32 devices in a mesh: row: 8 (over y, x, core), col: 4 (over z).
Axes of the slice: x: 2, y: 2, z: 4, core: 2. Of those that a mesh axis runs over, the one named last changes fastest.
Arguments:
- query_tokens: bfloat16 [128, 128, 768], P(('row', 'col')), may hold values from -5 to 5
- passage_tokens: bfloat16 [64, 512, 768], P(('row', 'col')), may hold values from -5 to 5
- query_lengths: int32 [128], P(('row', 'col')), may hold values from 102 to 128, as said below
- passage_lengths: int32 [64], P(('row', 'col')), may hold values from 409 to 512, as said below
- positives: int32 [128], P(('row', 'col')), may hold values from 0 to 63
- w_query: bfloat16 [768, 768], replicated, may hold values from -0.21875 to 0.21875
- w_key: bfloat16 [768, 768], replicated, may hold values from -0.21875 to 0.21875
- w_value: bfloat16 [768, 768], replicated, may hold values from -0.21875 to 0.21875
- w_attn_out: bfloat16 [768, 768], replicated, may hold values from -0.21875 to 0.21875
- w_inner: bfloat16 [768, 3072], replicated, may hold values from -0.21875 to 0.21875
- w_outer: bfloat16 [3072, 768], replicated, may hold values from -0.109375 to 0.109375
- bias_query: float32 [768], replicated, may hold values from -3 to 3
- bias_value: float32 [768], replicated, may hold values from -0.3 to 0.3
- bias_attn_out: float32 [768], replicated, may hold values from -0.6 to 0.6
- bias_inner: float32 [3072], replicated, may hold values from -0.6 to 0.6
- bias_outer: float32 [768], replicated, may hold values from -0.6 to 0.6
- gain_one: float32 [768], replicated, may hold values from 0.5 to 1.5
- shift_one: float32 [768], replicated, may hold values from -0.6 to 0.6
- gain_two: float32 [768], replicated, may hold values from 0.5 to 1.5
- shift_two: float32 [768], replicated, may hold values from -0.3 to 0.3
Outputs:
- loss: float32 [], replicated
- query_out: bfloat16 [128, 128, 768], P(('row', 'col'))
- passage_out: bfloat16 [64, 512, 768], P(('row', 'col'))
- query_grad: bfloat16 [128, 128, 768], P(('row', 'col'))
- passage_grad: bfloat16 [64, 512, 768], P(('row', 'col'))
- grad_w_query: float32 [768, 768], P('row')
- grad_w_key: float32 [768, 768], P('row')
- grad_w_value: float32 [768, 768], P('row')
- grad_w_attn_out: float32 [768, 768], P('row')
- grad_w_inner: float32 [768, 3072], P('row')
- grad_w_outer: float32 [3072, 768], P('row')
- grad_bias_query: float32 [768], P('row')
- grad_bias_value: float32 [768], P('row')
- grad_bias_attn_out: float32 [768], P('row')
- grad_bias_inner: float32 [3072], P('row')
- grad_bias_outer: float32 [768], P('row')
- grad_gain_one: float32 [768], P('row')
- grad_shift_one: float32 [768], P('row')
- grad_gain_two: float32 [768], P('row')
- grad_shift_two: float32 [768], P('row')
The draws below stay inside these ranges and needn't reach their ends.
Inputs may be any that keep to these rules, and one draw needn't show every extreme that they name: `query_lengths`: each query has 102 to 128 live tokens, the first ones of its slots; some query has exactly 128. `passage_lengths`: each passage has 409 to 512 live tokens, the first ones of its slots; some passage has exactly 512.
All inputs are finite; a program needn't handle non-finite values.
Results may differ from the reference program's by a relative error of at most 0.029.
Values may be sent and summed in bfloat16 or wider, within the bound.
No kernel may reach another device: no remote copies, remote signals or barrier semaphores. Data moves between devices by JAX's collectives and lax.ppermute only.
A program may use at most 256 MiB of HBM per device.

```python
import math
import jax
import jax.numpy as jnp
from jax import lax

HEADS = 12
D = 768
FF = 3072
Q_LEN = 128
P_LEN = 512
QUERIES = 128
PASSAGES = 64


link_share = 0.8


def ragged_lengths(key, amount, longest):
    key_len, key_pick = jax.random.split(key)
    values = jax.random.randint(key_len, (amount,), longest * 4 // 5, longest + 1, dtype=jnp.int32)
    chosen_slot = jax.random.randint(key_pick, (), 0, amount, dtype=jnp.int32)
    return jnp.where(jnp.arange(amount, dtype=jnp.int32) == chosen_slot, longest, values).astype(jnp.int32)


def draw_query_lengths(key, part):
    key = jax.random.fold_in(key, 11)
    return ragged_lengths(key, QUERIES, Q_LEN)


def draw_passage_lengths(key, part):
    key = jax.random.fold_in(key, 23)
    return ragged_lengths(key, PASSAGES, P_LEN)


def cluster_vectors(key):
    return jax.random.normal(jax.random.fold_in(key, 103), (PASSAGES, D), dtype=jnp.float32)


def positive_draw(key):
    key_values, key_first, key_second = jax.random.split(jax.random.fold_in(key, 101), 3)
    values = jax.random.randint(key_values, (QUERIES,), 0, PASSAGES, dtype=jnp.int32)
    first_slot = jax.random.randint(key_first, (), 0, QUERIES, dtype=jnp.int32)
    second_slot = (first_slot + 1 + jax.random.randint(key_second, (), 0, QUERIES - 1, dtype=jnp.int32)) % QUERIES
    slots = jnp.arange(QUERIES, dtype=jnp.int32)
    values = jnp.where(slots == first_slot, 0, values)
    values = jnp.where(slots == second_slot, PASSAGES - 1, values)
    return values.astype(jnp.int32)


def token_signs(key, amount, slots):
    key_share, key_bits = jax.random.split(key)
    share = jax.random.randint(key_share, (amount, 1), 20, 81, dtype=jnp.int32)
    bits = jax.random.randint(key_bits, (amount, slots), 0, 100, dtype=jnp.int32)
    return jnp.where(bits < share, 1.0, -1.0).astype(jnp.float32)


def clustered_tokens(key, directions, slots, noise_scale, cluster_scale):
    amount = directions.shape[0]
    key_noise, key_signs = jax.random.split(key)
    signs = token_signs(key_signs, amount, slots)
    noise = noise_scale * jax.random.normal(key_noise, (amount, slots, D), dtype=jnp.float32)
    mixed = noise + cluster_scale * signs[:, :, None] * directions[:, None, :]
    return jnp.clip(mixed, -5.0, 5.0).astype(jnp.bfloat16)


def draw_positives(key, part):
    return positive_draw(key)


def draw_query_tokens(key, part):
    shared_vectors = cluster_vectors(key)
    chosen = positive_draw(key)
    key = jax.random.fold_in(key, 31)
    key_fresh, key_tokens = jax.random.split(key)
    noise_scale = 0.5
    cluster_scale = 1.2
    fresh = jax.random.normal(key_fresh, (QUERIES, D), dtype=jnp.float32)
    linked = jnp.take(shared_vectors, chosen, axis=0)
    directions = link_share * linked + math.sqrt(1.0 - link_share * link_share) * fresh
    return clustered_tokens(key_tokens, directions, Q_LEN, noise_scale, cluster_scale)


def draw_passage_tokens(key, part):
    shared_vectors = cluster_vectors(key)
    key = jax.random.fold_in(key, 37)
    noise_scale = 0.5
    cluster_scale = 1.2
    return clustered_tokens(key, shared_vectors, P_LEN, noise_scale, cluster_scale)


def centred(stream_key, shape, deviation, limit, kind=jnp.bfloat16):
    entries = deviation * jax.random.normal(stream_key, shape, jnp.float32)
    return jnp.clip(entries, min=-limit, max=limit).astype(kind)


def setup_inputs(seed: int = 0) -> dict:
    key_list = jax.random.split(jax.random.key(seed), 21)
    return {
        "query_tokens": draw_query_tokens(jax.random.fold_in(key_list[20], 71), 0),
        "passage_tokens": draw_passage_tokens(jax.random.fold_in(key_list[20], 71), 0),
        "query_lengths": draw_query_lengths(jax.random.fold_in(key_list[20], 71), 0),
        "passage_lengths": draw_passage_lengths(jax.random.fold_in(key_list[20], 71), 0),
        "positives": draw_positives(jax.random.fold_in(key_list[20], 71), 0),
        "w_query": centred(key_list[5], (D, D), D ** -0.5, 0.21875),
        "w_key": centred(key_list[6], (D, D), D ** -0.5, 0.21875),
        "w_value": centred(key_list[7], (D, D), D ** -0.5, 0.21875),
        "w_attn_out": centred(key_list[8], (D, D), D ** -0.5, 0.21875),
        "w_inner": centred(key_list[9], (D, FF), D ** -0.5, 0.21875),
        "w_outer": centred(key_list[10], (FF, D), FF ** -0.5, 0.109375),
        "bias_query": centred(key_list[11], (D,), 0.5, 3.0, jnp.float32),
        "bias_value": centred(key_list[12], (D,), 0.05, 0.3, jnp.float32),
        "bias_attn_out": centred(key_list[13], (D,), 0.1, 0.6, jnp.float32),
        "bias_inner": centred(key_list[14], (FF,), 0.1, 0.6, jnp.float32),
        "bias_outer": centred(key_list[15], (D,), 0.1, 0.6, jnp.float32),
        "gain_one": jnp.clip(1.0 + 0.1 * jax.random.normal(key_list[16], (D,), jnp.float32), 0.5, 1.5),
        "shift_one": centred(key_list[17], (D,), 0.1, 0.6, jnp.float32),
        "gain_two": jnp.clip(1.0 + 0.1 * jax.random.normal(key_list[18], (D,), jnp.float32), 0.5, 1.5),
        "shift_two": centred(key_list[19], (D,), 0.05, 0.3, jnp.float32),
    }


@jax.custom_vjp
def low(v):
    return lax.optimization_barrier(v.astype(jnp.bfloat16)).astype(jnp.float32)

@jax.custom_vjp
def low_back(v):
    return v

def low_keep(v):
    return (low(v), None)

def low_pass(kept, grad):
    return (grad,)

def back_keep(v):
    return (v, None)

def back_low(kept, grad):
    return (low(grad),)
low.defvjp(low_keep, low_pass)
low_back.defvjp(back_keep, back_low)
HIGH = lax.Precision.HIGHEST
EPS_NORM = 1e-12
EPS_POOL = 1e-06
SCALE_LOSS = 128.0
INV_TEMP = 100.0

def matmul(left, right):
    return jnp.dot(left, right, precision=HIGH)

def normalize(hidden, gain, shift):
    center = hidden - lax.optimization_barrier(jnp.mean(hidden, -1, keepdims=True))
    spread = lax.optimization_barrier(jnp.mean(center * center, -1, keepdims=True))
    return center * lax.rsqrt(spread + EPS_NORM) * gain + shift

def sequence_layer(params, tokens, length):
    w_query, w_key, w_value, w_attn_out, w_inner, w_outer, bias_query, bias_value, bias_attn_out, bias_inner, bias_outer, gain_one, shift_one, gain_two, shift_two = params
    seq_len, model_width = tokens.shape
    head_dim = model_width // HEADS
    query_rows = low_back(low(matmul(tokens, w_query) + bias_query)).reshape(seq_len, HEADS, head_dim)
    key_rows = low_back(low(matmul(tokens, w_key))).reshape(seq_len, HEADS, head_dim)
    value_rows = low_back(low(matmul(tokens, w_value) + bias_value)).reshape(seq_len, HEADS, head_dim)
    raw_scores = jnp.einsum('qhd,khd->hqk', query_rows, key_rows, precision=HIGH)
    scores = low_back(raw_scores * head_dim ** (-0.5))
    positions = jnp.arange(seq_len, dtype=jnp.int32)
    live_keys = positions < length
    masked = jnp.where(live_keys[None, None, :], scores, -1e+30)
    probs = low(jax.nn.softmax(masked, axis=-1))
    context = jnp.einsum('hqk,khd->qhd', probs, value_rows, precision=HIGH).reshape(seq_len, model_width)
    context = low_back(low(context))
    attn_out = low_back(matmul(context, w_attn_out) + bias_attn_out)
    normed_one = normalize(tokens + attn_out, gain_one, shift_one)
    inner_pre = low_back(matmul(low(normed_one), w_inner) + bias_inner)
    active = low(jax.nn.gelu(inner_pre, approximate=False))
    ffn_out = low_back(matmul(active, w_outer) + bias_outer)
    normed_two = normalize(normed_one + ffn_out, gain_two, shift_two)
    live_rows = live_keys.astype(normed_two.dtype)
    pooled = lax.optimization_barrier(jnp.sum(normed_two * live_rows[:, None], 0)) / length.astype(normed_two.dtype)
    embedding = pooled * lax.rsqrt(jnp.sum(pooled * pooled) + EPS_POOL)
    return (normed_two, embedding)

def forward(params, queries, passages, query_lengths, passage_lengths, positives):
    step_fn = jax.checkpoint(lambda item: sequence_layer(params, item[0], item[1]))
    query_out, query_embed = lax.map(step_fn, (queries, query_lengths))
    passage_out, passage_embed = lax.map(step_fn, (passages, passage_lengths))
    raw_scores = jnp.dot(low(query_embed), low(passage_embed).T, precision=HIGH)
    scores = low_back(raw_scores) * INV_TEMP
    totals = jax.nn.logsumexp(scores, axis=1)
    columns = jnp.arange(scores.shape[1], dtype=jnp.int32)
    target = (columns[None, :] == positives[:, None]).astype(scores.dtype)
    picked = lax.optimization_barrier(jnp.sum(scores * target, 1))
    losses = totals - picked
    return (SCALE_LOSS * jnp.sum(losses), (query_out, passage_out, jnp.mean(losses)))

def reference(query_tokens, passage_tokens, query_lengths, passage_lengths, positives, w_query, w_key, w_value, w_attn_out, w_inner, w_outer, bias_query, bias_value, bias_attn_out, bias_inner, bias_outer, gain_one, shift_one, gain_two, shift_two):
    params = tuple((item.astype(jnp.float32) for item in (w_query, w_key, w_value, w_attn_out, w_inner, w_outer, bias_query, bias_value, bias_attn_out, bias_inner, bias_outer, gain_one, shift_one, gain_two, shift_two)))

    def wrapped(prm, queries, passages):
        return forward(prm, queries, passages, query_lengths, passage_lengths, positives)
    objective, pull_back, aux = jax.vjp(wrapped, params, query_tokens.astype(jnp.float32), passage_tokens.astype(jnp.float32), has_aux=True)
    grads, query_grad, passage_grad = pull_back(jnp.ones_like(objective))
    query_out, passage_out, loss = aux
    return (loss, query_out.astype(jnp.bfloat16), passage_out.astype(jnp.bfloat16), query_grad.astype(jnp.bfloat16), passage_grad.astype(jnp.bfloat16), grads[0], grads[1], grads[2], grads[3], grads[4], grads[5], grads[6], grads[7], grads[8], grads[9], grads[10], grads[11], grads[12], grads[13], grads[14])
```

```python
from functools import partial

import jax
import jax.numpy as jnp
from jax import lax
from jax.experimental import pallas as pl
from jax.experimental.pallas import tpu as pltpu
from jax.sharding import PartitionSpec as P

HEADS = 12
EPS_NORM = 1e-12
EPS_POOL = 1e-06
SCALE_LOSS = 128.0
INV_TEMP = 100.0
TILE = 256
SLOTS = 8
VMEM = 60 * 1024 * 1024
LOW = jnp.bfloat16
F32 = jnp.float32


def mm(left, right):
    return lax.dot_general(left, right, (((1,), (0,)), ((), ())), preferred_element_type=F32)


def mm_nt(left, right):
    return lax.dot_general(left, right, (((1,), (1,)), ((), ())), preferred_element_type=F32)


def norm_parts(hidden):
    center = hidden - jnp.mean(hidden, -1, keepdims=True)
    spread = jnp.mean(center * center, -1, keepdims=True)
    scale = lax.rsqrt(spread + EPS_NORM)
    return center * scale, scale


def gelu_parts(u):
    square = u * u
    q = 1.4250060785476853e-06
    for factor in (-3.669345091379551e-05, -8.782652731110375e-05, 0.03639228618131223, 0.7978697123041883):
        q = q * square + factor
    share = 0.5 + 0.5 * jnp.tanh(u * q)
    bell = jnp.exp(-0.5 * square)
    return u * share, share + (0.3989422804014327 * u) * bell


def vec(ref, cols=slice(None)):
    return ref[cols].reshape(1, -1)


def rows_of(step, size):
    return pl.ds(pl.multiple_of(step * size, size), size)


def part_owner(part, q_dev, q_len, p_len, qlen_ref, plen_ref):
    per = p_len // q_len
    beyond = jnp.maximum(part - q_dev, 0)
    is_query = part < q_dev
    slot = jnp.where(is_query, part, q_dev + beyond // per)
    length = jnp.where(is_query, qlen_ref[jnp.where(is_query, part, 0)], plen_ref[beyond // per])
    first = jnp.where(is_query, 0, beyond % per * q_len)
    return slot, length, first


def live_rows(first, length, size):
    return (first + lax.broadcasted_iota(jnp.int32, (size, 1), 0)) < length


def sure_rows(size):
    return size * 4 // 5 // 16 * 16


def half_only(pair_t, which):
    half = pair_t.shape[0] // 2
    zeros = jnp.zeros((half, pair_t.shape[1]), pair_t.dtype)
    if which == 0:
        return jnp.concatenate([pair_t[:half], zeros], 0)
    return jnp.concatenate([zeros, pair_t[half:]], 0)


def staged(count, *stages):
    for step in range(count + len(stages) - 1):
        for late, stage in enumerate(stages):
            if 0 <= step - late < count:
                stage(step - late)


def fetch(source, target, sems, index):
    return pltpu.make_async_copy(source, target, sems.at[index])


def attend_kernel(
    dims, qlen_ref, plen_ref, xq_ref, xp_ref, wq_ref, wk_ref, wv_ref, bq_ref, bv_ref,
    q_ref, k_ref, v_ref, ctx_t_ref, lse_ref,
):
    q_dev, q_len, rows_all, width = dims
    block = pl.program_id(0)
    head_dim = width // HEADS
    x = jnp.where(block == 0, xq_ref[...], xp_ref[...])
    q = ((mm(x, wq_ref[...]) + vec(bq_ref)) * head_dim**-0.5).astype(LOW)
    k = mm(x, wk_ref[...]).astype(LOW)
    v = (mm(x, wv_ref[...]) + vec(bv_ref)).astype(LOW)
    q_ref[...] = q
    k_ref[...] = k
    v_ref[...] = v
    q_t, v_t = q.T, v.T

    def attend(size, starts, lengths):
        items = [(start, length, head) for head in range(HEADS) for start, length in zip(starts, lengths)]
        scores, weights = {}, {}

        def compare(i):
            start, length, head = items[i]
            cols = slice(head // 2 * 2 * head_dim, (head // 2 + 1) * 2 * head_dim)
            here = slice(start, start + size)
            scores[i] = mm(k[here, cols], half_only(q_t[cols, here], head % 2))

        def weigh(i):
            start, length, head = items[i]
            edge = sure_rows(size)
            early, late = scores[i][:edge], scores.pop(i)[edge:]
            late = jnp.where(live_rows(edge, length, size - edge), late, -1e30)
            top = jnp.maximum(jnp.max(early, 0, keepdims=True), jnp.max(late, 0, keepdims=True))
            weights[i] = top, jnp.concatenate([jnp.exp(early - top).astype(LOW), jnp.exp(late - top).astype(LOW)], 0)

        def combine(i):
            start, length, head = items[i]
            here, rows = slice(start, start + size), slice(head * head_dim, (head + 1) * head_dim)
            top, weight = weights.pop(i)
            values = jnp.concatenate([v_t[rows, here], jnp.ones((16, size), LOW)], 0)
            result = mm(values, weight)
            total = result[head_dim : head_dim + 1]
            lse_ref[0, head // 2, head % 2 : head % 2 + 1, here] = top + jnp.log(total)
            ctx_t_ref[rows, here] = (result[:head_dim] * (1.0 / total)).astype(LOW)

        staged(len(items), compare, weigh, combine)

    @pl.when(block == 0)
    def _():
        attend(q_len, [s * q_len for s in range(q_dev)], [qlen_ref[s] for s in range(q_dev)])

    @pl.when(block > 0)
    def _():
        attend(rows_all, [0], [plen_ref[jnp.maximum(block - 1, 0)]])


def dense_kernel(
    dims, qlen_ref, plen_ref, pos_ref, xq_ref, xp_ref, ctx_t_ref, wo_hbm, wi_hbm, wf_hbm,
    bo_ref, bi_ref, bf_ref, g1_ref, s1_ref, g2_ref, s2_ref,
    h1_ref, y1_ref, act_ref, dg_ref, h2_ref, yq_ref, yp_ref, pool_ref, pay_ref,
    wo_ref, wi_ref, wf_ref, sems,
):
    q_dev, q_len, p_len, width, inner = dims
    block = pl.program_id(0)
    rows_all = xq_ref.shape[0]
    query_blocks = q_dev * q_len // rows_all
    copies = [
        fetch(source, target, sems, index)
        for index, (source, target) in enumerate([(wo_hbm, wo_ref), (wi_hbm, wi_ref), (wf_hbm, wf_ref)])
    ]

    @pl.when(block == 0)
    def _():
        for copy in copies:
            copy.start()
        pool_ref[...] = jnp.zeros_like(pool_ref)
        copies[0].wait()

    x = jnp.where(block < query_blocks, xq_ref[...], xp_ref[...])
    hidden = x.astype(F32) + (mm(ctx_t_ref[...].T, wo_ref[...]) + vec(bo_ref))
    h1_ref[...] = hidden.astype(LOW)
    y1 = norm_parts(hidden)[0] * vec(g1_ref) + vec(s1_ref)
    y1_low = y1.astype(LOW)
    y1_ref[...] = y1_low

    @pl.when(block == 0)
    def _():
        copies[1].wait()
        copies[2].wait()

    group = width // TILE
    raw, made = {}, {}
    sums = [y1[:, n * TILE : (n + 1) * TILE] + vec(bf_ref, slice(n * TILE, (n + 1) * TILE)) for n in range(group)]

    def expand(i):
        cols = slice(i * TILE, (i + 1) * TILE)
        raw[i] = mm(y1_low, wi_ref[:, cols]) + vec(bi_ref, cols)

    def activate(i):
        cols = slice(i * TILE, (i + 1) * TILE)
        act, slope = gelu_parts(raw.pop(i))
        made[i] = act.astype(LOW)
        act_ref[:, cols] = made[i]
        dg_ref[:, cols] = slope.astype(LOW)

    def contract(i):
        first, n = i // group * group, i % group
        left = jnp.concatenate([made[first + j] for j in range(group)], 1)
        cols = slice(n * TILE, (n + 1) * TILE)
        sums[n] = sums[n] + mm(left, wf_ref[first * TILE : (first + group) * TILE, cols])

    late = [lambda i: None] * (group - 1)
    staged(inner // TILE, expand, activate, *late, contract)

    total = jnp.concatenate(sums, 1)
    h2_ref[...] = total.astype(LOW)
    y2 = norm_parts(total)[0] * vec(g2_ref) + vec(s2_ref)
    for part in range(rows_all // q_len):
        number = block * (rows_all // q_len) + part
        slot, length, first = part_owner(number, q_dev, q_len, p_len, qlen_ref, plen_ref)
        piece = y2[part * q_len : (part + 1) * q_len]
        summed = jnp.sum(jnp.where(live_rows(first, length, q_len), piece, 0.0), 0, keepdims=True)
        in_slot = lax.broadcasted_iota(jnp.int32, (SLOTS, 1), 0) == slot
        pool_ref[...] += jnp.where(in_slot, summed / length.astype(F32), 0.0)

    @pl.when(block < query_blocks)
    def _():
        yq_ref[...] = y2.astype(LOW)

    @pl.when(block >= query_blocks)
    def _():
        yp_ref[...] = y2.astype(LOW)

    @pl.when(block == pl.num_programs(0) - 1)
    def _():
        pooled = pool_ref[...]
        emb = pooled * lax.rsqrt(jnp.sum(pooled * pooled, -1, keepdims=True) + EPS_POOL)
        pay_ref[:, :width] = emb.astype(LOW)
        row = lax.broadcasted_iota(jnp.int32, (SLOTS, 128), 0)
        col = lax.broadcasted_iota(jnp.int32, (SLOTS, 128), 1)
        place = jnp.zeros((SLOTS, 128), jnp.int32)
        for j in range(q_dev):
            high = pos_ref[j] // 128
            low = pos_ref[j] - high * 128
            place = jnp.where(row == j, jnp.where(col == 0, high, jnp.where(col == 1, low, 0)), place)
        pay_ref[:, width:] = place.astype(F32).astype(LOW)


def loss_kernel(
    dims, me_ref, qlen_ref, plen_ref, own_ref, all_ref, pool_ref, loss_ref, gvec_ref
):
    q_dev, p_dev, width, col_count = dims
    count = all_ref.shape[0]
    every = all_ref[:, :width]
    own = own_ref[:, :width]

    def passage_mask(index):
        spot, place = index % SLOTS, index // SLOTS
        per_core = count // SLOTS // 2
        core, rest = place // per_core, place % per_core
        device = (rest // col_count * 2 + core) * col_count + rest % col_count
        return (spot >= q_dev) & (spot < q_dev + p_dev), device * p_dev + spot - q_dev

    scores = mm_nt(own, every) * INV_TEMP
    valid, ident = passage_mask(lax.broadcasted_iota(jnp.int32, (SLOTS, count), 1))
    scores = jnp.where(valid, scores, -1e30)
    top = jnp.max(scores, -1, keepdims=True)
    totals = top + jnp.log(jnp.sum(jnp.exp(scores - top), -1, keepdims=True))
    marks = own_ref[:, width:].astype(F32)
    wanted = marks[:, 0:1] * 128.0 + marks[:, 1:2]
    target = (valid & (ident.astype(F32) == wanted)).astype(F32)
    raw = (INV_TEMP * (SCALE_LOSS * (jnp.exp(scores - totals) - target))).astype(LOW)
    grad_q = mm(raw, every)

    picker_col = lax.broadcasted_iota(jnp.int32, (SLOTS, 128), 1)
    picker = jnp.where(picker_col == 0, 128.0, jnp.where(picker_col == 1, 1.0, 0.0)).astype(LOW)
    own_row = lax.broadcasted_iota(jnp.int32, (SLOTS, TILE), 0)
    own_valid = (own_row >= q_dev) & (own_row < q_dev + p_dev)
    own_ident = (me_ref[0] * p_dev + own_row - q_dev).astype(F32)

    def body(step, carry):
        total_loss, grad_p = carry
        rows = rows_of(step, TILE)
        some = all_ref[rows, :width]
        place = mm_nt(picker, all_ref[rows, width:])[0:1]
        table = mm_nt(every, some) * INV_TEMP
        ok, names = passage_mask(lax.broadcasted_iota(jnp.int32, (count, TILE), 0))
        picked = jnp.sum(jnp.where(ok & (names.astype(F32) == place), table, 0.0), 0, keepdims=True)
        table = jnp.where(ok, table, -1e30)
        high = jnp.max(table, 0, keepdims=True)
        lse = high + jnp.log(jnp.sum(jnp.exp(table - high), 0, keepdims=True))
        is_query = lax.broadcasted_iota(jnp.int32, (1, TILE), 1) % SLOTS < q_dev
        losses = jnp.where(is_query, lse - picked, 0.0)
        mine = mm_nt(own, some) * INV_TEMP
        hit = (own_ident == place).astype(F32)
        grads = INV_TEMP * (SCALE_LOSS * (jnp.exp(mine - lse) - hit))
        grads = jnp.where(own_valid & is_query, grads, 0.0).astype(LOW)
        return total_loss + jnp.sum(losses, 1, keepdims=True), grad_p + mm(grads, some)

    start = (jnp.zeros((1, 1), F32), jnp.zeros((SLOTS, width), F32))
    total_loss, grad_p = lax.fori_loop(0, count // TILE, body, start)
    loss_ref[...] = jnp.broadcast_to(total_loss / float(count // SLOTS * q_dev), loss_ref.shape)

    slot = lax.broadcasted_iota(jnp.int32, (SLOTS, 1), 0)
    grad = jnp.where(slot < q_dev, grad_q, grad_p)
    pooled = pool_ref[...]
    r = lax.rsqrt(jnp.sum(pooled * pooled, -1, keepdims=True) + EPS_POOL)
    inside = jnp.sum(pooled * grad, -1, keepdims=True)
    length = jnp.ones((SLOTS, 1), F32)
    for j in range(q_dev):
        length = jnp.where(slot == j, qlen_ref[j].astype(F32), length)
    for j in range(p_dev):
        length = jnp.where(slot == q_dev + j, plen_ref[j].astype(F32), length)
    gvec_ref[...] = (r * grad - r * r * r * inside * pooled) / length


def norm_two_kernel(dims, qlen_ref, plen_ref, gvec_ref, h2_ref, g2_ref, gf_ref, gf_t_ref, stat_ref):
    q_dev, q_len, rows_all, width = dims
    block = pl.program_id(0)

    @pl.when(block == 0)
    def _():
        stat_ref[...] = jnp.zeros_like(stat_ref)

    def body(part, carry):
        rows = rows_of(part, q_len)
        number = block * (rows_all // q_len) + part
        slot, length, first = part_owner(number, q_dev, q_len, rows_all, qlen_ref, plen_ref)
        in_slot = lax.broadcasted_iota(jnp.int32, (SLOTS, 1), 0) == slot
        grad_y = jnp.sum(jnp.where(in_slot, gvec_ref[...], 0.0), 0, keepdims=True)
        live = live_rows(first, length, q_len)
        n2, r2 = norm_parts(h2_ref[rows, :].astype(F32))
        g = grad_y * vec(g2_ref)
        grad = r2 * (g - jnp.mean(g, -1, keepdims=True) - n2 * jnp.mean(g * n2, -1, keepdims=True))
        grad = jnp.where(live, grad, 0.0)
        low = grad.astype(LOW)
        gf_ref[rows, :] = low
        gf_t_ref[:, rows] = low.T
        stat_ref[0:1, :] += grad_y * jnp.sum(jnp.where(live, n2, 0.0), 0, keepdims=True)
        stat_ref[1:2, :] += grad_y * jnp.sum(live.astype(F32), 0, keepdims=True)
        stat_ref[2:3, :] += jnp.sum(low.astype(F32), 0, keepdims=True)
        return carry

    lax.fori_loop(0, rows_all // q_len, body, 0)


def dense_back_kernel(
    dims, gf_ref, dg_ref, h1_ref, wf_hbm, wi_hbm, wo_hbm, g1_ref,
    gu_ref, gh1_ref, ga_ref, gc_ref, stat_ref, bi_ref,
    wf_ref, wi_ref, wo_ref, sems,
):
    rows_all, width, inner = dims
    block = pl.program_id(0)
    chunk = TILE
    group = width // chunk
    copies = [
        fetch(wf_hbm.at[pl.ds(0, width), :], wf_ref.at[pl.ds(0, width), :], sems, 0),
        fetch(wi_hbm.at[:, pl.ds(0, width)], wi_ref.at[:, pl.ds(0, width)], sems, 1),
        fetch(wf_hbm.at[pl.ds(width, inner - width), :], wf_ref.at[pl.ds(width, inner - width), :], sems, 2),
        fetch(wi_hbm.at[:, pl.ds(width, inner - width)], wi_ref.at[:, pl.ds(width, inner - width)], sems, 3),
        fetch(wo_hbm, wo_ref, sems, 4),
    ]

    @pl.when(block == 0)
    def _():
        for copy in copies:
            copy.start()
        stat_ref[...] = jnp.zeros_like(stat_ref)
        bi_ref[...] = jnp.zeros_like(bi_ref)
        copies[0].wait()
        copies[1].wait()

    gf = gf_ref[...]
    raw, made = {}, {}
    sums = [gf[:, n * chunk : (n + 1) * chunk].astype(F32) for n in range(group)]
    biases = []

    def spread(i):
        raw[i] = mm_nt(gf, wf_ref[i * chunk : (i + 1) * chunk, :])

    def slope(i):
        cols = slice(i * chunk, (i + 1) * chunk)
        made[i] = (raw.pop(i) * dg_ref[:, cols].astype(F32)).astype(LOW)
        gu_ref[:, cols] = made[i]
        biases.append(jnp.sum(made[i].astype(F32), 0, keepdims=True))

    def gather(i):
        first, n = i // group * group, i % group
        left = jnp.concatenate([made[first + j] for j in range(group)], 1)
        cols = slice(n * chunk, (n + 1) * chunk)
        sums[n] = sums[n] + mm_nt(left, wi_ref[cols, first * chunk : (first + group) * chunk])

    staged(group, spread, slope)

    @pl.when(block == 0)
    def _():
        for copy in copies[2:]:
            copy.wait()

    count = inner // chunk
    staged(
        count,
        lambda i: spread(i + group) if i + group < count else None,
        lambda i: slope(i + group) if i + group < count else None,
        gather,
    )
    bi_ref[0:1, :] += jnp.concatenate(biases, 1)
    total = jnp.concatenate(sums, 1)
    n1, r1 = norm_parts(h1_ref[...].astype(F32))
    stat_ref[0:1, :] += jnp.sum(total * n1, 0, keepdims=True)
    stat_ref[1:2, :] += jnp.sum(total, 0, keepdims=True)
    g = total * vec(g1_ref)
    grad = r1 * (g - jnp.mean(g, -1, keepdims=True) - n1 * jnp.mean(g * n1, -1, keepdims=True))
    gh1_ref[...] = grad
    low = grad.astype(LOW)
    ga_ref[...] = low
    stat_ref[2:3, :] += jnp.sum(low.astype(F32), 0, keepdims=True)
    gc_ref[...] = mm_nt(low, wo_ref[...]).astype(LOW)


def attend_back_kernel(
    dims, qlen_ref, plen_ref, q_ref, k_ref, v_ref, ctx_t_ref, lse_ref, gc_ref, out_ref, stat_ref
):
    q_dev, q_len, rows_all, head_dim = dims
    block = pl.program_id(0)
    pair_dim = 2 * head_dim
    width = q_ref.shape[1]
    pairs = width // pair_dim

    @pl.when(block == 0)
    def _():
        stat_ref[...] = jnp.zeros_like(stat_ref)

    def attend(size, starts, lengths):
        lane = lax.broadcasted_iota(jnp.int32, (size, pair_dim), 1)
        items = [(s, p, which) for s in range(len(starts)) for p in range(pairs) for which in range(2)]
        held, raw, made = {}, {}, {}

        def pair_of(s, p):
            if (s, p) not in held:
                here, cols = slice(starts[s], starts[s] + size), slice(p * pair_dim, (p + 1) * pair_dim)
                q, k, v, gc = q_ref[here, cols], k_ref[here, cols], v_ref[here, cols], gc_ref[here, cols]
                held[s, p] = here, cols, q, k, v, gc, q.T, k.T, gc.T
            return held[s, p]

        def compare(i):
            s, p, which = items[i]
            here, cols, q, k, v, gc, q_t, k_t, gc_t = pair_of(s, p)
            raw[i] = mm(k, half_only(q_t, which)), mm(v, half_only(gc_t, which))

        def weigh(i):
            s, p, which = items[i]
            here, cols, q, k, v, gc, q_t, k_t, gc_t = pair_of(s, p)
            head = slice((p * 2 + which) * head_dim, (p * 2 + which + 1) * head_dim)
            scores, grad_p = raw.pop(i)
            lse = lse_ref[0, p, which : which + 1, here]
            edge = sure_rows(size)
            late = jnp.where(live_rows(edge, lengths[s], size - edge), scores[edge:], -1e30)
            probs = jnp.concatenate([jnp.exp(scores[:edge] - lse), jnp.exp(late - lse)], 0)
            half = slice(which * head_dim, (which + 1) * head_dim)
            delta = jnp.sum(gc_t[half].astype(F32) * ctx_t_ref[head, here].astype(F32), 0, keepdims=True)
            made[i] = probs.astype(LOW), (probs * (grad_p - delta)).astype(LOW)

        def combine(i):
            s, p, which = items[i]
            here, cols, q, k, v, gc, q_t, k_t, gc_t = pair_of(s, p)
            mine = (lane >= head_dim) if which else (lane < head_dim)
            zero = jnp.zeros_like(q)
            probs, grad_s = made.pop(i)
            add_v = mm(probs, jnp.where(mine, gc, zero))
            add_k = mm(grad_s, jnp.where(mine, q, zero))
            add_q = mm(k_t[which * head_dim : (which + 1) * head_dim], grad_s)
            if which == 0:
                made[s, p] = add_v, add_k, add_q
                return
            old_v, old_k, old_q = made.pop((s, p))
            grad_q = (jnp.concatenate([old_q, add_q], 0).T * head_dim**-0.5).astype(LOW)
            grad_v = (old_v + add_v).astype(LOW)
            out_ref[here, cols] = grad_q
            out_ref[here, width + cols.start : width + cols.stop] = (old_k + add_k).astype(LOW)
            out_ref[here, 2 * width + cols.start : 2 * width + cols.stop] = grad_v
            stat_ref[0:1, cols] += jnp.sum(grad_q.astype(F32), 0, keepdims=True)
            stat_ref[1:2, cols] += jnp.sum(grad_v.astype(F32), 0, keepdims=True)

        staged(len(items), compare, weigh, combine)

    @pl.when(block == 0)
    def _():
        attend(q_len, [s * q_len for s in range(q_dev)], [qlen_ref[s] for s in range(q_dev)])

    @pl.when(block > 0)
    def _():
        attend(rows_all, [0], [plen_ref[jnp.maximum(block - 1, 0)]])


def input_grad_kernel(groups, *refs):
    grads, (gh1_ref, wq_ref, wk_ref, wv_ref, gq_ref, gp_ref) = refs[: len(groups)], refs[len(groups) :]
    block = pl.program_id(0)
    total = gh1_ref[...]
    for grad_ref, (start, wide) in zip(grads, groups):
        for number, w_ref in enumerate((wq_ref, wk_ref, wv_ref)):
            total = total + mm_nt(grad_ref[:, number * wide : (number + 1) * wide], w_ref[:, start : start + wide])
    low = total.astype(LOW)

    @pl.when(block == 0)
    def _():
        gq_ref[...] = low

    @pl.when(block > 0)
    def _():
        gp_ref[...] = low


def weight_grad_kernel(shards, by_row, tile, core_ref, left_ref, right_ref, *refs):
    *extra, send_ref, keep_ref = refs
    high, wide = left_ref.shape[0], right_ref.shape[1]
    result = [
        [
            mm(left_ref[row : row + tile[0], :], right_ref[:, col : col + tile[1]]).astype(LOW)
            for col in range(0, wide, tile[1])
        ]
        for row in range(0, high, tile[0])
    ]
    result = jnp.concatenate([jnp.concatenate(items, 1) for items in result], 0)
    count = shards if by_row else send_ref.shape[0] * 2
    size = result.shape[0 if by_row else 1] // count
    tail = [None] * count
    if extra:
        tail = small_rows(extra, count, result.shape[1])

    def store(even, odd):
        for shard in range(count):
            spot = slice(shard * size, (shard + 1) * size)
            piece = result[spot, :] if by_row else result[:, spot]
            target = odd if shard % 2 else even
            if tail[shard] is None:
                target[shard // 2] = piece
            else:
                target[shard // 2, :size] = piece
                target[shard // 2, size:] = tail[shard]

    @pl.when(core_ref[0] == 0)
    def _():
        store(keep_ref, send_ref)

    @pl.when(core_ref[0] == 1)
    def _():
        store(send_ref, keep_ref)


def small_rows(refs, count, wide):
    two, one, inner, *attn = [ref[...] for ref in refs]
    eight = jnp.concatenate(
        [jnp.concatenate([item[0:2] for item in attn], 1), one[2:3], two[2:3], one[0:2], two[0:2]], 0
    )
    inner = inner[0:1]
    short, long = eight.shape[1] // count, inner.shape[1] // count
    rows = []
    for shard in range(count):
        top = eight[:, shard * short : (shard + 1) * short]
        low = inner[:, shard * long : (shard + 1) * long]
        top = jnp.concatenate([top, jnp.zeros((8, wide - short), F32)], 1)
        low = jnp.concatenate([low, jnp.zeros((1, wide - long), F32)], 1)
        rows.append(jnp.concatenate([top, low, jnp.zeros((7, wide), F32)], 0).astype(LOW))
    return rows


def turn_kernel(part_ref, out_ref):
    out_ref[...] = part_ref[...].astype(F32).T


def turn_low_kernel(*refs):
    *inputs, out_ref = refs
    if len(inputs) == 1:
        out_ref[...] = inputs[0][...].T
        return

    @pl.when(pl.program_id(0) == 0)
    def _():
        out_ref[...] = inputs[0][...].T

    @pl.when(pl.program_id(0) > 0)
    def _():
        out_ref[...] = inputs[1][...].T


def const_spec(shape):
    return pl.BlockSpec(shape, lambda i: (0,) * len(shape), pipeline_mode=pl.Buffered(1))


def call(body, operands, in_specs, outs, grid, room, deps=(), old=(), name=None, scratch=(), us=10):
    count, extra = len(operands), len(old)
    if deps:
        tied = min(range(count), key=lambda i: operands[i].size)
        operands = list(operands)
        operands[tied] = lax.optimization_barrier((operands[tied], *deps))[0]

    def kernel(*refs):
        body(*refs[:count], *refs[count + extra :])

    return pl.pallas_call(
        kernel,
        grid=grid,
        in_specs=list(in_specs) + [pl.BlockSpec(memory_space=pl.ANY)] * extra,
        out_specs=[spec for spec, _ in outs],
        out_shape=[kind for _, kind in outs],
        scratch_shapes=scratch,
        input_output_aliases={count + i: i for i in range(extra)},
        compiler_params=pltpu.CompilerParams(vmem_limit_bytes=room * 1024 * 1024),
        cost_estimate=pl.CostEstimate(flops=int(us * 1.15e7), bytes_accessed=0, transcendentals=0),
        name=name,
    )(*operands, *old)


def weight_grad(left_t, right, by_row, row_count, core, deps=(), extra=(), old=(), room=None, tile=(256, 256)):
    height, depth = left_t.shape
    wide = right.shape[1]
    cut = (height if by_row else wide) // row_count
    block = 768
    per_block = row_count if by_row else block // cut if block % cut == 0 else 0
    if wide % block or cut % (16 if by_row else 128) or per_block % 2:
        whole = jnp.dot(left_t, right, preferred_element_type=F32).astype(LOW)
        if by_row:
            whole = whole.reshape(row_count // 2, 2, cut, wide)
        else:
            whole = whole.reshape(height, row_count // 2, 2, cut).transpose(1, 2, 0, 3)
        if extra:

            def rows_kernel(*refs):
                for shard, item in enumerate(small_rows(refs[:-1], row_count, wide)):
                    refs[-1][shard] = item

            rows = pl.pallas_call(
                rows_kernel,
                out_shape=jax.ShapeDtypeStruct((row_count, 16, wide), LOW),
                compiler_params=pltpu.CompilerParams(vmem_limit_bytes=VMEM),
            )(*extra)
            whole = jnp.concatenate([whole, rows.reshape(row_count // 2, 2, 16, wide)], 2)
        result = [lax.dynamic_index_in_dim(whole, side, 1, keepdims=False) for side in (1 - core, core)]
        return [jnp.concatenate([a, b], 2) for a, b in zip(old, result)] if old else result
    if by_row:
        rows = cut + (16 if extra else 0)
        shape = (row_count // 2, rows, room or wide)
        after = (room - wide) // block if old else 0
        spec = pl.BlockSpec((row_count // 2, rows, block), lambda i: (0, 0, i + after))
    else:
        shape = (row_count // 2, height, cut)
        spec = pl.BlockSpec((per_block // 2, height, cut), lambda i: (i, 0, 0))
    return call(
        partial(weight_grad_kernel, row_count, by_row, tile),
        (core.reshape(1), left_t, right, *extra),
        [
            pl.BlockSpec(memory_space=pltpu.SMEM),
            const_spec((height, depth)),
            pl.BlockSpec((depth, block), lambda i: (0, i)),
        ]
        + [const_spec(item.shape) for item in extra],
        [(spec, jax.ShapeDtypeStruct(shape, LOW))] * 2,
        (wide // block,),
        56,
        deps,
        old,
        name="weight_grad",
        us=height * depth * wide * 3.3e-9,
    )


class Flow:
    def __init__(self, sent, kept, line=False):
        bits = lax.axis_size("row").bit_length() - 1
        self.order = [(0,)] + [tuple(range(i, min(i + 2, bits))) for i in range(1, bits, 2)]
        self.left = list(range(bits - 1, 0, -1))
        count = lax.axis_size("col")
        self.line = [(None, [(i, i ^ (1 << bit)) for i in range(count)]) for bit in range(count.bit_length() - 1)]
        if line:
            half = count // 2
            self.line = [(None, [(i, i + 1), (count - 1 - i, count - 2 - i)]) for i in range(half - 1)]
            self.line += [(None, [(half - 1, half), (half, half - 1)])]
            self.line += [
                ((i, count - 1 - i), [(i + 1, i), (count - 2 - i, count - 1 - i)])
                for i in range(half - 2, -1, -1)
            ]
        self.sent, self.kept, self.got = [sent], kept, None

    def shard(self, terms, bits, mask):
        here = lax.axis_index("row")
        order = [self.left.index(bit) for bit in bits]
        total = None
        for term in terms:
            starts, sizes = [0] * term.ndim, list(term.shape)
            for axis, bit in zip(order, bits):
                starts[axis], sizes[axis] = ((here ^ mask) >> bit) & 1, 1
            piece = lax.dynamic_slice(term, starts, sizes)
            piece = piece.reshape([size for i, size in enumerate(sizes) if i not in order]).astype(F32)
            total = piece if total is None else total + piece
        return total.astype(LOW)

    def step(self):
        if self.order:
            bits = self.order[0]
            masks = [
                sum(1 << bit for i, bit in enumerate(bits) if other >> i & 1)
                for other in range(1, 1 << len(bits))
            ]
            if bits != (0,):
                terms = [self.kept, *self.got]
                self.sent = [self.shard(terms, bits, mask) for mask in masks]
                self.kept = self.shard(terms, bits, 0)
                self.left = [bit for bit in self.left if bit not in bits]
            size = lax.axis_size("row")
            self.got = [
                lax.ppermute(sent, "row", [(i, i ^ mask) for i in range(size)])
                for sent, mask in zip(self.sent, masks)
            ]
        else:
            self.sent = [self.kept]
            self.got = [lax.ppermute(self.kept, "col", self.line[0][1])]

    def land(self, token=None):
        if token is not None:
            self.kept = lax.optimization_barrier((self.kept, token))[0]
        got = self.got
        if self.order:
            bits = self.order.pop(0)
            if bits == (0,):
                dims = (2,) * len(self.left) + self.kept.shape[1:]
                self.kept, self.got = self.kept.reshape(dims), [item.reshape(dims) for item in self.got]
            if not self.order:
                self.kept = sum([item.astype(F32) for item in self.got], self.kept.astype(F32)).astype(LOW)
        else:
            ends, _ = self.line.pop(0)
            if ends is None:
                self.kept = self.kept + self.got[0]
            else:
                here = lax.axis_index("col")
                self.kept = jnp.where((here == ends[0]) | (here == ends[1]), self.got[0], self.kept)
        return got

    def turn(self, token=None):
        got = self.land(token)
        if self.done:
            return got
        self.step()
        return got + self.sent

    @property
    def done(self):
        return not self.order and not self.line


def gather_all(piece):
    row_bits = lax.axis_size("row").bit_length() - 1
    col_bits = lax.axis_size("col").bit_length() - 1
    steps = [("col", tuple(range(i, min(i + 2, col_bits)))) for i in range(0, col_bits, 2)]
    steps += [("row", tuple(range(i, min(i + 2, row_bits)))) for i in range(1, row_bits, 2)]
    for name, bits in steps + [("row", (0,))]:
        here = lax.axis_index(name)
        pieces = [piece]
        for other in range(1, 1 << len(bits)):
            mask = sum(1 << bit for i, bit in enumerate(bits) if other >> i & 1)
            pairs = [(i, i ^ mask) for i in range(lax.axis_size(name))]
            pieces.append(lax.ppermute(piece, name, pairs))
        for i, bit in enumerate(bits):
            high = ((here >> bit) & 1) == 1
            pieces = [
                jnp.where(high, pieces[place ^ (1 << i)], pieces[place]) for place in range(len(pieces))
            ]
        piece = jnp.concatenate(pieces, 0)
    return piece


def per_device(
    query_tokens, passage_tokens, query_lengths, passage_lengths, positives,
    w_query, w_key, w_value, w_attn_out, w_inner, w_outer,
    bias_query, bias_value, bias_attn_out, bias_inner, bias_outer,
    gain_one, shift_one, gain_two, shift_two,
):
    q_dev, q_len, width = query_tokens.shape
    p_dev, p_len, _ = passage_tokens.shape
    inner = w_inner.shape[1]
    rows_all = p_len
    assert q_dev * q_len == rows_all and q_dev + p_dev <= SLOTS
    blocks = 1 + p_dev
    total_rows = blocks * rows_all
    row_count = lax.axis_size("row")
    col_count = lax.axis_size("col")
    row_here = lax.axis_index("row")
    core = row_here & 1
    me = (row_here * col_count + lax.axis_index("col")).reshape(1)
    params = pltpu.CompilerParams(vmem_limit_bytes=VMEM)
    smem = pl.BlockSpec(memory_space=pltpu.SMEM)

    def line(item):
        return item

    def by_block(wide):
        return pl.BlockSpec((rows_all, wide), lambda i: (i, 0))

    def by_block_t(high):
        return pl.BlockSpec((high, rows_all), lambda i: (0, i))

    def fixed(shape):
        return pl.BlockSpec(shape, lambda i: (0,) * len(shape))

    queries_spec = pl.BlockSpec((rows_all, width), lambda i: (0, 0))
    passages_spec = pl.BlockSpec((rows_all, width), lambda i: (jnp.maximum(i - 1, 0), 0))

    lse_spec = pl.BlockSpec((1, HEADS // 2, 8, rows_all), lambda i: (i, 0, 0, 0))

    def shape(*dims, kind=LOW):
        return jax.ShapeDtypeStruct(dims, kind)

    queries = query_tokens.reshape(rows_all, width)
    passages = passage_tokens.reshape(p_dev * rows_all, width)
    square = const_spec((width, width))
    anywhere = pl.BlockSpec(memory_space=pl.ANY)
    thin = const_spec((width,))

    q, k, v, ctx_t, lse = call(
        partial(attend_kernel, (q_dev, q_len, rows_all, width)),
        (query_lengths, passage_lengths, queries, passages, w_query, w_key, w_value, bias_query, bias_value),
        [smem, smem, queries_spec, passages_spec, square, square, square, thin, thin],
        [(by_block(width), shape(total_rows, width))] * 3
        + [
            (by_block_t(width), shape(width, total_rows)),
            (lse_spec, shape(blocks, HEADS // 2, 8, rows_all, kind=F32)),
        ],
        (blocks,),
        56,
        name="attend",
        us=25,
    )

    rows_part = rows_all
    parts = blocks

    def by_part(wide):
        return pl.BlockSpec((rows_part, wide), lambda i: (i, 0))

    queries_part = pl.BlockSpec((rows_part, width), lambda i: (0, 0))
    passages_part = pl.BlockSpec((rows_part, width), lambda i: (jnp.maximum(i - 1, 0), 0))
    h1, y1, act, slope, h2, query_out, passage_out, pooled, payload = call(
        partial(dense_kernel, (q_dev, q_len, p_len, width, inner)),
        (
            query_lengths, passage_lengths, positives, queries, passages, ctx_t, w_attn_out, w_inner, w_outer,
            bias_attn_out, bias_inner, bias_outer, gain_one, shift_one, gain_two, shift_two,
        ),
        [smem, smem, smem, queries_part, passages_part, pl.BlockSpec((width, rows_part), lambda i: (0, i))]
        + [anywhere] * 3
        + [thin, const_spec((inner,))]
        + [thin] * 5,
        [
            (by_part(width), shape(total_rows, width)),
            (by_part(width), shape(total_rows, width)),
            (by_part(inner), shape(total_rows, inner)),
            (by_part(inner), shape(total_rows, inner)),
            (by_part(width), shape(total_rows, width)),
            (queries_part, shape(rows_all, width)),
            (passages_part, shape(p_dev * rows_all, width)),
            (fixed((SLOTS, width)), shape(SLOTS, width, kind=F32)),
            (fixed((SLOTS, width + 128)), shape(SLOTS, width + 128)),
        ],
        (parts,),
        56,
        name="dense",
        scratch=[
            pltpu.VMEM((width, width), LOW),
            pltpu.VMEM((width, inner), LOW),
            pltpu.VMEM((inner, width), LOW),
            pltpu.SemaphoreType.DMA((3,)),
        ],
        us=40,
    )

    gathered = gather_all(payload)
    loss, gvec = pl.pallas_call(
        partial(loss_kernel, (q_dev, p_dev, width, col_count)),
        in_specs=[smem] * 3 + [pl.BlockSpec(memory_space=pltpu.VMEM)] * 3,
        out_specs=[pl.BlockSpec(memory_space=pltpu.VMEM)] * 2,
        out_shape=[shape(8, 128, kind=F32), shape(SLOTS, width, kind=F32)],
        compiler_params=params,
        name="loss",
    )(me, query_lengths, passage_lengths, payload, gathered, pooled)

    smalls = shape(8, width, kind=F32)
    grad_f, grad_f_t, stat_two = call(
        partial(norm_two_kernel, (q_dev, q_len, rows_all, width)),
        (query_lengths, passage_lengths, gvec, h2, line(gain_two)),
        [smem, smem, fixed((SLOTS, width)), by_block(width), thin],
        [
            (by_block(width), shape(total_rows, width)),
            (by_block_t(width), shape(width, total_rows)),
            (fixed((8, width)), smalls),
        ],
        (blocks,),
        60,
        name="norm_two",
        us=9,
    )

    outer = Flow(*weight_grad(grad_f_t, act, False, row_count, core), line=True)
    outer.step()

    def dense_back(deps):
        return call(
            partial(dense_back_kernel, (rows_part, width, inner)),
            (grad_f, slope, h1, w_outer, w_inner, w_attn_out, line(gain_one)),
            [by_part(width), by_part(inner), by_part(width), anywhere, anywhere, anywhere, thin],
            [
                (by_part(inner), shape(total_rows, inner)),
                (by_part(width), shape(total_rows, width, kind=F32)),
                (by_part(width), shape(total_rows, width)),
                (by_part(width), shape(total_rows, width)),
                (fixed((8, width)), smalls),
                (fixed((8, inner)), shape(8, inner, kind=F32)),
            ],
            (parts,),
            58,
            deps,
            name="dense_back",
            scratch=[
                pltpu.VMEM((inner, width), LOW),
                pltpu.VMEM((width, inner), LOW),
                pltpu.VMEM((width, width), LOW),
                pltpu.SemaphoreType.DMA((5,)),
            ],
            us=30,
        )

    def turn(arrays, specs, deps):
        outs = [(by_block_t(width), shape(width, total_rows))]
        return call(turn_low_kernel, arrays, specs, outs, (blocks,), 56, deps, name="turn", us=3)[0]

    y1_t = turn([y1], [by_block(width)], outer.sent)
    deps = outer.turn(y1_t)
    grad_u, grad_h1, grad_attn, grad_ctx, stat_one, grad_bias_inner = dense_back(deps)
    deps = outer.turn(stat_one)
    up_flow = Flow(*weight_grad(y1_t, grad_u, True, row_count, core, deps, tile=(128, 256)))
    up_flow.step()
    deps = up_flow.sent
    x_t = turn([queries, passages], [queries_spec, passages_spec], deps)
    deps = up_flow.turn(x_t)

    head_dim = width // HEADS
    third = 4 * head_dim
    groups = [(0, 2 * third), (2 * third, third)]

    def attend_back(start, wide, deps):
        pairs = wide // (2 * head_dim)
        index = start // wide
        cols = pl.BlockSpec((rows_all, wide), lambda i: (i, index))
        return call(
            partial(attend_back_kernel, (q_dev, q_len, rows_all, head_dim)),
            (query_lengths, passage_lengths, q, k, v, ctx_t, lse, grad_ctx),
            [smem, smem]
            + [cols] * 3
            + [
                pl.BlockSpec((wide, rows_all), lambda i: (index, i)),
                pl.BlockSpec((1, pairs, 8, rows_all), lambda i: (i, index, 0, 0)),
                cols,
            ],
            [
                (by_block(3 * wide), shape(total_rows, 3 * wide)),
                (fixed((8, wide)), shape(8, wide, kind=F32)),
            ],
            (blocks,),
            56,
            deps,
            name="attend_back",
            us=12,
        )

    grad_a, stat_a = attend_back(*groups[0], deps)
    mixed = weight_grad(ctx_t, grad_attn, True, row_count, core, [stat_a], room=3 * width, tile=(768, 256))
    deps = outer.turn(mixed[0]) + up_flow.turn(mixed[0])
    mixed = weight_grad(x_t, grad_a, True, row_count, core, deps, old=mixed, room=3 * width, tile=(256, 768))
    mixed_flow = Flow(*mixed)
    mixed_flow.step()
    grad_b, stat_b = attend_back(*groups[1], mixed_flow.sent)
    deps = [stat_b, *outer.turn(stat_b), *up_flow.turn(stat_b), *mixed_flow.turn(stat_b)]

    extra = (stat_two, stat_one, grad_bias_inner, stat_a, stat_b)
    last_flow = Flow(*weight_grad(x_t, grad_b, True, row_count, core, deps, extra))
    last_flow.step()
    deps = last_flow.sent

    query_grad, passage_grad = call(
        partial(input_grad_kernel, groups),
        (grad_a, grad_b, grad_h1, w_query, w_key, w_value),
        [by_block(3 * wide) for _, wide in groups] + [by_block(width), square, square, square],
        [
            (queries_spec, shape(rows_all, width)),
            (passages_spec, shape(p_dev * rows_all, width)),
        ],
        (blocks,),
        56,
        deps,
        name="input_grad",
        us=8,
    )
    mixed_flow.turn(passage_grad)
    last_flow.turn(mixed_flow.kept)
    outer.turn(last_flow.kept)
    up_flow.turn(outer.kept)
    mixed_flow.turn(up_flow.kept)
    last_flow.turn(mixed_flow.kept)
    last_flow.turn()
    mixed_flow.turn()
    last_flow.turn(mixed_flow.kept)
    flows = [outer, up_flow, mixed_flow, last_flow]
    while not all(flow.done for flow in flows):
        for flow in flows:
            if not flow.done:
                flow.turn()
    cut = width // row_count
    turned = pl.pallas_call(
        turn_kernel,
        out_shape=shape(inner // row_count, width, kind=F32),
        compiler_params=params,
        name="turn",
    )(outer.kept)
    mixed, last = mixed_flow.kept.astype(F32), last_flow.kept.astype(F32)
    qkv = [
        jnp.concatenate(
            [mixed[:, width + i * 2 * third : width + (i + 1) * 2 * third], last[:cut, i * third : (i + 1) * third]],
            1,
        )
        for i in range(3)
    ]
    small = last[cut:]
    return (
        loss[0, 0],
        query_out.reshape(query_tokens.shape),
        passage_out.reshape(passage_tokens.shape),
        query_grad.reshape(query_tokens.shape),
        passage_grad.reshape(passage_tokens.shape),
        *qkv,
        mixed[:, :width],
        up_flow.kept.astype(F32),
        turned,
        *[small[i, :cut] for i in range(3)],
        small[8, : inner // row_count],
        *[small[i, :cut] for i in range(3, 8)],
    )


def solution(mesh):
    in_specs = (
        P(("row", "col"), None, None),
        P(("row", "col"), None, None),
        P(("row", "col")),
        P(("row", "col")),
        P(("row", "col")),
        P(),
        P(),
        P(),
        P(),
        P(),
        P(),
        P(),
        P(),
        P(),
        P(),
        P(),
        P(),
        P(),
        P(),
        P(),
    )
    out_specs = (
        P(),
        P(("row", "col"), None, None),
        P(("row", "col"), None, None),
        P(("row", "col"), None, None),
        P(("row", "col"), None, None),
        P("row", None),
        P("row", None),
        P("row", None),
        P("row", None),
        P("row", None),
        P("row", None),
        P("row"),
        P("row"),
        P("row"),
        P("row"),
        P("row"),
        P("row"),
        P("row"),
        P("row"),
        P("row"),
    )
    return jax.shard_map(
        per_device, mesh=mesh, in_specs=in_specs, out_specs=out_specs, check_vma=False
    )
```

```python
from functools import partial

import jax
import jax.numpy as jnp
from jax import lax
from jax.experimental import pallas as pl
from jax.experimental.pallas import tpu as pltpu
from jax.sharding import PartitionSpec as P

HEADS = 12
EPS_NORM = 1e-12
EPS_POOL = 1e-06
SCALE_LOSS = 128.0
INV_TEMP = 100.0
TILE = 256
SLOTS = 8
VMEM = 60 * 1024 * 1024
LOW = jnp.bfloat16
F32 = jnp.float32


def mm(left, right):
    return lax.dot_general(left, right, (((1,), (0,)), ((), ())), preferred_element_type=F32)


def mm_nt(left, right):
    return lax.dot_general(left, right, (((1,), (1,)), ((), ())), preferred_element_type=F32)


def norm_parts(hidden):
    center = hidden - jnp.mean(hidden, -1, keepdims=True)
    spread = jnp.mean(center * center, -1, keepdims=True)
    scale = lax.rsqrt(spread + EPS_NORM)
    return center * scale, scale


def gelu_parts(u):
    square = u * u
    q = 1.4250060785476853e-06
    for factor in (-3.669345091379551e-05, -8.782652731110375e-05, 0.03639228618131223, 0.7978697123041883):
        q = q * square + factor
    share = 0.5 + 0.5 * jnp.tanh(u * q)
    bell = jnp.exp(-0.5 * square)
    return u * share, share + (0.3989422804014327 * u) * bell


def vec(ref, cols=slice(None)):
    return ref[cols].reshape(1, -1)


def rows_of(step, size):
    return pl.ds(pl.multiple_of(step * size, size), size)


def part_owner(part, q_dev, q_len, p_len, qlen_ref, plen_ref):
    per = p_len // q_len
    beyond = jnp.maximum(part - q_dev, 0)
    is_query = part < q_dev
    slot = jnp.where(is_query, part, q_dev + beyond // per)
    length = jnp.where(is_query, qlen_ref[jnp.where(is_query, part, 0)], plen_ref[beyond // per])
    first = jnp.where(is_query, 0, beyond % per * q_len)
    return slot, length, first


def live_rows(first, length, size):
    return (first + lax.broadcasted_iota(jnp.int32, (size, 1), 0)) < length


def sure_rows(size):
    return size * 4 // 5 // 16 * 16


def half_only(pair_t, which):
    half = pair_t.shape[0] // 2
    zeros = jnp.zeros((half, pair_t.shape[1]), pair_t.dtype)
    if which == 0:
        return jnp.concatenate([pair_t[:half], zeros], 0)
    return jnp.concatenate([zeros, pair_t[half:]], 0)


def staged(count, *stages):
    for step in range(count + len(stages) - 1):
        for late, stage in enumerate(stages):
            if 0 <= step - late < count:
                stage(step - late)


def fetch(source, target, sems, index):
    return pltpu.make_async_copy(source, target, sems.at[index])


def attend_kernel(
    dims, qlen_ref, plen_ref, xq_ref, xp_ref, wq_ref, wk_ref, wv_ref, bq_ref, bv_ref,
    q_ref, k_ref, v_ref, ctx_t_ref, lse_ref,
):
    q_dev, q_len, rows_all, width = dims
    block = pl.program_id(0)
    head_dim = width // HEADS
    x = jnp.where(block == 0, xq_ref[...], xp_ref[...])
    q = ((mm(x, wq_ref[...]) + vec(bq_ref)) * head_dim**-0.5).astype(LOW)
    k = mm(x, wk_ref[...]).astype(LOW)
    v = (mm(x, wv_ref[...]) + vec(bv_ref)).astype(LOW)
    q_ref[...] = q
    k_ref[...] = k
    v_ref[...] = v
    q_t, v_t = q.T, v.T

    def attend(size, starts, lengths):
        items = [(start, length, head) for head in range(HEADS) for start, length in zip(starts, lengths)]
        scores, weights = {}, {}

        def compare(i):
            start, length, head = items[i]
            cols = slice(head // 2 * 2 * head_dim, (head // 2 + 1) * 2 * head_dim)
            here = slice(start, start + size)
            scores[i] = mm(k[here, cols], half_only(q_t[cols, here], head % 2))

        def weigh(i):
            start, length, head = items[i]
            edge = sure_rows(size)
            early, late = scores[i][:edge], scores.pop(i)[edge:]
            late = jnp.where(live_rows(edge, length, size - edge), late, -1e30)
            top = jnp.maximum(jnp.max(early, 0, keepdims=True), jnp.max(late, 0, keepdims=True))
            weights[i] = top, jnp.concatenate([jnp.exp(early - top).astype(LOW), jnp.exp(late - top).astype(LOW)], 0)

        def combine(i):
            start, length, head = items[i]
            here, rows = slice(start, start + size), slice(head * head_dim, (head + 1) * head_dim)
            top, weight = weights.pop(i)
            values = jnp.concatenate([v_t[rows, here], jnp.ones((16, size), LOW)], 0)
            result = mm(values, weight)
            total = result[head_dim : head_dim + 1]
            lse_ref[0, head // 2, head % 2 : head % 2 + 1, here] = top + jnp.log(total)
            ctx_t_ref[rows, here] = (result[:head_dim] * (1.0 / total)).astype(LOW)

        staged(len(items), compare, weigh, combine)

    @pl.when(block == 0)
    def _():
        attend(q_len, [s * q_len for s in range(q_dev)], [qlen_ref[s] for s in range(q_dev)])

    @pl.when(block > 0)
    def _():
        attend(rows_all, [0], [plen_ref[jnp.maximum(block - 1, 0)]])


def dense_kernel(
    dims, qlen_ref, plen_ref, pos_ref, xq_ref, xp_ref, ctx_t_ref, wo_hbm, wi_hbm, wf_hbm,
    bo_ref, bi_ref, bf_ref, g1_ref, s1_ref, g2_ref, s2_ref,
    h1_ref, y1_ref, act_ref, dg_ref, h2_ref, yq_ref, yp_ref, pool_ref, pay_ref,
    wo_ref, wi_ref, wf_ref, sems,
):
    q_dev, q_len, p_len, width, inner = dims
    block = pl.program_id(0)
    rows_all = xq_ref.shape[0]
    query_blocks = q_dev * q_len // rows_all
    copies = [
        fetch(source, target, sems, index)
        for index, (source, target) in enumerate([(wo_hbm, wo_ref), (wi_hbm, wi_ref), (wf_hbm, wf_ref)])
    ]

    @pl.when(block == 0)
    def _():
        for copy in copies:
            copy.start()
        pool_ref[...] = jnp.zeros_like(pool_ref)
        copies[0].wait()

    x = jnp.where(block < query_blocks, xq_ref[...], xp_ref[...])
    hidden = x.astype(F32) + (mm(ctx_t_ref[...].T, wo_ref[...]) + vec(bo_ref))
    h1_ref[...] = hidden.astype(LOW)
    y1 = norm_parts(hidden)[0] * vec(g1_ref) + vec(s1_ref)
    y1_low = y1.astype(LOW)
    y1_ref[...] = y1_low

    @pl.when(block == 0)
    def _():
        copies[1].wait()
        copies[2].wait()

    group = width // TILE
    raw, made = {}, {}
    sums = [y1[:, n * TILE : (n + 1) * TILE] + vec(bf_ref, slice(n * TILE, (n + 1) * TILE)) for n in range(group)]

    def expand(i):
        cols = slice(i * TILE, (i + 1) * TILE)
        raw[i] = mm(y1_low, wi_ref[:, cols]) + vec(bi_ref, cols)

    def activate(i):
        cols = slice(i * TILE, (i + 1) * TILE)
        act, slope = gelu_parts(raw.pop(i))
        made[i] = act.astype(LOW)
        act_ref[:, cols] = made[i]
        dg_ref[:, cols] = slope.astype(LOW)

    def contract(i):
        first, n = i // group * group, i % group
        left = jnp.concatenate([made[first + j] for j in range(group)], 1)
        cols = slice(n * TILE, (n + 1) * TILE)
        sums[n] = sums[n] + mm(left, wf_ref[first * TILE : (first + group) * TILE, cols])

    late = [lambda i: None] * (group - 1)
    staged(inner // TILE, expand, activate, *late, contract)

    total = jnp.concatenate(sums, 1)
    h2_ref[...] = total.astype(LOW)
    y2 = norm_parts(total)[0] * vec(g2_ref) + vec(s2_ref)
    for part in range(rows_all // q_len):
        number = block * (rows_all // q_len) + part
        slot, length, first = part_owner(number, q_dev, q_len, p_len, qlen_ref, plen_ref)
        piece = y2[part * q_len : (part + 1) * q_len]
        summed = jnp.sum(jnp.where(live_rows(first, length, q_len), piece, 0.0), 0, keepdims=True)
        in_slot = lax.broadcasted_iota(jnp.int32, (SLOTS, 1), 0) == slot
        pool_ref[...] += jnp.where(in_slot, summed / length.astype(F32), 0.0)

    @pl.when(block < query_blocks)
    def _():
        yq_ref[...] = y2.astype(LOW)

    @pl.when(block >= query_blocks)
    def _():
        yp_ref[...] = y2.astype(LOW)

    @pl.when(block == pl.num_programs(0) - 1)
    def _():
        pooled = pool_ref[...]
        emb = pooled * lax.rsqrt(jnp.sum(pooled * pooled, -1, keepdims=True) + EPS_POOL)
        pay_ref[:, :width] = emb.astype(LOW)
        row = lax.broadcasted_iota(jnp.int32, (SLOTS, 128), 0)
        col = lax.broadcasted_iota(jnp.int32, (SLOTS, 128), 1)
        place = jnp.zeros((SLOTS, 128), jnp.int32)
        for j in range(q_dev):
            high = pos_ref[j] // 128
            low = pos_ref[j] - high * 128
            place = jnp.where(row == j, jnp.where(col == 0, high, jnp.where(col == 1, low, 0)), place)
        pay_ref[:, width:] = place.astype(F32).astype(LOW)


def loss_kernel(
    dims, me_ref, qlen_ref, plen_ref, own_ref, all_ref, pool_ref, loss_ref, gvec_ref
):
    q_dev, p_dev, width, col_count = dims
    count = all_ref.shape[0]
    every = all_ref[:, :width]
    own = own_ref[:, :width]

    def passage_mask(index):
        spot, place = index % SLOTS, index // SLOTS
        per_core = count // SLOTS // 2
        core, rest = place // per_core, place % per_core
        device = (rest // col_count * 2 + core) * col_count + rest % col_count
        return (spot >= q_dev) & (spot < q_dev + p_dev), device * p_dev + spot - q_dev

    scores = mm_nt(own, every) * INV_TEMP
    valid, ident = passage_mask(lax.broadcasted_iota(jnp.int32, (SLOTS, count), 1))
    scores = jnp.where(valid, scores, -1e30)
    top = jnp.max(scores, -1, keepdims=True)
    totals = top + jnp.log(jnp.sum(jnp.exp(scores - top), -1, keepdims=True))
    marks = own_ref[:, width:].astype(F32)
    wanted = marks[:, 0:1] * 128.0 + marks[:, 1:2]
    target = (valid & (ident.astype(F32) == wanted)).astype(F32)
    raw = (INV_TEMP * (SCALE_LOSS * (jnp.exp(scores - totals) - target))).astype(LOW)
    grad_q = mm(raw, every)

    picker_col = lax.broadcasted_iota(jnp.int32, (SLOTS, 128), 1)
    picker = jnp.where(picker_col == 0, 128.0, jnp.where(picker_col == 1, 1.0, 0.0)).astype(LOW)
    own_row = lax.broadcasted_iota(jnp.int32, (SLOTS, TILE), 0)
    own_valid = (own_row >= q_dev) & (own_row < q_dev + p_dev)
    own_ident = (me_ref[0] * p_dev + own_row - q_dev).astype(F32)

    def body(step, carry):
        total_loss, grad_p = carry
        rows = rows_of(step, TILE)
        some = all_ref[rows, :width]
        place = mm_nt(picker, all_ref[rows, width:])[0:1]
        table = mm_nt(every, some) * INV_TEMP
        ok, names = passage_mask(lax.broadcasted_iota(jnp.int32, (count, TILE), 0))
        picked = jnp.sum(jnp.where(ok & (names.astype(F32) == place), table, 0.0), 0, keepdims=True)
        table = jnp.where(ok, table, -1e30)
        high = jnp.max(table, 0, keepdims=True)
        lse = high + jnp.log(jnp.sum(jnp.exp(table - high), 0, keepdims=True))
        is_query = lax.broadcasted_iota(jnp.int32, (1, TILE), 1) % SLOTS < q_dev
        losses = jnp.where(is_query, lse - picked, 0.0)
        mine = mm_nt(own, some) * INV_TEMP
        hit = (own_ident == place).astype(F32)
        grads = INV_TEMP * (SCALE_LOSS * (jnp.exp(mine - lse) - hit))
        grads = jnp.where(own_valid & is_query, grads, 0.0).astype(LOW)
        return total_loss + jnp.sum(losses, 1, keepdims=True), grad_p + mm(grads, some)

    start = (jnp.zeros((1, 1), F32), jnp.zeros((SLOTS, width), F32))
    total_loss, grad_p = lax.fori_loop(0, count // TILE, body, start)
    loss_ref[...] = jnp.broadcast_to(total_loss / float(count // SLOTS * q_dev), loss_ref.shape)

    slot = lax.broadcasted_iota(jnp.int32, (SLOTS, 1), 0)
    grad = jnp.where(slot < q_dev, grad_q, grad_p)
    pooled = pool_ref[...]
    r = lax.rsqrt(jnp.sum(pooled * pooled, -1, keepdims=True) + EPS_POOL)
    inside = jnp.sum(pooled * grad, -1, keepdims=True)
    length = jnp.ones((SLOTS, 1), F32)
    for j in range(q_dev):
        length = jnp.where(slot == j, qlen_ref[j].astype(F32), length)
    for j in range(p_dev):
        length = jnp.where(slot == q_dev + j, plen_ref[j].astype(F32), length)
    gvec_ref[...] = (r * grad - r * r * r * inside * pooled) / length


def store_shards(core_ref, result, send_ref, keep_ref, by_row=True, tails=None):
    count = send_ref.shape[0] * 2
    size = result.shape[0 if by_row else 1] // count

    def store(even, odd):
        for shard in range(count):
            spot = slice(shard * size, (shard + 1) * size)
            piece = (result[spot, :] if by_row else result[:, spot]).astype(LOW)
            target = odd if shard % 2 else even
            if tails is None:
                target[shard // 2] = piece
            else:
                target[shard // 2, :size] = piece
                target[shard // 2, size:] = tails[shard]

    @pl.when(core_ref[0] == 0)
    def _():
        store(keep_ref, send_ref)

    @pl.when(core_ref[0] == 1)
    def _():
        store(send_ref, keep_ref)


def outer_grad_kernel(
    dims, core_ref, qlen_ref, plen_ref, gvec_ref, h2_ref, g2_ref, act_ref,
    gf_ref, stat_ref, send_ref, keep_ref, gf_t_ref,
):
    q_dev, q_len, p_len = dims

    @pl.when(pl.program_id(0) == 0)
    def _():
        stat_ref[...] = jnp.zeros_like(stat_ref)

        def body(part, carry):
            rows = rows_of(part, q_len)
            slot, length, first = part_owner(part, q_dev, q_len, p_len, qlen_ref, plen_ref)
            in_slot = lax.broadcasted_iota(jnp.int32, (SLOTS, 1), 0) == slot
            grad_y = jnp.sum(jnp.where(in_slot, gvec_ref[...], 0.0), 0, keepdims=True)
            live = live_rows(first, length, q_len)
            n2, r2 = norm_parts(h2_ref[rows, :].astype(F32))
            g = grad_y * vec(g2_ref)
            grad = r2 * (g - jnp.mean(g, -1, keepdims=True) - n2 * jnp.mean(g * n2, -1, keepdims=True))
            grad = jnp.where(live, grad, 0.0)
            low = grad.astype(LOW)
            gf_ref[rows, :] = low
            gf_t_ref[:, rows] = low.T
            stat_ref[0:1, :] += grad_y * jnp.sum(jnp.where(live, n2, 0.0), 0, keepdims=True)
            stat_ref[1:2, :] += grad_y * jnp.sum(live.astype(F32), 0, keepdims=True)
            stat_ref[2:3, :] += jnp.sum(low.astype(F32), 0, keepdims=True)
            return carry

        lax.fori_loop(0, h2_ref.shape[0] // q_len, body, 0)

    store_shards(core_ref, mm(gf_t_ref[...], act_ref[...]), send_ref, keep_ref, by_row=False)


def dense_back_kernel(
    dims, core_ref, gf_ref, dg_ref, h1_ref, ctx_t_ref, wf_hbm, wi_hbm, wo_hbm, g1_ref,
    gu_ref, ga_ref, gc_ref, stat_ref, bi_ref, send_ref, keep_ref,
    sum_ref, wf_ref, wi_ref, wo_ref, sems,
):
    rows_all, width, inner = dims
    block = pl.program_id(0)
    chunk = TILE
    group = width // chunk
    copies = [
        fetch(wf_hbm.at[pl.ds(0, width), :], wf_ref.at[pl.ds(0, width), :], sems, 0),
        fetch(wi_hbm.at[:, pl.ds(0, width)], wi_ref.at[:, pl.ds(0, width)], sems, 1),
        fetch(wf_hbm.at[pl.ds(width, inner - width), :], wf_ref.at[pl.ds(width, inner - width), :], sems, 2),
        fetch(wi_hbm.at[:, pl.ds(width, inner - width)], wi_ref.at[:, pl.ds(width, inner - width)], sems, 3),
        fetch(wo_hbm, wo_ref, sems, 4),
    ]

    @pl.when(block == 0)
    def _():
        for copy in copies:
            copy.start()
        stat_ref[...] = jnp.zeros_like(stat_ref)
        bi_ref[...] = jnp.zeros_like(bi_ref)
        copies[0].wait()
        copies[1].wait()

    gf = gf_ref[...]
    raw, made = {}, {}
    sums = [gf[:, n * chunk : (n + 1) * chunk].astype(F32) for n in range(group)]
    biases = []

    def spread(i):
        raw[i] = mm_nt(gf, wf_ref[i * chunk : (i + 1) * chunk, :])

    def slope(i):
        cols = slice(i * chunk, (i + 1) * chunk)
        made[i] = (raw.pop(i) * dg_ref[:, cols].astype(F32)).astype(LOW)
        gu_ref[:, cols] = made[i]
        biases.append(jnp.sum(made[i].astype(F32), 0, keepdims=True))

    def gather(i):
        first, n = i // group * group, i % group
        left = jnp.concatenate([made[first + j] for j in range(group)], 1)
        cols = slice(n * chunk, (n + 1) * chunk)
        sums[n] = sums[n] + mm_nt(left, wi_ref[cols, first * chunk : (first + group) * chunk])

    staged(group, spread, slope)

    @pl.when(block == 0)
    def _():
        for copy in copies[2:]:
            copy.wait()

    count = inner // chunk
    staged(
        count,
        lambda i: spread(i + group) if i + group < count else None,
        lambda i: slope(i + group) if i + group < count else None,
        gather,
    )
    bi_ref[0:1, :] += jnp.concatenate(biases, 1)
    total = jnp.concatenate(sums, 1)
    n1, r1 = norm_parts(h1_ref[...].astype(F32))
    stat_ref[0:1, :] += jnp.sum(total * n1, 0, keepdims=True)
    stat_ref[1:2, :] += jnp.sum(total, 0, keepdims=True)
    g = total * vec(g1_ref)
    grad = r1 * (g - jnp.mean(g, -1, keepdims=True) - n1 * jnp.mean(g * n1, -1, keepdims=True))
    low = grad.astype(LOW)
    ga_ref[...] = low
    stat_ref[2:3, :] += jnp.sum(low.astype(F32), 0, keepdims=True)
    gc_ref[...] = mm_nt(low, wo_ref[...]).astype(LOW)
    product = mm(ctx_t_ref[...], low)

    @pl.when(block == 0)
    def _():
        sum_ref[...] = product

    @pl.when(block > 0)
    def _():
        sum_ref[...] += product

    @pl.when(block == pl.num_programs(0) - 1)
    def _():
        store_shards(core_ref, sum_ref[...], send_ref, keep_ref)


def attend_back_kernel(
    dims, core_ref, qlen_ref, plen_ref, q_ref, k_ref, v_ref, ctx_t_ref, lse_ref, gc_ref, x_t_ref, *refs
):
    *extra, out_ref, stat_ref, send_ref, keep_ref, sum_ref = refs
    q_dev, q_len, rows_all, head_dim = dims
    block = pl.program_id(0)
    pair_dim = 2 * head_dim
    width = q_ref.shape[1]
    pairs = width // pair_dim

    @pl.when(block == 0)
    def _():
        stat_ref[...] = jnp.zeros_like(stat_ref)

    def attend(size, starts, lengths, fresh):
        lane = lax.broadcasted_iota(jnp.int32, (size, pair_dim), 1)
        items = [(s, p, which) for p in range(pairs) for s in range(len(starts)) for which in range(2)]
        held, raw, made, grads = {}, {}, {}, {}

        def pair_of(s, p):
            if (s, p) not in held:
                here, cols = slice(starts[s], starts[s] + size), slice(p * pair_dim, (p + 1) * pair_dim)
                q, k, v, gc = q_ref[here, cols], k_ref[here, cols], v_ref[here, cols], gc_ref[here, cols]
                held[s, p] = here, cols, q, k, v, gc, q.T, k.T, gc.T
            return held[s, p]

        def compare(i):
            s, p, which = items[i]
            here, cols, q, k, v, gc, q_t, k_t, gc_t = pair_of(s, p)
            raw[i] = mm(k, half_only(q_t, which)), mm(v, half_only(gc_t, which))

        def weigh(i):
            s, p, which = items[i]
            here, cols, q, k, v, gc, q_t, k_t, gc_t = pair_of(s, p)
            head = slice((p * 2 + which) * head_dim, (p * 2 + which + 1) * head_dim)
            scores, grad_p = raw.pop(i)
            lse = lse_ref[0, p, which : which + 1, here]
            edge = sure_rows(size)
            late = jnp.where(live_rows(edge, lengths[s], size - edge), scores[edge:], -1e30)
            probs = jnp.concatenate([jnp.exp(scores[:edge] - lse), jnp.exp(late - lse)], 0)
            half = slice(which * head_dim, (which + 1) * head_dim)
            delta = jnp.sum(gc_t[half].astype(F32) * ctx_t_ref[head, here].astype(F32), 0, keepdims=True)
            made[i] = probs.astype(LOW), (probs * (grad_p - delta)).astype(LOW)

        def combine(i):
            s, p, which = items[i]
            here, cols, q, k, v, gc, q_t, k_t, gc_t = pair_of(s, p)
            mine = (lane >= head_dim) if which else (lane < head_dim)
            zero = jnp.zeros_like(q)
            probs, grad_s = made.pop(i)
            add_v = mm(probs, jnp.where(mine, gc, zero))
            add_k = mm(grad_s, jnp.where(mine, q, zero))
            add_q = mm(k_t[which * head_dim : (which + 1) * head_dim], grad_s)
            if which == 0:
                made[s, p] = add_v, add_k, add_q
                return
            old_v, old_k, old_q = made.pop((s, p))
            grad_q = (jnp.concatenate([old_q, add_q], 0).T * head_dim**-0.5).astype(LOW)
            grad_k = (old_k + add_k).astype(LOW)
            grad_v = (old_v + add_v).astype(LOW)
            for number, grad in enumerate((grad_q, grad_k, grad_v)):
                out_ref[here, number * width + cols.start : number * width + cols.stop] = grad
                grads[number, s, p] = grad
            stat_ref[0:1, cols] += jnp.sum(grad_q.astype(F32), 0, keepdims=True)
            stat_ref[1:2, cols] += jnp.sum(grad_v.astype(F32), 0, keepdims=True)

            if p % 2 and s == len(starts) - 1:
                project(p - 1)

        def project(p):
            for number in range(3):
                rows = [
                    jnp.concatenate([grads.pop((number, s, p)), grads.pop((number, s, p + 1))], 1)
                    for s in range(len(starts))
                ]
                product = mm(x_t_ref[...], jnp.concatenate(rows, 0))
                cols = slice(number * width + p * pair_dim, number * width + (p + 2) * pair_dim)
                if fresh:
                    sum_ref[:, cols] = product
                else:
                    sum_ref[:, cols] += product

        staged(len(items), compare, weigh, combine)

    @pl.when(block == 0)
    def _():
        attend(q_len, [s * q_len for s in range(q_dev)], [qlen_ref[s] for s in range(q_dev)], True)

    @pl.when(block > 0)
    def _():
        attend(rows_all, [0], [plen_ref[jnp.maximum(block - 1, 0)]], False)

    @pl.when(block == pl.num_programs(0) - 1)
    def _():
        tails = None
        if extra:
            tails = small_rows([*extra, stat_ref], send_ref.shape[0] * 2, send_ref.shape[2])
        store_shards(core_ref, sum_ref[...], send_ref, keep_ref, tails=tails)


def input_grad_kernel(grad_ref, base_ref, wq_ref, wk_ref, wv_ref, *out_refs):
    wide = wq_ref.shape[1]
    total = base_ref[...].astype(F32)
    for number, w_ref in enumerate((wq_ref, wk_ref, wv_ref)):
        total = total + mm_nt(grad_ref[:, number * wide : (number + 1) * wide], w_ref[...])
    low = total.astype(LOW)
    if len(out_refs) == 1:
        out_refs[0][...] = low
        return

    @pl.when(pl.program_id(0) == 0)
    def _():
        out_refs[0][...] = low

    @pl.when(pl.program_id(0) > 0)
    def _():
        out_refs[1][...] = low


def weight_grad_kernel(core_ref, left_ref, right_ref, send_ref, keep_ref):
    store_shards(core_ref, mm(left_ref[...], right_ref[...]), send_ref, keep_ref)


def small_rows(refs, count, wide):
    two, one, inner, *attn = [ref[...] for ref in refs]
    eight = jnp.concatenate(
        [jnp.concatenate([item[0:2] for item in attn], 1), one[2:3], two[2:3], one[0:2], two[0:2]], 0
    )
    inner = inner[0:1]
    short, long = eight.shape[1] // count, inner.shape[1] // count
    rows = []
    for shard in range(count):
        top = eight[:, shard * short : (shard + 1) * short]
        low = inner[:, shard * long : (shard + 1) * long]
        top = jnp.concatenate([top, jnp.zeros((8, wide - short), F32)], 1)
        low = jnp.concatenate([low, jnp.zeros((1, wide - long), F32)], 1)
        rows.append(jnp.concatenate([top, low, jnp.zeros((7, wide), F32)], 0).astype(LOW))
    return rows


def turn_kernel(part_ref, out_ref):
    out_ref[...] = part_ref[...].astype(F32).T


def turn_low_kernel(*refs):
    *inputs, out_ref = refs
    if len(inputs) == 1:
        out_ref[...] = inputs[0][...].T
        return

    @pl.when(pl.program_id(0) == 0)
    def _():
        out_ref[...] = inputs[0][...].T

    @pl.when(pl.program_id(0) > 0)
    def _():
        out_ref[...] = inputs[1][...].T


def const_spec(shape):
    return pl.BlockSpec(shape, lambda i: (0,) * len(shape), pipeline_mode=pl.Buffered(1))


def call(body, operands, in_specs, outs, grid, room, deps=(), old=(), name=None, scratch=(), us=10):
    count, extra = len(operands), len(old)
    if deps:
        tied = min(range(count), key=lambda i: operands[i].size)
        operands = list(operands)
        operands[tied] = lax.optimization_barrier((operands[tied], *deps))[0]

    def kernel(*refs):
        body(*refs[:count], *refs[count + extra :])

    return pl.pallas_call(
        kernel,
        grid=grid,
        in_specs=list(in_specs) + [pl.BlockSpec(memory_space=pl.ANY)] * extra,
        out_specs=[spec for spec, _ in outs],
        out_shape=[kind for _, kind in outs],
        scratch_shapes=scratch,
        input_output_aliases={count + i: i for i in range(extra)},
        compiler_params=pltpu.CompilerParams(vmem_limit_bytes=room * 1024 * 1024),
        cost_estimate=pl.CostEstimate(flops=int(us * 1.15e7), bytes_accessed=0, transcendentals=0),
        name=name,
    )(*operands, *old)


def weight_grad(left_t, right, row_count, core, deps, old):
    height, depth = left_t.shape
    wide = right.shape[1]
    block = min(wide, 768)
    shape = old[0].shape
    spec = pl.BlockSpec((*shape[:2], block), lambda i: (0, 0, i))
    return call(
        weight_grad_kernel,
        (core, left_t, right),
        [
            pl.BlockSpec(memory_space=pltpu.SMEM),
            const_spec((height, depth)),
            pl.BlockSpec((depth, block), lambda i: (0, i)),
        ],
        [(spec, jax.ShapeDtypeStruct(shape, LOW))] * 2,
        (wide // block,),
        56,
        deps,
        old,
        name="weight_grad",
        us=12,
    )


def add_kernel(*refs):
    *terms, out_ref = refs
    out_ref[...] = sum([ref[...].astype(F32) for ref in terms[1:]], terms[0][...].astype(F32)).astype(LOW)


def add_all(terms):
    shape = terms[0].shape
    spec = pl.BlockSpec(shape, lambda i: (0,) * len(shape), pipeline_mode=pl.Buffered(1))
    outs = [(spec, jax.ShapeDtypeStruct(shape, LOW))]
    return call(add_kernel, terms, [spec] * len(terms), outs, (1,), 24, name="add_all", us=20_000)[0]


class Flow:
    def __init__(self, sent, kept, line=False, fused=False):
        bits = lax.axis_size("row").bit_length() - 1
        self.order = [(0,)] + [tuple(range(i, min(i + 2, bits))) for i in range(1, bits, 2)]
        self.left = list(range(bits - 1, 0, -1))
        count = lax.axis_size("col")
        self.line = [(None, [(i, i ^ (1 << bit)) for i in range(count)]) for bit in range(count.bit_length() - 1)]
        if line:
            half = count // 2
            self.line = [(None, [(i, i + 1), (count - 1 - i, count - 2 - i)]) for i in range(half - 1)]
            self.line += [(None, [(half - 1, half), (half, half - 1)])]
            self.line += [
                ((i, count - 1 - i), [(i + 1, i), (count - 2 - i, count - 1 - i)])
                for i in range(half - 2, -1, -1)
            ]
        self.sent, self.kept, self.got, self.fused = [sent], kept, None, fused

    def shard(self, terms, bits, mask):
        here = lax.axis_index("row")
        order = [self.left.index(bit) for bit in bits]
        total = None
        for term in terms:
            starts, sizes = [0] * term.ndim, list(term.shape)
            for axis, bit in zip(order, bits):
                starts[axis], sizes[axis] = ((here ^ mask) >> bit) & 1, 1
            piece = lax.dynamic_slice(term, starts, sizes)
            piece = piece.reshape([size for i, size in enumerate(sizes) if i not in order]).astype(F32)
            total = piece if total is None else total + piece
        return total.astype(LOW)

    def step(self):
        if self.order:
            bits = self.order[0]
            masks = [
                sum(1 << bit for i, bit in enumerate(bits) if other >> i & 1)
                for other in range(1, 1 << len(bits))
            ]
            if bits != (0,):
                terms = [self.kept, *self.got]
                self.sent = [self.shard(terms, bits, mask) for mask in masks]
                self.kept = self.shard(terms, bits, 0)
                self.left = [bit for bit in self.left if bit not in bits]
            size = lax.axis_size("row")
            self.got = [
                lax.ppermute(sent, "row", [(i, i ^ mask) for i in range(size)])
                for sent, mask in zip(self.sent, masks)
            ]
        else:
            self.sent = [self.kept]
            self.got = [lax.ppermute(self.kept, "col", self.line[0][1])]

    def land(self, token=None):
        if token is not None:
            self.kept = lax.optimization_barrier((self.kept, token))[0]
        got = self.got
        if self.order:
            bits = self.order.pop(0)
            if bits == (0,):
                dims = (2,) * len(self.left) + self.kept.shape[1:]
                self.kept, self.got = self.kept.reshape(dims), [item.reshape(dims) for item in self.got]
            if not self.order and self.fused:
                self.kept = add_all([self.kept, *self.got])
            elif not self.order:
                self.kept = sum([item.astype(F32) for item in self.got], self.kept.astype(F32)).astype(LOW)
        else:
            ends, _ = self.line.pop(0)
            if ends is None:
                self.kept = self.kept + self.got[0]
            else:
                here = lax.axis_index("col")
                self.kept = jnp.where((here == ends[0]) | (here == ends[1]), self.got[0], self.kept)
        return got

    def turn(self, token=None):
        got = self.land(token)
        if self.done:
            return got
        self.step()
        return got + self.sent

    @property
    def done(self):
        return not self.order and not self.line


def gather_all(piece):
    row_bits = lax.axis_size("row").bit_length() - 1
    col_bits = lax.axis_size("col").bit_length() - 1
    steps = [("col", tuple(range(i, min(i + 2, col_bits)))) for i in range(0, col_bits, 2)]
    steps += [("row", tuple(range(i, min(i + 2, row_bits)))) for i in range(1, row_bits, 2)]
    for name, bits in steps + [("row", (0,))]:
        here = lax.axis_index(name)
        pieces = [piece]
        for other in range(1, 1 << len(bits)):
            mask = sum(1 << bit for i, bit in enumerate(bits) if other >> i & 1)
            pairs = [(i, i ^ mask) for i in range(lax.axis_size(name))]
            pieces.append(lax.ppermute(piece, name, pairs))
        for i, bit in enumerate(bits):
            high = ((here >> bit) & 1) == 1
            pieces = [
                jnp.where(high, pieces[place ^ (1 << i)], pieces[place]) for place in range(len(pieces))
            ]
        piece = jnp.concatenate(pieces, 0)
    return piece


def per_device(
    query_tokens, passage_tokens, query_lengths, passage_lengths, positives,
    w_query, w_key, w_value, w_attn_out, w_inner, w_outer,
    bias_query, bias_value, bias_attn_out, bias_inner, bias_outer,
    gain_one, shift_one, gain_two, shift_two,
):
    q_dev, q_len, width = query_tokens.shape
    p_dev, p_len, _ = passage_tokens.shape
    inner = w_inner.shape[1]
    rows_all = p_len
    assert q_dev * q_len == rows_all and q_dev + p_dev <= SLOTS
    blocks = 1 + p_dev
    total_rows = blocks * rows_all
    row_count = lax.axis_size("row")
    col_count = lax.axis_size("col")
    row_here = lax.axis_index("row")
    core = (row_here & 1).reshape(1)
    me = (row_here * col_count + lax.axis_index("col")).reshape(1)
    params = pltpu.CompilerParams(vmem_limit_bytes=VMEM)
    smem = pl.BlockSpec(memory_space=pltpu.SMEM)

    def by_block(wide):
        return pl.BlockSpec((rows_all, wide), lambda i: (i, 0))

    def by_block_t(high):
        return pl.BlockSpec((high, rows_all), lambda i: (0, i))

    def fixed(shape):
        return pl.BlockSpec(shape, lambda i: (0,) * len(shape))

    queries_spec = pl.BlockSpec((rows_all, width), lambda i: (0, 0))
    passages_spec = pl.BlockSpec((rows_all, width), lambda i: (jnp.maximum(i - 1, 0), 0))

    lse_spec = pl.BlockSpec((1, HEADS // 2, 8, rows_all), lambda i: (i, 0, 0, 0))

    def shape(*dims, kind=LOW):
        return jax.ShapeDtypeStruct(dims, kind)

    queries = query_tokens.reshape(rows_all, width)
    passages = passage_tokens.reshape(p_dev * rows_all, width)
    square = const_spec((width, width))
    anywhere = pl.BlockSpec(memory_space=pl.ANY)
    thin = const_spec((width,))

    q, k, v, ctx_t, lse = call(
        partial(attend_kernel, (q_dev, q_len, rows_all, width)),
        (query_lengths, passage_lengths, queries, passages, w_query, w_key, w_value, bias_query, bias_value),
        [smem, smem, queries_spec, passages_spec, square, square, square, thin, thin],
        [(by_block(width), shape(total_rows, width))] * 3
        + [
            (by_block_t(width), shape(width, total_rows)),
            (lse_spec, shape(blocks, HEADS // 2, 8, rows_all, kind=F32)),
        ],
        (blocks,),
        56,
        name="attend",
        us=25,
    )

    rows_part = rows_all // 2
    parts = 2 * blocks

    def by_part(wide):
        return pl.BlockSpec((rows_part, wide), lambda i: (i, 0))

    queries_part = pl.BlockSpec((rows_part, width), lambda i: (jnp.minimum(i, 1), 0))
    passages_part = pl.BlockSpec((rows_part, width), lambda i: (jnp.maximum(i - 2, 0), 0))
    h1, y1, act, slope, h2, query_out, passage_out, pooled, payload = call(
        partial(dense_kernel, (q_dev, q_len, p_len, width, inner)),
        (
            query_lengths, passage_lengths, positives, queries, passages, ctx_t, w_attn_out, w_inner, w_outer,
            bias_attn_out, bias_inner, bias_outer, gain_one, shift_one, gain_two, shift_two,
        ),
        [smem, smem, smem, queries_part, passages_part, pl.BlockSpec((width, rows_part), lambda i: (0, i))]
        + [anywhere] * 3
        + [thin, const_spec((inner,))]
        + [thin] * 5,
        [
            (by_part(width), shape(total_rows, width)),
            (by_part(width), shape(total_rows, width)),
            (by_part(inner), shape(total_rows, inner)),
            (by_part(inner), shape(total_rows, inner)),
            (by_part(width), shape(total_rows, width)),
            (queries_part, shape(rows_all, width)),
            (passages_part, shape(p_dev * rows_all, width)),
            (fixed((SLOTS, width)), shape(SLOTS, width, kind=F32)),
            (fixed((SLOTS, width + 128)), shape(SLOTS, width + 128)),
        ],
        (parts,),
        56,
        name="dense",
        scratch=[
            pltpu.VMEM((width, width), LOW),
            pltpu.VMEM((width, inner), LOW),
            pltpu.VMEM((inner, width), LOW),
            pltpu.SemaphoreType.DMA((3,)),
        ],
        us=40,
    )

    gathered = gather_all(payload)
    loss, gvec = pl.pallas_call(
        partial(loss_kernel, (q_dev, p_dev, width, col_count)),
        in_specs=[smem] * 3 + [pl.BlockSpec(memory_space=pltpu.VMEM)] * 3,
        out_specs=[pl.BlockSpec(memory_space=pltpu.VMEM)] * 2,
        out_shape=[shape(8, 128, kind=F32), shape(SLOTS, width, kind=F32)],
        compiler_params=params,
        name="loss",
    )(me, query_lengths, passage_lengths, payload, gathered, pooled)

    smalls = shape(8, width, kind=F32)
    cut = width // row_count
    cut_inner = inner // row_count
    half = row_count // 2
    step_cols = 768
    per_step = step_cols // cut_inner
    outer_spec = pl.BlockSpec((per_step // 2, width, cut_inner), lambda i: (i, 0, 0))
    grad_f, stat_two, *outer_parts = call(
        partial(outer_grad_kernel, (q_dev, q_len, p_len)),
        (core, query_lengths, passage_lengths, gvec, h2, gain_two, act),
        [smem, smem, smem, fixed((SLOTS, width)), const_spec((total_rows, width)), thin]
        + [pl.BlockSpec((total_rows, step_cols), lambda i: (0, i))],
        [
            (fixed((total_rows, width)), shape(total_rows, width)),
            (fixed((8, width)), smalls),
            (outer_spec, shape(half, width, cut_inner)),
            (outer_spec, shape(half, width, cut_inner)),
        ],
        (inner // step_cols,),
        56,
        name="outer_grad",
        scratch=[pltpu.VMEM((width, total_rows), LOW)],
        us=16,
    )
    outer = Flow(*outer_parts, line=True)
    outer.step()

    def turn(arrays, specs, deps):
        outs = [(by_block_t(width), shape(width, total_rows))]
        return call(turn_low_kernel, arrays, specs, outs, (blocks,), 56, deps, name="turn", us=3)[0]

    y1_t = turn([y1], [by_block(width)], outer.sent)
    deps = outer.turn(y1_t)
    attn_spec = pl.BlockSpec((half, cut, width), lambda i: (0, 0, inner // width))
    grad_u, grad_attn, grad_ctx, stat_one, grad_bias_inner, *up_parts = call(
        partial(dense_back_kernel, (rows_all, width, inner)),
        (core, grad_f, slope, h1, ctx_t, w_outer, w_inner, w_attn_out, gain_one),
        [smem, by_block(width), by_block(inner), by_block(width), by_block_t(width)]
        + [anywhere, anywhere, anywhere, thin],
        [
            (by_block(inner), shape(total_rows, inner)),
            (by_block(width), shape(total_rows, width)),
            (by_block(width), shape(total_rows, width)),
            (fixed((8, width)), smalls),
            (fixed((8, inner)), shape(8, inner, kind=F32)),
            (attn_spec, shape(half, cut, inner + width)),
            (attn_spec, shape(half, cut, inner + width)),
        ],
        (blocks,),
        60,
        deps,
        name="dense_back",
        scratch=[
            pltpu.VMEM((width, width), F32),
            pltpu.VMEM((inner, width), LOW),
            pltpu.VMEM((width, inner), LOW),
            pltpu.VMEM((width, width), LOW),
            pltpu.SemaphoreType.DMA((5,)),
        ],
        us=30,
    )
    deps = outer.turn(stat_one)
    up_flow = Flow(*weight_grad(y1_t, grad_u, row_count, core, deps, up_parts), line=True, fused=True)
    up_flow.step()
    x_t = turn([queries, passages], [queries_spec, passages_spec], up_flow.sent)
    deps = up_flow.turn(x_t)

    head_dim = width // HEADS
    third = 4 * head_dim
    groups = [(0, 2 * third), (2 * third, third)]

    def attend_back(start, wide, deps, extra=()):
        pairs = wide // (2 * head_dim)
        index = start // wide
        cols = pl.BlockSpec((rows_all, wide), lambda i: (i, index))
        rows = cut + (16 if extra else 0)
        return call(
            partial(attend_back_kernel, (q_dev, q_len, rows_all, head_dim)),
            (core, query_lengths, passage_lengths, q, k, v, ctx_t, lse, grad_ctx, x_t, *extra),
            [smem, smem, smem]
            + [cols] * 3
            + [
                pl.BlockSpec((wide, rows_all), lambda i: (index, i)),
                pl.BlockSpec((1, pairs, 8, rows_all), lambda i: (i, index, 0, 0)),
                cols,
                by_block_t(width),
            ]
            + [const_spec(item.shape) for item in extra],
            [
                (by_block(3 * wide), shape(total_rows, 3 * wide)),
                (fixed((8, wide)), shape(8, wide, kind=F32)),
            ]
            + [(fixed((half, rows, 3 * wide)), shape(half, rows, 3 * wide))] * 2,
            (blocks,),
            56,
            deps,
            name="attend_back",
            scratch=[pltpu.VMEM((width, 3 * wide), F32)],
            us=12,
        )

    def input_grad(start, wide, grad, base, outs, deps):
        index = start // wide
        cols = pl.BlockSpec((width, wide), lambda i: (0, index), pipeline_mode=pl.Buffered(1))
        return call(
            input_grad_kernel,
            (grad, base, w_query, w_key, w_value),
            [by_block(3 * wide), by_block(width), cols, cols, cols],
            outs,
            (blocks,),
            56,
            deps,
            name="input_grad",
            us=6,
        )

    grad_a, stat_a, *mixed_parts = attend_back(*groups[0], deps)
    mixed_flow = Flow(*mixed_parts)
    mixed_flow.step()
    deps = mixed_flow.sent + outer.turn(stat_a)
    (part_grad,) = input_grad(
        *groups[0], grad_a, grad_attn, [(by_block(width), shape(total_rows, width))], deps
    )
    deps = up_flow.turn(part_grad) + mixed_flow.turn(up_flow.kept)
    extra = (stat_two, stat_one, grad_bias_inner, stat_a)
    grad_b, stat_b, *last_parts = attend_back(*groups[1], deps, extra)
    last_flow = Flow(*last_parts)
    last_flow.step()
    deps = last_flow.sent + outer.turn(stat_b) + mixed_flow.turn(stat_b) + up_flow.turn(stat_b)
    query_grad, passage_grad = input_grad(
        *groups[1],
        grad_b,
        part_grad,
        [
            (queries_spec, shape(rows_all, width)),
            (passages_spec, shape(p_dev * rows_all, width)),
        ],
        deps,
    )
    last_flow.turn(passage_grad)
    mixed_flow.turn(last_flow.kept)
    outer.turn(mixed_flow.kept)
    last_flow.turn(outer.kept)
    up_flow.turn(last_flow.kept)
    last_flow.turn(up_flow.kept)
    mixed_flow.turn(last_flow.kept)
    last_flow.turn(mixed_flow.kept)
    flows = [outer, up_flow, mixed_flow, last_flow]
    while not all(flow.done for flow in flows):
        for flow in flows:
            if not flow.done:
                flow.turn()
    turned = pl.pallas_call(
        turn_kernel,
        out_shape=shape(cut_inner, width, kind=F32),
        compiler_params=params,
        name="turn",
    )(outer.kept)
    mixed, last = mixed_flow.kept.astype(F32), last_flow.kept.astype(F32)
    qkv = [
        jnp.concatenate(
            [mixed[:, i * 2 * third : (i + 1) * 2 * third], last[:cut, i * third : (i + 1) * third]], 1
        )
        for i in range(3)
    ]
    up_sum = up_flow.kept.astype(F32)
    small = last[cut:]
    return (
        loss[0, 0],
        query_out.reshape(query_tokens.shape),
        passage_out.reshape(passage_tokens.shape),
        query_grad.reshape(query_tokens.shape),
        passage_grad.reshape(passage_tokens.shape),
        *qkv,
        up_sum[:, inner:],
        up_sum[:, :inner],
        turned,
        *[small[i, :cut] for i in range(3)],
        small[8, : inner // row_count],
        *[small[i, :cut] for i in range(3, 8)],
    )


def solution(mesh):
    in_specs = (
        P(("row", "col"), None, None),
        P(("row", "col"), None, None),
        P(("row", "col")),
        P(("row", "col")),
        P(("row", "col")),
        P(),
        P(),
        P(),
        P(),
        P(),
        P(),
        P(),
        P(),
        P(),
        P(),
        P(),
        P(),
        P(),
        P(),
        P(),
    )
    out_specs = (
        P(),
        P(("row", "col"), None, None),
        P(("row", "col"), None, None),
        P(("row", "col"), None, None),
        P(("row", "col"), None, None),
        P("row", None),
        P("row", None),
        P("row", None),
        P("row", None),
        P("row", None),
        P("row", None),
        P("row"),
        P("row"),
        P("row"),
        P("row"),
        P("row"),
        P("row"),
        P("row"),
        P("row"),
        P("row"),
    )
    return jax.shard_map(
        per_device, mesh=mesh, in_specs=in_specs, out_specs=out_specs, check_vma=False
    )
```

```python
from functools import partial

import jax
import jax.numpy as jnp
from jax import lax
from jax.experimental import pallas as pl
from jax.experimental.pallas import tpu as pltpu
from jax.sharding import PartitionSpec as P

HEADS = 12
EPS_NORM = 1e-12
EPS_POOL = 1e-06
SCALE_LOSS = 128.0
INV_TEMP = 100.0
TILE = 256
SLOTS = 8
VMEM = 60 * 1024 * 1024
LOW = jnp.bfloat16
F32 = jnp.float32


def mm(left, right):
    return lax.dot_general(left, right, (((1,), (0,)), ((), ())), preferred_element_type=F32)


def mm_nt(left, right):
    return lax.dot_general(left, right, (((1,), (1,)), ((), ())), preferred_element_type=F32)


def norm_parts(hidden):
    center = hidden - jnp.mean(hidden, -1, keepdims=True)
    spread = jnp.mean(center * center, -1, keepdims=True)
    scale = lax.rsqrt(spread + EPS_NORM)
    return center * scale, scale


def gelu_parts(u):
    square = u * u
    q = 1.4250060785476853e-06
    for factor in (-3.669345091379551e-05, -8.782652731110375e-05, 0.03639228618131223, 0.7978697123041883):
        q = q * square + factor
    share = 0.5 + 0.5 * jnp.tanh(u * q)
    bell = jnp.exp(-0.5 * square)
    return u * share, share + (0.3989422804014327 * u) * bell


def vec(ref, cols=slice(None)):
    return ref[cols].reshape(1, -1)


def rows_of(step, size):
    return pl.ds(pl.multiple_of(step * size, size), size)


def part_owner(part, q_dev, q_len, p_len, qlen_ref, plen_ref):
    per = p_len // q_len
    beyond = jnp.maximum(part - q_dev, 0)
    is_query = part < q_dev
    slot = jnp.where(is_query, part, q_dev + beyond // per)
    length = jnp.where(is_query, qlen_ref[jnp.where(is_query, part, 0)], plen_ref[beyond // per])
    first = jnp.where(is_query, 0, beyond % per * q_len)
    return slot, length, first


def live_rows(first, length, size):
    return (first + lax.broadcasted_iota(jnp.int32, (size, 1), 0)) < length


def sure_rows(size):
    return size * 4 // 5 // 16 * 16


def half_only(pair_t, which):
    half = pair_t.shape[0] // 2
    zeros = jnp.zeros((half, pair_t.shape[1]), pair_t.dtype)
    if which == 0:
        return jnp.concatenate([pair_t[:half], zeros], 0)
    return jnp.concatenate([zeros, pair_t[half:]], 0)


def staged(count, *stages):
    for step in range(count + len(stages) - 1):
        for late, stage in enumerate(stages):
            if 0 <= step - late < count:
                stage(step - late)


def fetch(source, target, sems, index):
    return pltpu.make_async_copy(source, target, sems.at[index])


def attend_kernel(
    dims, qlen_ref, plen_ref, xq_ref, xp_ref, wq_ref, wk_ref, wv_ref, bq_ref, bv_ref,
    q_ref, k_ref, v_ref, ctx_t_ref, lse_ref,
):
    q_dev, q_len, rows_all, width = dims
    block = pl.program_id(0)
    head_dim = width // HEADS
    x = jnp.where(block == 0, xq_ref[...], xp_ref[...])
    q = ((mm(x, wq_ref[...]) + vec(bq_ref)) * head_dim**-0.5).astype(LOW)
    k = mm(x, wk_ref[...]).astype(LOW)
    v = (mm(x, wv_ref[...]) + vec(bv_ref)).astype(LOW)
    q_ref[...] = q
    k_ref[...] = k
    v_ref[...] = v
    q_t, v_t = q.T, v.T

    def attend(size, starts, lengths):
        items = [(start, length, head) for head in range(HEADS) for start, length in zip(starts, lengths)]
        scores, weights = {}, {}

        def compare(i):
            start, length, head = items[i]
            cols = slice(head // 2 * 2 * head_dim, (head // 2 + 1) * 2 * head_dim)
            here = slice(start, start + size)
            scores[i] = mm(k[here, cols], half_only(q_t[cols, here], head % 2))

        def weigh(i):
            start, length, head = items[i]
            edge = sure_rows(size)
            early, late = scores[i][:edge], scores.pop(i)[edge:]
            late = jnp.where(live_rows(edge, length, size - edge), late, -1e30)
            top = jnp.maximum(jnp.max(early, 0, keepdims=True), jnp.max(late, 0, keepdims=True))
            weights[i] = top, jnp.concatenate([jnp.exp(early - top).astype(LOW), jnp.exp(late - top).astype(LOW)], 0)

        def combine(i):
            start, length, head = items[i]
            here, rows = slice(start, start + size), slice(head * head_dim, (head + 1) * head_dim)
            top, weight = weights.pop(i)
            values = jnp.concatenate([v_t[rows, here], jnp.ones((16, size), LOW)], 0)
            result = mm(values, weight)
            total = result[head_dim : head_dim + 1]
            lse_ref[0, head // 2, head % 2 : head % 2 + 1, here] = top + jnp.log(total)
            ctx_t_ref[rows, here] = (result[:head_dim] * (1.0 / total)).astype(LOW)

        staged(len(items), compare, weigh, combine)

    @pl.when(block == 0)
    def _():
        attend(q_len, [s * q_len for s in range(q_dev)], [qlen_ref[s] for s in range(q_dev)])

    @pl.when(block > 0)
    def _():
        attend(rows_all, [0], [plen_ref[jnp.maximum(block - 1, 0)]])


def dense_kernel(
    dims, qlen_ref, plen_ref, pos_ref, xq_ref, xp_ref, ctx_t_ref, wo_hbm, wi_hbm, wf_hbm,
    bo_ref, bi_ref, bf_ref, g1_ref, s1_ref, g2_ref, s2_ref,
    h1_ref, y1_ref, act_ref, dg_ref, h2_ref, yq_ref, yp_ref, pool_ref, pay_ref,
    wo_ref, wi_ref, wf_ref, sems,
):
    q_dev, q_len, p_len, width, inner = dims
    block = pl.program_id(0)
    rows_all = xq_ref.shape[0]
    query_blocks = q_dev * q_len // rows_all
    copies = [
        fetch(source, target, sems, index)
        for index, (source, target) in enumerate([(wo_hbm, wo_ref), (wi_hbm, wi_ref), (wf_hbm, wf_ref)])
    ]

    @pl.when(block == 0)
    def _():
        for copy in copies:
            copy.start()
        pool_ref[...] = jnp.zeros_like(pool_ref)
        copies[0].wait()

    x = jnp.where(block < query_blocks, xq_ref[...], xp_ref[...])
    hidden = x.astype(F32) + (mm(ctx_t_ref[...].T, wo_ref[...]) + vec(bo_ref))
    h1_ref[...] = hidden.astype(LOW)
    y1 = norm_parts(hidden)[0] * vec(g1_ref) + vec(s1_ref)
    y1_low = y1.astype(LOW)
    y1_ref[...] = y1_low

    @pl.when(block == 0)
    def _():
        copies[1].wait()
        copies[2].wait()

    group = width // TILE
    raw, made = {}, {}
    sums = [y1[:, n * TILE : (n + 1) * TILE] + vec(bf_ref, slice(n * TILE, (n + 1) * TILE)) for n in range(group)]

    def expand(i):
        cols = slice(i * TILE, (i + 1) * TILE)
        raw[i] = mm(y1_low, wi_ref[:, cols]) + vec(bi_ref, cols)

    def activate(i):
        cols = slice(i * TILE, (i + 1) * TILE)
        act, slope = gelu_parts(raw.pop(i))
        made[i] = act.astype(LOW)
        act_ref[:, cols] = made[i]
        dg_ref[:, cols] = slope.astype(LOW)

    def contract(i):
        first, n = i // group * group, i % group
        left = jnp.concatenate([made[first + j] for j in range(group)], 1)
        cols = slice(n * TILE, (n + 1) * TILE)
        sums[n] = sums[n] + mm(left, wf_ref[first * TILE : (first + group) * TILE, cols])

    late = [lambda i: None] * (group - 1)
    staged(inner // TILE, expand, activate, *late, contract)

    total = jnp.concatenate(sums, 1)
    h2_ref[...] = total.astype(LOW)
    y2 = norm_parts(total)[0] * vec(g2_ref) + vec(s2_ref)
    for part in range(rows_all // q_len):
        number = block * (rows_all // q_len) + part
        slot, length, first = part_owner(number, q_dev, q_len, p_len, qlen_ref, plen_ref)
        piece = y2[part * q_len : (part + 1) * q_len]
        summed = jnp.sum(jnp.where(live_rows(first, length, q_len), piece, 0.0), 0, keepdims=True)
        in_slot = lax.broadcasted_iota(jnp.int32, (SLOTS, 1), 0) == slot
        pool_ref[...] += jnp.where(in_slot, summed / length.astype(F32), 0.0)

    @pl.when(block < query_blocks)
    def _():
        yq_ref[...] = y2.astype(LOW)

    @pl.when(block >= query_blocks)
    def _():
        yp_ref[...] = y2.astype(LOW)

    @pl.when(block == pl.num_programs(0) - 1)
    def _():
        pooled = pool_ref[...]
        emb = pooled * lax.rsqrt(jnp.sum(pooled * pooled, -1, keepdims=True) + EPS_POOL)
        pay_ref[:, :width] = emb.astype(LOW)
        row = lax.broadcasted_iota(jnp.int32, (SLOTS, 128), 0)
        col = lax.broadcasted_iota(jnp.int32, (SLOTS, 128), 1)
        place = jnp.zeros((SLOTS, 128), jnp.int32)
        for j in range(q_dev):
            high = pos_ref[j] // 128
            low = pos_ref[j] - high * 128
            place = jnp.where(row == j, jnp.where(col == 0, high, jnp.where(col == 1, low, 0)), place)
        pay_ref[:, width:] = place.astype(F32).astype(LOW)


def loss_kernel(
    dims, me_ref, qlen_ref, plen_ref, own_ref, all_ref, pool_ref, loss_ref, gvec_ref
):
    q_dev, p_dev, width, col_count = dims
    count = all_ref.shape[0]
    every = all_ref[:, :width]
    own = own_ref[:, :width]

    def passage_mask(index):
        spot, place = index % SLOTS, index // SLOTS
        per_core = count // SLOTS // 2
        core, rest = place // per_core, place % per_core
        device = (rest // col_count * 2 + core) * col_count + rest % col_count
        return (spot >= q_dev) & (spot < q_dev + p_dev), device * p_dev + spot - q_dev

    scores = mm_nt(own, every) * INV_TEMP
    valid, ident = passage_mask(lax.broadcasted_iota(jnp.int32, (SLOTS, count), 1))
    scores = jnp.where(valid, scores, -1e30)
    top = jnp.max(scores, -1, keepdims=True)
    totals = top + jnp.log(jnp.sum(jnp.exp(scores - top), -1, keepdims=True))
    marks = own_ref[:, width:].astype(F32)
    wanted = marks[:, 0:1] * 128.0 + marks[:, 1:2]
    target = (valid & (ident.astype(F32) == wanted)).astype(F32)
    raw = (INV_TEMP * (SCALE_LOSS * (jnp.exp(scores - totals) - target))).astype(LOW)
    grad_q = mm(raw, every)

    picker_col = lax.broadcasted_iota(jnp.int32, (SLOTS, 128), 1)
    picker = jnp.where(picker_col == 0, 128.0, jnp.where(picker_col == 1, 1.0, 0.0)).astype(LOW)
    own_row = lax.broadcasted_iota(jnp.int32, (SLOTS, TILE), 0)
    own_valid = (own_row >= q_dev) & (own_row < q_dev + p_dev)
    own_ident = (me_ref[0] * p_dev + own_row - q_dev).astype(F32)

    def body(step, carry):
        total_loss, grad_p = carry
        rows = rows_of(step, TILE)
        some = all_ref[rows, :width]
        place = mm_nt(picker, all_ref[rows, width:])[0:1]
        table = mm_nt(every, some) * INV_TEMP
        ok, names = passage_mask(lax.broadcasted_iota(jnp.int32, (count, TILE), 0))
        picked = jnp.sum(jnp.where(ok & (names.astype(F32) == place), table, 0.0), 0, keepdims=True)
        table = jnp.where(ok, table, -1e30)
        high = jnp.max(table, 0, keepdims=True)
        lse = high + jnp.log(jnp.sum(jnp.exp(table - high), 0, keepdims=True))
        is_query = lax.broadcasted_iota(jnp.int32, (1, TILE), 1) % SLOTS < q_dev
        losses = jnp.where(is_query, lse - picked, 0.0)
        mine = mm_nt(own, some) * INV_TEMP
        hit = (own_ident == place).astype(F32)
        grads = INV_TEMP * (SCALE_LOSS * (jnp.exp(mine - lse) - hit))
        grads = jnp.where(own_valid & is_query, grads, 0.0).astype(LOW)
        return total_loss + jnp.sum(losses, 1, keepdims=True), grad_p + mm(grads, some)

    start = (jnp.zeros((1, 1), F32), jnp.zeros((SLOTS, width), F32))
    total_loss, grad_p = lax.fori_loop(0, count // TILE, body, start)
    loss_ref[...] = jnp.broadcast_to(total_loss / float(count // SLOTS * q_dev), loss_ref.shape)

    slot = lax.broadcasted_iota(jnp.int32, (SLOTS, 1), 0)
    grad = jnp.where(slot < q_dev, grad_q, grad_p)
    pooled = pool_ref[...]
    r = lax.rsqrt(jnp.sum(pooled * pooled, -1, keepdims=True) + EPS_POOL)
    inside = jnp.sum(pooled * grad, -1, keepdims=True)
    length = jnp.ones((SLOTS, 1), F32)
    for j in range(q_dev):
        length = jnp.where(slot == j, qlen_ref[j].astype(F32), length)
    for j in range(p_dev):
        length = jnp.where(slot == q_dev + j, plen_ref[j].astype(F32), length)
    gvec_ref[...] = (r * grad - r * r * r * inside * pooled) / length


def store_shards(core_ref, result, send_ref, keep_ref, by_row=True, tails=None):
    count = send_ref.shape[0] * 2
    size = result.shape[0 if by_row else 1] // count

    def store(even, odd):
        for shard in range(count):
            spot = slice(shard * size, (shard + 1) * size)
            piece = (result[spot, :] if by_row else result[:, spot]).astype(LOW)
            target = odd if shard % 2 else even
            if tails is None:
                target[shard // 2] = piece
            else:
                target[shard // 2, :size] = piece
                target[shard // 2, size:] = tails[shard]

    @pl.when(core_ref[0] == 0)
    def _():
        store(keep_ref, send_ref)

    @pl.when(core_ref[0] == 1)
    def _():
        store(send_ref, keep_ref)


def outer_grad_kernel(
    dims, core_ref, qlen_ref, plen_ref, gvec_ref, h2_ref, g2_ref, act_ref,
    gf_ref, stat_ref, send_ref, keep_ref, gf_t_ref,
):
    q_dev, q_len, p_len = dims

    @pl.when(pl.program_id(0) == 0)
    def _():
        stat_ref[...] = jnp.zeros_like(stat_ref)

        def body(part, carry):
            rows = rows_of(part, q_len)
            slot, length, first = part_owner(part, q_dev, q_len, p_len, qlen_ref, plen_ref)
            in_slot = lax.broadcasted_iota(jnp.int32, (SLOTS, 1), 0) == slot
            grad_y = jnp.sum(jnp.where(in_slot, gvec_ref[...], 0.0), 0, keepdims=True)
            live = live_rows(first, length, q_len)
            n2, r2 = norm_parts(h2_ref[rows, :].astype(F32))
            g = grad_y * vec(g2_ref)
            grad = r2 * (g - jnp.mean(g, -1, keepdims=True) - n2 * jnp.mean(g * n2, -1, keepdims=True))
            grad = jnp.where(live, grad, 0.0)
            low = grad.astype(LOW)
            gf_ref[rows, :] = low
            gf_t_ref[:, rows] = low.T
            stat_ref[0:1, :] += grad_y * jnp.sum(jnp.where(live, n2, 0.0), 0, keepdims=True)
            stat_ref[1:2, :] += grad_y * jnp.sum(live.astype(F32), 0, keepdims=True)
            stat_ref[2:3, :] += jnp.sum(low.astype(F32), 0, keepdims=True)
            return carry

        lax.fori_loop(0, h2_ref.shape[0] // q_len, body, 0)

    store_shards(core_ref, mm(gf_t_ref[...], act_ref[...]), send_ref, keep_ref, by_row=False)


def dense_back_kernel(
    dims, core_ref, gf_ref, dg_ref, h1_ref, ctx_t_ref, wf_hbm, wi_hbm, wo_hbm, g1_ref,
    gu_ref, ga_ref, gc_ref, stat_ref, bi_ref, send_ref, keep_ref,
    sum_ref, wf_ref, wi_ref, wo_ref, sems,
):
    rows_all, width, inner = dims
    block = pl.program_id(0)
    chunk = TILE
    group = width // chunk
    copies = [
        fetch(wf_hbm.at[pl.ds(0, width), :], wf_ref.at[pl.ds(0, width), :], sems, 0),
        fetch(wi_hbm.at[:, pl.ds(0, width)], wi_ref.at[:, pl.ds(0, width)], sems, 1),
        fetch(wf_hbm.at[pl.ds(width, inner - width), :], wf_ref.at[pl.ds(width, inner - width), :], sems, 2),
        fetch(wi_hbm.at[:, pl.ds(width, inner - width)], wi_ref.at[:, pl.ds(width, inner - width)], sems, 3),
        fetch(wo_hbm, wo_ref, sems, 4),
    ]

    @pl.when(block == 0)
    def _():
        for copy in copies:
            copy.start()
        stat_ref[...] = jnp.zeros_like(stat_ref)
        bi_ref[...] = jnp.zeros_like(bi_ref)
        copies[0].wait()
        copies[1].wait()

    gf = gf_ref[...]
    raw, made = {}, {}
    sums = [gf[:, n * chunk : (n + 1) * chunk].astype(F32) for n in range(group)]
    biases = []

    def spread(i):
        raw[i] = mm_nt(gf, wf_ref[i * chunk : (i + 1) * chunk, :])

    def slope(i):
        cols = slice(i * chunk, (i + 1) * chunk)
        made[i] = (raw.pop(i) * dg_ref[:, cols].astype(F32)).astype(LOW)
        gu_ref[:, cols] = made[i]
        biases.append(jnp.sum(made[i].astype(F32), 0, keepdims=True))

    def gather(i):
        first, n = i // group * group, i % group
        left = jnp.concatenate([made[first + j] for j in range(group)], 1)
        cols = slice(n * chunk, (n + 1) * chunk)
        sums[n] = sums[n] + mm_nt(left, wi_ref[cols, first * chunk : (first + group) * chunk])

    staged(group, spread, slope)

    @pl.when(block == 0)
    def _():
        for copy in copies[2:]:
            copy.wait()

    count = inner // chunk
    staged(
        count,
        lambda i: spread(i + group) if i + group < count else None,
        lambda i: slope(i + group) if i + group < count else None,
        gather,
    )
    bi_ref[0:1, :] += jnp.concatenate(biases, 1)
    total = jnp.concatenate(sums, 1)
    n1, r1 = norm_parts(h1_ref[...].astype(F32))
    stat_ref[0:1, :] += jnp.sum(total * n1, 0, keepdims=True)
    stat_ref[1:2, :] += jnp.sum(total, 0, keepdims=True)
    g = total * vec(g1_ref)
    grad = r1 * (g - jnp.mean(g, -1, keepdims=True) - n1 * jnp.mean(g * n1, -1, keepdims=True))
    low = grad.astype(LOW)
    ga_ref[...] = low
    stat_ref[2:3, :] += jnp.sum(low.astype(F32), 0, keepdims=True)
    gc_ref[...] = mm_nt(low, wo_ref[...]).astype(LOW)
    product = mm(ctx_t_ref[...], low)

    @pl.when(block == 0)
    def _():
        sum_ref[...] = product

    @pl.when(block > 0)
    def _():
        sum_ref[...] += product

    @pl.when(block == pl.num_programs(0) - 1)
    def _():
        store_shards(core_ref, sum_ref[...], send_ref, keep_ref)


def attend_back_kernel(
    dims, core_ref, qlen_ref, plen_ref, q_ref, k_ref, v_ref, ctx_t_ref, lse_ref, gc_ref, x_t_ref, *refs
):
    *extra, out_ref, stat_ref, send_ref, keep_ref, sum_ref = refs
    q_dev, q_len, rows_all, head_dim = dims
    block = pl.program_id(0)
    pair_dim = 2 * head_dim
    width = q_ref.shape[1]
    pairs = width // pair_dim

    @pl.when(block == 0)
    def _():
        stat_ref[...] = jnp.zeros_like(stat_ref)

    def attend(size, starts, lengths, fresh):
        lane = lax.broadcasted_iota(jnp.int32, (size, pair_dim), 1)
        items = [(s, p, which) for p in range(pairs) for s in range(len(starts)) for which in range(2)]
        held, raw, made, grads = {}, {}, {}, {}

        def pair_of(s, p):
            if (s, p) not in held:
                here, cols = slice(starts[s], starts[s] + size), slice(p * pair_dim, (p + 1) * pair_dim)
                q, k, v, gc = q_ref[here, cols], k_ref[here, cols], v_ref[here, cols], gc_ref[here, cols]
                held[s, p] = here, cols, q, k, v, gc, q.T, k.T, gc.T
            return held[s, p]

        def compare(i):
            s, p, which = items[i]
            here, cols, q, k, v, gc, q_t, k_t, gc_t = pair_of(s, p)
            raw[i] = mm(k, half_only(q_t, which)), mm(v, half_only(gc_t, which))

        def weigh(i):
            s, p, which = items[i]
            here, cols, q, k, v, gc, q_t, k_t, gc_t = pair_of(s, p)
            head = slice((p * 2 + which) * head_dim, (p * 2 + which + 1) * head_dim)
            scores, grad_p = raw.pop(i)
            lse = lse_ref[0, p, which : which + 1, here]
            edge = sure_rows(size)
            late = jnp.where(live_rows(edge, lengths[s], size - edge), scores[edge:], -1e30)
            probs = jnp.concatenate([jnp.exp(scores[:edge] - lse), jnp.exp(late - lse)], 0)
            half = slice(which * head_dim, (which + 1) * head_dim)
            delta = jnp.sum(gc_t[half].astype(F32) * ctx_t_ref[head, here].astype(F32), 0, keepdims=True)
            made[i] = probs.astype(LOW), (probs * (grad_p - delta)).astype(LOW)

        def combine(i):
            s, p, which = items[i]
            here, cols, q, k, v, gc, q_t, k_t, gc_t = pair_of(s, p)
            mine = (lane >= head_dim) if which else (lane < head_dim)
            zero = jnp.zeros_like(q)
            probs, grad_s = made.pop(i)
            add_v = mm(probs, jnp.where(mine, gc, zero))
            add_k = mm(grad_s, jnp.where(mine, q, zero))
            add_q = mm(k_t[which * head_dim : (which + 1) * head_dim], grad_s)
            if which == 0:
                made[s, p] = add_v, add_k, add_q
                return
            old_v, old_k, old_q = made.pop((s, p))
            grad_q = (jnp.concatenate([old_q, add_q], 0).T * head_dim**-0.5).astype(LOW)
            grad_k = (old_k + add_k).astype(LOW)
            grad_v = (old_v + add_v).astype(LOW)
            for number, grad in enumerate((grad_q, grad_k, grad_v)):
                out_ref[here, number * width + cols.start : number * width + cols.stop] = grad
                grads[number, s, p] = grad
            stat_ref[0:1, cols] += jnp.sum(grad_q.astype(F32), 0, keepdims=True)
            stat_ref[1:2, cols] += jnp.sum(grad_v.astype(F32), 0, keepdims=True)

            if p % 2 and s == len(starts) - 1:
                project(p - 1)

        def project(p):
            for number in range(3):
                rows = [
                    jnp.concatenate([grads.pop((number, s, p)), grads.pop((number, s, p + 1))], 1)
                    for s in range(len(starts))
                ]
                product = mm(x_t_ref[...], jnp.concatenate(rows, 0))
                cols = slice(number * width + p * pair_dim, number * width + (p + 2) * pair_dim)
                if fresh:
                    sum_ref[:, cols] = product
                else:
                    sum_ref[:, cols] += product

        staged(len(items), compare, weigh, combine)

    @pl.when(block == 0)
    def _():
        attend(q_len, [s * q_len for s in range(q_dev)], [qlen_ref[s] for s in range(q_dev)], True)

    @pl.when(block > 0)
    def _():
        attend(rows_all, [0], [plen_ref[jnp.maximum(block - 1, 0)]], False)

    @pl.when(block == pl.num_programs(0) - 1)
    def _():
        tails = None
        if extra:
            tails = small_rows([*extra, stat_ref], send_ref.shape[0] * 2, send_ref.shape[2])
        store_shards(core_ref, sum_ref[...], send_ref, keep_ref, tails=tails)


def input_grad_kernel(grad_ref, base_ref, wq_ref, wk_ref, wv_ref, *out_refs):
    wide = wq_ref.shape[1]
    total = base_ref[...].astype(F32)
    for number, w_ref in enumerate((wq_ref, wk_ref, wv_ref)):
        total = total + mm_nt(grad_ref[:, number * wide : (number + 1) * wide], w_ref[...])
    low = total.astype(LOW)
    if len(out_refs) == 1:
        out_refs[0][...] = low
        return

    @pl.when(pl.program_id(0) == 0)
    def _():
        out_refs[0][...] = low

    @pl.when(pl.program_id(0) > 0)
    def _():
        out_refs[1][...] = low


def weight_grad_kernel(core_ref, left_ref, right_ref, send_ref, keep_ref):
    store_shards(core_ref, mm(left_ref[...], right_ref[...]), send_ref, keep_ref)


def small_rows(refs, count, wide):
    two, one, inner, *attn = [ref[...] for ref in refs]
    eight = jnp.concatenate(
        [jnp.concatenate([item[0:2] for item in attn], 1), one[2:3], two[2:3], one[0:2], two[0:2]], 0
    )
    inner = inner[0:1]
    short, long = eight.shape[1] // count, inner.shape[1] // count
    rows = []
    for shard in range(count):
        top = eight[:, shard * short : (shard + 1) * short]
        low = inner[:, shard * long : (shard + 1) * long]
        top = jnp.concatenate([top, jnp.zeros((8, wide - short), F32)], 1)
        low = jnp.concatenate([low, jnp.zeros((1, wide - long), F32)], 1)
        rows.append(jnp.concatenate([top, low, jnp.zeros((7, wide), F32)], 0).astype(LOW))
    return rows


def turn_kernel(part_ref, out_ref):
    out_ref[...] = part_ref[...].astype(F32).T


def turn_low_kernel(*refs):
    *inputs, out_ref = refs
    if len(inputs) == 1:
        out_ref[...] = inputs[0][...].T
        return

    @pl.when(pl.program_id(0) == 0)
    def _():
        out_ref[...] = inputs[0][...].T

    @pl.when(pl.program_id(0) > 0)
    def _():
        out_ref[...] = inputs[1][...].T


def const_spec(shape):
    return pl.BlockSpec(shape, lambda i: (0,) * len(shape), pipeline_mode=pl.Buffered(1))


def call(body, operands, in_specs, outs, grid, room, deps=(), old=(), name=None, scratch=(), us=20_000):
    count, extra = len(operands), len(old)
    if deps:
        tied = min(range(count), key=lambda i: operands[i].size)
        operands = list(operands)
        operands[tied] = lax.optimization_barrier((operands[tied], *deps))[0]

    def kernel(*refs):
        body(*refs[:count], *refs[count + extra :])

    return pl.pallas_call(
        kernel,
        grid=grid,
        in_specs=list(in_specs) + [pl.BlockSpec(memory_space=pl.ANY)] * extra,
        out_specs=[spec for spec, _ in outs],
        out_shape=[kind for _, kind in outs],
        scratch_shapes=scratch,
        input_output_aliases={count + i: i for i in range(extra)},
        compiler_params=pltpu.CompilerParams(vmem_limit_bytes=room * 1024 * 1024),
        cost_estimate=pl.CostEstimate(flops=int(us * 1.15e7), bytes_accessed=0, transcendentals=0),
        name=name,
    )(*operands, *old)


def weight_grad(left_t, right, row_count, core, deps, old):
    height, depth = left_t.shape
    wide = right.shape[1]
    block = min(wide, 768)
    shape = old[0].shape
    spec = pl.BlockSpec((*shape[:2], block), lambda i: (0, 0, i))
    return call(
        weight_grad_kernel,
        (core, left_t, right),
        [
            pl.BlockSpec(memory_space=pltpu.SMEM),
            const_spec((height, depth)),
            pl.BlockSpec((depth, block), lambda i: (0, i)),
        ],
        [(spec, jax.ShapeDtypeStruct(shape, LOW))] * 2,
        (wide // block,),
        56,
        deps,
        old,
        name="weight_grad",
    )


def add_kernel(*refs):
    *terms, out_ref = refs
    out_ref[...] = sum([ref[...].astype(F32) for ref in terms[1:]], terms[0][...].astype(F32)).astype(LOW)


def add_all(terms):
    shape = terms[0].shape
    spec = pl.BlockSpec(shape, lambda i: (0,) * len(shape), pipeline_mode=pl.Buffered(1))
    outs = [(spec, jax.ShapeDtypeStruct(shape, LOW))]
    return call(add_kernel, terms, [spec] * len(terms), outs, (1,), 24, name="add_all", us=20_000)[0]


class Flow:
    def __init__(self, sent, kept, line=False, fused=False):
        bits = lax.axis_size("row").bit_length() - 1
        self.order = [(0,)] + [tuple(range(i, min(i + 2, bits))) for i in range(1, bits, 2)]
        self.left = list(range(bits - 1, 0, -1))
        count = lax.axis_size("col")
        self.line = [(None, [(i, i ^ (1 << bit)) for i in range(count)]) for bit in range(count.bit_length() - 1)]
        if line:
            half = count // 2
            self.line = [(None, [(i, i + 1), (count - 1 - i, count - 2 - i)]) for i in range(half - 1)]
            self.line += [(None, [(half - 1, half), (half, half - 1)])]
            self.line += [
                ((i, count - 1 - i), [(i + 1, i), (count - 2 - i, count - 1 - i)])
                for i in range(half - 2, -1, -1)
            ]
        self.sent, self.kept, self.got, self.fused = [sent], kept, None, fused

    def shard(self, terms, bits, mask):
        here = lax.axis_index("row")
        order = [self.left.index(bit) for bit in bits]
        total = None
        for term in terms:
            starts, sizes = [0] * term.ndim, list(term.shape)
            for axis, bit in zip(order, bits):
                starts[axis], sizes[axis] = ((here ^ mask) >> bit) & 1, 1
            piece = lax.dynamic_slice(term, starts, sizes)
            piece = piece.reshape([size for i, size in enumerate(sizes) if i not in order]).astype(F32)
            total = piece if total is None else total + piece
        return total.astype(LOW)

    def step(self):
        if self.order:
            bits = self.order[0]
            masks = [
                sum(1 << bit for i, bit in enumerate(bits) if other >> i & 1)
                for other in range(1, 1 << len(bits))
            ]
            if bits != (0,):
                terms = [self.kept, *self.got]
                self.sent = [self.shard(terms, bits, mask) for mask in masks]
                self.kept = self.shard(terms, bits, 0)
                self.left = [bit for bit in self.left if bit not in bits]
            size = lax.axis_size("row")
            self.got = [
                lax.ppermute(sent, "row", [(i, i ^ mask) for i in range(size)])
                for sent, mask in zip(self.sent, masks)
            ]
        else:
            self.sent = [self.kept]
            self.got = [lax.ppermute(self.kept, "col", self.line[0][1])]

    def land(self, token=None):
        if token is not None:
            self.kept = lax.optimization_barrier((self.kept, token))[0]
        got = self.got
        if self.order:
            bits = self.order.pop(0)
            if bits == (0,):
                dims = (2,) * len(self.left) + self.kept.shape[1:]
                self.kept, self.got = self.kept.reshape(dims), [item.reshape(dims) for item in self.got]
            if not self.order and self.fused:
                self.kept = add_all([self.kept, *self.got])
            elif not self.order:
                self.kept = sum([item.astype(F32) for item in self.got], self.kept.astype(F32)).astype(LOW)
        else:
            ends, _ = self.line.pop(0)
            if ends is None:
                self.kept = self.kept + self.got[0]
            else:
                here = lax.axis_index("col")
                self.kept = jnp.where((here == ends[0]) | (here == ends[1]), self.got[0], self.kept)
        return got

    def turn(self, token=None):
        got = self.land(token)
        if self.done:
            return got
        self.step()
        return got + self.sent

    @property
    def done(self):
        return not self.order and not self.line


def gather_all(piece):
    row_bits = lax.axis_size("row").bit_length() - 1
    col_bits = lax.axis_size("col").bit_length() - 1
    steps = [("col", tuple(range(i, min(i + 2, col_bits)))) for i in range(0, col_bits, 2)]
    steps += [("row", tuple(range(i, min(i + 2, row_bits)))) for i in range(1, row_bits, 2)]
    for name, bits in steps + [("row", (0,))]:
        here = lax.axis_index(name)
        pieces = [piece]
        for other in range(1, 1 << len(bits)):
            mask = sum(1 << bit for i, bit in enumerate(bits) if other >> i & 1)
            pairs = [(i, i ^ mask) for i in range(lax.axis_size(name))]
            pieces.append(lax.ppermute(piece, name, pairs))
        for i, bit in enumerate(bits):
            high = ((here >> bit) & 1) == 1
            pieces = [
                jnp.where(high, pieces[place ^ (1 << i)], pieces[place]) for place in range(len(pieces))
            ]
        piece = jnp.concatenate(pieces, 0)
    return piece


def per_device(
    query_tokens, passage_tokens, query_lengths, passage_lengths, positives,
    w_query, w_key, w_value, w_attn_out, w_inner, w_outer,
    bias_query, bias_value, bias_attn_out, bias_inner, bias_outer,
    gain_one, shift_one, gain_two, shift_two,
):
    q_dev, q_len, width = query_tokens.shape
    p_dev, p_len, _ = passage_tokens.shape
    inner = w_inner.shape[1]
    rows_all = p_len
    assert q_dev * q_len == rows_all and q_dev + p_dev <= SLOTS
    blocks = 1 + p_dev
    total_rows = blocks * rows_all
    row_count = lax.axis_size("row")
    col_count = lax.axis_size("col")
    row_here = lax.axis_index("row")
    core = (row_here & 1).reshape(1)
    me = (row_here * col_count + lax.axis_index("col")).reshape(1)
    params = pltpu.CompilerParams(vmem_limit_bytes=VMEM)
    smem = pl.BlockSpec(memory_space=pltpu.SMEM)

    def by_block(wide):
        return pl.BlockSpec((rows_all, wide), lambda i: (i, 0))

    def by_block_t(high):
        return pl.BlockSpec((high, rows_all), lambda i: (0, i))

    def fixed(shape):
        return pl.BlockSpec(shape, lambda i: (0,) * len(shape))

    queries_spec = pl.BlockSpec((rows_all, width), lambda i: (0, 0))
    passages_spec = pl.BlockSpec((rows_all, width), lambda i: (jnp.maximum(i - 1, 0), 0))

    lse_spec = pl.BlockSpec((1, HEADS // 2, 8, rows_all), lambda i: (i, 0, 0, 0))

    def shape(*dims, kind=LOW):
        return jax.ShapeDtypeStruct(dims, kind)

    queries = query_tokens.reshape(rows_all, width)
    passages = passage_tokens.reshape(p_dev * rows_all, width)
    square = const_spec((width, width))
    anywhere = pl.BlockSpec(memory_space=pl.ANY)
    thin = const_spec((width,))

    q, k, v, ctx_t, lse = call(
        partial(attend_kernel, (q_dev, q_len, rows_all, width)),
        (query_lengths, passage_lengths, queries, passages, w_query, w_key, w_value, bias_query, bias_value),
        [smem, smem, queries_spec, passages_spec, square, square, square, thin, thin],
        [(by_block(width), shape(total_rows, width))] * 3
        + [
            (by_block_t(width), shape(width, total_rows)),
            (lse_spec, shape(blocks, HEADS // 2, 8, rows_all, kind=F32)),
        ],
        (blocks,),
        56,
        name="attend",

    )

    rows_part = rows_all // 2
    parts = 2 * blocks

    def by_part(wide):
        return pl.BlockSpec((rows_part, wide), lambda i: (i, 0))

    queries_part = pl.BlockSpec((rows_part, width), lambda i: (jnp.minimum(i, 1), 0))
    passages_part = pl.BlockSpec((rows_part, width), lambda i: (jnp.maximum(i - 2, 0), 0))
    h1, y1, act, slope, h2, query_out, passage_out, pooled, payload = call(
        partial(dense_kernel, (q_dev, q_len, p_len, width, inner)),
        (
            query_lengths, passage_lengths, positives, queries, passages, ctx_t, w_attn_out, w_inner, w_outer,
            bias_attn_out, bias_inner, bias_outer, gain_one, shift_one, gain_two, shift_two,
        ),
        [smem, smem, smem, queries_part, passages_part, pl.BlockSpec((width, rows_part), lambda i: (0, i))]
        + [anywhere] * 3
        + [thin, const_spec((inner,))]
        + [thin] * 5,
        [
            (by_part(width), shape(total_rows, width)),
            (by_part(width), shape(total_rows, width)),
            (by_part(inner), shape(total_rows, inner)),
            (by_part(inner), shape(total_rows, inner)),
            (by_part(width), shape(total_rows, width)),
            (queries_part, shape(rows_all, width)),
            (passages_part, shape(p_dev * rows_all, width)),
            (fixed((SLOTS, width)), shape(SLOTS, width, kind=F32)),
            (fixed((SLOTS, width + 128)), shape(SLOTS, width + 128)),
        ],
        (parts,),
        56,
        name="dense",
        scratch=[
            pltpu.VMEM((width, width), LOW),
            pltpu.VMEM((width, inner), LOW),
            pltpu.VMEM((inner, width), LOW),
            pltpu.SemaphoreType.DMA((3,)),
        ],

    )

    gathered = gather_all(payload)
    loss, gvec = pl.pallas_call(
        partial(loss_kernel, (q_dev, p_dev, width, col_count)),
        in_specs=[smem] * 3 + [pl.BlockSpec(memory_space=pltpu.VMEM)] * 3,
        out_specs=[pl.BlockSpec(memory_space=pltpu.VMEM)] * 2,
        out_shape=[shape(8, 128, kind=F32), shape(SLOTS, width, kind=F32)],
        compiler_params=params,
        name="loss",
    )(me, query_lengths, passage_lengths, payload, gathered, pooled)

    smalls = shape(8, width, kind=F32)
    cut = width // row_count
    cut_inner = inner // row_count
    half = row_count // 2
    step_cols = 768
    per_step = step_cols // cut_inner
    outer_spec = pl.BlockSpec((per_step // 2, width, cut_inner), lambda i: (i, 0, 0))
    grad_f, stat_two, *outer_parts = call(
        partial(outer_grad_kernel, (q_dev, q_len, p_len)),
        (core, query_lengths, passage_lengths, gvec, h2, gain_two, act),
        [smem, smem, smem, fixed((SLOTS, width)), const_spec((total_rows, width)), thin]
        + [pl.BlockSpec((total_rows, step_cols), lambda i: (0, i))],
        [
            (fixed((total_rows, width)), shape(total_rows, width)),
            (fixed((8, width)), smalls),
            (outer_spec, shape(half, width, cut_inner)),
            (outer_spec, shape(half, width, cut_inner)),
        ],
        (inner // step_cols,),
        56,
        name="outer_grad",
        scratch=[pltpu.VMEM((width, total_rows), LOW)],
    )
    outer = Flow(*outer_parts, line=True)
    outer.step()

    def turn(arrays, specs, deps):
        outs = [(by_block_t(width), shape(width, total_rows))]
        return call(turn_low_kernel, arrays, specs, outs, (blocks,), 56, deps, name="turn")[0]

    y1_t = turn([y1], [by_block(width)], outer.sent)
    deps = outer.turn(y1_t)
    attn_spec = pl.BlockSpec((half, cut, width), lambda i: (0, 0, inner // width))
    grad_u, grad_attn, grad_ctx, stat_one, grad_bias_inner, *up_parts = call(
        partial(dense_back_kernel, (rows_all, width, inner)),
        (core, grad_f, slope, h1, ctx_t, w_outer, w_inner, w_attn_out, gain_one),
        [smem, by_block(width), by_block(inner), by_block(width), by_block_t(width)]
        + [anywhere, anywhere, anywhere, thin],
        [
            (by_block(inner), shape(total_rows, inner)),
            (by_block(width), shape(total_rows, width)),
            (by_block(width), shape(total_rows, width)),
            (fixed((8, width)), smalls),
            (fixed((8, inner)), shape(8, inner, kind=F32)),
            (attn_spec, shape(half, cut, inner + width)),
            (attn_spec, shape(half, cut, inner + width)),
        ],
        (blocks,),
        60,
        deps,
        name="dense_back",
        scratch=[
            pltpu.VMEM((width, width), F32),
            pltpu.VMEM((inner, width), LOW),
            pltpu.VMEM((width, inner), LOW),
            pltpu.VMEM((width, width), LOW),
            pltpu.SemaphoreType.DMA((5,)),
        ],
    )
    deps = outer.turn(stat_one)
    up_flow = Flow(*weight_grad(y1_t, grad_u, row_count, core, deps, up_parts), line=True, fused=True)
    up_flow.step()
    deps = up_flow.sent + outer.turn(up_flow.sent[0])
    x_t = turn([queries, passages], [queries_spec, passages_spec], deps)
    deps = up_flow.turn(x_t)

    head_dim = width // HEADS
    third = 4 * head_dim
    groups = [(0, 2 * third), (2 * third, third)]

    def attend_back(start, wide, deps, extra=()):
        pairs = wide // (2 * head_dim)
        index = start // wide
        cols = pl.BlockSpec((rows_all, wide), lambda i: (i, index))
        rows = cut + (16 if extra else 0)
        return call(
            partial(attend_back_kernel, (q_dev, q_len, rows_all, head_dim)),
            (core, query_lengths, passage_lengths, q, k, v, ctx_t, lse, grad_ctx, x_t, *extra),
            [smem, smem, smem]
            + [cols] * 3
            + [
                pl.BlockSpec((wide, rows_all), lambda i: (index, i)),
                pl.BlockSpec((1, pairs, 8, rows_all), lambda i: (i, index, 0, 0)),
                cols,
                by_block_t(width),
            ]
            + [const_spec(item.shape) for item in extra],
            [
                (by_block(3 * wide), shape(total_rows, 3 * wide)),
                (fixed((8, wide)), shape(8, wide, kind=F32)),
            ]
            + [(fixed((half, rows, 3 * wide)), shape(half, rows, 3 * wide))] * 2,
            (blocks,),
            56,
            deps,
            name="attend_back",
            scratch=[pltpu.VMEM((width, 3 * wide), F32)],
        )

    def input_grad(start, wide, grad, base, outs, deps, us):
        index = start // wide
        cols = pl.BlockSpec((width, wide), lambda i: (0, index), pipeline_mode=pl.Buffered(1))
        return call(
            input_grad_kernel,
            (grad, base, w_query, w_key, w_value),
            [by_block(3 * wide), by_block(width), cols, cols, cols],
            outs,
            (blocks,),
            56,
            deps,
            name="input_grad",
            us=us,
        )

    grad_a, stat_a, *mixed_parts = attend_back(*groups[0], deps)
    mixed_flow = Flow(*mixed_parts)
    mixed_flow.step()
    deps = mixed_flow.sent + outer.turn(stat_a)
    (part_grad,) = input_grad(
        *groups[0], grad_a, grad_attn, [(by_block(width), shape(total_rows, width))], deps, 0
    )
    deps = up_flow.turn(part_grad) + mixed_flow.turn(up_flow.kept)
    extra = (stat_two, stat_one, grad_bias_inner, stat_a)
    grad_b, stat_b, *last_parts = attend_back(*groups[1], deps, extra)
    last_flow = Flow(*last_parts)
    last_flow.step()
    deps = last_flow.sent + outer.turn(stat_b) + mixed_flow.turn(stat_b) + up_flow.turn(stat_b)
    query_grad, passage_grad = input_grad(
        *groups[1],
        grad_b,
        part_grad,
        [
            (queries_spec, shape(rows_all, width)),
            (passages_spec, shape(p_dev * rows_all, width)),
        ],
        deps,
        20_000,
    )
    last_flow.turn(passage_grad)
    mixed_flow.turn(last_flow.kept)
    up_flow.turn(mixed_flow.kept)
    outs = [(fixed((cut_inner, width)), shape(cut_inner, width, kind=F32))]
    (turned,) = call(
        turn_kernel, (outer.kept,), [const_spec((width, cut_inner))], outs, (1,), 56, [up_flow.kept], name="turn"
    )
    last_flow.turn(turned)
    last_flow.turn()
    mixed_flow.turn(last_flow.kept)
    last_flow.turn(mixed_flow.kept)
    flows = [outer, up_flow, mixed_flow, last_flow]
    while not all(flow.done for flow in flows):
        for flow in flows:
            if not flow.done:
                flow.turn()
    mixed, last = mixed_flow.kept.astype(F32), last_flow.kept.astype(F32)
    qkv = [
        jnp.concatenate(
            [mixed[:, i * 2 * third : (i + 1) * 2 * third], last[:cut, i * third : (i + 1) * third]], 1
        )
        for i in range(3)
    ]
    up_sum = up_flow.kept.astype(F32)
    small = last[cut:]
    return (
        loss[0, 0],
        query_out.reshape(query_tokens.shape),
        passage_out.reshape(passage_tokens.shape),
        query_grad.reshape(query_tokens.shape),
        passage_grad.reshape(passage_tokens.shape),
        *qkv,
        up_sum[:, inner:],
        up_sum[:, :inner],
        turned,
        *[small[i, :cut] for i in range(3)],
        small[8, : inner // row_count],
        *[small[i, :cut] for i in range(3, 8)],
    )


def solution(mesh):
    in_specs = (
        P(("row", "col"), None, None),
        P(("row", "col"), None, None),
        P(("row", "col")),
        P(("row", "col")),
        P(("row", "col")),
        P(),
        P(),
        P(),
        P(),
        P(),
        P(),
        P(),
        P(),
        P(),
        P(),
        P(),
        P(),
        P(),
        P(),
        P(),
    )
    out_specs = (
        P(),
        P(("row", "col"), None, None),
        P(("row", "col"), None, None),
        P(("row", "col"), None, None),
        P(("row", "col"), None, None),
        P("row", None),
        P("row", None),
        P("row", None),
        P("row", None),
        P("row", None),
        P("row", None),
        P("row"),
        P("row"),
        P("row"),
        P("row"),
        P("row"),
        P("row"),
        P("row"),
        P("row"),
        P("row"),
    )
    return jax.shard_map(
        per_device, mesh=mesh, in_specs=in_specs, out_specs=out_specs, check_vma=False
    )
```

```python
from functools import partial

import jax
import jax.numpy as jnp
from jax import lax
from jax.experimental import pallas as pl
from jax.experimental.pallas import tpu as pltpu
from jax.sharding import PartitionSpec as P

HEADS = 12
EPS_NORM = 1e-12
EPS_POOL = 1e-06
SCALE_LOSS = 128.0
INV_TEMP = 100.0
TILE = 256
SLOTS = 8
VMEM = 60 * 1024 * 1024
LOW = jnp.bfloat16
F32 = jnp.float32


def mm(left, right):
    return lax.dot_general(left, right, (((1,), (0,)), ((), ())), preferred_element_type=F32)


def mm_nt(left, right):
    return lax.dot_general(left, right, (((1,), (1,)), ((), ())), preferred_element_type=F32)


def norm_parts(hidden):
    center = hidden - jnp.mean(hidden, -1, keepdims=True)
    spread = jnp.mean(center * center, -1, keepdims=True)
    scale = lax.rsqrt(spread + EPS_NORM)
    return center * scale, scale


def gelu_parts(u):
    square = u * u
    q = 1.4250060785476853e-06
    for factor in (-3.669345091379551e-05, -8.782652731110375e-05, 0.03639228618131223, 0.7978697123041883):
        q = q * square + factor
    share = 0.5 + 0.5 * jnp.tanh(u * q)
    bell = jnp.exp(-0.5 * square)
    return u * share, share + (0.3989422804014327 * u) * bell


def vec(ref, cols=slice(None)):
    return ref[cols].reshape(1, -1)


def rows_of(step, size):
    return pl.ds(pl.multiple_of(step * size, size), size)


def part_owner(part, q_dev, q_len, p_len, qlen_ref, plen_ref):
    per = p_len // q_len
    beyond = jnp.maximum(part - q_dev, 0)
    is_query = part < q_dev
    slot = jnp.where(is_query, part, q_dev + beyond // per)
    length = jnp.where(is_query, qlen_ref[jnp.where(is_query, part, 0)], plen_ref[beyond // per])
    first = jnp.where(is_query, 0, beyond % per * q_len)
    return slot, length, first


def live_rows(first, length, size):
    return (first + lax.broadcasted_iota(jnp.int32, (size, 1), 0)) < length


def sure_rows(size):
    return size * 4 // 5 // 16 * 16


def half_only(pair_t, which):
    half = pair_t.shape[0] // 2
    zeros = jnp.zeros((half, pair_t.shape[1]), pair_t.dtype)
    if which == 0:
        return jnp.concatenate([pair_t[:half], zeros], 0)
    return jnp.concatenate([zeros, pair_t[half:]], 0)


def staged(count, *stages):
    for step in range(count + len(stages) - 1):
        for late, stage in enumerate(stages):
            if 0 <= step - late < count:
                stage(step - late)


def fetch(source, target, sems, index):
    return pltpu.make_async_copy(source, target, sems.at[index])


def attend_kernel(
    dims, qlen_ref, plen_ref, xq_ref, xp_ref, wq_ref, wk_ref, wv_ref, bq_ref, bv_ref,
    q_ref, k_ref, v_ref, ctx_t_ref, lse_ref,
):
    q_dev, q_len, rows_all, width = dims
    block = pl.program_id(0)
    head_dim = width // HEADS
    x = jnp.where(block == 0, xq_ref[...], xp_ref[...])
    q = ((mm(x, wq_ref[...]) + vec(bq_ref)) * head_dim**-0.5).astype(LOW)
    k = mm(x, wk_ref[...]).astype(LOW)
    v = (mm(x, wv_ref[...]) + vec(bv_ref)).astype(LOW)
    q_ref[...] = q
    k_ref[...] = k
    v_ref[...] = v
    q_t, v_t = q.T, v.T

    def attend(size, starts, lengths):
        items = [(start, length, head) for head in range(HEADS) for start, length in zip(starts, lengths)]
        scores, weights = {}, {}

        def compare(i):
            start, length, head = items[i]
            cols = slice(head // 2 * 2 * head_dim, (head // 2 + 1) * 2 * head_dim)
            here = slice(start, start + size)
            scores[i] = mm(k[here, cols], half_only(q_t[cols, here], head % 2))

        def weigh(i):
            start, length, head = items[i]
            edge = sure_rows(size)
            early, late = scores[i][:edge], scores.pop(i)[edge:]
            late = jnp.where(live_rows(edge, length, size - edge), late, -1e30)
            top = jnp.maximum(jnp.max(early, 0, keepdims=True), jnp.max(late, 0, keepdims=True))
            weights[i] = top, jnp.concatenate([jnp.exp(early - top).astype(LOW), jnp.exp(late - top).astype(LOW)], 0)

        def combine(i):
            start, length, head = items[i]
            here, rows = slice(start, start + size), slice(head * head_dim, (head + 1) * head_dim)
            top, weight = weights.pop(i)
            values = jnp.concatenate([v_t[rows, here], jnp.ones((16, size), LOW)], 0)
            result = mm(values, weight)
            total = result[head_dim : head_dim + 1]
            lse_ref[0, head // 2, head % 2 : head % 2 + 1, here] = top + jnp.log(total)
            ctx_t_ref[rows, here] = (result[:head_dim] * (1.0 / total)).astype(LOW)

        staged(len(items), compare, weigh, combine)

    @pl.when(block == 0)
    def _():
        attend(q_len, [s * q_len for s in range(q_dev)], [qlen_ref[s] for s in range(q_dev)])

    @pl.when(block > 0)
    def _():
        attend(rows_all, [0], [plen_ref[jnp.maximum(block - 1, 0)]])


def dense_kernel(
    dims, qlen_ref, plen_ref, pos_ref, xq_ref, xp_ref, ctx_t_ref, wo_hbm, wi_hbm, wf_hbm,
    bo_ref, bi_ref, bf_ref, g1_ref, s1_ref, g2_ref, s2_ref,
    h1_ref, y1_ref, act_ref, dg_ref, h2_ref, yq_ref, yp_ref, pool_ref, pay_ref,
    wo_ref, wi_ref, wf_ref, sems,
):
    q_dev, q_len, p_len, width, inner = dims
    block = pl.program_id(0)
    rows_all = xq_ref.shape[0]
    query_blocks = q_dev * q_len // rows_all
    copies = [
        fetch(source, target, sems, index)
        for index, (source, target) in enumerate([(wo_hbm, wo_ref), (wi_hbm, wi_ref), (wf_hbm, wf_ref)])
    ]

    @pl.when(block == 0)
    def _():
        for copy in copies:
            copy.start()
        pool_ref[...] = jnp.zeros_like(pool_ref)
        copies[0].wait()

    x = jnp.where(block < query_blocks, xq_ref[...], xp_ref[...])
    hidden = x.astype(F32) + (mm(ctx_t_ref[...].T, wo_ref[...]) + vec(bo_ref))
    h1_ref[...] = hidden.astype(LOW)
    y1 = norm_parts(hidden)[0] * vec(g1_ref) + vec(s1_ref)
    y1_low = y1.astype(LOW)
    y1_ref[...] = y1_low

    @pl.when(block == 0)
    def _():
        copies[1].wait()
        copies[2].wait()

    group = width // TILE
    raw, made = {}, {}
    sums = [y1[:, n * TILE : (n + 1) * TILE] + vec(bf_ref, slice(n * TILE, (n + 1) * TILE)) for n in range(group)]

    def expand(i):
        cols = slice(i * TILE, (i + 1) * TILE)
        raw[i] = mm(y1_low, wi_ref[:, cols]) + vec(bi_ref, cols)

    def activate(i):
        cols = slice(i * TILE, (i + 1) * TILE)
        act, slope = gelu_parts(raw.pop(i))
        made[i] = act.astype(LOW)
        act_ref[:, cols] = made[i]
        dg_ref[:, cols] = slope.astype(LOW)

    def contract(i):
        first, n = i // group * group, i % group
        left = jnp.concatenate([made[first + j] for j in range(group)], 1)
        cols = slice(n * TILE, (n + 1) * TILE)
        sums[n] = sums[n] + mm(left, wf_ref[first * TILE : (first + group) * TILE, cols])

    late = [lambda i: None] * (group - 1)
    staged(inner // TILE, expand, activate, *late, contract)

    total = jnp.concatenate(sums, 1)
    h2_ref[...] = total.astype(LOW)
    y2 = norm_parts(total)[0] * vec(g2_ref) + vec(s2_ref)
    for part in range(rows_all // q_len):
        number = block * (rows_all // q_len) + part
        slot, length, first = part_owner(number, q_dev, q_len, p_len, qlen_ref, plen_ref)
        piece = y2[part * q_len : (part + 1) * q_len]
        summed = jnp.sum(jnp.where(live_rows(first, length, q_len), piece, 0.0), 0, keepdims=True)
        in_slot = lax.broadcasted_iota(jnp.int32, (SLOTS, 1), 0) == slot
        pool_ref[...] += jnp.where(in_slot, summed / length.astype(F32), 0.0)

    @pl.when(block < query_blocks)
    def _():
        yq_ref[...] = y2.astype(LOW)

    @pl.when(block >= query_blocks)
    def _():
        yp_ref[...] = y2.astype(LOW)

    @pl.when(block == pl.num_programs(0) - 1)
    def _():
        pooled = pool_ref[...]
        emb = pooled * lax.rsqrt(jnp.sum(pooled * pooled, -1, keepdims=True) + EPS_POOL)
        pay_ref[:, :width] = emb.astype(LOW)
        row = lax.broadcasted_iota(jnp.int32, (SLOTS, 128), 0)
        col = lax.broadcasted_iota(jnp.int32, (SLOTS, 128), 1)
        place = jnp.zeros((SLOTS, 128), jnp.int32)
        for j in range(q_dev):
            high = pos_ref[j] // 128
            low = pos_ref[j] - high * 128
            place = jnp.where(row == j, jnp.where(col == 0, high, jnp.where(col == 1, low, 0)), place)
        pay_ref[:, width:] = place.astype(F32).astype(LOW)


def loss_kernel(
    dims, me_ref, qlen_ref, plen_ref, own_ref, all_ref, pool_ref, loss_ref, gvec_ref
):
    q_dev, p_dev, width, col_count = dims
    count = all_ref.shape[0]
    every = all_ref[:, :width]
    own = own_ref[:, :width]

    def passage_mask(index):
        spot, place = index % SLOTS, index // SLOTS
        per_core = count // SLOTS // 2
        core, rest = place // per_core, place % per_core
        device = (rest // col_count * 2 + core) * col_count + rest % col_count
        return (spot >= q_dev) & (spot < q_dev + p_dev), device * p_dev + spot - q_dev

    scores = mm_nt(own, every) * INV_TEMP
    valid, ident = passage_mask(lax.broadcasted_iota(jnp.int32, (SLOTS, count), 1))
    scores = jnp.where(valid, scores, -1e30)
    top = jnp.max(scores, -1, keepdims=True)
    totals = top + jnp.log(jnp.sum(jnp.exp(scores - top), -1, keepdims=True))
    marks = own_ref[:, width:].astype(F32)
    wanted = marks[:, 0:1] * 128.0 + marks[:, 1:2]
    target = (valid & (ident.astype(F32) == wanted)).astype(F32)
    raw = (INV_TEMP * (SCALE_LOSS * (jnp.exp(scores - totals) - target))).astype(LOW)
    grad_q = mm(raw, every)

    picker_col = lax.broadcasted_iota(jnp.int32, (SLOTS, 128), 1)
    picker = jnp.where(picker_col == 0, 128.0, jnp.where(picker_col == 1, 1.0, 0.0)).astype(LOW)
    own_row = lax.broadcasted_iota(jnp.int32, (SLOTS, TILE), 0)
    own_valid = (own_row >= q_dev) & (own_row < q_dev + p_dev)
    own_ident = (me_ref[0] * p_dev + own_row - q_dev).astype(F32)

    def body(step, carry):
        total_loss, grad_p = carry
        rows = rows_of(step, TILE)
        some = all_ref[rows, :width]
        place = mm_nt(picker, all_ref[rows, width:])[0:1]
        table = mm_nt(every, some) * INV_TEMP
        ok, names = passage_mask(lax.broadcasted_iota(jnp.int32, (count, TILE), 0))
        picked = jnp.sum(jnp.where(ok & (names.astype(F32) == place), table, 0.0), 0, keepdims=True)
        table = jnp.where(ok, table, -1e30)
        high = jnp.max(table, 0, keepdims=True)
        lse = high + jnp.log(jnp.sum(jnp.exp(table - high), 0, keepdims=True))
        is_query = lax.broadcasted_iota(jnp.int32, (1, TILE), 1) % SLOTS < q_dev
        losses = jnp.where(is_query, lse - picked, 0.0)
        mine = mm_nt(own, some) * INV_TEMP
        hit = (own_ident == place).astype(F32)
        grads = INV_TEMP * (SCALE_LOSS * (jnp.exp(mine - lse) - hit))
        grads = jnp.where(own_valid & is_query, grads, 0.0).astype(LOW)
        return total_loss + jnp.sum(losses, 1, keepdims=True), grad_p + mm(grads, some)

    start = (jnp.zeros((1, 1), F32), jnp.zeros((SLOTS, width), F32))
    total_loss, grad_p = lax.fori_loop(0, count // TILE, body, start)
    loss_ref[...] = jnp.broadcast_to(total_loss / float(count // SLOTS * q_dev), loss_ref.shape)

    slot = lax.broadcasted_iota(jnp.int32, (SLOTS, 1), 0)
    grad = jnp.where(slot < q_dev, grad_q, grad_p)
    pooled = pool_ref[...]
    r = lax.rsqrt(jnp.sum(pooled * pooled, -1, keepdims=True) + EPS_POOL)
    inside = jnp.sum(pooled * grad, -1, keepdims=True)
    length = jnp.ones((SLOTS, 1), F32)
    for j in range(q_dev):
        length = jnp.where(slot == j, qlen_ref[j].astype(F32), length)
    for j in range(p_dev):
        length = jnp.where(slot == q_dev + j, plen_ref[j].astype(F32), length)
    gvec_ref[...] = (r * grad - r * r * r * inside * pooled) / length


def store_shards(core_ref, result, send_ref, keep_ref, by_row=True, tails=None):
    count = send_ref.shape[0] * 2
    size = result.shape[0 if by_row else 1] // count

    def store(even, odd):
        for shard in range(count):
            spot = slice(shard * size, (shard + 1) * size)
            piece = (result[spot, :] if by_row else result[:, spot]).astype(LOW)
            target = odd if shard % 2 else even
            if tails is None:
                target[shard // 2] = piece
            else:
                target[shard // 2, :size] = piece
                target[shard // 2, size:] = tails[shard]

    @pl.when(core_ref[0] == 0)
    def _():
        store(keep_ref, send_ref)

    @pl.when(core_ref[0] == 1)
    def _():
        store(send_ref, keep_ref)


def outer_grad_kernel(
    dims, core_ref, qlen_ref, plen_ref, gvec_ref, h2_ref, g2_ref, act_ref,
    gf_ref, stat_ref, send_ref, keep_ref, gf_t_ref,
):
    q_dev, q_len, p_len = dims

    @pl.when(pl.program_id(0) == 0)
    def _():
        stat_ref[...] = jnp.zeros_like(stat_ref)

        def body(part, carry):
            rows = rows_of(part, q_len)
            slot, length, first = part_owner(part, q_dev, q_len, p_len, qlen_ref, plen_ref)
            in_slot = lax.broadcasted_iota(jnp.int32, (SLOTS, 1), 0) == slot
            grad_y = jnp.sum(jnp.where(in_slot, gvec_ref[...], 0.0), 0, keepdims=True)
            live = live_rows(first, length, q_len)
            n2, r2 = norm_parts(h2_ref[rows, :].astype(F32))
            g = grad_y * vec(g2_ref)
            grad = r2 * (g - jnp.mean(g, -1, keepdims=True) - n2 * jnp.mean(g * n2, -1, keepdims=True))
            grad = jnp.where(live, grad, 0.0)
            low = grad.astype(LOW)
            gf_ref[rows, :] = low
            gf_t_ref[:, rows] = low.T
            stat_ref[0:1, :] += grad_y * jnp.sum(jnp.where(live, n2, 0.0), 0, keepdims=True)
            stat_ref[1:2, :] += grad_y * jnp.sum(live.astype(F32), 0, keepdims=True)
            stat_ref[2:3, :] += jnp.sum(low.astype(F32), 0, keepdims=True)
            return carry

        lax.fori_loop(0, h2_ref.shape[0] // q_len, body, 0)

    store_shards(core_ref, mm(gf_t_ref[...], act_ref[...]), send_ref, keep_ref, by_row=False)


def dense_back_kernel(
    dims, core_ref, gf_ref, dg_ref, h1_ref, ctx_t_ref, wf_hbm, wi_hbm, wo_hbm, g1_ref,
    gu_ref, ga_ref, gc_ref, stat_ref, bi_ref, send_ref, keep_ref,
    sum_ref, wf_ref, wi_ref, wo_ref, sems,
):
    rows_all, width, inner = dims
    block = pl.program_id(0)
    chunk = TILE
    group = width // chunk
    copies = [
        fetch(wf_hbm.at[pl.ds(0, width), :], wf_ref.at[pl.ds(0, width), :], sems, 0),
        fetch(wi_hbm.at[:, pl.ds(0, width)], wi_ref.at[:, pl.ds(0, width)], sems, 1),
        fetch(wf_hbm.at[pl.ds(width, inner - width), :], wf_ref.at[pl.ds(width, inner - width), :], sems, 2),
        fetch(wi_hbm.at[:, pl.ds(width, inner - width)], wi_ref.at[:, pl.ds(width, inner - width)], sems, 3),
        fetch(wo_hbm, wo_ref, sems, 4),
    ]

    @pl.when(block == 0)
    def _():
        for copy in copies:
            copy.start()
        stat_ref[...] = jnp.zeros_like(stat_ref)
        bi_ref[...] = jnp.zeros_like(bi_ref)
        copies[0].wait()
        copies[1].wait()

    gf = gf_ref[...]
    raw, made = {}, {}
    sums = [gf[:, n * chunk : (n + 1) * chunk].astype(F32) for n in range(group)]
    biases = []

    def spread(i):
        raw[i] = mm_nt(gf, wf_ref[i * chunk : (i + 1) * chunk, :])

    def slope(i):
        cols = slice(i * chunk, (i + 1) * chunk)
        made[i] = (raw.pop(i) * dg_ref[:, cols].astype(F32)).astype(LOW)
        gu_ref[:, cols] = made[i]
        biases.append(jnp.sum(made[i].astype(F32), 0, keepdims=True))

    def gather(i):
        first, n = i // group * group, i % group
        left = jnp.concatenate([made[first + j] for j in range(group)], 1)
        cols = slice(n * chunk, (n + 1) * chunk)
        sums[n] = sums[n] + mm_nt(left, wi_ref[cols, first * chunk : (first + group) * chunk])

    staged(group, spread, slope)

    @pl.when(block == 0)
    def _():
        for copy in copies[2:]:
            copy.wait()

    count = inner // chunk
    staged(
        count,
        lambda i: spread(i + group) if i + group < count else None,
        lambda i: slope(i + group) if i + group < count else None,
        gather,
    )
    bi_ref[0:1, :] += jnp.concatenate(biases, 1)
    total = jnp.concatenate(sums, 1)
    n1, r1 = norm_parts(h1_ref[...].astype(F32))
    stat_ref[0:1, :] += jnp.sum(total * n1, 0, keepdims=True)
    stat_ref[1:2, :] += jnp.sum(total, 0, keepdims=True)
    g = total * vec(g1_ref)
    grad = r1 * (g - jnp.mean(g, -1, keepdims=True) - n1 * jnp.mean(g * n1, -1, keepdims=True))
    low = grad.astype(LOW)
    ga_ref[...] = low
    stat_ref[2:3, :] += jnp.sum(low.astype(F32), 0, keepdims=True)
    gc_ref[...] = mm_nt(low, wo_ref[...]).astype(LOW)
    product = mm(ctx_t_ref[...], low)

    @pl.when(block == 0)
    def _():
        sum_ref[...] = product

    @pl.when(block > 0)
    def _():
        sum_ref[...] += product

    @pl.when(block == pl.num_programs(0) - 1)
    def _():
        store_shards(core_ref, sum_ref[...], send_ref, keep_ref)


def attend_back_kernel(
    dims, core_ref, qlen_ref, plen_ref, q_ref, k_ref, v_ref, ctx_t_ref, lse_ref, gc_ref, x_t_ref, *refs
):
    *extra, out_ref, stat_ref, send_ref, keep_ref, sum_ref = refs
    q_dev, q_len, rows_all, head_dim = dims
    block = pl.program_id(0)
    pair_dim = 2 * head_dim
    width = q_ref.shape[1]
    pairs = width // pair_dim

    @pl.when(block == 0)
    def _():
        stat_ref[...] = jnp.zeros_like(stat_ref)

    def attend(size, starts, lengths, fresh):
        lane = lax.broadcasted_iota(jnp.int32, (size, pair_dim), 1)
        items = [(s, p, which) for p in range(pairs) for s in range(len(starts)) for which in range(2)]
        held, raw, made, grads = {}, {}, {}, {}

        def pair_of(s, p):
            if (s, p) not in held:
                here, cols = slice(starts[s], starts[s] + size), slice(p * pair_dim, (p + 1) * pair_dim)
                q, k, v, gc = q_ref[here, cols], k_ref[here, cols], v_ref[here, cols], gc_ref[here, cols]
                held[s, p] = here, cols, q, k, v, gc, q.T, k.T, gc.T
            return held[s, p]

        def compare(i):
            s, p, which = items[i]
            here, cols, q, k, v, gc, q_t, k_t, gc_t = pair_of(s, p)
            raw[i] = mm(k, half_only(q_t, which)), mm(v, half_only(gc_t, which))

        def weigh(i):
            s, p, which = items[i]
            here, cols, q, k, v, gc, q_t, k_t, gc_t = pair_of(s, p)
            head = slice((p * 2 + which) * head_dim, (p * 2 + which + 1) * head_dim)
            scores, grad_p = raw.pop(i)
            lse = lse_ref[0, p, which : which + 1, here]
            edge = sure_rows(size)
            late = jnp.where(live_rows(edge, lengths[s], size - edge), scores[edge:], -1e30)
            probs = jnp.concatenate([jnp.exp(scores[:edge] - lse), jnp.exp(late - lse)], 0)
            half = slice(which * head_dim, (which + 1) * head_dim)
            delta = jnp.sum(gc_t[half].astype(F32) * ctx_t_ref[head, here].astype(F32), 0, keepdims=True)
            made[i] = probs.astype(LOW), (probs * (grad_p - delta)).astype(LOW)

        def combine(i):
            s, p, which = items[i]
            here, cols, q, k, v, gc, q_t, k_t, gc_t = pair_of(s, p)
            mine = (lane >= head_dim) if which else (lane < head_dim)
            zero = jnp.zeros_like(q)
            probs, grad_s = made.pop(i)
            add_v = mm(probs, jnp.where(mine, gc, zero))
            add_k = mm(grad_s, jnp.where(mine, q, zero))
            add_q = mm(k_t[which * head_dim : (which + 1) * head_dim], grad_s)
            if which == 0:
                made[s, p] = add_v, add_k, add_q
                return
            old_v, old_k, old_q = made.pop((s, p))
            grad_q = (jnp.concatenate([old_q, add_q], 0).T * head_dim**-0.5).astype(LOW)
            grad_k = (old_k + add_k).astype(LOW)
            grad_v = (old_v + add_v).astype(LOW)
            for number, grad in enumerate((grad_q, grad_k, grad_v)):
                out_ref[here, number * width + cols.start : number * width + cols.stop] = grad
                grads[number, s, p] = grad
            stat_ref[0:1, cols] += jnp.sum(grad_q.astype(F32), 0, keepdims=True)
            stat_ref[1:2, cols] += jnp.sum(grad_v.astype(F32), 0, keepdims=True)

            if p % 2 and s == len(starts) - 1:
                project(p - 1)

        def project(p):
            for number in range(3):
                rows = [
                    jnp.concatenate([grads.pop((number, s, p)), grads.pop((number, s, p + 1))], 1)
                    for s in range(len(starts))
                ]
                product = mm(x_t_ref[...], jnp.concatenate(rows, 0))
                cols = slice(number * width + p * pair_dim, number * width + (p + 2) * pair_dim)
                if fresh:
                    sum_ref[:, cols] = product
                else:
                    sum_ref[:, cols] += product

        staged(len(items), compare, weigh, combine)

    @pl.when(block == 0)
    def _():
        attend(q_len, [s * q_len for s in range(q_dev)], [qlen_ref[s] for s in range(q_dev)], True)

    @pl.when(block > 0)
    def _():
        attend(rows_all, [0], [plen_ref[jnp.maximum(block - 1, 0)]], False)

    @pl.when(block == pl.num_programs(0) - 1)
    def _():
        tails = None
        if extra:
            tails = small_rows([*extra, stat_ref], send_ref.shape[0] * 2, send_ref.shape[2])
        store_shards(core_ref, sum_ref[...], send_ref, keep_ref, tails=tails)


def input_grad_kernel(grad_ref, base_ref, wq_ref, wk_ref, wv_ref, *out_refs):
    wide = wq_ref.shape[1]
    total = base_ref[...].astype(F32)
    for number, w_ref in enumerate((wq_ref, wk_ref, wv_ref)):
        total = total + mm_nt(grad_ref[:, number * wide : (number + 1) * wide], w_ref[...])
    low = total.astype(LOW)
    if len(out_refs) == 1:
        out_refs[0][...] = low
        return

    @pl.when(pl.program_id(0) == 0)
    def _():
        out_refs[0][...] = low

    @pl.when(pl.program_id(0) > 0)
    def _():
        out_refs[1][...] = low


def weight_grad_kernel(core_ref, left_ref, right_ref, send_ref, keep_ref):
    store_shards(core_ref, mm(left_ref[...], right_ref[...]), send_ref, keep_ref)


def small_rows(refs, count, wide):
    two, one, inner, *attn = [ref[...] for ref in refs]
    eight = jnp.concatenate(
        [jnp.concatenate([item[0:2] for item in attn], 1), one[2:3], two[2:3], one[0:2], two[0:2]], 0
    )
    inner = inner[0:1]
    short, long = eight.shape[1] // count, inner.shape[1] // count
    rows = []
    for shard in range(count):
        top = eight[:, shard * short : (shard + 1) * short]
        low = inner[:, shard * long : (shard + 1) * long]
        top = jnp.concatenate([top, jnp.zeros((8, wide - short), F32)], 1)
        low = jnp.concatenate([low, jnp.zeros((1, wide - long), F32)], 1)
        rows.append(jnp.concatenate([top, low, jnp.zeros((7, wide), F32)], 0).astype(LOW))
    return rows


def turn_kernel(part_ref, out_ref):
    out_ref[...] = part_ref[...].astype(F32).T


def turn_low_kernel(*refs):
    *inputs, out_ref = refs
    if len(inputs) == 1:
        out_ref[...] = inputs[0][...].T
        return

    @pl.when(pl.program_id(0) == 0)
    def _():
        out_ref[...] = inputs[0][...].T

    @pl.when(pl.program_id(0) > 0)
    def _():
        out_ref[...] = inputs[1][...].T


def const_spec(shape):
    return pl.BlockSpec(shape, lambda i: (0,) * len(shape), pipeline_mode=pl.Buffered(1))


def call(body, operands, in_specs, outs, grid, room, deps=(), old=(), name=None, scratch=(), us=12):
    count, extra = len(operands), len(old)
    if deps:
        tied = min(range(count), key=lambda i: operands[i].size)
        operands = list(operands)
        operands[tied] = lax.optimization_barrier((operands[tied], *deps))[0]

    def kernel(*refs):
        body(*refs[:count], *refs[count + extra :])

    return pl.pallas_call(
        kernel,
        grid=grid,
        in_specs=list(in_specs) + [pl.BlockSpec(memory_space=pl.ANY)] * extra,
        out_specs=[spec for spec, _ in outs],
        out_shape=[kind for _, kind in outs],
        scratch_shapes=scratch,
        input_output_aliases={count + i: i for i in range(extra)},
        compiler_params=pltpu.CompilerParams(vmem_limit_bytes=room * 1024 * 1024),
        cost_estimate=pl.CostEstimate(flops=int(us * 1.15e9), bytes_accessed=0, transcendentals=0),
        name=name,
    )(*operands, *old)


def weight_grad(left_t, right, row_count, core, deps, old):
    height, depth = left_t.shape
    wide = right.shape[1]
    block = min(wide, 768)
    shape = old[0].shape
    spec = pl.BlockSpec((*shape[:2], block), lambda i: (0, 0, i))
    return call(
        weight_grad_kernel,
        (core, left_t, right),
        [
            pl.BlockSpec(memory_space=pltpu.SMEM),
            const_spec((height, depth)),
            pl.BlockSpec((depth, block), lambda i: (0, i)),
        ],
        [(spec, jax.ShapeDtypeStruct(shape, LOW))] * 2,
        (wide // block,),
        56,
        deps,
        old,
        name="weight_grad",
    )


def add_kernel(*refs):
    *terms, out_ref = refs
    out_ref[...] = sum([ref[...].astype(F32) for ref in terms[1:]], terms[0][...].astype(F32)).astype(LOW)


def add_all(terms):
    shape = terms[0].shape
    spec = pl.BlockSpec(shape, lambda i: (0,) * len(shape), pipeline_mode=pl.Buffered(1))
    outs = [(spec, jax.ShapeDtypeStruct(shape, LOW))]
    return call(add_kernel, terms, [spec] * len(terms), outs, (1,), 24, name="add_all", us=12)[0]


class Flow:
    def __init__(self, sent, kept, line=False, fused=False):
        bits = lax.axis_size("row").bit_length() - 1
        self.order = [(0,)] + [tuple(range(i, min(i + 2, bits))) for i in range(1, bits, 2)]
        self.left = list(range(bits - 1, 0, -1))
        count = lax.axis_size("col")
        self.line = [(None, [(i, i ^ (1 << bit)) for i in range(count)]) for bit in range(count.bit_length() - 1)]
        if line:
            half = count // 2
            self.line = [(None, [(i, i + 1), (count - 1 - i, count - 2 - i)]) for i in range(half - 1)]
            self.line += [(None, [(half - 1, half), (half, half - 1)])]
            self.line += [
                ((i, count - 1 - i), [(i + 1, i), (count - 2 - i, count - 1 - i)])
                for i in range(half - 2, -1, -1)
            ]
        self.sent, self.kept, self.got, self.fused = [sent], kept, None, fused

    def shard(self, terms, bits, mask):
        here = lax.axis_index("row")
        order = [self.left.index(bit) for bit in bits]
        total = None
        for term in terms:
            starts, sizes = [0] * term.ndim, list(term.shape)
            for axis, bit in zip(order, bits):
                starts[axis], sizes[axis] = ((here ^ mask) >> bit) & 1, 1
            piece = lax.dynamic_slice(term, starts, sizes)
            piece = piece.reshape([size for i, size in enumerate(sizes) if i not in order]).astype(F32)
            total = piece if total is None else total + piece
        return total.astype(LOW)

    def step(self):
        if self.order:
            bits = self.order[0]
            masks = [
                sum(1 << bit for i, bit in enumerate(bits) if other >> i & 1)
                for other in range(1, 1 << len(bits))
            ]
            if bits != (0,):
                terms = [self.kept, *self.got]
                self.sent = [self.shard(terms, bits, mask) for mask in masks]
                self.kept = self.shard(terms, bits, 0)
                self.left = [bit for bit in self.left if bit not in bits]
            size = lax.axis_size("row")
            self.got = [
                lax.ppermute(sent, "row", [(i, i ^ mask) for i in range(size)])
                for sent, mask in zip(self.sent, masks)
            ]
        else:
            self.sent = [self.kept]
            self.got = [lax.ppermute(self.kept, "col", self.line[0][1])]

    def land(self, token=None):
        if token is not None:
            self.kept = lax.optimization_barrier((self.kept, token))[0]
        got = self.got
        if self.order:
            bits = self.order.pop(0)
            if bits == (0,):
                dims = (2,) * len(self.left) + self.kept.shape[1:]
                self.kept, self.got = self.kept.reshape(dims), [item.reshape(dims) for item in self.got]
            if not self.order and self.fused:
                self.kept = add_all([self.kept, *self.got])
            elif not self.order:
                self.kept = sum([item.astype(F32) for item in self.got], self.kept.astype(F32)).astype(LOW)
        else:
            ends, _ = self.line.pop(0)
            if ends is None:
                self.kept = self.kept + self.got[0]
            else:
                here = lax.axis_index("col")
                self.kept = jnp.where((here == ends[0]) | (here == ends[1]), self.got[0], self.kept)
        return got

    def turn(self, token=None):
        got = self.land(token)
        if self.done:
            return got
        self.step()
        return got + self.sent

    @property
    def done(self):
        return not self.order and not self.line


def gather_all(piece):
    row_bits = lax.axis_size("row").bit_length() - 1
    col_bits = lax.axis_size("col").bit_length() - 1
    steps = [("col", tuple(range(i, min(i + 2, col_bits)))) for i in range(0, col_bits, 2)]
    steps += [("row", tuple(range(i, min(i + 2, row_bits)))) for i in range(1, row_bits, 2)]
    for name, bits in steps + [("row", (0,))]:
        here = lax.axis_index(name)
        pieces = [piece]
        for other in range(1, 1 << len(bits)):
            mask = sum(1 << bit for i, bit in enumerate(bits) if other >> i & 1)
            pairs = [(i, i ^ mask) for i in range(lax.axis_size(name))]
            pieces.append(lax.ppermute(piece, name, pairs))
        for i, bit in enumerate(bits):
            high = ((here >> bit) & 1) == 1
            pieces = [
                jnp.where(high, pieces[place ^ (1 << i)], pieces[place]) for place in range(len(pieces))
            ]
        piece = jnp.concatenate(pieces, 0)
    return piece


def per_device(
    query_tokens, passage_tokens, query_lengths, passage_lengths, positives,
    w_query, w_key, w_value, w_attn_out, w_inner, w_outer,
    bias_query, bias_value, bias_attn_out, bias_inner, bias_outer,
    gain_one, shift_one, gain_two, shift_two,
):
    q_dev, q_len, width = query_tokens.shape
    p_dev, p_len, _ = passage_tokens.shape
    inner = w_inner.shape[1]
    rows_all = p_len
    assert q_dev * q_len == rows_all and q_dev + p_dev <= SLOTS
    blocks = 1 + p_dev
    total_rows = blocks * rows_all
    row_count = lax.axis_size("row")
    col_count = lax.axis_size("col")
    row_here = lax.axis_index("row")
    core = (row_here & 1).reshape(1)
    me = (row_here * col_count + lax.axis_index("col")).reshape(1)
    params = pltpu.CompilerParams(vmem_limit_bytes=VMEM)
    smem = pl.BlockSpec(memory_space=pltpu.SMEM)

    def by_block(wide):
        return pl.BlockSpec((rows_all, wide), lambda i: (i, 0))

    def by_block_t(high):
        return pl.BlockSpec((high, rows_all), lambda i: (0, i))

    def fixed(shape):
        return pl.BlockSpec(shape, lambda i: (0,) * len(shape))

    queries_spec = pl.BlockSpec((rows_all, width), lambda i: (0, 0))
    passages_spec = pl.BlockSpec((rows_all, width), lambda i: (jnp.maximum(i - 1, 0), 0))

    lse_spec = pl.BlockSpec((1, HEADS // 2, 8, rows_all), lambda i: (i, 0, 0, 0))

    def shape(*dims, kind=LOW):
        return jax.ShapeDtypeStruct(dims, kind)

    queries = query_tokens.reshape(rows_all, width)
    passages = passage_tokens.reshape(p_dev * rows_all, width)
    square = const_spec((width, width))
    anywhere = pl.BlockSpec(memory_space=pl.ANY)
    thin = const_spec((width,))

    q, k, v, ctx_t, lse = call(
        partial(attend_kernel, (q_dev, q_len, rows_all, width)),
        (query_lengths, passage_lengths, queries, passages, w_query, w_key, w_value, bias_query, bias_value),
        [smem, smem, queries_spec, passages_spec, square, square, square, thin, thin],
        [(by_block(width), shape(total_rows, width))] * 3
        + [
            (by_block_t(width), shape(width, total_rows)),
            (lse_spec, shape(blocks, HEADS // 2, 8, rows_all, kind=F32)),
        ],
        (blocks,),
        56,
        name="attend",

    )

    rows_part = rows_all // 2
    parts = 2 * blocks

    def by_part(wide):
        return pl.BlockSpec((rows_part, wide), lambda i: (i, 0))

    queries_part = pl.BlockSpec((rows_part, width), lambda i: (jnp.minimum(i, 1), 0))
    passages_part = pl.BlockSpec((rows_part, width), lambda i: (jnp.maximum(i - 2, 0), 0))
    h1, y1, act, slope, h2, query_out, passage_out, pooled, payload = call(
        partial(dense_kernel, (q_dev, q_len, p_len, width, inner)),
        (
            query_lengths, passage_lengths, positives, queries, passages, ctx_t, w_attn_out, w_inner, w_outer,
            bias_attn_out, bias_inner, bias_outer, gain_one, shift_one, gain_two, shift_two,
        ),
        [smem, smem, smem, queries_part, passages_part, pl.BlockSpec((width, rows_part), lambda i: (0, i))]
        + [anywhere] * 3
        + [thin, const_spec((inner,))]
        + [thin] * 5,
        [
            (by_part(width), shape(total_rows, width)),
            (by_part(width), shape(total_rows, width)),
            (by_part(inner), shape(total_rows, inner)),
            (by_part(inner), shape(total_rows, inner)),
            (by_part(width), shape(total_rows, width)),
            (queries_part, shape(rows_all, width)),
            (passages_part, shape(p_dev * rows_all, width)),
            (fixed((SLOTS, width)), shape(SLOTS, width, kind=F32)),
            (fixed((SLOTS, width + 128)), shape(SLOTS, width + 128)),
        ],
        (parts,),
        56,
        name="dense",
        scratch=[
            pltpu.VMEM((width, width), LOW),
            pltpu.VMEM((width, inner), LOW),
            pltpu.VMEM((inner, width), LOW),
            pltpu.SemaphoreType.DMA((3,)),
        ],

    )

    gathered = gather_all(payload)
    loss, gvec = pl.pallas_call(
        partial(loss_kernel, (q_dev, p_dev, width, col_count)),
        in_specs=[smem] * 3 + [pl.BlockSpec(memory_space=pltpu.VMEM)] * 3,
        out_specs=[pl.BlockSpec(memory_space=pltpu.VMEM)] * 2,
        out_shape=[shape(8, 128, kind=F32), shape(SLOTS, width, kind=F32)],
        compiler_params=params,
        name="loss",
    )(me, query_lengths, passage_lengths, payload, gathered, pooled)

    smalls = shape(8, width, kind=F32)
    cut = width // row_count
    cut_inner = inner // row_count
    half = row_count // 2
    step_cols = 768
    per_step = step_cols // cut_inner
    outer_spec = pl.BlockSpec((per_step // 2, width, cut_inner), lambda i: (i, 0, 0))
    grad_f, stat_two, *outer_parts = call(
        partial(outer_grad_kernel, (q_dev, q_len, p_len)),
        (core, query_lengths, passage_lengths, gvec, h2, gain_two, act),
        [smem, smem, smem, fixed((SLOTS, width)), const_spec((total_rows, width)), thin]
        + [pl.BlockSpec((total_rows, step_cols), lambda i: (0, i))],
        [
            (fixed((total_rows, width)), shape(total_rows, width)),
            (fixed((8, width)), smalls),
            (outer_spec, shape(half, width, cut_inner)),
            (outer_spec, shape(half, width, cut_inner)),
        ],
        (inner // step_cols,),
        56,
        name="outer_grad",
        scratch=[pltpu.VMEM((width, total_rows), LOW)],
    )
    outer = Flow(*outer_parts, line=True)
    outer.step()

    def turn(arrays, specs, deps):
        outs = [(by_block_t(width), shape(width, total_rows))]
        return call(turn_low_kernel, arrays, specs, outs, (blocks,), 56, deps, name="turn", us=40)[0]

    y1_t = turn([y1], [by_block(width)], outer.sent)
    deps = outer.turn(y1_t)
    attn_spec = pl.BlockSpec((half, cut, width), lambda i: (0, 0, inner // width))
    grad_u, grad_attn, grad_ctx, stat_one, grad_bias_inner, *up_parts = call(
        partial(dense_back_kernel, (rows_all, width, inner)),
        (core, grad_f, slope, h1, ctx_t, w_outer, w_inner, w_attn_out, gain_one),
        [smem, by_block(width), by_block(inner), by_block(width), by_block_t(width)]
        + [anywhere, anywhere, anywhere, thin],
        [
            (by_block(inner), shape(total_rows, inner)),
            (by_block(width), shape(total_rows, width)),
            (by_block(width), shape(total_rows, width)),
            (fixed((8, width)), smalls),
            (fixed((8, inner)), shape(8, inner, kind=F32)),
            (attn_spec, shape(half, cut, inner + width)),
            (attn_spec, shape(half, cut, inner + width)),
        ],
        (blocks,),
        60,
        deps,
        name="dense_back",
        scratch=[
            pltpu.VMEM((width, width), F32),
            pltpu.VMEM((inner, width), LOW),
            pltpu.VMEM((width, inner), LOW),
            pltpu.VMEM((width, width), LOW),
            pltpu.SemaphoreType.DMA((5,)),
        ],
    )
    deps = outer.turn(stat_one)
    up_flow = Flow(*weight_grad(y1_t, grad_u, row_count, core, deps, up_parts), line=True, fused=True)
    up_flow.step()
    deps = up_flow.sent + outer.turn(up_flow.sent[0])
    x_t = turn([queries, passages], [queries_spec, passages_spec], deps)
    deps = up_flow.turn(x_t)

    head_dim = width // HEADS
    third = 4 * head_dim
    groups = [(0, 2 * third), (2 * third, third)]

    def attend_back(start, wide, deps, extra=()):
        pairs = wide // (2 * head_dim)
        index = start // wide
        cols = pl.BlockSpec((rows_all, wide), lambda i: (i, index))
        rows = cut + (16 if extra else 0)
        return call(
            partial(attend_back_kernel, (q_dev, q_len, rows_all, head_dim)),
            (core, query_lengths, passage_lengths, q, k, v, ctx_t, lse, grad_ctx, x_t, *extra),
            [smem, smem, smem]
            + [cols] * 3
            + [
                pl.BlockSpec((wide, rows_all), lambda i: (index, i)),
                pl.BlockSpec((1, pairs, 8, rows_all), lambda i: (i, index, 0, 0)),
                cols,
                by_block_t(width),
            ]
            + [const_spec(item.shape) for item in extra],
            [
                (by_block(3 * wide), shape(total_rows, 3 * wide)),
                (fixed((8, wide)), shape(8, wide, kind=F32)),
            ]
            + [(fixed((half, rows, 3 * wide)), shape(half, rows, 3 * wide))] * 2,
            (blocks,),
            56,
            deps,
            name="attend_back",
            scratch=[pltpu.VMEM((width, 3 * wide), F32)],
        )

    def input_grad(start, wide, grad, base, outs, deps, us):
        index = start // wide
        cols = pl.BlockSpec((width, wide), lambda i: (0, index), pipeline_mode=pl.Buffered(1))
        return call(
            input_grad_kernel,
            (grad, base, w_query, w_key, w_value),
            [by_block(3 * wide), by_block(width), cols, cols, cols],
            outs,
            (blocks,),
            56,
            deps,
            name="input_grad",
            us=us,
        )

    grad_a, stat_a, *mixed_parts = attend_back(*groups[0], deps)
    mixed_flow = Flow(*mixed_parts)
    mixed_flow.step()
    deps = mixed_flow.sent + outer.turn(stat_a)
    (part_grad,) = input_grad(
        *groups[0], grad_a, grad_attn, [(by_block(width), shape(total_rows, width))], deps, 0
    )
    deps = up_flow.turn(part_grad) + mixed_flow.turn(up_flow.kept)
    extra = (stat_two, stat_one, grad_bias_inner, stat_a)
    grad_b, stat_b, *last_parts = attend_back(*groups[1], deps, extra)
    last_flow = Flow(*last_parts)
    last_flow.step()
    deps = last_flow.sent + outer.turn(stat_b) + mixed_flow.turn(stat_b) + up_flow.turn(stat_b)
    query_grad, passage_grad = input_grad(
        *groups[1],
        grad_b,
        part_grad,
        [
            (queries_spec, shape(rows_all, width)),
            (passages_spec, shape(p_dev * rows_all, width)),
        ],
        deps,
        12,
    )
    last_flow.turn(passage_grad)
    mixed_flow.turn(last_flow.kept)
    up_flow.turn(mixed_flow.kept)
    outs = [(fixed((cut_inner, width)), shape(cut_inner, width, kind=F32))]
    (turned,) = call(
        turn_kernel, (outer.kept,), [const_spec((width, cut_inner))], outs, (1,), 56, [up_flow.kept], name="turn", us=40
    )
    last_flow.turn(turned)
    last_flow.turn()
    mixed_flow.turn(last_flow.kept)
    last_flow.turn(mixed_flow.kept)
    flows = [outer, up_flow, mixed_flow, last_flow]
    while not all(flow.done for flow in flows):
        for flow in flows:
            if not flow.done:
                flow.turn()
    mixed, last = mixed_flow.kept, last_flow.kept
    qkv = [
        jnp.concatenate(
            [mixed[:, i * 2 * third : (i + 1) * 2 * third], last[:cut, i * third : (i + 1) * third]], 1
        ).astype(F32)
        for i in range(3)
    ]
    up_sum = up_flow.kept
    small = last[cut:].astype(F32)
    return (
        loss[0, 0],
        query_out.reshape(query_tokens.shape),
        passage_out.reshape(passage_tokens.shape),
        query_grad.reshape(query_tokens.shape),
        passage_grad.reshape(passage_tokens.shape),
        *qkv,
        up_sum[:, inner:].astype(F32),
        up_sum[:, :inner].astype(F32),
        turned,
        *[small[i, :cut] for i in range(3)],
        small[8, : inner // row_count],
        *[small[i, :cut] for i in range(3, 8)],
    )


def solution(mesh):
    in_specs = (
        P(("row", "col"), None, None),
        P(("row", "col"), None, None),
        P(("row", "col")),
        P(("row", "col")),
        P(("row", "col")),
        P(),
        P(),
        P(),
        P(),
        P(),
        P(),
        P(),
        P(),
        P(),
        P(),
        P(),
        P(),
        P(),
        P(),
        P(),
    )
    out_specs = (
        P(),
        P(("row", "col"), None, None),
        P(("row", "col"), None, None),
        P(("row", "col"), None, None),
        P(("row", "col"), None, None),
        P("row", None),
        P("row", None),
        P("row", None),
        P("row", None),
        P("row", None),
        P("row", None),
        P("row"),
        P("row"),
        P("row"),
        P("row"),
        P("row"),
        P("row"),
        P("row"),
        P("row"),
        P("row"),
    )
    return jax.shard_map(
        per_device, mesh=mesh, in_specs=in_specs, out_specs=out_specs, check_vma=False
    )
```

```python
from functools import partial

import jax
import jax.numpy as jnp
from jax import lax
from jax.experimental import pallas as pl
from jax.experimental.pallas import tpu as pltpu
from jax.sharding import PartitionSpec as P

HEADS = 12
EPS_NORM = 1e-12
EPS_POOL = 1e-06
SCALE_LOSS = 128.0
INV_TEMP = 100.0
TILE = 256
SLOTS = 8
VMEM = 60 * 1024 * 1024
LOW = jnp.bfloat16
F32 = jnp.float32


def mm(left, right):
    return lax.dot_general(left, right, (((1,), (0,)), ((), ())), preferred_element_type=F32)


def mm_nt(left, right):
    return lax.dot_general(left, right, (((1,), (1,)), ((), ())), preferred_element_type=F32)


def norm_parts(hidden):
    center = hidden - jnp.mean(hidden, -1, keepdims=True)
    spread = jnp.mean(center * center, -1, keepdims=True)
    scale = lax.rsqrt(spread + EPS_NORM)
    return center * scale, scale


def gelu_parts(u):
    square = u * u
    q = 1.4250060785476853e-06
    for factor in (-3.669345091379551e-05, -8.782652731110375e-05, 0.03639228618131223, 0.7978697123041883):
        q = q * square + factor
    share = 0.5 + 0.5 * jnp.tanh(u * q)
    bell = jnp.exp(-0.5 * square)
    return u * share, share + (0.3989422804014327 * u) * bell


def vec(ref, cols=slice(None)):
    return ref[cols].reshape(1, -1)


def rows_of(step, size):
    return pl.ds(pl.multiple_of(step * size, size), size)


def part_owner(part, q_dev, q_len, p_len, qlen_ref, plen_ref):
    per = p_len // q_len
    beyond = jnp.maximum(part - q_dev, 0)
    is_query = part < q_dev
    slot = jnp.where(is_query, part, q_dev + beyond // per)
    length = jnp.where(is_query, qlen_ref[jnp.where(is_query, part, 0)], plen_ref[beyond // per])
    first = jnp.where(is_query, 0, beyond % per * q_len)
    return slot, length, first


def live_rows(first, length, size):
    return (first + lax.broadcasted_iota(jnp.int32, (size, 1), 0)) < length


def sure_rows(size):
    return size * 4 // 5 // 16 * 16


def half_only(pair_t, which):
    half = pair_t.shape[0] // 2
    zeros = jnp.zeros((half, pair_t.shape[1]), pair_t.dtype)
    if which == 0:
        return jnp.concatenate([pair_t[:half], zeros], 0)
    return jnp.concatenate([zeros, pair_t[half:]], 0)


def staged(count, *stages):
    for step in range(count + len(stages) - 1):
        for late, stage in enumerate(stages):
            if 0 <= step - late < count:
                stage(step - late)


def fetch(source, target, sems, index):
    return pltpu.make_async_copy(source, target, sems.at[index])


def attend_kernel(
    dims, qlen_ref, plen_ref, xq_ref, xp_ref, wq_ref, wk_ref, wv_ref, bq_ref, bv_ref,
    q_ref, k_ref, v_ref, ctx_t_ref, lse_ref,
):
    q_dev, q_len, rows_all, width = dims
    block = pl.program_id(0)
    head_dim = width // HEADS
    x = jnp.where(block == 0, xq_ref[...], xp_ref[...])
    q = ((mm(x, wq_ref[...]) + vec(bq_ref)) * head_dim**-0.5).astype(LOW)
    k = mm(x, wk_ref[...]).astype(LOW)
    v = (mm(x, wv_ref[...]) + vec(bv_ref)).astype(LOW)
    q_ref[...] = q
    k_ref[...] = k
    v_ref[...] = v
    q_t, v_t = q.T, v.T

    def attend(size, starts, lengths):
        items = [(start, length, head) for head in range(HEADS) for start, length in zip(starts, lengths)]
        scores, weights = {}, {}

        def compare(i):
            start, length, head = items[i]
            cols = slice(head // 2 * 2 * head_dim, (head // 2 + 1) * 2 * head_dim)
            here = slice(start, start + size)
            scores[i] = mm(k[here, cols], half_only(q_t[cols, here], head % 2))

        def weigh(i):
            start, length, head = items[i]
            edge = sure_rows(size)
            early, late = scores[i][:edge], scores.pop(i)[edge:]
            late = jnp.where(live_rows(edge, length, size - edge), late, -1e30)
            top = jnp.maximum(jnp.max(early, 0, keepdims=True), jnp.max(late, 0, keepdims=True))
            weights[i] = top, jnp.concatenate([jnp.exp(early - top).astype(LOW), jnp.exp(late - top).astype(LOW)], 0)

        def combine(i):
            start, length, head = items[i]
            here, rows = slice(start, start + size), slice(head * head_dim, (head + 1) * head_dim)
            top, weight = weights.pop(i)
            values = jnp.concatenate([v_t[rows, here], jnp.ones((16, size), LOW)], 0)
            result = mm(values, weight)
            total = result[head_dim : head_dim + 1]
            lse_ref[0, head // 2, head % 2 : head % 2 + 1, here] = top + jnp.log(total)
            ctx_t_ref[rows, here] = (result[:head_dim] * (1.0 / total)).astype(LOW)

        staged(len(items), compare, weigh, combine)

    @pl.when(block == 0)
    def _():
        attend(q_len, [s * q_len for s in range(q_dev)], [qlen_ref[s] for s in range(q_dev)])

    @pl.when(block > 0)
    def _():
        attend(rows_all, [0], [plen_ref[jnp.maximum(block - 1, 0)]])


def dense_kernel(
    dims, qlen_ref, plen_ref, pos_ref, xq_ref, xp_ref, ctx_t_ref, wo_hbm, wi_hbm, wf_hbm,
    bo_ref, bi_ref, bf_ref, g1_ref, s1_ref, g2_ref, s2_ref,
    h1_ref, y1_ref, act_ref, dg_ref, h2_ref, yq_ref, yp_ref, pool_ref, pay_ref,
    wo_ref, wi_ref, wf_ref, sems,
):
    q_dev, q_len, p_len, width, inner = dims
    block = pl.program_id(0)
    rows_all = xq_ref.shape[0]
    query_blocks = q_dev * q_len // rows_all
    copies = [
        fetch(source, target, sems, index)
        for index, (source, target) in enumerate([(wo_hbm, wo_ref), (wi_hbm, wi_ref), (wf_hbm, wf_ref)])
    ]

    @pl.when(block == 0)
    def _():
        for copy in copies:
            copy.start()
        pool_ref[...] = jnp.zeros_like(pool_ref)
        copies[0].wait()

    x = jnp.where(block < query_blocks, xq_ref[...], xp_ref[...])
    hidden = x.astype(F32) + (mm(ctx_t_ref[...].T, wo_ref[...]) + vec(bo_ref))
    h1_ref[...] = hidden.astype(LOW)
    y1 = norm_parts(hidden)[0] * vec(g1_ref) + vec(s1_ref)
    y1_low = y1.astype(LOW)
    y1_ref[...] = y1_low

    @pl.when(block == 0)
    def _():
        copies[1].wait()
        copies[2].wait()

    raw, made = {}, {}

    def expand(i):
        cols = slice(i * TILE, (i + 1) * TILE)
        raw[i] = mm(y1_low, wi_ref[:, cols]) + vec(bi_ref, cols)

    def activate(i):
        cols = slice(i * TILE, (i + 1) * TILE)
        act, slope = gelu_parts(raw.pop(i))
        made[i] = act.astype(LOW)
        act_ref[:, cols] = made[i]
        dg_ref[:, cols] = slope.astype(LOW)

    staged(inner // TILE, expand, activate)
    left = jnp.concatenate([made[i] for i in range(inner // TILE)], 1)
    total = (y1 + vec(bf_ref)) + mm(left, wf_ref[...])
    h2_ref[...] = total.astype(LOW)
    y2 = norm_parts(total)[0] * vec(g2_ref) + vec(s2_ref)
    for part in range(rows_all // q_len):
        number = block * (rows_all // q_len) + part
        slot, length, first = part_owner(number, q_dev, q_len, p_len, qlen_ref, plen_ref)
        piece = y2[part * q_len : (part + 1) * q_len]
        summed = jnp.sum(jnp.where(live_rows(first, length, q_len), piece, 0.0), 0, keepdims=True)
        in_slot = lax.broadcasted_iota(jnp.int32, (SLOTS, 1), 0) == slot
        pool_ref[...] += jnp.where(in_slot, summed / length.astype(F32), 0.0)

    @pl.when(block < query_blocks)
    def _():
        yq_ref[...] = y2.astype(LOW)

    @pl.when(block >= query_blocks)
    def _():
        yp_ref[...] = y2.astype(LOW)

    @pl.when(block == pl.num_programs(0) - 1)
    def _():
        pooled = pool_ref[...]
        emb = pooled * lax.rsqrt(jnp.sum(pooled * pooled, -1, keepdims=True) + EPS_POOL)
        pay_ref[:, :width] = emb.astype(LOW)
        row = lax.broadcasted_iota(jnp.int32, (SLOTS, 128), 0)
        col = lax.broadcasted_iota(jnp.int32, (SLOTS, 128), 1)
        place = jnp.zeros((SLOTS, 128), jnp.int32)
        for j in range(q_dev):
            high = pos_ref[j] // 128
            low = pos_ref[j] - high * 128
            place = jnp.where(row == j, jnp.where(col == 0, high, jnp.where(col == 1, low, 0)), place)
        pay_ref[:, width:] = place.astype(F32).astype(LOW)


def loss_kernel(
    dims, me_ref, qlen_ref, plen_ref, own_ref, all_ref, pool_ref, loss_ref, gvec_ref
):
    q_dev, p_dev, width, col_count = dims
    count = all_ref.shape[0]
    every = all_ref[:, :width]
    own = own_ref[:, :width]

    def passage_mask(index):
        spot, place = index % SLOTS, index // SLOTS
        per_core = count // SLOTS // 2
        core, rest = place // per_core, place % per_core
        device = (rest // col_count * 2 + core) * col_count + rest % col_count
        return (spot >= q_dev) & (spot < q_dev + p_dev), device * p_dev + spot - q_dev

    scores = mm_nt(own, every) * INV_TEMP
    valid, ident = passage_mask(lax.broadcasted_iota(jnp.int32, (SLOTS, count), 1))
    scores = jnp.where(valid, scores, -1e30)
    top = jnp.max(scores, -1, keepdims=True)
    totals = top + jnp.log(jnp.sum(jnp.exp(scores - top), -1, keepdims=True))
    marks = own_ref[:, width:].astype(F32)
    wanted = marks[:, 0:1] * 128.0 + marks[:, 1:2]
    target = (valid & (ident.astype(F32) == wanted)).astype(F32)
    raw = (INV_TEMP * (SCALE_LOSS * (jnp.exp(scores - totals) - target))).astype(LOW)
    grad_q = mm(raw, every)

    picker_col = lax.broadcasted_iota(jnp.int32, (SLOTS, 128), 1)
    picker = jnp.where(picker_col == 0, 128.0, jnp.where(picker_col == 1, 1.0, 0.0)).astype(LOW)
    own_row = lax.broadcasted_iota(jnp.int32, (SLOTS, TILE), 0)
    own_valid = (own_row >= q_dev) & (own_row < q_dev + p_dev)
    own_ident = (me_ref[0] * p_dev + own_row - q_dev).astype(F32)

    def body(step, carry):
        total_loss, grad_p = carry
        rows = rows_of(step, TILE)
        some = all_ref[rows, :width]
        place = mm_nt(picker, all_ref[rows, width:])[0:1]
        table = mm_nt(every, some) * INV_TEMP
        ok, names = passage_mask(lax.broadcasted_iota(jnp.int32, (count, TILE), 0))
        picked = jnp.sum(jnp.where(ok & (names.astype(F32) == place), table, 0.0), 0, keepdims=True)
        table = jnp.where(ok, table, -1e30)
        high = jnp.max(table, 0, keepdims=True)
        lse = high + jnp.log(jnp.sum(jnp.exp(table - high), 0, keepdims=True))
        is_query = lax.broadcasted_iota(jnp.int32, (1, TILE), 1) % SLOTS < q_dev
        losses = jnp.where(is_query, lse - picked, 0.0)
        mine = mm_nt(own, some) * INV_TEMP
        hit = (own_ident == place).astype(F32)
        grads = INV_TEMP * (SCALE_LOSS * (jnp.exp(mine - lse) - hit))
        grads = jnp.where(own_valid & is_query, grads, 0.0).astype(LOW)
        return total_loss + jnp.sum(losses, 1, keepdims=True), grad_p + mm(grads, some)

    start = (jnp.zeros((1, 1), F32), jnp.zeros((SLOTS, width), F32))
    total_loss, grad_p = lax.fori_loop(0, count // TILE, body, start)
    loss_ref[...] = jnp.broadcast_to(total_loss / float(count // SLOTS * q_dev), loss_ref.shape)

    slot = lax.broadcasted_iota(jnp.int32, (SLOTS, 1), 0)
    grad = jnp.where(slot < q_dev, grad_q, grad_p)
    pooled = pool_ref[...]
    r = lax.rsqrt(jnp.sum(pooled * pooled, -1, keepdims=True) + EPS_POOL)
    inside = jnp.sum(pooled * grad, -1, keepdims=True)
    length = jnp.ones((SLOTS, 1), F32)
    for j in range(q_dev):
        length = jnp.where(slot == j, qlen_ref[j].astype(F32), length)
    for j in range(p_dev):
        length = jnp.where(slot == q_dev + j, plen_ref[j].astype(F32), length)
    gvec_ref[...] = (r * grad - r * r * r * inside * pooled) / length


def store_shards(core_ref, result, send_ref, keep_ref, by_row=True, tails=None):
    count = send_ref.shape[0] * 2
    size = result.shape[0 if by_row else 1] // count

    def store(even, odd):
        for shard in range(count):
            spot = slice(shard * size, (shard + 1) * size)
            piece = (result[spot, :] if by_row else result[:, spot]).astype(LOW)
            target = odd if shard % 2 else even
            if tails is None:
                target[shard // 2] = piece
            else:
                target[shard // 2, :size] = piece
                target[shard // 2, size:] = tails[shard]

    @pl.when(core_ref[0] == 0)
    def _():
        store(keep_ref, send_ref)

    @pl.when(core_ref[0] == 1)
    def _():
        store(send_ref, keep_ref)


def outer_grad_kernel(
    dims, core_ref, qlen_ref, plen_ref, gvec_ref, h2_ref, g2_ref, act_ref,
    gf_ref, stat_ref, send_ref, keep_ref, gf_t_ref,
):
    q_dev, q_len, p_len = dims

    @pl.when(pl.program_id(0) == 0)
    def _():
        stat_ref[...] = jnp.zeros_like(stat_ref)

        def body(part, carry):
            rows = rows_of(part, q_len)
            slot, length, first = part_owner(part, q_dev, q_len, p_len, qlen_ref, plen_ref)
            in_slot = lax.broadcasted_iota(jnp.int32, (SLOTS, 1), 0) == slot
            grad_y = jnp.sum(jnp.where(in_slot, gvec_ref[...], 0.0), 0, keepdims=True)
            live = live_rows(first, length, q_len)
            n2, r2 = norm_parts(h2_ref[rows, :].astype(F32))
            g = grad_y * vec(g2_ref)
            grad = r2 * (g - jnp.mean(g, -1, keepdims=True) - n2 * jnp.mean(g * n2, -1, keepdims=True))
            grad = jnp.where(live, grad, 0.0)
            low = grad.astype(LOW)
            gf_ref[rows, :] = low
            gf_t_ref[:, rows] = low.T
            stat_ref[0:1, :] += grad_y * jnp.sum(jnp.where(live, n2, 0.0), 0, keepdims=True)
            stat_ref[1:2, :] += grad_y * jnp.sum(live.astype(F32), 0, keepdims=True)
            stat_ref[2:3, :] += jnp.sum(low.astype(F32), 0, keepdims=True)
            return carry

        lax.fori_loop(0, h2_ref.shape[0] // q_len, body, 0)

    store_shards(core_ref, mm(gf_t_ref[...], act_ref[...]), send_ref, keep_ref, by_row=False)


def dense_back_kernel(
    dims, gf_ref, dg_ref, h1_ref, wf_hbm, wi_hbm, wo_hbm, g1_ref,
    gu_ref, ga_ref, gc_ref, stat_ref, bi_ref,
    wf_ref, wi_ref, wo_ref, sems,
):
    inner = dims
    block = pl.program_id(0)
    copies = [
        fetch(source, target, sems, index)
        for index, (source, target) in enumerate([(wf_hbm, wf_ref), (wi_hbm, wi_ref), (wo_hbm, wo_ref)])
    ]

    @pl.when(block == 0)
    def _():
        for copy in copies:
            copy.start()
        stat_ref[...] = jnp.zeros_like(stat_ref)
        bi_ref[...] = jnp.zeros_like(bi_ref)
        copies[0].wait()

    gf = gf_ref[...]
    raw, made, biases = {}, {}, []

    def spread(i):
        raw[i] = mm_nt(gf, wf_ref[i * TILE : (i + 1) * TILE, :])

    def slope(i):
        cols = slice(i * TILE, (i + 1) * TILE)
        made[i] = (raw.pop(i) * dg_ref[:, cols].astype(F32)).astype(LOW)
        gu_ref[:, cols] = made[i]
        biases.append(jnp.sum(made[i].astype(F32), 0, keepdims=True))

    staged(inner // TILE, spread, slope)
    bi_ref[0:1, :] += jnp.concatenate(biases, 1)
    left = jnp.concatenate([made[i] for i in range(inner // TILE)], 1)

    @pl.when(block == 0)
    def _():
        for copy in copies[1:]:
            copy.wait()

    total = gf.astype(F32) + mm_nt(left, wi_ref[...])
    n1, r1 = norm_parts(h1_ref[...].astype(F32))
    stat_ref[0:1, :] += jnp.sum(total * n1, 0, keepdims=True)
    stat_ref[1:2, :] += jnp.sum(total, 0, keepdims=True)
    g = total * vec(g1_ref)
    grad = r1 * (g - jnp.mean(g, -1, keepdims=True) - n1 * jnp.mean(g * n1, -1, keepdims=True))
    low = grad.astype(LOW)
    ga_ref[...] = low
    stat_ref[2:3, :] += jnp.sum(low.astype(F32), 0, keepdims=True)
    gc_ref[...] = mm_nt(low, wo_ref[...]).astype(LOW)


def attend_back_kernel(
    dims, core_ref, qlen_ref, plen_ref, q_ref, k_ref, v_ref, ctx_t_ref, lse_ref, gc_ref, x_t_ref, *refs
):
    *extra, out_ref, stat_ref, send_ref, keep_ref, sum_ref = refs
    q_dev, q_len, rows_all, head_dim = dims
    block = pl.program_id(0)
    pair_dim = 2 * head_dim
    width = q_ref.shape[1]
    pairs = width // pair_dim

    @pl.when(block == 0)
    def _():
        stat_ref[...] = jnp.zeros_like(stat_ref)

    def attend(size, starts, lengths, fresh):
        lane = lax.broadcasted_iota(jnp.int32, (size, pair_dim), 1)
        items = [(s, p, which) for p in range(pairs) for s in range(len(starts)) for which in range(2)]
        held, raw, made, grads = {}, {}, {}, {}

        def pair_of(s, p):
            if (s, p) not in held:
                here, cols = slice(starts[s], starts[s] + size), slice(p * pair_dim, (p + 1) * pair_dim)
                q, k, v, gc = q_ref[here, cols], k_ref[here, cols], v_ref[here, cols], gc_ref[here, cols]
                held[s, p] = here, cols, q, k, v, gc, q.T, k.T, gc.T
            return held[s, p]

        def compare(i):
            s, p, which = items[i]
            here, cols, q, k, v, gc, q_t, k_t, gc_t = pair_of(s, p)
            raw[i] = mm(k, half_only(q_t, which)), mm(v, half_only(gc_t, which))

        def weigh(i):
            s, p, which = items[i]
            here, cols, q, k, v, gc, q_t, k_t, gc_t = pair_of(s, p)
            head = slice((p * 2 + which) * head_dim, (p * 2 + which + 1) * head_dim)
            scores, grad_p = raw.pop(i)
            lse = lse_ref[0, p, which : which + 1, here]
            edge = sure_rows(size)
            late = jnp.where(live_rows(edge, lengths[s], size - edge), scores[edge:], -1e30)
            probs = jnp.concatenate([jnp.exp(scores[:edge] - lse), jnp.exp(late - lse)], 0)
            half = slice(which * head_dim, (which + 1) * head_dim)
            delta = jnp.sum(gc_t[half].astype(F32) * ctx_t_ref[head, here].astype(F32), 0, keepdims=True)
            made[i] = probs.astype(LOW), (probs * (grad_p - delta)).astype(LOW)

        def combine(i):
            s, p, which = items[i]
            here, cols, q, k, v, gc, q_t, k_t, gc_t = pair_of(s, p)
            mine = (lane >= head_dim) if which else (lane < head_dim)
            zero = jnp.zeros_like(q)
            probs, grad_s = made.pop(i)
            add_v = mm(probs, jnp.where(mine, gc, zero))
            add_k = mm(grad_s, jnp.where(mine, q, zero))
            add_q = mm(k_t[which * head_dim : (which + 1) * head_dim], grad_s)
            if which == 0:
                made[s, p] = add_v, add_k, add_q
                return
            old_v, old_k, old_q = made.pop((s, p))
            grad_q = (jnp.concatenate([old_q, add_q], 0).T * head_dim**-0.5).astype(LOW)
            grad_k = (old_k + add_k).astype(LOW)
            grad_v = (old_v + add_v).astype(LOW)
            for number, grad in enumerate((grad_q, grad_k, grad_v)):
                out_ref[here, number * width + cols.start : number * width + cols.stop] = grad
                grads[number, s, p] = grad
            stat_ref[0:1, cols] += jnp.sum(grad_q.astype(F32), 0, keepdims=True)
            stat_ref[1:2, cols] += jnp.sum(grad_v.astype(F32), 0, keepdims=True)

            if p % 2 and s == len(starts) - 1:
                project(p - 1)

        def project(p):
            for number in range(3):
                rows = [
                    jnp.concatenate([grads.pop((number, s, p)), grads.pop((number, s, p + 1))], 1)
                    for s in range(len(starts))
                ]
                product = mm(x_t_ref[...], jnp.concatenate(rows, 0))
                cols = slice(number * width + p * pair_dim, number * width + (p + 2) * pair_dim)
                if fresh:
                    sum_ref[:, cols] = product
                else:
                    sum_ref[:, cols] += product

        staged(len(items), compare, weigh, combine)

    @pl.when(block == 0)
    def _():
        attend(q_len, [s * q_len for s in range(q_dev)], [qlen_ref[s] for s in range(q_dev)], True)

    @pl.when(block > 0)
    def _():
        attend(rows_all, [0], [plen_ref[jnp.maximum(block - 1, 0)]], False)

    @pl.when(block == pl.num_programs(0) - 1)
    def _():
        tails = None
        if extra:
            tails = small_rows([*extra, stat_ref], send_ref.shape[0] * 2, send_ref.shape[2])
        store_shards(core_ref, sum_ref[...], send_ref, keep_ref, tails=tails)


def input_grad_kernel(groups, *refs):
    grads, (base_ref, wq_ref, wk_ref, wv_ref, gq_ref, gp_ref) = refs[: len(groups)], refs[len(groups) :]
    total = base_ref[...].astype(F32)
    for grad_ref, (start, wide) in zip(grads, groups):
        for number, w_ref in enumerate((wq_ref, wk_ref, wv_ref)):
            total = total + mm_nt(grad_ref[:, number * wide : (number + 1) * wide], w_ref[:, start : start + wide])
    low = total.astype(LOW)

    @pl.when(pl.program_id(0) == 0)
    def _():
        gq_ref[...] = low

    @pl.when(pl.program_id(0) > 0)
    def _():
        gp_ref[...] = low


def weight_grad_kernel(core_ref, left_ref, right_ref, send_ref, keep_ref):
    store_shards(core_ref, mm(left_ref[...], right_ref[...]), send_ref, keep_ref)


def small_rows(refs, count, wide):
    two, one, inner, *attn = [ref[...] for ref in refs]
    eight = jnp.concatenate(
        [jnp.concatenate([item[0:2] for item in attn], 1), one[2:3], two[2:3], one[0:2], two[0:2]], 0
    )
    inner = inner[0:1]
    short, long = eight.shape[1] // count, inner.shape[1] // count
    rows = []
    for shard in range(count):
        top = eight[:, shard * short : (shard + 1) * short]
        low = inner[:, shard * long : (shard + 1) * long]
        top = jnp.concatenate([top, jnp.zeros((8, wide - short), F32)], 1)
        low = jnp.concatenate([low, jnp.zeros((1, wide - long), F32)], 1)
        rows.append(jnp.concatenate([top, low, jnp.zeros((7, wide), F32)], 0).astype(LOW))
    return rows


def turn_kernel(part_ref, out_ref):
    out_ref[...] = part_ref[...].astype(F32).T


def turn_low_kernel(*refs):
    *inputs, out_ref = refs
    if len(inputs) == 1:
        out_ref[...] = inputs[0][...].T
        return

    @pl.when(pl.program_id(0) == 0)
    def _():
        out_ref[...] = inputs[0][...].T

    @pl.when(pl.program_id(0) > 0)
    def _():
        out_ref[...] = inputs[1][...].T


def const_spec(shape):
    return pl.BlockSpec(shape, lambda i: (0,) * len(shape), pipeline_mode=pl.Buffered(1))


def call(body, operands, in_specs, outs, grid, room, deps=(), old=(), into=0, name=None, scratch=(), us=12):
    count, extra = len(operands), len(old)
    if deps:
        tied = min(range(count), key=lambda i: operands[i].size)
        operands = list(operands)
        operands[tied] = lax.optimization_barrier((operands[tied], *deps))[0]

    def kernel(*refs):
        body(*refs[:count], *refs[count + extra :])

    return pl.pallas_call(
        kernel,
        grid=grid,
        in_specs=list(in_specs) + [pl.BlockSpec(memory_space=pl.ANY)] * extra,
        out_specs=[spec for spec, _ in outs],
        out_shape=[jax.ShapeDtypeStruct(kind.shape, kind.dtype) for _, kind in outs],
        scratch_shapes=scratch,
        input_output_aliases={count + i: into + i for i in range(extra)},
        compiler_params=pltpu.CompilerParams(vmem_limit_bytes=room * 1024 * 1024),
        cost_estimate=pl.CostEstimate(flops=int(us * 1.15e9), bytes_accessed=0, transcendentals=0),
        name=name,
    )(*operands, *old)


def weight_grad(left_t, right, row_count, core, deps, old=(), at=0, us=12):
    height, depth = left_t.shape
    wide = right.shape[1]
    block = min(wide, 768)
    shape = old[0].shape if old else (row_count // 2, height // row_count, wide)
    spec = pl.BlockSpec((*shape[:2], block), lambda i: (0, 0, i + at))
    return call(
        weight_grad_kernel,
        (core, left_t, right),
        [
            pl.BlockSpec(memory_space=pltpu.SMEM),
            const_spec((height, depth)),
            pl.BlockSpec((depth, block), lambda i: (0, i)),
        ],
        [(spec, jax.ShapeDtypeStruct(shape, LOW))] * 2,
        (wide // block,),
        56,
        deps,
        old,
        name="weight_grad",
        us=us,
    )


def add_kernel(*refs):
    *terms, out_ref = refs
    out_ref[...] = sum([ref[...].astype(F32) for ref in terms[1:]], terms[0][...].astype(F32)).astype(LOW)


def add_all(terms):
    shape = terms[0].shape
    spec = pl.BlockSpec(shape, lambda i: (0,) * len(shape), pipeline_mode=pl.Buffered(1))
    outs = [(spec, jax.ShapeDtypeStruct(shape, LOW))]
    return call(add_kernel, terms, [spec] * len(terms), outs, (1,), 24, name="add_all", us=12)[0]


class Flow:
    def __init__(self, sent, kept, line=False, fused=False):
        bits = lax.axis_size("row").bit_length() - 1
        self.order = [(0,)] + [tuple(range(i, min(i + 2, bits))) for i in range(1, bits, 2)]
        self.left = list(range(bits - 1, 0, -1))
        count = lax.axis_size("col")
        self.line = [(None, [(i, i ^ (1 << bit)) for i in range(count)]) for bit in range(count.bit_length() - 1)]
        if line:
            half = count // 2
            self.line = [(None, [(i, i + 1), (count - 1 - i, count - 2 - i)]) for i in range(half - 1)]
            self.line += [(None, [(half - 1, half), (half, half - 1)])]
            self.line += [
                ((i, count - 1 - i), [(i + 1, i), (count - 2 - i, count - 1 - i)])
                for i in range(half - 2, -1, -1)
            ]
        self.sent, self.kept, self.got, self.fused = [sent], kept, None, fused

    def shard(self, terms, bits, mask):
        here = lax.axis_index("row")
        order = [self.left.index(bit) for bit in bits]
        total = None
        for term in terms:
            starts, sizes = [0] * term.ndim, list(term.shape)
            for axis, bit in zip(order, bits):
                starts[axis], sizes[axis] = ((here ^ mask) >> bit) & 1, 1
            piece = lax.dynamic_slice(term, starts, sizes)
            piece = piece.reshape([size for i, size in enumerate(sizes) if i not in order]).astype(F32)
            total = piece if total is None else total + piece
        return total.astype(LOW)

    def step(self):
        if self.order:
            bits = self.order[0]
            masks = [
                sum(1 << bit for i, bit in enumerate(bits) if other >> i & 1)
                for other in range(1, 1 << len(bits))
            ]
            if bits != (0,):
                terms = [self.kept, *self.got]
                self.sent = [self.shard(terms, bits, mask) for mask in masks]
                self.kept = self.shard(terms, bits, 0)
                self.left = [bit for bit in self.left if bit not in bits]
            size = lax.axis_size("row")
            self.got = [
                lax.ppermute(sent, "row", [(i, i ^ mask) for i in range(size)])
                for sent, mask in zip(self.sent, masks)
            ]
        else:
            self.sent = [self.kept]
            self.got = [lax.ppermute(self.kept, "col", self.line[0][1])]

    def land(self, token=None):
        if token is not None:
            self.kept = lax.optimization_barrier((self.kept, token))[0]
        got = self.got
        if self.order:
            bits = self.order.pop(0)
            if bits == (0,):
                dims = (2,) * len(self.left) + self.kept.shape[1:]
                self.kept, self.got = self.kept.reshape(dims), [item.reshape(dims) for item in self.got]
            if not self.order and self.fused:
                self.kept = add_all([self.kept, *self.got])
            elif not self.order:
                self.kept = sum([item.astype(F32) for item in self.got], self.kept.astype(F32)).astype(LOW)
        else:
            ends, _ = self.line.pop(0)
            if ends is None:
                self.kept = self.kept + self.got[0]
            else:
                here = lax.axis_index("col")
                self.kept = jnp.where((here == ends[0]) | (here == ends[1]), self.got[0], self.kept)
        return got

    def turn(self, token=None):
        got = self.land(token)
        if self.done:
            return got
        self.step()
        return got + self.sent

    @property
    def done(self):
        return not self.order and not self.line


def gather_all(piece):
    row_bits = lax.axis_size("row").bit_length() - 1
    col_bits = lax.axis_size("col").bit_length() - 1
    steps = [("col", tuple(range(i, min(i + 2, col_bits)))) for i in range(0, col_bits, 2)]
    steps += [("row", tuple(range(i, min(i + 2, row_bits)))) for i in range(1, row_bits, 2)]
    for name, bits in steps + [("row", (0,))]:
        here = lax.axis_index(name)
        pieces = [piece]
        for other in range(1, 1 << len(bits)):
            mask = sum(1 << bit for i, bit in enumerate(bits) if other >> i & 1)
            pairs = [(i, i ^ mask) for i in range(lax.axis_size(name))]
            pieces.append(lax.ppermute(piece, name, pairs))
        for i, bit in enumerate(bits):
            high = ((here >> bit) & 1) == 1
            pieces = [
                jnp.where(high, pieces[place ^ (1 << i)], pieces[place]) for place in range(len(pieces))
            ]
        piece = jnp.concatenate(pieces, 0)
    return piece


def per_device(
    query_tokens, passage_tokens, query_lengths, passage_lengths, positives,
    w_query, w_key, w_value, w_attn_out, w_inner, w_outer,
    bias_query, bias_value, bias_attn_out, bias_inner, bias_outer,
    gain_one, shift_one, gain_two, shift_two,
):
    q_dev, q_len, width = query_tokens.shape
    p_dev, p_len, _ = passage_tokens.shape
    inner = w_inner.shape[1]
    rows_all = p_len
    assert q_dev * q_len == rows_all and q_dev + p_dev <= SLOTS
    blocks = 1 + p_dev
    total_rows = blocks * rows_all
    row_count = lax.axis_size("row")
    col_count = lax.axis_size("col")
    row_here = lax.axis_index("row")
    core = (row_here & 1).reshape(1)
    me = (row_here * col_count + lax.axis_index("col")).reshape(1)
    params = pltpu.CompilerParams(vmem_limit_bytes=VMEM)
    smem = pl.BlockSpec(memory_space=pltpu.SMEM)

    def by_block(wide):
        return pl.BlockSpec((rows_all, wide), lambda i: (i, 0))

    def by_block_t(high):
        return pl.BlockSpec((high, rows_all), lambda i: (0, i))

    def fixed(shape):
        return pl.BlockSpec(shape, lambda i: (0,) * len(shape))

    queries_spec = pl.BlockSpec((rows_all, width), lambda i: (0, 0))
    passages_spec = pl.BlockSpec((rows_all, width), lambda i: (jnp.maximum(i - 1, 0), 0))

    lse_spec = pl.BlockSpec((1, HEADS // 2, 8, rows_all), lambda i: (i, 0, 0, 0))

    def shape(*dims, kind=LOW):
        return jax.ShapeDtypeStruct(dims, kind)

    queries = query_tokens.reshape(rows_all, width)
    passages = passage_tokens.reshape(p_dev * rows_all, width)
    square = const_spec((width, width))
    anywhere = pl.BlockSpec(memory_space=pl.ANY)
    thin = const_spec((width,))

    q, k, v, ctx_t, lse = call(
        partial(attend_kernel, (q_dev, q_len, rows_all, width)),
        (query_lengths, passage_lengths, queries, passages, w_query, w_key, w_value, bias_query, bias_value),
        [smem, smem, queries_spec, passages_spec, square, square, square, thin, thin],
        [(by_block(width), shape(total_rows, width))] * 3
        + [
            (by_block_t(width), shape(width, total_rows)),
            (lse_spec, shape(blocks, HEADS // 2, 8, rows_all, kind=F32)),
        ],
        (blocks,),
        56,
        name="attend",

    )

    rows_part = rows_all
    parts = blocks

    def by_part(wide):
        return pl.BlockSpec((rows_part, wide), lambda i: (i, 0))

    queries_part = pl.BlockSpec((rows_part, width), lambda i: (0, 0))
    passages_part = pl.BlockSpec((rows_part, width), lambda i: (jnp.maximum(i - 1, 0), 0))
    h1, y1, act, slope, h2, query_out, passage_out, pooled, payload = call(
        partial(dense_kernel, (q_dev, q_len, p_len, width, inner)),
        (
            query_lengths, passage_lengths, positives, queries, passages, ctx_t, w_attn_out, w_inner, w_outer,
            bias_attn_out, bias_inner, bias_outer, gain_one, shift_one, gain_two, shift_two,
        ),
        [smem, smem, smem, queries_part, passages_part, pl.BlockSpec((width, rows_part), lambda i: (0, i))]
        + [anywhere] * 3
        + [thin, const_spec((inner,))]
        + [thin] * 5,
        [
            (by_part(width), shape(total_rows, width)),
            (by_part(width), shape(total_rows, width)),
            (by_part(inner), shape(total_rows, inner)),
            (by_part(inner), shape(total_rows, inner)),
            (by_part(width), shape(total_rows, width)),
            (queries_part, shape(rows_all, width)),
            (passages_part, shape(p_dev * rows_all, width)),
            (fixed((SLOTS, width)), shape(SLOTS, width, kind=F32)),
            (fixed((SLOTS, width + 128)), shape(SLOTS, width + 128)),
        ],
        (parts,),
        56,
        name="dense",
        scratch=[
            pltpu.VMEM((width, width), LOW),
            pltpu.VMEM((width, inner), LOW),
            pltpu.VMEM((inner, width), LOW),
            pltpu.SemaphoreType.DMA((3,)),
        ],

    )

    gathered = gather_all(payload)
    loss, gvec = pl.pallas_call(
        partial(loss_kernel, (q_dev, p_dev, width, col_count)),
        in_specs=[smem] * 3 + [pl.BlockSpec(memory_space=pltpu.VMEM)] * 3,
        out_specs=[pl.BlockSpec(memory_space=pltpu.VMEM)] * 2,
        out_shape=[shape(8, 128, kind=F32), shape(SLOTS, width, kind=F32)],
        compiler_params=params,
        name="loss",
    )(me, query_lengths, passage_lengths, payload, gathered, pooled)

    smalls = shape(8, width, kind=F32)
    cut = width // row_count
    cut_inner = inner // row_count
    half = row_count // 2
    step_cols = 768
    per_step = step_cols // cut_inner
    outer_spec = pl.BlockSpec((per_step // 2, width, cut_inner), lambda i: (i, 0, 0))
    grad_f, stat_two, *outer_parts = call(
        partial(outer_grad_kernel, (q_dev, q_len, p_len)),
        (core, query_lengths, passage_lengths, gvec, h2, gain_two, act),
        [smem, smem, smem, fixed((SLOTS, width)), const_spec((total_rows, width)), thin]
        + [pl.BlockSpec((total_rows, step_cols), lambda i: (0, i))],
        [
            (fixed((total_rows, width)), shape(total_rows, width)),
            (fixed((8, width)), smalls),
            (outer_spec, shape(half, width, cut_inner)),
            (outer_spec, shape(half, width, cut_inner)),
        ],
        (inner // step_cols,),
        56,
        name="outer_grad",
        scratch=[pltpu.VMEM((width, total_rows), LOW)],
    )
    outer = Flow(*outer_parts, line=True)
    outer.step()

    def turn(arrays, specs, deps):
        outs = [(by_block_t(width), shape(width, total_rows))]
        return call(turn_low_kernel, arrays, specs, outs, (blocks,), 56, deps, name="turn", us=40)[0]

    y1_t = turn([y1], [by_block(width)], outer.sent)
    deps = outer.turn(y1_t)
    head_dim = width // HEADS
    third = 4 * head_dim
    groups = [(0, 2 * third), (2 * third, third)]
    grad_u, grad_attn, grad_ctx, stat_one, grad_bias_inner = call(
        partial(dense_back_kernel, inner),
        (grad_f, slope, h1, w_outer, w_inner, w_attn_out, gain_one),
        [by_block(width), by_block(inner), by_block(width), anywhere, anywhere, anywhere, thin],
        [
            (by_block(inner), shape(total_rows, inner)),
            (by_block(width), shape(total_rows, width)),
            (by_block(width), shape(total_rows, width)),
            (fixed((8, width)), smalls),
            (fixed((8, inner)), shape(8, inner, kind=F32)),
        ],
        (blocks,),
        60,
        deps,
        name="dense_back",
        scratch=[
            pltpu.VMEM((inner, width), LOW),
            pltpu.VMEM((width, inner), LOW),
            pltpu.VMEM((width, width), LOW),
            pltpu.SemaphoreType.DMA((3,)),
        ],
    )
    deps = outer.turn(stat_one)
    up_flow = Flow(*weight_grad(y1_t, grad_u, row_count, core, deps), fused=True)
    up_flow.step()
    deps = up_flow.sent + outer.turn(up_flow.sent[0])
    x_t = turn([queries, passages], [queries_spec, passages_spec], deps)
    deps = up_flow.turn(x_t)

    def attend_back(start, wide, deps, extra=(), room=None):
        pairs = wide // (2 * head_dim)
        index = start // wide
        cols = pl.BlockSpec((rows_all, wide), lambda i: (i, index))
        rows = cut + (16 if extra else 0)
        return call(
            partial(attend_back_kernel, (q_dev, q_len, rows_all, head_dim)),
            (core, query_lengths, passage_lengths, q, k, v, ctx_t, lse, grad_ctx, x_t, *extra),
            [smem, smem, smem]
            + [cols] * 3
            + [
                pl.BlockSpec((wide, rows_all), lambda i: (index, i)),
                pl.BlockSpec((1, pairs, 8, rows_all), lambda i: (i, index, 0, 0)),
                cols,
                by_block_t(width),
            ]
            + [const_spec(item.shape) for item in extra],
            [
                (by_block(3 * wide), shape(total_rows, 3 * wide)),
                (fixed((8, wide)), shape(8, wide, kind=F32)),
            ]
            + [(fixed((half, rows, 3 * wide)), shape(half, rows, room or 3 * wide))] * 2,
            (blocks,),
            56,
            deps,
            name="attend_back",
            scratch=[pltpu.VMEM((width, 3 * wide), F32)],
            us=12 if room else 40,
        )

    grad_a, stat_a, *mixed_parts = attend_back(*groups[0], deps, room=6 * third + width)
    at = 6 * third // width
    mixed_parts = weight_grad(ctx_t, grad_attn, row_count, core, [stat_a], mixed_parts, at, us=0)
    mixed_flow = Flow(*mixed_parts)
    mixed_flow.step()
    token = mixed_flow.sent[0]
    deps = mixed_flow.sent + outer.turn(token) + up_flow.turn(token)
    extra = (stat_two, stat_one, grad_bias_inner, stat_a)
    grad_b, stat_b, *last_parts = attend_back(*groups[1], deps, extra)
    last_flow = Flow(*last_parts)
    last_flow.step()
    deps = last_flow.sent + outer.turn(stat_b) + mixed_flow.turn(stat_b) + up_flow.turn(stat_b)
    query_grad, passage_grad = call(
        partial(input_grad_kernel, groups),
        (grad_a, grad_b, grad_attn, w_query, w_key, w_value),
        [by_block(3 * wide) for _, wide in groups] + [by_block(width), square, square, square],
        [
            (queries_spec, shape(rows_all, width)),
            (passages_spec, shape(p_dev * rows_all, width)),
        ],
        (blocks,),
        56,
        deps,
        name="input_grad",
        us=40,
    )
    last_flow.turn(passage_grad)
    mixed_flow.turn(last_flow.kept)
    up_flow.turn(mixed_flow.kept)
    outs = [(fixed((cut_inner, width)), shape(cut_inner, width, kind=F32))]
    (turned,) = call(
        turn_kernel, (outer.kept,), [const_spec((width, cut_inner))], outs, (1,), 56, [up_flow.kept], name="turn", us=40
    )
    mixed_flow.turn(turned)
    last_flow.turn(mixed_flow.kept)
    last_flow.turn()
    mixed_flow.turn(last_flow.kept)
    flows = [outer, up_flow, mixed_flow, last_flow]
    while not all(flow.done for flow in flows):
        for flow in flows:
            if not flow.done:
                flow.turn()
    mixed, last = mixed_flow.kept, last_flow.kept
    qkv = [
        jnp.concatenate(
            [mixed[:, i * 2 * third : (i + 1) * 2 * third], last[:cut, i * third : (i + 1) * third]], 1
        ).astype(F32)
        for i in range(3)
    ]
    small = last[cut:].astype(F32)
    return (
        loss[0, 0],
        query_out.reshape(query_tokens.shape),
        passage_out.reshape(passage_tokens.shape),
        query_grad.reshape(query_tokens.shape),
        passage_grad.reshape(passage_tokens.shape),
        *qkv,
        mixed[:, 6 * third :].astype(F32),
        up_flow.kept.astype(F32),
        turned,
        *[small[i, :cut] for i in range(3)],
        small[8, : inner // row_count],
        *[small[i, :cut] for i in range(3, 8)],
    )


def solution(mesh):
    in_specs = (
        P(("row", "col"), None, None),
        P(("row", "col"), None, None),
        P(("row", "col")),
        P(("row", "col")),
        P(("row", "col")),
        P(),
        P(),
        P(),
        P(),
        P(),
        P(),
        P(),
        P(),
        P(),
        P(),
        P(),
        P(),
        P(),
        P(),
        P(),
    )
    out_specs = (
        P(),
        P(("row", "col"), None, None),
        P(("row", "col"), None, None),
        P(("row", "col"), None, None),
        P(("row", "col"), None, None),
        P("row", None),
        P("row", None),
        P("row", None),
        P("row", None),
        P("row", None),
        P("row", None),
        P("row"),
        P("row"),
        P("row"),
        P("row"),
        P("row"),
        P("row"),
        P("row"),
        P("row"),
        P("row"),
    )
    return jax.shard_map(
        per_device, mesh=mesh, in_specs=in_specs, out_specs=out_specs, check_vma=False
    )
```

```python
from functools import partial

import jax
import jax.numpy as jnp
from jax import lax
from jax.experimental import pallas as pl
from jax.experimental.pallas import tpu as pltpu
from jax.sharding import PartitionSpec as P

HEADS = 12
EPS_NORM = 1e-12
EPS_POOL = 1e-06
SCALE_LOSS = 128.0
INV_TEMP = 100.0
TILE = 256
SLOTS = 8
VMEM = 60 * 1024 * 1024
LOW = jnp.bfloat16
F32 = jnp.float32


def mm(left, right):
    return lax.dot_general(left, right, (((1,), (0,)), ((), ())), preferred_element_type=F32)


def mm_nt(left, right):
    return lax.dot_general(left, right, (((1,), (1,)), ((), ())), preferred_element_type=F32)


def norm_parts(hidden):
    center = hidden - jnp.mean(hidden, -1, keepdims=True)
    spread = jnp.mean(center * center, -1, keepdims=True)
    scale = lax.rsqrt(spread + EPS_NORM)
    return center * scale, scale


def gelu_parts(u):
    square = u * u
    q = 1.4250060785476853e-06
    for factor in (-3.669345091379551e-05, -8.782652731110375e-05, 0.03639228618131223, 0.7978697123041883):
        q = q * square + factor
    share = 0.5 + 0.5 * jnp.tanh(u * q)
    bell = jnp.exp(-0.5 * square)
    return u * share, share + (0.3989422804014327 * u) * bell


def vec(ref, cols=slice(None)):
    return ref[cols].reshape(1, -1)


def rows_of(step, size):
    return pl.ds(pl.multiple_of(step * size, size), size)


def part_owner(part, q_dev, q_len, p_len, qlen_ref, plen_ref):
    per = p_len // q_len
    beyond = jnp.maximum(part - q_dev, 0)
    is_query = part < q_dev
    slot = jnp.where(is_query, part, q_dev + beyond // per)
    length = jnp.where(is_query, qlen_ref[jnp.where(is_query, part, 0)], plen_ref[beyond // per])
    first = jnp.where(is_query, 0, beyond % per * q_len)
    return slot, length, first


def live_rows(first, length, size):
    return (first + lax.broadcasted_iota(jnp.int32, (size, 1), 0)) < length


def sure_rows(size):
    return size * 4 // 5 // 16 * 16


def half_only(pair_t, which):
    half = pair_t.shape[0] // 2
    zeros = jnp.zeros((half, pair_t.shape[1]), pair_t.dtype)
    if which == 0:
        return jnp.concatenate([pair_t[:half], zeros], 0)
    return jnp.concatenate([zeros, pair_t[half:]], 0)


def staged(count, *stages):
    for step in range(count + len(stages) - 1):
        for late, stage in enumerate(stages):
            if 0 <= step - late < count:
                stage(step - late)


def fetch(source, target, sems, index):
    return pltpu.make_async_copy(source, target, sems.at[index])


def attend_kernel(
    dims, qlen_ref, plen_ref, xq_ref, xp_ref, wq_ref, wk_ref, wv_ref, bq_ref, bv_ref,
    q_ref, k_ref, v_ref, ctx_t_ref, lse_ref,
):
    q_dev, q_len, rows_all, width = dims
    block = pl.program_id(0)
    head_dim = width // HEADS
    x = jnp.where(block == 0, xq_ref[...], xp_ref[...])
    q = ((mm(x, wq_ref[...]) + vec(bq_ref)) * head_dim**-0.5).astype(LOW)
    k = mm(x, wk_ref[...]).astype(LOW)
    v = (mm(x, wv_ref[...]) + vec(bv_ref)).astype(LOW)
    q_ref[...] = q
    k_ref[...] = k
    v_ref[...] = v
    q_t, v_t = q.T, v.T

    def attend(size, starts, lengths):
        items = [(start, length, head) for head in range(HEADS) for start, length in zip(starts, lengths)]
        scores, weights = {}, {}

        def compare(i):
            start, length, head = items[i]
            cols = slice(head // 2 * 2 * head_dim, (head // 2 + 1) * 2 * head_dim)
            here = slice(start, start + size)
            scores[i] = mm(k[here, cols], half_only(q_t[cols, here], head % 2))

        def weigh(i):
            start, length, head = items[i]
            edge = sure_rows(size)
            early, late = scores[i][:edge], scores.pop(i)[edge:]
            late = jnp.where(live_rows(edge, length, size - edge), late, -1e30)
            top = jnp.maximum(jnp.max(early, 0, keepdims=True), jnp.max(late, 0, keepdims=True))
            weights[i] = top, jnp.concatenate([jnp.exp(early - top).astype(LOW), jnp.exp(late - top).astype(LOW)], 0)

        def combine(i):
            start, length, head = items[i]
            here, rows = slice(start, start + size), slice(head * head_dim, (head + 1) * head_dim)
            top, weight = weights.pop(i)
            values = jnp.concatenate([v_t[rows, here], jnp.ones((16, size), LOW)], 0)
            result = mm(values, weight)
            total = result[head_dim : head_dim + 1]
            lse_ref[0, head // 2, head % 2 : head % 2 + 1, here] = top + jnp.log(total)
            ctx_t_ref[rows, here] = (result[:head_dim] * (1.0 / total)).astype(LOW)

        staged(len(items), compare, weigh, combine)

    @pl.when(block == 0)
    def _():
        attend(q_len, [s * q_len for s in range(q_dev)], [qlen_ref[s] for s in range(q_dev)])

    @pl.when(block > 0)
    def _():
        attend(rows_all, [0], [plen_ref[jnp.maximum(block - 1, 0)]])


def dense_kernel(
    dims, qlen_ref, plen_ref, pos_ref, xq_ref, xp_ref, ctx_t_ref, wo_hbm, wi_hbm, wf_hbm,
    bo_ref, bi_ref, bf_ref, g1_ref, s1_ref, g2_ref, s2_ref,
    h1_ref, y1_ref, act_ref, dg_ref, h2_ref, yq_ref, yp_ref, pool_ref, pay_ref,
    wo_ref, wi_ref, wf_ref, sems,
):
    q_dev, q_len, p_len, width, inner = dims
    block = pl.program_id(0)
    rows_all = xq_ref.shape[0]
    query_blocks = q_dev * q_len // rows_all
    copies = [
        fetch(source, target, sems, index)
        for index, (source, target) in enumerate([(wo_hbm, wo_ref), (wi_hbm, wi_ref), (wf_hbm, wf_ref)])
    ]

    @pl.when(block == 0)
    def _():
        for copy in copies:
            copy.start()
        pool_ref[...] = jnp.zeros_like(pool_ref)
        copies[0].wait()

    x = jnp.where(block < query_blocks, xq_ref[...], xp_ref[...])
    hidden = x.astype(F32) + (mm(ctx_t_ref[...].T, wo_ref[...]) + vec(bo_ref))
    h1_ref[...] = hidden.astype(LOW)
    y1 = norm_parts(hidden)[0] * vec(g1_ref) + vec(s1_ref)
    y1_low = y1.astype(LOW)
    y1_ref[...] = y1_low

    @pl.when(block == 0)
    def _():
        copies[1].wait()
        copies[2].wait()

    raw, made = {}, {}

    def expand(i):
        cols = slice(i * TILE, (i + 1) * TILE)
        raw[i] = mm(y1_low, wi_ref[:, cols]) + vec(bi_ref, cols)

    def activate(i):
        cols = slice(i * TILE, (i + 1) * TILE)
        act, slope = gelu_parts(raw.pop(i))
        made[i] = act.astype(LOW)
        act_ref[:, cols] = made[i]
        dg_ref[:, cols] = slope.astype(LOW)

    staged(inner // TILE, expand, activate)
    left = jnp.concatenate([made[i] for i in range(inner // TILE)], 1)
    total = (y1 + vec(bf_ref)) + mm(left, wf_ref[...])
    h2_ref[...] = total.astype(LOW)
    y2 = norm_parts(total)[0] * vec(g2_ref) + vec(s2_ref)
    for part in range(rows_all // q_len):
        number = block * (rows_all // q_len) + part
        slot, length, first = part_owner(number, q_dev, q_len, p_len, qlen_ref, plen_ref)
        piece = y2[part * q_len : (part + 1) * q_len]
        summed = jnp.sum(jnp.where(live_rows(first, length, q_len), piece, 0.0), 0, keepdims=True)
        in_slot = lax.broadcasted_iota(jnp.int32, (SLOTS, 1), 0) == slot
        pool_ref[...] += jnp.where(in_slot, summed / length.astype(F32), 0.0)

    @pl.when(block < query_blocks)
    def _():
        yq_ref[...] = y2.astype(LOW)

    @pl.when(block >= query_blocks)
    def _():
        yp_ref[...] = y2.astype(LOW)

    @pl.when(block == pl.num_programs(0) - 1)
    def _():
        pooled = pool_ref[...]
        emb = pooled * lax.rsqrt(jnp.sum(pooled * pooled, -1, keepdims=True) + EPS_POOL)
        pay_ref[:, :width] = emb.astype(LOW)
        row = lax.broadcasted_iota(jnp.int32, (SLOTS, 128), 0)
        col = lax.broadcasted_iota(jnp.int32, (SLOTS, 128), 1)
        place = jnp.zeros((SLOTS, 128), jnp.int32)
        for j in range(q_dev):
            high = pos_ref[j] // 128
            low = pos_ref[j] - high * 128
            place = jnp.where(row == j, jnp.where(col == 0, high, jnp.where(col == 1, low, 0)), place)
        pay_ref[:, width:] = place.astype(F32).astype(LOW)


def loss_kernel(
    dims, me_ref, qlen_ref, plen_ref, own_ref, all_ref, pool_ref, loss_ref, gvec_ref
):
    q_dev, p_dev, width, col_count = dims
    count = all_ref.shape[0]
    every = all_ref[:, :width]
    own = own_ref[:, :width]

    def passage_mask(index):
        spot, place = index % SLOTS, index // SLOTS
        per_core = count // SLOTS // 2
        core, rest = place // per_core, place % per_core
        device = (rest // col_count * 2 + core) * col_count + rest % col_count
        return (spot >= q_dev) & (spot < q_dev + p_dev), device * p_dev + spot - q_dev

    scores = mm_nt(own, every) * INV_TEMP
    valid, ident = passage_mask(lax.broadcasted_iota(jnp.int32, (SLOTS, count), 1))
    scores = jnp.where(valid, scores, -1e30)
    top = jnp.max(scores, -1, keepdims=True)
    totals = top + jnp.log(jnp.sum(jnp.exp(scores - top), -1, keepdims=True))
    marks = own_ref[:, width:].astype(F32)
    wanted = marks[:, 0:1] * 128.0 + marks[:, 1:2]
    target = (valid & (ident.astype(F32) == wanted)).astype(F32)
    raw = (INV_TEMP * (SCALE_LOSS * (jnp.exp(scores - totals) - target))).astype(LOW)
    grad_q = mm(raw, every)

    picker_col = lax.broadcasted_iota(jnp.int32, (SLOTS, 128), 1)
    picker = jnp.where(picker_col == 0, 128.0, jnp.where(picker_col == 1, 1.0, 0.0)).astype(LOW)
    own_row = lax.broadcasted_iota(jnp.int32, (SLOTS, TILE), 0)
    own_valid = (own_row >= q_dev) & (own_row < q_dev + p_dev)
    own_ident = (me_ref[0] * p_dev + own_row - q_dev).astype(F32)

    def body(step, carry):
        total_loss, grad_p = carry
        rows = rows_of(step, TILE)
        some = all_ref[rows, :width]
        place = mm_nt(picker, all_ref[rows, width:])[0:1]
        table = mm_nt(every, some) * INV_TEMP
        ok, names = passage_mask(lax.broadcasted_iota(jnp.int32, (count, TILE), 0))
        picked = jnp.sum(jnp.where(ok & (names.astype(F32) == place), table, 0.0), 0, keepdims=True)
        table = jnp.where(ok, table, -1e30)
        high = jnp.max(table, 0, keepdims=True)
        lse = high + jnp.log(jnp.sum(jnp.exp(table - high), 0, keepdims=True))
        is_query = lax.broadcasted_iota(jnp.int32, (1, TILE), 1) % SLOTS < q_dev
        losses = jnp.where(is_query, lse - picked, 0.0)
        mine = mm_nt(own, some) * INV_TEMP
        hit = (own_ident == place).astype(F32)
        grads = INV_TEMP * (SCALE_LOSS * (jnp.exp(mine - lse) - hit))
        grads = jnp.where(own_valid & is_query, grads, 0.0).astype(LOW)
        return total_loss + jnp.sum(losses, 1, keepdims=True), grad_p + mm(grads, some)

    start = (jnp.zeros((1, 1), F32), jnp.zeros((SLOTS, width), F32))
    total_loss, grad_p = lax.fori_loop(0, count // TILE, body, start)
    loss_ref[...] = jnp.broadcast_to(total_loss / float(count // SLOTS * q_dev), loss_ref.shape)

    slot = lax.broadcasted_iota(jnp.int32, (SLOTS, 1), 0)
    grad = jnp.where(slot < q_dev, grad_q, grad_p)
    pooled = pool_ref[...]
    r = lax.rsqrt(jnp.sum(pooled * pooled, -1, keepdims=True) + EPS_POOL)
    inside = jnp.sum(pooled * grad, -1, keepdims=True)
    length = jnp.ones((SLOTS, 1), F32)
    for j in range(q_dev):
        length = jnp.where(slot == j, qlen_ref[j].astype(F32), length)
    for j in range(p_dev):
        length = jnp.where(slot == q_dev + j, plen_ref[j].astype(F32), length)
    gvec_ref[...] = (r * grad - r * r * r * inside * pooled) / length


def store_shards(core_ref, result, send_ref, keep_ref, by_row=True, tails=None):
    count = send_ref.shape[0] * 2
    size = result.shape[0 if by_row else 1] // count

    def store(even, odd):
        for shard in range(count):
            spot = slice(shard * size, (shard + 1) * size)
            piece = (result[spot, :] if by_row else result[:, spot]).astype(LOW)
            target = odd if shard % 2 else even
            if tails is None:
                target[shard // 2] = piece
            else:
                target[shard // 2, :size] = piece
                target[shard // 2, size:] = tails[shard]

    @pl.when(core_ref[0] == 0)
    def _():
        store(keep_ref, send_ref)

    @pl.when(core_ref[0] == 1)
    def _():
        store(send_ref, keep_ref)


def outer_grad_kernel(
    dims, core_ref, qlen_ref, plen_ref, gvec_ref, h2_ref, g2_ref, act_ref,
    gf_ref, stat_ref, send_ref, keep_ref, gf_t_ref,
):
    q_dev, q_len, p_len = dims

    @pl.when(pl.program_id(0) == 0)
    def _():
        stat_ref[...] = jnp.zeros_like(stat_ref)

        def body(part, carry):
            rows = rows_of(part, q_len)
            slot, length, first = part_owner(part, q_dev, q_len, p_len, qlen_ref, plen_ref)
            in_slot = lax.broadcasted_iota(jnp.int32, (SLOTS, 1), 0) == slot
            grad_y = jnp.sum(jnp.where(in_slot, gvec_ref[...], 0.0), 0, keepdims=True)
            live = live_rows(first, length, q_len)
            n2, r2 = norm_parts(h2_ref[rows, :].astype(F32))
            g = grad_y * vec(g2_ref)
            grad = r2 * (g - jnp.mean(g, -1, keepdims=True) - n2 * jnp.mean(g * n2, -1, keepdims=True))
            grad = jnp.where(live, grad, 0.0)
            low = grad.astype(LOW)
            gf_ref[rows, :] = low
            gf_t_ref[:, rows] = low.T
            stat_ref[0:1, :] += grad_y * jnp.sum(jnp.where(live, n2, 0.0), 0, keepdims=True)
            stat_ref[1:2, :] += grad_y * jnp.sum(live.astype(F32), 0, keepdims=True)
            stat_ref[2:3, :] += jnp.sum(low.astype(F32), 0, keepdims=True)
            return carry

        lax.fori_loop(0, h2_ref.shape[0] // q_len, body, 0)

    store_shards(core_ref, mm(gf_t_ref[...], act_ref[...]), send_ref, keep_ref, by_row=False)


def dense_back_kernel(
    dims, gf_ref, dg_ref, h1_ref, wf_hbm, wi_hbm, wo_hbm, g1_ref,
    gu_ref, ga_ref, gc_ref, stat_ref, bi_ref,
    wf_ref, wi_ref, wo_ref, sems,
):
    inner = dims
    block = pl.program_id(0)
    copies = [
        fetch(source, target, sems, index)
        for index, (source, target) in enumerate([(wf_hbm, wf_ref), (wi_hbm, wi_ref), (wo_hbm, wo_ref)])
    ]

    @pl.when(block == 0)
    def _():
        for copy in copies:
            copy.start()
        stat_ref[...] = jnp.zeros_like(stat_ref)
        bi_ref[...] = jnp.zeros_like(bi_ref)
        copies[0].wait()

    gf = gf_ref[...]
    raw, made, biases = {}, {}, []

    def spread(i):
        raw[i] = mm_nt(gf, wf_ref[i * TILE : (i + 1) * TILE, :])

    def slope(i):
        cols = slice(i * TILE, (i + 1) * TILE)
        made[i] = (raw.pop(i) * dg_ref[:, cols].astype(F32)).astype(LOW)
        gu_ref[:, cols] = made[i]
        biases.append(jnp.sum(made[i].astype(F32), 0, keepdims=True))

    staged(inner // TILE, spread, slope)
    bi_ref[0:1, :] += jnp.concatenate(biases, 1)
    left = jnp.concatenate([made[i] for i in range(inner // TILE)], 1)

    @pl.when(block == 0)
    def _():
        for copy in copies[1:]:
            copy.wait()

    total = gf.astype(F32) + mm_nt(left, wi_ref[...])
    n1, r1 = norm_parts(h1_ref[...].astype(F32))
    stat_ref[0:1, :] += jnp.sum(total * n1, 0, keepdims=True)
    stat_ref[1:2, :] += jnp.sum(total, 0, keepdims=True)
    g = total * vec(g1_ref)
    grad = r1 * (g - jnp.mean(g, -1, keepdims=True) - n1 * jnp.mean(g * n1, -1, keepdims=True))
    low = grad.astype(LOW)
    ga_ref[...] = low
    stat_ref[2:3, :] += jnp.sum(low.astype(F32), 0, keepdims=True)
    gc_ref[...] = mm_nt(low, wo_ref[...]).astype(LOW)


def attend_back_kernel(
    dims, core_ref, qlen_ref, plen_ref, q_ref, k_ref, v_ref, ctx_t_ref, lse_ref, gc_ref, x_t_ref, *refs
):
    *extra, out_ref, stat_ref, send_ref, keep_ref, sum_ref = refs
    q_dev, q_len, rows_all, head_dim = dims
    block = pl.program_id(0)
    pair_dim = 2 * head_dim
    width = q_ref.shape[1]
    pairs = width // pair_dim

    @pl.when(block == 0)
    def _():
        stat_ref[...] = jnp.zeros_like(stat_ref)

    def attend(size, starts, lengths, fresh):
        lane = lax.broadcasted_iota(jnp.int32, (size, pair_dim), 1)
        items = [(s, p, which) for p in range(pairs) for s in range(len(starts)) for which in range(2)]
        held, raw, made, grads = {}, {}, {}, {}

        def pair_of(s, p):
            if (s, p) not in held:
                here, cols = slice(starts[s], starts[s] + size), slice(p * pair_dim, (p + 1) * pair_dim)
                q, k, v, gc = q_ref[here, cols], k_ref[here, cols], v_ref[here, cols], gc_ref[here, cols]
                held[s, p] = here, cols, q, k, v, gc, q.T, k.T, gc.T
            return held[s, p]

        def compare(i):
            s, p, which = items[i]
            here, cols, q, k, v, gc, q_t, k_t, gc_t = pair_of(s, p)
            raw[i] = mm(k, half_only(q_t, which)), mm(v, half_only(gc_t, which))

        def weigh(i):
            s, p, which = items[i]
            here, cols, q, k, v, gc, q_t, k_t, gc_t = pair_of(s, p)
            head = slice((p * 2 + which) * head_dim, (p * 2 + which + 1) * head_dim)
            scores, grad_p = raw.pop(i)
            lse = lse_ref[0, p, which : which + 1, here]
            edge = sure_rows(size)
            late = jnp.where(live_rows(edge, lengths[s], size - edge), scores[edge:], -1e30)
            probs = jnp.concatenate([jnp.exp(scores[:edge] - lse), jnp.exp(late - lse)], 0)
            half = slice(which * head_dim, (which + 1) * head_dim)
            delta = jnp.sum(gc_t[half].astype(F32) * ctx_t_ref[head, here].astype(F32), 0, keepdims=True)
            made[i] = probs.astype(LOW), (probs * (grad_p - delta)).astype(LOW)

        def combine(i):
            s, p, which = items[i]
            here, cols, q, k, v, gc, q_t, k_t, gc_t = pair_of(s, p)
            mine = (lane >= head_dim) if which else (lane < head_dim)
            zero = jnp.zeros_like(q)
            probs, grad_s = made.pop(i)
            add_v = mm(probs, jnp.where(mine, gc, zero))
            add_k = mm(grad_s, jnp.where(mine, q, zero))
            add_q = mm(k_t[which * head_dim : (which + 1) * head_dim], grad_s)
            if which == 0:
                made[s, p] = add_v, add_k, add_q
                return
            old_v, old_k, old_q = made.pop((s, p))
            grad_q = (jnp.concatenate([old_q, add_q], 0).T * head_dim**-0.5).astype(LOW)
            grad_k = (old_k + add_k).astype(LOW)
            grad_v = (old_v + add_v).astype(LOW)
            for number, grad in enumerate((grad_q, grad_k, grad_v)):
                out_ref[here, number * width + cols.start : number * width + cols.stop] = grad
                grads[number, s, p] = grad
            stat_ref[0:1, cols] += jnp.sum(grad_q.astype(F32), 0, keepdims=True)
            stat_ref[1:2, cols] += jnp.sum(grad_v.astype(F32), 0, keepdims=True)

            if p % 2 and s == len(starts) - 1:
                project(p - 1)

        def project(p):
            for number in range(3):
                rows = [
                    jnp.concatenate([grads.pop((number, s, p)), grads.pop((number, s, p + 1))], 1)
                    for s in range(len(starts))
                ]
                product = mm(x_t_ref[...], jnp.concatenate(rows, 0))
                cols = slice(number * width + p * pair_dim, number * width + (p + 2) * pair_dim)
                if fresh:
                    sum_ref[:, cols] = product
                else:
                    sum_ref[:, cols] += product

        staged(len(items), compare, weigh, combine)

    @pl.when(block == 0)
    def _():
        attend(q_len, [s * q_len for s in range(q_dev)], [qlen_ref[s] for s in range(q_dev)], True)

    @pl.when(block > 0)
    def _():
        attend(rows_all, [0], [plen_ref[jnp.maximum(block - 1, 0)]], False)

    @pl.when(block == pl.num_programs(0) - 1)
    def _():
        tails = None
        if extra:
            tails = small_rows([*extra, stat_ref], send_ref.shape[0] * 2, send_ref.shape[2])
        store_shards(core_ref, sum_ref[...], send_ref, keep_ref, tails=tails)


def input_grad_kernel(groups, *refs):
    grads, (base_ref, wq_ref, wk_ref, wv_ref, gq_ref, gp_ref) = refs[: len(groups)], refs[len(groups) :]
    total = base_ref[...].astype(F32)
    for grad_ref, (start, wide) in zip(grads, groups):
        for number, w_ref in enumerate((wq_ref, wk_ref, wv_ref)):
            total = total + mm_nt(grad_ref[:, number * wide : (number + 1) * wide], w_ref[:, start : start + wide])
    low = total.astype(LOW)

    @pl.when(pl.program_id(0) == 0)
    def _():
        gq_ref[...] = low

    @pl.when(pl.program_id(0) > 0)
    def _():
        gp_ref[...] = low


def weight_grad_kernel(core_ref, left_ref, right_ref, send_ref, keep_ref):
    store_shards(core_ref, mm(left_ref[...], right_ref[...]), send_ref, keep_ref)


def small_rows(refs, count, wide):
    two, one, inner, *attn = [ref[...] for ref in refs]
    eight = jnp.concatenate(
        [jnp.concatenate([item[0:2] for item in attn], 1), one[2:3], two[2:3], one[0:2], two[0:2]], 0
    )
    inner = inner[0:1]
    short, long = eight.shape[1] // count, inner.shape[1] // count
    rows = []
    for shard in range(count):
        top = eight[:, shard * short : (shard + 1) * short]
        low = inner[:, shard * long : (shard + 1) * long]
        top = jnp.concatenate([top, jnp.zeros((8, wide - short), F32)], 1)
        low = jnp.concatenate([low, jnp.zeros((1, wide - long), F32)], 1)
        rows.append(jnp.concatenate([top, low, jnp.zeros((7, wide), F32)], 0).astype(LOW))
    return rows


def turn_kernel(part_ref, out_ref):
    out_ref[...] = part_ref[...].astype(F32).T


def turn_low_kernel(*refs):
    *inputs, out_ref = refs
    if len(inputs) == 1:
        out_ref[...] = inputs[0][...].T
        return

    @pl.when(pl.program_id(0) == 0)
    def _():
        out_ref[...] = inputs[0][...].T

    @pl.when(pl.program_id(0) > 0)
    def _():
        out_ref[...] = inputs[1][...].T


def const_spec(shape):
    return pl.BlockSpec(shape, lambda i: (0,) * len(shape), pipeline_mode=pl.Buffered(1))


def call(body, operands, in_specs, outs, grid, room, deps=(), old=(), into=0, name=None, scratch=(), us=12):
    count, extra = len(operands), len(old)
    if deps:
        tied = min(range(count), key=lambda i: operands[i].size)
        operands = list(operands)
        operands[tied] = lax.optimization_barrier((operands[tied], *deps))[0]

    def kernel(*refs):
        body(*refs[:count], *refs[count + extra :])

    return pl.pallas_call(
        kernel,
        grid=grid,
        in_specs=list(in_specs) + [pl.BlockSpec(memory_space=pl.ANY)] * extra,
        out_specs=[spec for spec, _ in outs],
        out_shape=[jax.ShapeDtypeStruct(kind.shape, kind.dtype) for _, kind in outs],
        scratch_shapes=scratch,
        input_output_aliases={count + i: into + i for i in range(extra)},
        compiler_params=pltpu.CompilerParams(vmem_limit_bytes=room * 1024 * 1024),
        cost_estimate=pl.CostEstimate(flops=int(us * 1.15e9), bytes_accessed=0, transcendentals=0),
        name=name,
    )(*operands, *old)


def weight_grad(left_t, right, row_count, core, deps, old=(), at=0, us=12):
    height, depth = left_t.shape
    wide = right.shape[1]
    block = min(wide, 768)
    shape = old[0].shape if old else (row_count // 2, height // row_count, wide)
    spec = pl.BlockSpec((*shape[:2], block), lambda i: (0, 0, i + at))
    return call(
        weight_grad_kernel,
        (core, left_t, right),
        [
            pl.BlockSpec(memory_space=pltpu.SMEM),
            const_spec((height, depth)),
            pl.BlockSpec((depth, block), lambda i: (0, i)),
        ],
        [(spec, jax.ShapeDtypeStruct(shape, LOW))] * 2,
        (wide // block,),
        56,
        deps,
        old,
        name="weight_grad",
        us=us,
    )


def add_kernel(*refs):
    *terms, out_ref = refs
    out_ref[...] = sum([ref[...].astype(F32) for ref in terms[1:]], terms[0][...].astype(F32)).astype(LOW)


def add_all(terms):
    shape = terms[0].shape
    spec = pl.BlockSpec(shape, lambda i: (0,) * len(shape), pipeline_mode=pl.Buffered(1))
    outs = [(spec, jax.ShapeDtypeStruct(shape, LOW))]
    return call(add_kernel, terms, [spec] * len(terms), outs, (1,), 24, name="add_all", us=12)[0]


class Flow:
    def __init__(self, sent, kept, line=False, fused=False):
        bits = lax.axis_size("row").bit_length() - 1
        self.order = [(0,)] + [tuple(range(i, min(i + 2, bits))) for i in range(1, bits, 2)]
        self.left = list(range(bits - 1, 0, -1))
        count = lax.axis_size("col")
        self.line = [(None, [(i, i ^ (1 << bit)) for i in range(count)]) for bit in range(count.bit_length() - 1)]
        if line:
            half = count // 2
            self.line = [(None, [(i, i + 1), (count - 1 - i, count - 2 - i)]) for i in range(half - 1)]
            self.line += [(None, [(half - 1, half), (half, half - 1)])]
            self.line += [
                ((i, count - 1 - i), [(i + 1, i), (count - 2 - i, count - 1 - i)])
                for i in range(half - 2, -1, -1)
            ]
        self.sent, self.kept, self.got, self.fused = [sent], kept, None, fused

    def shard(self, terms, bits, mask):
        here = lax.axis_index("row")
        order = [self.left.index(bit) for bit in bits]
        total = None
        for term in terms:
            starts, sizes = [0] * term.ndim, list(term.shape)
            for axis, bit in zip(order, bits):
                starts[axis], sizes[axis] = ((here ^ mask) >> bit) & 1, 1
            piece = lax.dynamic_slice(term, starts, sizes)
            piece = piece.reshape([size for i, size in enumerate(sizes) if i not in order]).astype(F32)
            total = piece if total is None else total + piece
        return total.astype(LOW)

    def step(self):
        if self.order:
            bits = self.order[0]
            masks = [
                sum(1 << bit for i, bit in enumerate(bits) if other >> i & 1)
                for other in range(1, 1 << len(bits))
            ]
            if bits != (0,):
                terms = [self.kept, *self.got]
                self.sent = [self.shard(terms, bits, mask) for mask in masks]
                self.kept = self.shard(terms, bits, 0)
                self.left = [bit for bit in self.left if bit not in bits]
            size = lax.axis_size("row")
            self.got = [
                lax.ppermute(sent, "row", [(i, i ^ mask) for i in range(size)])
                for sent, mask in zip(self.sent, masks)
            ]
        else:
            self.sent = [self.kept]
            self.got = [lax.ppermute(self.kept, "col", self.line[0][1])]

    def land(self, token=None):
        if token is not None:
            self.kept = lax.optimization_barrier((self.kept, token))[0]
        got = self.got
        if self.order:
            bits = self.order.pop(0)
            if bits == (0,):
                dims = (2,) * len(self.left) + self.kept.shape[1:]
                self.kept, self.got = self.kept.reshape(dims), [item.reshape(dims) for item in self.got]
            if not self.order and self.fused:
                self.kept = add_all([self.kept, *self.got])
            elif not self.order:
                self.kept = sum([item.astype(F32) for item in self.got], self.kept.astype(F32)).astype(LOW)
        else:
            ends, _ = self.line.pop(0)
            if ends is None:
                self.kept = self.kept + self.got[0]
            else:
                here = lax.axis_index("col")
                self.kept = jnp.where((here == ends[0]) | (here == ends[1]), self.got[0], self.kept)
        return got

    def turn(self, token=None):
        got = self.land(token)
        if self.done:
            return got
        self.step()
        return got + self.sent

    @property
    def done(self):
        return not self.order and not self.line


def gather_all(piece):
    row_bits = lax.axis_size("row").bit_length() - 1
    col_bits = lax.axis_size("col").bit_length() - 1
    steps = [("col", tuple(range(i, min(i + 2, col_bits)))) for i in range(0, col_bits, 2)]
    steps += [("row", tuple(range(i, min(i + 2, row_bits)))) for i in range(1, row_bits, 2)]
    for name, bits in steps + [("row", (0,))]:
        here = lax.axis_index(name)
        pieces = [piece]
        for other in range(1, 1 << len(bits)):
            mask = sum(1 << bit for i, bit in enumerate(bits) if other >> i & 1)
            pairs = [(i, i ^ mask) for i in range(lax.axis_size(name))]
            pieces.append(lax.ppermute(piece, name, pairs))
        for i, bit in enumerate(bits):
            high = ((here >> bit) & 1) == 1
            pieces = [
                jnp.where(high, pieces[place ^ (1 << i)], pieces[place]) for place in range(len(pieces))
            ]
        piece = jnp.concatenate(pieces, 0)
    return piece


def per_device(
    query_tokens, passage_tokens, query_lengths, passage_lengths, positives,
    w_query, w_key, w_value, w_attn_out, w_inner, w_outer,
    bias_query, bias_value, bias_attn_out, bias_inner, bias_outer,
    gain_one, shift_one, gain_two, shift_two,
):
    q_dev, q_len, width = query_tokens.shape
    p_dev, p_len, _ = passage_tokens.shape
    inner = w_inner.shape[1]
    rows_all = p_len
    assert q_dev * q_len == rows_all and q_dev + p_dev <= SLOTS
    blocks = 1 + p_dev
    total_rows = blocks * rows_all
    row_count = lax.axis_size("row")
    col_count = lax.axis_size("col")
    row_here = lax.axis_index("row")
    core = (row_here & 1).reshape(1)
    me = (row_here * col_count + lax.axis_index("col")).reshape(1)
    params = pltpu.CompilerParams(vmem_limit_bytes=VMEM)
    smem = pl.BlockSpec(memory_space=pltpu.SMEM)

    def by_block(wide):
        return pl.BlockSpec((rows_all, wide), lambda i: (i, 0))

    def by_block_t(high):
        return pl.BlockSpec((high, rows_all), lambda i: (0, i))

    def fixed(shape):
        return pl.BlockSpec(shape, lambda i: (0,) * len(shape))

    queries_spec = pl.BlockSpec((rows_all, width), lambda i: (0, 0))
    passages_spec = pl.BlockSpec((rows_all, width), lambda i: (jnp.maximum(i - 1, 0), 0))

    lse_spec = pl.BlockSpec((1, HEADS // 2, 8, rows_all), lambda i: (i, 0, 0, 0))

    def shape(*dims, kind=LOW):
        return jax.ShapeDtypeStruct(dims, kind)

    queries = query_tokens.reshape(rows_all, width)
    passages = passage_tokens.reshape(p_dev * rows_all, width)
    square = const_spec((width, width))
    anywhere = pl.BlockSpec(memory_space=pl.ANY)
    thin = const_spec((width,))

    q, k, v, ctx_t, lse = call(
        partial(attend_kernel, (q_dev, q_len, rows_all, width)),
        (query_lengths, passage_lengths, queries, passages, w_query, w_key, w_value, bias_query, bias_value),
        [smem, smem, queries_spec, passages_spec, square, square, square, thin, thin],
        [(by_block(width), shape(total_rows, width))] * 3
        + [
            (by_block_t(width), shape(width, total_rows)),
            (lse_spec, shape(blocks, HEADS // 2, 8, rows_all, kind=F32)),
        ],
        (blocks,),
        56,
        name="attend",

    )

    rows_part = rows_all
    parts = blocks

    def by_part(wide):
        return pl.BlockSpec((rows_part, wide), lambda i: (i, 0))

    queries_part = pl.BlockSpec((rows_part, width), lambda i: (0, 0))
    passages_part = pl.BlockSpec((rows_part, width), lambda i: (jnp.maximum(i - 1, 0), 0))
    h1, y1, act, slope, h2, query_out, passage_out, pooled, payload = call(
        partial(dense_kernel, (q_dev, q_len, p_len, width, inner)),
        (
            query_lengths, passage_lengths, positives, queries, passages, ctx_t, w_attn_out, w_inner, w_outer,
            bias_attn_out, bias_inner, bias_outer, gain_one, shift_one, gain_two, shift_two,
        ),
        [smem, smem, smem, queries_part, passages_part, pl.BlockSpec((width, rows_part), lambda i: (0, i))]
        + [anywhere] * 3
        + [thin, const_spec((inner,))]
        + [thin] * 5,
        [
            (by_part(width), shape(total_rows, width)),
            (by_part(width), shape(total_rows, width)),
            (by_part(inner), shape(total_rows, inner)),
            (by_part(inner), shape(total_rows, inner)),
            (by_part(width), shape(total_rows, width)),
            (queries_part, shape(rows_all, width)),
            (passages_part, shape(p_dev * rows_all, width)),
            (fixed((SLOTS, width)), shape(SLOTS, width, kind=F32)),
            (fixed((SLOTS, width + 128)), shape(SLOTS, width + 128)),
        ],
        (parts,),
        56,
        name="dense",
        scratch=[
            pltpu.VMEM((width, width), LOW),
            pltpu.VMEM((width, inner), LOW),
            pltpu.VMEM((inner, width), LOW),
            pltpu.SemaphoreType.DMA((3,)),
        ],

    )

    gathered = gather_all(payload)
    loss, gvec = pl.pallas_call(
        partial(loss_kernel, (q_dev, p_dev, width, col_count)),
        in_specs=[smem] * 3 + [pl.BlockSpec(memory_space=pltpu.VMEM)] * 3,
        out_specs=[pl.BlockSpec(memory_space=pltpu.VMEM)] * 2,
        out_shape=[shape(8, 128, kind=F32), shape(SLOTS, width, kind=F32)],
        compiler_params=params,
        name="loss",
    )(me, query_lengths, passage_lengths, payload, gathered, pooled)

    smalls = shape(8, width, kind=F32)
    cut = width // row_count
    cut_inner = inner // row_count
    half = row_count // 2
    step_cols = 768
    per_step = step_cols // cut_inner
    outer_spec = pl.BlockSpec((per_step // 2, width, cut_inner), lambda i: (i, 0, 0))
    grad_f, stat_two, *outer_parts = call(
        partial(outer_grad_kernel, (q_dev, q_len, p_len)),
        (core, query_lengths, passage_lengths, gvec, h2, gain_two, act),
        [smem, smem, smem, fixed((SLOTS, width)), const_spec((total_rows, width)), thin]
        + [pl.BlockSpec((total_rows, step_cols), lambda i: (0, i))],
        [
            (fixed((total_rows, width)), shape(total_rows, width)),
            (fixed((8, width)), smalls),
            (outer_spec, shape(half, width, cut_inner)),
            (outer_spec, shape(half, width, cut_inner)),
        ],
        (inner // step_cols,),
        56,
        name="outer_grad",
        scratch=[pltpu.VMEM((width, total_rows), LOW)],
    )
    outer = Flow(*outer_parts, line=True)
    outer.step()

    def turn(arrays, specs, deps):
        outs = [(by_block_t(width), shape(width, total_rows))]
        return call(turn_low_kernel, arrays, specs, outs, (blocks,), 56, deps, name="turn", us=40)[0]

    y1_t = turn([y1], [by_block(width)], outer.sent)
    deps = outer.turn(y1_t)
    head_dim = width // HEADS
    third = 4 * head_dim
    groups = [(0, 2 * third), (2 * third, third)]
    grad_u, grad_attn, grad_ctx, stat_one, grad_bias_inner = call(
        partial(dense_back_kernel, inner),
        (grad_f, slope, h1, w_outer, w_inner, w_attn_out, gain_one),
        [by_block(width), by_block(inner), by_block(width), anywhere, anywhere, anywhere, thin],
        [
            (by_block(inner), shape(total_rows, inner)),
            (by_block(width), shape(total_rows, width)),
            (by_block(width), shape(total_rows, width)),
            (fixed((8, width)), smalls),
            (fixed((8, inner)), shape(8, inner, kind=F32)),
        ],
        (blocks,),
        60,
        deps,
        name="dense_back",
        scratch=[
            pltpu.VMEM((inner, width), LOW),
            pltpu.VMEM((width, inner), LOW),
            pltpu.VMEM((width, width), LOW),
            pltpu.SemaphoreType.DMA((3,)),
        ],
    )
    deps = outer.turn(stat_one)
    up_flow = Flow(*weight_grad(y1_t, grad_u, row_count, core, deps), line=True, fused=True)
    up_flow.step()
    deps = up_flow.sent + outer.turn(up_flow.sent[0])
    x_t = turn([queries, passages], [queries_spec, passages_spec], deps)
    deps = up_flow.turn(x_t)

    def attend_back(start, wide, deps, extra=(), room=None):
        pairs = wide // (2 * head_dim)
        index = start // wide
        cols = pl.BlockSpec((rows_all, wide), lambda i: (i, index))
        rows = cut + (16 if extra else 0)
        return call(
            partial(attend_back_kernel, (q_dev, q_len, rows_all, head_dim)),
            (core, query_lengths, passage_lengths, q, k, v, ctx_t, lse, grad_ctx, x_t, *extra),
            [smem, smem, smem]
            + [cols] * 3
            + [
                pl.BlockSpec((wide, rows_all), lambda i: (index, i)),
                pl.BlockSpec((1, pairs, 8, rows_all), lambda i: (i, index, 0, 0)),
                cols,
                by_block_t(width),
            ]
            + [const_spec(item.shape) for item in extra],
            [
                (by_block(3 * wide), shape(total_rows, 3 * wide)),
                (fixed((8, wide)), shape(8, wide, kind=F32)),
            ]
            + [(fixed((half, rows, 3 * wide)), shape(half, rows, room or 3 * wide))] * 2,
            (blocks,),
            56,
            deps,
            name="attend_back",
            scratch=[pltpu.VMEM((width, 3 * wide), F32)],
            us=12 if room else 40,
        )

    grad_a, stat_a, *mixed_parts = attend_back(*groups[0], deps, room=6 * third + width)
    at = 6 * third // width
    mixed_parts = weight_grad(ctx_t, grad_attn, row_count, core, [stat_a], mixed_parts, at, us=0)
    mixed_flow = Flow(*mixed_parts, line=True)
    mixed_flow.step()
    token = mixed_flow.sent[0]
    deps = mixed_flow.sent + outer.turn(token) + up_flow.turn(token)
    extra = (stat_two, stat_one, grad_bias_inner, stat_a)
    grad_b, stat_b, *last_parts = attend_back(*groups[1], deps, extra)
    last_flow = Flow(*last_parts)
    last_flow.step()
    deps = last_flow.sent + outer.turn(stat_b) + mixed_flow.turn(stat_b) + up_flow.turn(stat_b)
    query_grad, passage_grad = call(
        partial(input_grad_kernel, groups),
        (grad_a, grad_b, grad_attn, w_query, w_key, w_value),
        [by_block(3 * wide) for _, wide in groups] + [by_block(width), square, square, square],
        [
            (queries_spec, shape(rows_all, width)),
            (passages_spec, shape(p_dev * rows_all, width)),
        ],
        (blocks,),
        56,
        deps,
        name="input_grad",
        us=40,
    )
    last_flow.turn(passage_grad)
    up_flow.turn(last_flow.kept)
    mixed_flow.turn(up_flow.kept)
    last_flow.turn(mixed_flow.kept)
    outs = [(fixed((cut_inner, width)), shape(cut_inner, width, kind=F32))]
    (turned,) = call(
        turn_kernel, (outer.kept,), [const_spec((width, cut_inner))], outs, (1,), 56, [last_flow.kept], name="turn", us=40
    )
    mixed_flow.turn(turned)
    last_flow.turn(mixed_flow.kept)
    up_flow.turn(last_flow.kept)
    mixed_flow.turn(up_flow.kept)
    last_flow.turn(mixed_flow.kept)
    flows = [outer, up_flow, mixed_flow, last_flow]
    while not all(flow.done for flow in flows):
        for flow in flows:
            if not flow.done:
                flow.turn()
    mixed, last = mixed_flow.kept, last_flow.kept
    qkv = [
        jnp.concatenate(
            [mixed[:, i * 2 * third : (i + 1) * 2 * third], last[:cut, i * third : (i + 1) * third]], 1
        ).astype(F32)
        for i in range(3)
    ]
    small = last[cut:].astype(F32)
    return (
        loss[0, 0],
        query_out.reshape(query_tokens.shape),
        passage_out.reshape(passage_tokens.shape),
        query_grad.reshape(query_tokens.shape),
        passage_grad.reshape(passage_tokens.shape),
        *qkv,
        mixed[:, 6 * third :].astype(F32),
        up_flow.kept.astype(F32),
        turned,
        *[small[i, :cut] for i in range(3)],
        small[8, : inner // row_count],
        *[small[i, :cut] for i in range(3, 8)],
    )


def solution(mesh):
    in_specs = (
        P(("row", "col"), None, None),
        P(("row", "col"), None, None),
        P(("row", "col")),
        P(("row", "col")),
        P(("row", "col")),
        P(),
        P(),
        P(),
        P(),
        P(),
        P(),
        P(),
        P(),
        P(),
        P(),
        P(),
        P(),
        P(),
        P(),
        P(),
    )
    out_specs = (
        P(),
        P(("row", "col"), None, None),
        P(("row", "col"), None, None),
        P(("row", "col"), None, None),
        P(("row", "col"), None, None),
        P("row", None),
        P("row", None),
        P("row", None),
        P("row", None),
        P("row", None),
        P("row", None),
        P("row"),
        P("row"),
        P("row"),
        P("row"),
        P("row"),
        P("row"),
        P("row"),
        P("row"),
        P("row"),
    )
    return jax.shard_map(
        per_device, mesh=mesh, in_specs=in_specs, out_specs=out_specs, check_vma=False
    )
```

```python
from functools import partial

import jax
import jax.numpy as jnp
from jax import lax
from jax.experimental import pallas as pl
from jax.experimental.pallas import tpu as pltpu
from jax.sharding import PartitionSpec as P

HEADS = 12
EPS_NORM = 1e-12
EPS_POOL = 1e-06
SCALE_LOSS = 128.0
INV_TEMP = 100.0
TILE = 256
SLOTS = 8
VMEM = 60 * 1024 * 1024
LOW = jnp.bfloat16
F32 = jnp.float32


def mm(left, right):
    return lax.dot_general(left, right, (((1,), (0,)), ((), ())), preferred_element_type=F32)


def mm_nt(left, right):
    return lax.dot_general(left, right, (((1,), (1,)), ((), ())), preferred_element_type=F32)


def norm_parts(hidden):
    center = hidden - jnp.mean(hidden, -1, keepdims=True)
    spread = jnp.mean(center * center, -1, keepdims=True)
    scale = lax.rsqrt(spread + EPS_NORM)
    return center * scale, scale


def gelu_parts(u):
    square = u * u
    q = 1.4250060785476853e-06
    for factor in (-3.669345091379551e-05, -8.782652731110375e-05, 0.03639228618131223, 0.7978697123041883):
        q = q * square + factor
    share = 0.5 + 0.5 * jnp.tanh(u * q)
    bell = jnp.exp(-0.5 * square)
    return u * share, share + (0.3989422804014327 * u) * bell


def vec(ref, cols=slice(None)):
    return ref[cols].reshape(1, -1)


def rows_of(step, size):
    return pl.ds(pl.multiple_of(step * size, size), size)


def part_owner(part, q_dev, q_len, p_len, qlen_ref, plen_ref):
    per = p_len // q_len
    beyond = jnp.maximum(part - q_dev, 0)
    is_query = part < q_dev
    slot = jnp.where(is_query, part, q_dev + beyond // per)
    length = jnp.where(is_query, qlen_ref[jnp.where(is_query, part, 0)], plen_ref[beyond // per])
    first = jnp.where(is_query, 0, beyond % per * q_len)
    return slot, length, first


def live_rows(first, length, size):
    return (first + lax.broadcasted_iota(jnp.int32, (size, 1), 0)) < length


def sure_rows(size):
    return size * 4 // 5 // 16 * 16


def half_only(pair_t, which):
    half = pair_t.shape[0] // 2
    zeros = jnp.zeros((half, pair_t.shape[1]), pair_t.dtype)
    if which == 0:
        return jnp.concatenate([pair_t[:half], zeros], 0)
    return jnp.concatenate([zeros, pair_t[half:]], 0)


def staged(count, *stages):
    for step in range(count + len(stages) - 1):
        for late, stage in enumerate(stages):
            if 0 <= step - late < count:
                stage(step - late)


def fetch(source, target, sems, index):
    return pltpu.make_async_copy(source, target, sems.at[index])


def attend_kernel(
    dims, qlen_ref, plen_ref, xq_ref, xp_ref, wq_ref, wk_ref, wv_ref, bq_ref, bv_ref,
    q_ref, k_ref, v_ref, ctx_t_ref, lse_ref,
):
    q_dev, q_len, rows_all, width = dims
    block = pl.program_id(0)
    head_dim = width // HEADS
    x = jnp.where(block == 0, xq_ref[...], xp_ref[...])
    q = ((mm(x, wq_ref[...]) + vec(bq_ref)) * head_dim**-0.5).astype(LOW)
    k = mm(x, wk_ref[...]).astype(LOW)
    v = (mm(x, wv_ref[...]) + vec(bv_ref)).astype(LOW)
    q_ref[...] = q
    k_ref[...] = k
    v_ref[...] = v
    q_t, v_t = q.T, v.T

    def attend(size, starts, lengths):
        items = [(start, length, head) for head in range(HEADS) for start, length in zip(starts, lengths)]
        scores, weights = {}, {}

        def compare(i):
            start, length, head = items[i]
            cols = slice(head // 2 * 2 * head_dim, (head // 2 + 1) * 2 * head_dim)
            here = slice(start, start + size)
            scores[i] = mm(k[here, cols], half_only(q_t[cols, here], head % 2))

        def weigh(i):
            start, length, head = items[i]
            edge = sure_rows(size)
            early, late = scores[i][:edge], scores.pop(i)[edge:]
            late = jnp.where(live_rows(edge, length, size - edge), late, -1e30)
            top = jnp.maximum(jnp.max(early, 0, keepdims=True), jnp.max(late, 0, keepdims=True))
            weights[i] = top, jnp.concatenate([jnp.exp(early - top).astype(LOW), jnp.exp(late - top).astype(LOW)], 0)

        def combine(i):
            start, length, head = items[i]
            here, rows = slice(start, start + size), slice(head * head_dim, (head + 1) * head_dim)
            top, weight = weights.pop(i)
            values = jnp.concatenate([v_t[rows, here], jnp.ones((16, size), LOW)], 0)
            result = mm(values, weight)
            total = result[head_dim : head_dim + 1]
            lse_ref[0, head // 2, head % 2 : head % 2 + 1, here] = top + jnp.log(total)
            ctx_t_ref[rows, here] = (result[:head_dim] * (1.0 / total)).astype(LOW)

        staged(len(items), compare, weigh, combine)

    @pl.when(block == 0)
    def _():
        attend(q_len, [s * q_len for s in range(q_dev)], [qlen_ref[s] for s in range(q_dev)])

    @pl.when(block > 0)
    def _():
        attend(rows_all, [0], [plen_ref[jnp.maximum(block - 1, 0)]])


def dense_kernel(
    dims, qlen_ref, plen_ref, pos_ref, xq_ref, xp_ref, ctx_t_ref, wo_hbm, wi_hbm, wf_hbm,
    bo_ref, bi_ref, bf_ref, g1_ref, s1_ref, g2_ref, s2_ref,
    h1_ref, y1_ref, act_ref, dg_ref, h2_ref, yq_ref, yp_ref, pool_ref, pay_ref,
    wo_ref, wi_ref, wf_ref, sems,
):
    q_dev, q_len, p_len, width, inner = dims
    block = pl.program_id(0)
    rows_all = xq_ref.shape[0]
    query_blocks = q_dev * q_len // rows_all
    copies = [
        fetch(source, target, sems, index)
        for index, (source, target) in enumerate([(wo_hbm, wo_ref), (wi_hbm, wi_ref), (wf_hbm, wf_ref)])
    ]

    @pl.when(block == 0)
    def _():
        for copy in copies:
            copy.start()
        pool_ref[...] = jnp.zeros_like(pool_ref)
        copies[0].wait()

    x = jnp.where(block < query_blocks, xq_ref[...], xp_ref[...])
    hidden = x.astype(F32) + (mm(ctx_t_ref[...].T, wo_ref[...]) + vec(bo_ref))
    h1_ref[...] = hidden.astype(LOW)
    y1 = norm_parts(hidden)[0] * vec(g1_ref) + vec(s1_ref)
    y1_low = y1.astype(LOW)
    y1_ref[...] = y1_low

    @pl.when(block == 0)
    def _():
        copies[1].wait()
        copies[2].wait()

    raw, made = {}, {}

    def expand(i):
        cols = slice(i * TILE, (i + 1) * TILE)
        raw[i] = mm(y1_low, wi_ref[:, cols]) + vec(bi_ref, cols)

    def activate(i):
        cols = slice(i * TILE, (i + 1) * TILE)
        act, slope = gelu_parts(raw.pop(i))
        made[i] = act.astype(LOW)
        act_ref[:, cols] = made[i]
        dg_ref[:, cols] = slope.astype(LOW)

    staged(inner // TILE, expand, activate)
    left = jnp.concatenate([made[i] for i in range(inner // TILE)], 1)
    total = (y1 + vec(bf_ref)) + mm(left, wf_ref[...])
    h2_ref[...] = total.astype(LOW)
    y2 = norm_parts(total)[0] * vec(g2_ref) + vec(s2_ref)
    for part in range(rows_all // q_len):
        number = block * (rows_all // q_len) + part
        slot, length, first = part_owner(number, q_dev, q_len, p_len, qlen_ref, plen_ref)
        piece = y2[part * q_len : (part + 1) * q_len]
        summed = jnp.sum(jnp.where(live_rows(first, length, q_len), piece, 0.0), 0, keepdims=True)
        in_slot = lax.broadcasted_iota(jnp.int32, (SLOTS, 1), 0) == slot
        pool_ref[...] += jnp.where(in_slot, summed / length.astype(F32), 0.0)

    @pl.when(block < query_blocks)
    def _():
        yq_ref[...] = y2.astype(LOW)

    @pl.when(block >= query_blocks)
    def _():
        yp_ref[...] = y2.astype(LOW)

    @pl.when(block == pl.num_programs(0) - 1)
    def _():
        pooled = pool_ref[...]
        emb = pooled * lax.rsqrt(jnp.sum(pooled * pooled, -1, keepdims=True) + EPS_POOL)
        pay_ref[:, :width] = emb.astype(LOW)
        row = lax.broadcasted_iota(jnp.int32, (SLOTS, 128), 0)
        col = lax.broadcasted_iota(jnp.int32, (SLOTS, 128), 1)
        place = jnp.zeros((SLOTS, 128), jnp.int32)
        for j in range(q_dev):
            high = pos_ref[j] // 128
            low = pos_ref[j] - high * 128
            place = jnp.where(row == j, jnp.where(col == 0, high, jnp.where(col == 1, low, 0)), place)
        pay_ref[:, width:] = place.astype(F32).astype(LOW)


def loss_kernel(
    dims, me_ref, qlen_ref, plen_ref, own_ref, all_ref, pool_ref, loss_ref, gvec_ref
):
    q_dev, p_dev, width, col_count = dims
    count = all_ref.shape[0]
    every = all_ref[:, :width]
    own = own_ref[:, :width]

    def passage_mask(index):
        spot, place = index % SLOTS, index // SLOTS
        per_core = count // SLOTS // 2
        core, rest = place // per_core, place % per_core
        device = (rest // col_count * 2 + core) * col_count + rest % col_count
        return (spot >= q_dev) & (spot < q_dev + p_dev), device * p_dev + spot - q_dev

    scores = mm_nt(own, every) * INV_TEMP
    valid, ident = passage_mask(lax.broadcasted_iota(jnp.int32, (SLOTS, count), 1))
    scores = jnp.where(valid, scores, -1e30)
    top = jnp.max(scores, -1, keepdims=True)
    totals = top + jnp.log(jnp.sum(jnp.exp(scores - top), -1, keepdims=True))
    marks = own_ref[:, width:].astype(F32)
    wanted = marks[:, 0:1] * 128.0 + marks[:, 1:2]
    target = (valid & (ident.astype(F32) == wanted)).astype(F32)
    raw = (INV_TEMP * (SCALE_LOSS * (jnp.exp(scores - totals) - target))).astype(LOW)
    grad_q = mm(raw, every)

    picker_col = lax.broadcasted_iota(jnp.int32, (SLOTS, 128), 1)
    picker = jnp.where(picker_col == 0, 128.0, jnp.where(picker_col == 1, 1.0, 0.0)).astype(LOW)
    own_row = lax.broadcasted_iota(jnp.int32, (SLOTS, TILE), 0)
    own_valid = (own_row >= q_dev) & (own_row < q_dev + p_dev)
    own_ident = (me_ref[0] * p_dev + own_row - q_dev).astype(F32)

    def body(step, carry):
        total_loss, grad_p = carry
        rows = rows_of(step, TILE)
        some = all_ref[rows, :width]
        place = mm_nt(picker, all_ref[rows, width:])[0:1]
        table = mm_nt(every, some) * INV_TEMP
        ok, names = passage_mask(lax.broadcasted_iota(jnp.int32, (count, TILE), 0))
        picked = jnp.sum(jnp.where(ok & (names.astype(F32) == place), table, 0.0), 0, keepdims=True)
        table = jnp.where(ok, table, -1e30)
        high = jnp.max(table, 0, keepdims=True)
        lse = high + jnp.log(jnp.sum(jnp.exp(table - high), 0, keepdims=True))
        is_query = lax.broadcasted_iota(jnp.int32, (1, TILE), 1) % SLOTS < q_dev
        losses = jnp.where(is_query, lse - picked, 0.0)
        mine = mm_nt(own, some) * INV_TEMP
        hit = (own_ident == place).astype(F32)
        grads = INV_TEMP * (SCALE_LOSS * (jnp.exp(mine - lse) - hit))
        grads = jnp.where(own_valid & is_query, grads, 0.0).astype(LOW)
        return total_loss + jnp.sum(losses, 1, keepdims=True), grad_p + mm(grads, some)

    start = (jnp.zeros((1, 1), F32), jnp.zeros((SLOTS, width), F32))
    total_loss, grad_p = lax.fori_loop(0, count // TILE, body, start)
    loss_ref[...] = jnp.broadcast_to(total_loss / float(count // SLOTS * q_dev), loss_ref.shape)

    slot = lax.broadcasted_iota(jnp.int32, (SLOTS, 1), 0)
    grad = jnp.where(slot < q_dev, grad_q, grad_p)
    pooled = pool_ref[...]
    r = lax.rsqrt(jnp.sum(pooled * pooled, -1, keepdims=True) + EPS_POOL)
    inside = jnp.sum(pooled * grad, -1, keepdims=True)
    length = jnp.ones((SLOTS, 1), F32)
    for j in range(q_dev):
        length = jnp.where(slot == j, qlen_ref[j].astype(F32), length)
    for j in range(p_dev):
        length = jnp.where(slot == q_dev + j, plen_ref[j].astype(F32), length)
    gvec_ref[...] = (r * grad - r * r * r * inside * pooled) / length


def store_shards(core_ref, result, send_ref, keep_ref, by_row=True, tails=None):
    count = send_ref.shape[0] * 2
    size = result.shape[0 if by_row else 1] // count

    def store(even, odd):
        for shard in range(count):
            spot = slice(shard * size, (shard + 1) * size)
            piece = (result[spot, :] if by_row else result[:, spot]).astype(LOW)
            target = odd if shard % 2 else even
            if tails is None:
                target[shard // 2] = piece
            else:
                target[shard // 2, :size] = piece
                target[shard // 2, size:] = tails[shard]

    @pl.when(core_ref[0] == 0)
    def _():
        store(keep_ref, send_ref)

    @pl.when(core_ref[0] == 1)
    def _():
        store(send_ref, keep_ref)


def outer_grad_kernel(
    dims, core_ref, qlen_ref, plen_ref, gvec_ref, h2_ref, g2_ref, act_ref,
    gf_ref, stat_ref, send_ref, keep_ref, gf_t_ref,
):
    q_dev, q_len, p_len = dims

    @pl.when(pl.program_id(0) == 0)
    def _():
        stat_ref[...] = jnp.zeros_like(stat_ref)

        def body(part, carry):
            rows = rows_of(part, q_len)
            slot, length, first = part_owner(part, q_dev, q_len, p_len, qlen_ref, plen_ref)
            in_slot = lax.broadcasted_iota(jnp.int32, (SLOTS, 1), 0) == slot
            grad_y = jnp.sum(jnp.where(in_slot, gvec_ref[...], 0.0), 0, keepdims=True)
            live = live_rows(first, length, q_len)
            n2, r2 = norm_parts(h2_ref[rows, :].astype(F32))
            g = grad_y * vec(g2_ref)
            grad = r2 * (g - jnp.mean(g, -1, keepdims=True) - n2 * jnp.mean(g * n2, -1, keepdims=True))
            grad = jnp.where(live, grad, 0.0)
            low = grad.astype(LOW)
            gf_ref[rows, :] = low
            gf_t_ref[:, rows] = low.T
            stat_ref[0:1, :] += grad_y * jnp.sum(jnp.where(live, n2, 0.0), 0, keepdims=True)
            stat_ref[1:2, :] += grad_y * jnp.sum(live.astype(F32), 0, keepdims=True)
            stat_ref[2:3, :] += jnp.sum(low.astype(F32), 0, keepdims=True)
            return carry

        lax.fori_loop(0, h2_ref.shape[0] // q_len, body, 0)

    store_shards(core_ref, mm(gf_t_ref[...], act_ref[...]), send_ref, keep_ref, by_row=False)


def dense_back_kernel(
    dims, gf_ref, dg_ref, h1_ref, wf_hbm, wi_hbm, wo_hbm, g1_ref,
    gu_ref, ga_ref, gc_ref, stat_ref, bi_ref,
    wf_ref, wi_ref, wo_ref, sems,
):
    inner = dims
    block = pl.program_id(0)
    copies = [
        fetch(source, target, sems, index)
        for index, (source, target) in enumerate([(wf_hbm, wf_ref), (wi_hbm, wi_ref), (wo_hbm, wo_ref)])
    ]

    @pl.when(block == 0)
    def _():
        for copy in copies:
            copy.start()
        stat_ref[...] = jnp.zeros_like(stat_ref)
        bi_ref[...] = jnp.zeros_like(bi_ref)
        copies[0].wait()

    gf = gf_ref[...]
    raw, made, biases = {}, {}, []

    def spread(i):
        raw[i] = mm_nt(gf, wf_ref[i * TILE : (i + 1) * TILE, :])

    def slope(i):
        cols = slice(i * TILE, (i + 1) * TILE)
        made[i] = (raw.pop(i) * dg_ref[:, cols].astype(F32)).astype(LOW)
        gu_ref[:, cols] = made[i]
        biases.append(jnp.sum(made[i].astype(F32), 0, keepdims=True))

    staged(inner // TILE, spread, slope)
    bi_ref[0:1, :] += jnp.concatenate(biases, 1)
    left = jnp.concatenate([made[i] for i in range(inner // TILE)], 1)

    @pl.when(block == 0)
    def _():
        for copy in copies[1:]:
            copy.wait()

    total = gf.astype(F32) + mm_nt(left, wi_ref[...])
    n1, r1 = norm_parts(h1_ref[...].astype(F32))
    stat_ref[0:1, :] += jnp.sum(total * n1, 0, keepdims=True)
    stat_ref[1:2, :] += jnp.sum(total, 0, keepdims=True)
    g = total * vec(g1_ref)
    grad = r1 * (g - jnp.mean(g, -1, keepdims=True) - n1 * jnp.mean(g * n1, -1, keepdims=True))
    low = grad.astype(LOW)
    ga_ref[...] = low
    stat_ref[2:3, :] += jnp.sum(low.astype(F32), 0, keepdims=True)
    gc_ref[...] = mm_nt(low, wo_ref[...]).astype(LOW)


def attend_back_kernel(
    dims, core_ref, qlen_ref, plen_ref, q_ref, k_ref, v_ref, ctx_t_ref, lse_ref, gc_ref, x_t_ref, *refs
):
    *extra, out_ref, stat_ref, send_ref, keep_ref, sum_ref = refs
    q_dev, q_len, rows_all, head_dim = dims
    block = pl.program_id(0)
    pair_dim = 2 * head_dim
    width = q_ref.shape[1]
    pairs = width // pair_dim

    @pl.when(block == 0)
    def _():
        stat_ref[...] = jnp.zeros_like(stat_ref)

    def attend(size, starts, lengths, fresh):
        lane = lax.broadcasted_iota(jnp.int32, (size, pair_dim), 1)
        items = [(s, p, which) for p in range(pairs) for s in range(len(starts)) for which in range(2)]
        held, raw, made, grads = {}, {}, {}, {}

        def pair_of(s, p):
            if (s, p) not in held:
                here, cols = slice(starts[s], starts[s] + size), slice(p * pair_dim, (p + 1) * pair_dim)
                q, k, v, gc = q_ref[here, cols], k_ref[here, cols], v_ref[here, cols], gc_ref[here, cols]
                held[s, p] = here, cols, q, k, v, gc, q.T, k.T, gc.T
            return held[s, p]

        def compare(i):
            s, p, which = items[i]
            here, cols, q, k, v, gc, q_t, k_t, gc_t = pair_of(s, p)
            raw[i] = mm(k, half_only(q_t, which)), mm(v, half_only(gc_t, which))

        def weigh(i):
            s, p, which = items[i]
            here, cols, q, k, v, gc, q_t, k_t, gc_t = pair_of(s, p)
            head = slice((p * 2 + which) * head_dim, (p * 2 + which + 1) * head_dim)
            scores, grad_p = raw.pop(i)
            lse = lse_ref[0, p, which : which + 1, here]
            edge = sure_rows(size)
            late = jnp.where(live_rows(edge, lengths[s], size - edge), scores[edge:], -1e30)
            probs = jnp.concatenate([jnp.exp(scores[:edge] - lse), jnp.exp(late - lse)], 0)
            half = slice(which * head_dim, (which + 1) * head_dim)
            delta = jnp.sum(gc_t[half].astype(F32) * ctx_t_ref[head, here].astype(F32), 0, keepdims=True)
            made[i] = probs.astype(LOW), (probs * (grad_p - delta)).astype(LOW)

        def combine(i):
            s, p, which = items[i]
            here, cols, q, k, v, gc, q_t, k_t, gc_t = pair_of(s, p)
            mine = (lane >= head_dim) if which else (lane < head_dim)
            zero = jnp.zeros_like(q)
            probs, grad_s = made.pop(i)
            add_v = mm(probs, jnp.where(mine, gc, zero))
            add_k = mm(grad_s, jnp.where(mine, q, zero))
            add_q = mm(k_t[which * head_dim : (which + 1) * head_dim], grad_s)
            if which == 0:
                made[s, p] = add_v, add_k, add_q
                return
            old_v, old_k, old_q = made.pop((s, p))
            grad_q = (jnp.concatenate([old_q, add_q], 0).T * head_dim**-0.5).astype(LOW)
            grad_k = (old_k + add_k).astype(LOW)
            grad_v = (old_v + add_v).astype(LOW)
            for number, grad in enumerate((grad_q, grad_k, grad_v)):
                out_ref[here, number * width + cols.start : number * width + cols.stop] = grad
                grads[number, s, p] = grad
            stat_ref[0:1, cols] += jnp.sum(grad_q.astype(F32), 0, keepdims=True)
            stat_ref[1:2, cols] += jnp.sum(grad_v.astype(F32), 0, keepdims=True)

            if p % 2 and s == len(starts) - 1:
                project(p - 1)

        def project(p):
            for number in range(3):
                rows = [
                    jnp.concatenate([grads.pop((number, s, p)), grads.pop((number, s, p + 1))], 1)
                    for s in range(len(starts))
                ]
                product = mm(x_t_ref[...], jnp.concatenate(rows, 0))
                cols = slice(number * width + p * pair_dim, number * width + (p + 2) * pair_dim)
                if fresh:
                    sum_ref[:, cols] = product
                else:
                    sum_ref[:, cols] += product

        staged(len(items), compare, weigh, combine)

    @pl.when(block == 0)
    def _():
        attend(q_len, [s * q_len for s in range(q_dev)], [qlen_ref[s] for s in range(q_dev)], True)

    @pl.when(block > 0)
    def _():
        attend(rows_all, [0], [plen_ref[jnp.maximum(block - 1, 0)]], False)

    @pl.when(block == pl.num_programs(0) - 1)
    def _():
        tails = None
        if extra:
            tails = small_rows([*extra, stat_ref], send_ref.shape[0] * 2, send_ref.shape[2])
        store_shards(core_ref, sum_ref[...], send_ref, keep_ref, tails=tails)


def input_grad_kernel(groups, *refs):
    grads, (base_ref, wq_ref, wk_ref, wv_ref, gq_ref, gp_ref) = refs[: len(groups)], refs[len(groups) :]
    total = base_ref[...].astype(F32)
    for grad_ref, (start, wide) in zip(grads, groups):
        for number, w_ref in enumerate((wq_ref, wk_ref, wv_ref)):
            total = total + mm_nt(grad_ref[:, number * wide : (number + 1) * wide], w_ref[:, start : start + wide])
    low = total.astype(LOW)

    @pl.when(pl.program_id(0) == 0)
    def _():
        gq_ref[...] = low

    @pl.when(pl.program_id(0) > 0)
    def _():
        gp_ref[...] = low


def weight_grad_kernel(core_ref, left_ref, right_ref, send_ref, keep_ref):
    store_shards(core_ref, mm(left_ref[...], right_ref[...]), send_ref, keep_ref)


def small_rows(refs, count, wide):
    two, one, inner, *attn = [ref[...] for ref in refs]
    eight = jnp.concatenate(
        [jnp.concatenate([item[0:2] for item in attn], 1), one[2:3], two[2:3], one[0:2], two[0:2]], 0
    )
    inner = inner[0:1]
    short, long = eight.shape[1] // count, inner.shape[1] // count
    rows = []
    for shard in range(count):
        top = eight[:, shard * short : (shard + 1) * short]
        low = inner[:, shard * long : (shard + 1) * long]
        top = jnp.concatenate([top, jnp.zeros((8, wide - short), F32)], 1)
        low = jnp.concatenate([low, jnp.zeros((1, wide - long), F32)], 1)
        rows.append(jnp.concatenate([top, low, jnp.zeros((7, wide), F32)], 0).astype(LOW))
    return rows


def turn_kernel(part_ref, out_ref):
    out_ref[...] = part_ref[...].astype(F32).T


def turn_low_kernel(*refs):
    *inputs, out_ref = refs
    if len(inputs) == 1:
        out_ref[...] = inputs[0][...].T
        return

    @pl.when(pl.program_id(0) == 0)
    def _():
        out_ref[...] = inputs[0][...].T

    @pl.when(pl.program_id(0) > 0)
    def _():
        out_ref[...] = inputs[1][...].T


def const_spec(shape):
    return pl.BlockSpec(shape, lambda i: (0,) * len(shape), pipeline_mode=pl.Buffered(1))


def call(body, operands, in_specs, outs, grid, room, deps=(), old=(), into=0, name=None, scratch=(), us=12):
    count, extra = len(operands), len(old)
    if deps:
        tied = min(range(count), key=lambda i: operands[i].size)
        operands = list(operands)
        operands[tied] = lax.optimization_barrier((operands[tied], *deps))[0]

    def kernel(*refs):
        body(*refs[:count], *refs[count + extra :])

    return pl.pallas_call(
        kernel,
        grid=grid,
        in_specs=list(in_specs) + [pl.BlockSpec(memory_space=pl.ANY)] * extra,
        out_specs=[spec for spec, _ in outs],
        out_shape=[jax.ShapeDtypeStruct(kind.shape, kind.dtype) for _, kind in outs],
        scratch_shapes=scratch,
        input_output_aliases={count + i: into + i for i in range(extra)},
        compiler_params=pltpu.CompilerParams(vmem_limit_bytes=room * 1024 * 1024),
        cost_estimate=pl.CostEstimate(flops=int(us * 1.15e9), bytes_accessed=0, transcendentals=0),
        name=name,
    )(*operands, *old)


def weight_grad(left_t, right, row_count, core, deps, old=(), at=0, us=12):
    height, depth = left_t.shape
    wide = right.shape[1]
    block = min(wide, 768)
    shape = old[0].shape if old else (row_count // 2, height // row_count, wide)
    spec = pl.BlockSpec((*shape[:2], block), lambda i: (0, 0, i + at))
    return call(
        weight_grad_kernel,
        (core, left_t, right),
        [
            pl.BlockSpec(memory_space=pltpu.SMEM),
            const_spec((height, depth)),
            pl.BlockSpec((depth, block), lambda i: (0, i)),
        ],
        [(spec, jax.ShapeDtypeStruct(shape, LOW))] * 2,
        (wide // block,),
        56,
        deps,
        old,
        name="weight_grad",
        us=us,
    )


def add_kernel(*refs):
    *terms, out_ref = refs
    out_ref[...] = sum([ref[...].astype(F32) for ref in terms[1:]], terms[0][...].astype(F32)).astype(LOW)


def add_all(terms):
    shape = terms[0].shape
    spec = pl.BlockSpec(shape, lambda i: (0,) * len(shape), pipeline_mode=pl.Buffered(1))
    outs = [(spec, jax.ShapeDtypeStruct(shape, LOW))]
    return call(add_kernel, terms, [spec] * len(terms), outs, (1,), 24, name="add_all", us=12)[0]


def masks_of(bits):
    return [
        sum(1 << bit for i, bit in enumerate(bits) if other >> i & 1) for other in range(1, 1 << len(bits))
    ]


def in_order(pieces, name, bits):
    here = lax.axis_index(name)
    for i, bit in enumerate(bits):
        high = ((here >> bit) & 1) == 1
        pieces = [jnp.where(high, pieces[place ^ (1 << i)], pieces[place]) for place in range(len(pieces))]
    return jnp.concatenate(pieces, 0)


class Flow:
    def __init__(self, sent, kept, line=False, fused=False, split=False):
        bits = lax.axis_size("row").bit_length() - 1
        self.order = [(0,)] + [tuple(range(i, min(i + 2, bits))) for i in range(1, bits, 2)]
        self.left = list(range(bits - 1, 0, -1))
        count = lax.axis_size("col")
        self.line = [(None, [(i, i ^ (1 << bit)) for i in range(count)]) for bit in range(count.bit_length() - 1)]
        if line:
            half = count // 2
            self.line = [(None, [(i, i + 1), (count - 1 - i, count - 2 - i)]) for i in range(half - 1)]
            self.line += [(None, [(half - 1, half), (half, half - 1)])]
            self.line += [
                ((i, count - 1 - i), [(i + 1, i), (count - 2 - i, count - 1 - i)])
                for i in range(half - 2, -1, -1)
            ]
        if split:
            bits = count.bit_length() - 1
            groups = [tuple(range(i, min(i + 2, bits))) for i in range(0, bits, 2)]
            self.line = [("scatter", group) for group in groups[::-1]] + [("gather", group) for group in groups]
        self.sent, self.kept, self.got, self.fused, self.split = [sent], kept, None, fused, split

    def shard(self, terms, bits, mask, name="row"):
        here = lax.axis_index(name)
        order = [self.left.index(bit) for bit in bits]
        total = None
        for term in terms:
            starts, sizes = [0] * term.ndim, list(term.shape)
            for axis, bit in zip(order, bits):
                starts[axis], sizes[axis] = ((here ^ mask) >> bit) & 1, 1
            piece = lax.dynamic_slice(term, starts, sizes)
            piece = piece.reshape([size for i, size in enumerate(sizes) if i not in order]).astype(F32)
            total = piece if total is None else total + piece
        return total.astype(LOW)

    def step(self):
        if self.order:
            bits = self.order[0]
            masks = masks_of(bits)
            if bits != (0,):
                terms = [self.kept, *self.got]
                self.sent = [self.shard(terms, bits, mask) for mask in masks]
                self.kept = self.shard(terms, bits, 0)
                self.left = [bit for bit in self.left if bit not in bits]
            size = lax.axis_size("row")
            self.got = [
                lax.ppermute(sent, "row", [(i, i ^ mask) for i in range(size)])
                for sent, mask in zip(self.sent, masks)
            ]
        elif self.split:
            kind, bits = self.line[0]
            masks = masks_of(bits)
            size = lax.axis_size("col")
            if kind == "scatter":
                terms = [self.kept, *self.got]
                if not self.left:
                    self.left = list(range(size.bit_length() - 2, -1, -1))
                    rows, wide = self.kept.shape
                    dims = (2,) * len(self.left) + (rows // size, wide)
                    terms = [term.reshape(dims) for term in terms]
                self.sent = [self.shard(terms, bits, mask, "col") for mask in masks]
                self.kept = self.shard(terms, bits, 0, "col")
                self.left = [bit for bit in self.left if bit not in bits]
            else:
                self.sent = [self.kept] * len(masks)
            self.got = [
                lax.ppermute(sent, "col", [(i, i ^ mask) for i in range(size)])
                for sent, mask in zip(self.sent, masks)
            ]
        else:
            self.sent = [self.kept]
            self.got = [lax.ppermute(self.kept, "col", self.line[0][1])]

    def land(self, token=None):
        if token is not None:
            self.kept = lax.optimization_barrier((self.kept, token))[0]
        got = self.got
        if self.order:
            bits = self.order.pop(0)
            if bits == (0,):
                dims = (2,) * len(self.left) + self.kept.shape[1:]
                self.kept, self.got = self.kept.reshape(dims), [item.reshape(dims) for item in self.got]
            if not self.order and self.fused:
                self.kept = add_all([self.kept, *self.got])
            elif not self.order and not self.split:
                self.kept = sum([item.astype(F32) for item in self.got], self.kept.astype(F32)).astype(LOW)
        elif self.split:
            kind, bits = self.line.pop(0)
            if kind == "gather":
                self.kept = in_order([self.kept, *self.got], "col", bits)
            elif self.line[0][0] == "gather":
                self.kept = sum([item.astype(F32) for item in self.got], self.kept.astype(F32)).astype(LOW)
        else:
            ends, _ = self.line.pop(0)
            if ends is None:
                self.kept = self.kept + self.got[0]
            else:
                here = lax.axis_index("col")
                self.kept = jnp.where((here == ends[0]) | (here == ends[1]), self.got[0], self.kept)
        return got

    def turn(self, token=None):
        got = self.land(token)
        if self.done:
            return got
        self.step()
        return got + self.sent

    @property
    def done(self):
        return not self.order and not self.line


def gather_all(piece):
    row_bits = lax.axis_size("row").bit_length() - 1
    col_bits = lax.axis_size("col").bit_length() - 1
    steps = [("col", tuple(range(i, min(i + 2, col_bits)))) for i in range(0, col_bits, 2)]
    steps += [("row", tuple(range(i, min(i + 2, row_bits)))) for i in range(1, row_bits, 2)]
    for name, bits in steps + [("row", (0,))]:
        size = lax.axis_size(name)
        got = [lax.ppermute(piece, name, [(i, i ^ mask) for i in range(size)]) for mask in masks_of(bits)]
        piece = in_order([piece, *got], name, bits)
    return piece


def per_device(
    query_tokens, passage_tokens, query_lengths, passage_lengths, positives,
    w_query, w_key, w_value, w_attn_out, w_inner, w_outer,
    bias_query, bias_value, bias_attn_out, bias_inner, bias_outer,
    gain_one, shift_one, gain_two, shift_two,
):
    q_dev, q_len, width = query_tokens.shape
    p_dev, p_len, _ = passage_tokens.shape
    inner = w_inner.shape[1]
    rows_all = p_len
    assert q_dev * q_len == rows_all and q_dev + p_dev <= SLOTS
    blocks = 1 + p_dev
    total_rows = blocks * rows_all
    row_count = lax.axis_size("row")
    col_count = lax.axis_size("col")
    row_here = lax.axis_index("row")
    core = (row_here & 1).reshape(1)
    me = (row_here * col_count + lax.axis_index("col")).reshape(1)
    params = pltpu.CompilerParams(vmem_limit_bytes=VMEM)
    smem = pl.BlockSpec(memory_space=pltpu.SMEM)

    def by_block(wide):
        return pl.BlockSpec((rows_all, wide), lambda i: (i, 0))

    def by_block_t(high):
        return pl.BlockSpec((high, rows_all), lambda i: (0, i))

    def fixed(shape):
        return pl.BlockSpec(shape, lambda i: (0,) * len(shape))

    queries_spec = pl.BlockSpec((rows_all, width), lambda i: (0, 0))
    passages_spec = pl.BlockSpec((rows_all, width), lambda i: (jnp.maximum(i - 1, 0), 0))

    lse_spec = pl.BlockSpec((1, HEADS // 2, 8, rows_all), lambda i: (i, 0, 0, 0))

    def shape(*dims, kind=LOW):
        return jax.ShapeDtypeStruct(dims, kind)

    queries = query_tokens.reshape(rows_all, width)
    passages = passage_tokens.reshape(p_dev * rows_all, width)
    square = const_spec((width, width))
    anywhere = pl.BlockSpec(memory_space=pl.ANY)
    thin = const_spec((width,))

    q, k, v, ctx_t, lse = call(
        partial(attend_kernel, (q_dev, q_len, rows_all, width)),
        (query_lengths, passage_lengths, queries, passages, w_query, w_key, w_value, bias_query, bias_value),
        [smem, smem, queries_spec, passages_spec, square, square, square, thin, thin],
        [(by_block(width), shape(total_rows, width))] * 3
        + [
            (by_block_t(width), shape(width, total_rows)),
            (lse_spec, shape(blocks, HEADS // 2, 8, rows_all, kind=F32)),
        ],
        (blocks,),
        56,
        name="attend",

    )

    rows_part = rows_all
    parts = blocks

    def by_part(wide):
        return pl.BlockSpec((rows_part, wide), lambda i: (i, 0))

    queries_part = pl.BlockSpec((rows_part, width), lambda i: (0, 0))
    passages_part = pl.BlockSpec((rows_part, width), lambda i: (jnp.maximum(i - 1, 0), 0))
    h1, y1, act, slope, h2, query_out, passage_out, pooled, payload = call(
        partial(dense_kernel, (q_dev, q_len, p_len, width, inner)),
        (
            query_lengths, passage_lengths, positives, queries, passages, ctx_t, w_attn_out, w_inner, w_outer,
            bias_attn_out, bias_inner, bias_outer, gain_one, shift_one, gain_two, shift_two,
        ),
        [smem, smem, smem, queries_part, passages_part, pl.BlockSpec((width, rows_part), lambda i: (0, i))]
        + [anywhere] * 3
        + [thin, const_spec((inner,))]
        + [thin] * 5,
        [
            (by_part(width), shape(total_rows, width)),
            (by_part(width), shape(total_rows, width)),
            (by_part(inner), shape(total_rows, inner)),
            (by_part(inner), shape(total_rows, inner)),
            (by_part(width), shape(total_rows, width)),
            (queries_part, shape(rows_all, width)),
            (passages_part, shape(p_dev * rows_all, width)),
            (fixed((SLOTS, width)), shape(SLOTS, width, kind=F32)),
            (fixed((SLOTS, width + 128)), shape(SLOTS, width + 128)),
        ],
        (parts,),
        56,
        name="dense",
        scratch=[
            pltpu.VMEM((width, width), LOW),
            pltpu.VMEM((width, inner), LOW),
            pltpu.VMEM((inner, width), LOW),
            pltpu.SemaphoreType.DMA((3,)),
        ],

    )

    gathered = gather_all(payload)
    loss, gvec = pl.pallas_call(
        partial(loss_kernel, (q_dev, p_dev, width, col_count)),
        in_specs=[smem] * 3 + [pl.BlockSpec(memory_space=pltpu.VMEM)] * 3,
        out_specs=[pl.BlockSpec(memory_space=pltpu.VMEM)] * 2,
        out_shape=[shape(8, 128, kind=F32), shape(SLOTS, width, kind=F32)],
        compiler_params=params,
        name="loss",
    )(me, query_lengths, passage_lengths, payload, gathered, pooled)

    smalls = shape(8, width, kind=F32)
    cut = width // row_count
    cut_inner = inner // row_count
    half = row_count // 2
    step_cols = 768
    per_step = step_cols // cut_inner
    outer_spec = pl.BlockSpec((per_step // 2, width, cut_inner), lambda i: (i, 0, 0))
    grad_f, stat_two, *outer_parts = call(
        partial(outer_grad_kernel, (q_dev, q_len, p_len)),
        (core, query_lengths, passage_lengths, gvec, h2, gain_two, act),
        [smem, smem, smem, fixed((SLOTS, width)), const_spec((total_rows, width)), thin]
        + [pl.BlockSpec((total_rows, step_cols), lambda i: (0, i))],
        [
            (fixed((total_rows, width)), shape(total_rows, width)),
            (fixed((8, width)), smalls),
            (outer_spec, shape(half, width, cut_inner)),
            (outer_spec, shape(half, width, cut_inner)),
        ],
        (inner // step_cols,),
        56,
        name="outer_grad",
        scratch=[pltpu.VMEM((width, total_rows), LOW)],
    )
    outer = Flow(*outer_parts)
    outer.step()

    def turn(arrays, specs, deps):
        outs = [(by_block_t(width), shape(width, total_rows))]
        return call(turn_low_kernel, arrays, specs, outs, (blocks,), 56, deps, name="turn", us=40)[0]

    y1_t = turn([y1], [by_block(width)], outer.sent)
    deps = outer.turn(y1_t)
    head_dim = width // HEADS
    third = 4 * head_dim
    groups = [(0, 2 * third), (2 * third, third)]
    grad_u, grad_attn, grad_ctx, stat_one, grad_bias_inner = call(
        partial(dense_back_kernel, inner),
        (grad_f, slope, h1, w_outer, w_inner, w_attn_out, gain_one),
        [by_block(width), by_block(inner), by_block(width), anywhere, anywhere, anywhere, thin],
        [
            (by_block(inner), shape(total_rows, inner)),
            (by_block(width), shape(total_rows, width)),
            (by_block(width), shape(total_rows, width)),
            (fixed((8, width)), smalls),
            (fixed((8, inner)), shape(8, inner, kind=F32)),
        ],
        (blocks,),
        60,
        deps,
        name="dense_back",
        scratch=[
            pltpu.VMEM((inner, width), LOW),
            pltpu.VMEM((width, inner), LOW),
            pltpu.VMEM((width, width), LOW),
            pltpu.SemaphoreType.DMA((3,)),
        ],
    )
    deps = outer.turn(stat_one)
    up_flow = Flow(*weight_grad(y1_t, grad_u, row_count, core, deps), line=True, fused=True)
    up_flow.step()
    deps = up_flow.sent + outer.turn(up_flow.sent[0])
    x_t = turn([queries, passages], [queries_spec, passages_spec], deps)
    deps = up_flow.turn(x_t)

    def attend_back(start, wide, deps, extra=(), room=None):
        pairs = wide // (2 * head_dim)
        index = start // wide
        cols = pl.BlockSpec((rows_all, wide), lambda i: (i, index))
        rows = cut + (16 if extra else 0)
        return call(
            partial(attend_back_kernel, (q_dev, q_len, rows_all, head_dim)),
            (core, query_lengths, passage_lengths, q, k, v, ctx_t, lse, grad_ctx, x_t, *extra),
            [smem, smem, smem]
            + [cols] * 3
            + [
                pl.BlockSpec((wide, rows_all), lambda i: (index, i)),
                pl.BlockSpec((1, pairs, 8, rows_all), lambda i: (i, index, 0, 0)),
                cols,
                by_block_t(width),
            ]
            + [const_spec(item.shape) for item in extra],
            [
                (by_block(3 * wide), shape(total_rows, 3 * wide)),
                (fixed((8, wide)), shape(8, wide, kind=F32)),
            ]
            + [(fixed((half, rows, 3 * wide)), shape(half, rows, room or 3 * wide))] * 2,
            (blocks,),
            56,
            deps,
            name="attend_back",
            scratch=[pltpu.VMEM((width, 3 * wide), F32)],
            us=12 if room else 40,
        )

    grad_a, stat_a, *mixed_parts = attend_back(*groups[0], deps, room=6 * third + width)
    at = 6 * third // width
    mixed_parts = weight_grad(ctx_t, grad_attn, row_count, core, [stat_a], mixed_parts, at, us=0)
    mixed_flow = Flow(*mixed_parts, split=True)
    mixed_flow.step()
    token = mixed_flow.sent[0]
    deps = mixed_flow.sent + outer.turn(token) + up_flow.turn(token)
    extra = (stat_two, stat_one, grad_bias_inner, stat_a)
    grad_b, stat_b, *last_parts = attend_back(*groups[1], deps, extra)
    last_flow = Flow(*last_parts)
    last_flow.step()
    deps = last_flow.sent + mixed_flow.turn(stat_b) + up_flow.turn(stat_b)
    query_grad, passage_grad = call(
        partial(input_grad_kernel, groups),
        (grad_a, grad_b, grad_attn, w_query, w_key, w_value),
        [by_block(3 * wide) for _, wide in groups] + [by_block(width), square, square, square],
        [
            (queries_spec, shape(rows_all, width)),
            (passages_spec, shape(p_dev * rows_all, width)),
        ],
        (blocks,),
        56,
        deps,
        name="input_grad",
        us=40,
    )
    last_flow.turn(passage_grad)
    up_flow.turn(last_flow.kept)
    mixed_flow.turn(up_flow.kept)
    last_flow.turn(mixed_flow.kept)
    outs = [(fixed((cut_inner, width)), shape(cut_inner, width, kind=F32))]
    (turned,) = call(
        turn_kernel, (outer.kept,), [const_spec((width, cut_inner))], outs, (1,), 56, [last_flow.kept], name="turn", us=40
    )
    mixed_flow.turn(turned)
    last_flow.turn(mixed_flow.kept)
    up_flow.turn(last_flow.kept)
    mixed_flow.turn(up_flow.kept)
    last_flow.turn(mixed_flow.kept)
    flows = [outer, up_flow, mixed_flow, last_flow]
    while not all(flow.done for flow in flows):
        for flow in flows:
            if not flow.done:
                flow.turn()
    mixed, last = mixed_flow.kept, last_flow.kept
    qkv = [
        jnp.concatenate(
            [mixed[:, i * 2 * third : (i + 1) * 2 * third], last[:cut, i * third : (i + 1) * third]], 1
        ).astype(F32)
        for i in range(3)
    ]
    small = last[cut:].astype(F32)
    return (
        loss[0, 0],
        query_out.reshape(query_tokens.shape),
        passage_out.reshape(passage_tokens.shape),
        query_grad.reshape(query_tokens.shape),
        passage_grad.reshape(passage_tokens.shape),
        *qkv,
        mixed[:, 6 * third :].astype(F32),
        up_flow.kept.astype(F32),
        turned,
        *[small[i, :cut] for i in range(3)],
        small[8, : inner // row_count],
        *[small[i, :cut] for i in range(3, 8)],
    )


def solution(mesh):
    in_specs = (
        P(("row", "col"), None, None),
        P(("row", "col"), None, None),
        P(("row", "col")),
        P(("row", "col")),
        P(("row", "col")),
        P(),
        P(),
        P(),
        P(),
        P(),
        P(),
        P(),
        P(),
        P(),
        P(),
        P(),
        P(),
        P(),
        P(),
        P(),
    )
    out_specs = (
        P(),
        P(("row", "col"), None, None),
        P(("row", "col"), None, None),
        P(("row", "col"), None, None),
        P(("row", "col"), None, None),
        P("row", None),
        P("row", None),
        P("row", None),
        P("row", None),
        P("row", None),
        P("row", None),
        P("row"),
        P("row"),
        P("row"),
        P("row"),
        P("row"),
        P("row"),
        P("row"),
        P("row"),
        P("row"),
    )
    return jax.shard_map(
        per_device, mesh=mesh, in_specs=in_specs, out_specs=out_specs, check_vma=False
    )
```

```python
from functools import partial

import jax
import jax.numpy as jnp
from jax import lax
from jax.experimental import pallas as pl
from jax.experimental.pallas import tpu as pltpu
from jax.sharding import PartitionSpec as P

HEADS = 12
EPS_NORM = 1e-12
EPS_POOL = 1e-06
SCALE_LOSS = 128.0
INV_TEMP = 100.0
TILE = 256
SLOTS = 8
VMEM = 60 * 1024 * 1024
LOW = jnp.bfloat16
F32 = jnp.float32


def mm(left, right):
    return lax.dot_general(left, right, (((1,), (0,)), ((), ())), preferred_element_type=F32)


def mm_nt(left, right):
    return lax.dot_general(left, right, (((1,), (1,)), ((), ())), preferred_element_type=F32)


def norm_parts(hidden):
    center = hidden - jnp.mean(hidden, -1, keepdims=True)
    spread = jnp.mean(center * center, -1, keepdims=True)
    scale = lax.rsqrt(spread + EPS_NORM)
    return center * scale, scale


def gelu_parts(u):
    square = u * u
    q = 1.4250060785476853e-06
    for factor in (-3.669345091379551e-05, -8.782652731110375e-05, 0.03639228618131223, 0.7978697123041883):
        q = q * square + factor
    share = 0.5 + 0.5 * jnp.tanh(u * q)
    bell = jnp.exp(-0.5 * square)
    return u * share, share + (0.3989422804014327 * u) * bell


def vec(ref, cols=slice(None)):
    return ref[cols].reshape(1, -1)


def rows_of(step, size):
    return pl.ds(pl.multiple_of(step * size, size), size)


def part_owner(part, q_dev, q_len, p_len, qlen_ref, plen_ref):
    per = p_len // q_len
    beyond = jnp.maximum(part - q_dev, 0)
    is_query = part < q_dev
    slot = jnp.where(is_query, part, q_dev + beyond // per)
    length = jnp.where(is_query, qlen_ref[jnp.where(is_query, part, 0)], plen_ref[beyond // per])
    first = jnp.where(is_query, 0, beyond % per * q_len)
    return slot, length, first


def live_rows(first, length, size):
    return (first + lax.broadcasted_iota(jnp.int32, (size, 1), 0)) < length


def sure_rows(size):
    return size * 4 // 5 // 16 * 16


def half_only(pair_t, which):
    half = pair_t.shape[0] // 2
    zeros = jnp.zeros((half, pair_t.shape[1]), pair_t.dtype)
    if which == 0:
        return jnp.concatenate([pair_t[:half], zeros], 0)
    return jnp.concatenate([zeros, pair_t[half:]], 0)


def staged(count, *stages):
    for step in range(count + len(stages) - 1):
        for late, stage in enumerate(stages):
            if 0 <= step - late < count:
                stage(step - late)


def fetch(source, target, sems, index):
    return pltpu.make_async_copy(source, target, sems.at[index])


def attend_kernel(
    dims, qlen_ref, plen_ref, xq_ref, xp_ref, wq_ref, wk_ref, wv_ref, bq_ref, bv_ref,
    q_ref, k_ref, v_ref, ctx_t_ref, lse_ref,
):
    q_dev, q_len, rows_all, width = dims
    block = pl.program_id(0)
    head_dim = width // HEADS
    x = jnp.where(block == 0, xq_ref[...], xp_ref[...])
    q = ((mm(x, wq_ref[...]) + vec(bq_ref)) * head_dim**-0.5).astype(LOW)
    k = mm(x, wk_ref[...]).astype(LOW)
    v = (mm(x, wv_ref[...]) + vec(bv_ref)).astype(LOW)
    q_ref[...] = q
    k_ref[...] = k
    v_ref[...] = v
    q_t, v_t = q.T, v.T

    def attend(size, starts, lengths):
        items = [(start, length, head) for head in range(HEADS) for start, length in zip(starts, lengths)]
        scores, weights = {}, {}

        def compare(i):
            start, length, head = items[i]
            cols = slice(head // 2 * 2 * head_dim, (head // 2 + 1) * 2 * head_dim)
            here = slice(start, start + size)
            scores[i] = mm(k[here, cols], half_only(q_t[cols, here], head % 2))

        def weigh(i):
            start, length, head = items[i]
            edge = sure_rows(size)
            early, late = scores[i][:edge], scores.pop(i)[edge:]
            late = jnp.where(live_rows(edge, length, size - edge), late, -1e30)
            top = jnp.maximum(jnp.max(early, 0, keepdims=True), jnp.max(late, 0, keepdims=True))
            weights[i] = top, jnp.concatenate([jnp.exp(early - top).astype(LOW), jnp.exp(late - top).astype(LOW)], 0)

        def combine(i):
            start, length, head = items[i]
            here, rows = slice(start, start + size), slice(head * head_dim, (head + 1) * head_dim)
            top, weight = weights.pop(i)
            values = jnp.concatenate([v_t[rows, here], jnp.ones((16, size), LOW)], 0)
            result = mm(values, weight)
            total = result[head_dim : head_dim + 1]
            lse_ref[0, head // 2, head % 2 : head % 2 + 1, here] = top + jnp.log(total)
            ctx_t_ref[rows, here] = (result[:head_dim] * (1.0 / total)).astype(LOW)

        staged(len(items), compare, weigh, combine)

    @pl.when(block == 0)
    def _():
        attend(q_len, [s * q_len for s in range(q_dev)], [qlen_ref[s] for s in range(q_dev)])

    @pl.when(block > 0)
    def _():
        attend(rows_all, [0], [plen_ref[jnp.maximum(block - 1, 0)]])


def dense_kernel(
    dims, qlen_ref, plen_ref, pos_ref, xq_ref, xp_ref, ctx_t_ref, wo_hbm, wi_hbm, wf_hbm,
    bo_ref, bi_ref, bf_ref, g1_ref, s1_ref, g2_ref, s2_ref,
    h1_ref, y1_ref, act_ref, dg_ref, h2_ref, yq_ref, yp_ref, pool_ref, pay_ref,
    wo_ref, wi_ref, wf_ref, sems,
):
    q_dev, q_len, p_len, width, inner = dims
    block = pl.program_id(0)
    rows_all = xq_ref.shape[0]
    query_blocks = q_dev * q_len // rows_all
    copies = [
        fetch(source, target, sems, index)
        for index, (source, target) in enumerate([(wo_hbm, wo_ref), (wi_hbm, wi_ref), (wf_hbm, wf_ref)])
    ]

    @pl.when(block == 0)
    def _():
        for copy in copies:
            copy.start()
        pool_ref[...] = jnp.zeros_like(pool_ref)
        copies[0].wait()

    x = jnp.where(block < query_blocks, xq_ref[...], xp_ref[...])
    hidden = x.astype(F32) + (mm(ctx_t_ref[...].T, wo_ref[...]) + vec(bo_ref))
    h1_ref[...] = hidden.astype(LOW)
    y1 = norm_parts(hidden)[0] * vec(g1_ref) + vec(s1_ref)
    y1_low = y1.astype(LOW)
    y1_ref[...] = y1_low

    @pl.when(block == 0)
    def _():
        copies[1].wait()
        copies[2].wait()

    raw, made = {}, {}

    def expand(i):
        cols = slice(i * TILE, (i + 1) * TILE)
        raw[i] = mm(y1_low, wi_ref[:, cols]) + vec(bi_ref, cols)

    def activate(i):
        cols = slice(i * TILE, (i + 1) * TILE)
        act, slope = gelu_parts(raw.pop(i))
        made[i] = act.astype(LOW)
        act_ref[:, cols] = made[i]
        dg_ref[:, cols] = slope.astype(LOW)

    staged(inner // TILE, expand, activate)
    left = jnp.concatenate([made[i] for i in range(inner // TILE)], 1)
    total = (y1 + vec(bf_ref)) + mm(left, wf_ref[...])
    h2_ref[...] = total.astype(LOW)
    y2 = norm_parts(total)[0] * vec(g2_ref) + vec(s2_ref)
    for part in range(rows_all // q_len):
        number = block * (rows_all // q_len) + part
        slot, length, first = part_owner(number, q_dev, q_len, p_len, qlen_ref, plen_ref)
        piece = y2[part * q_len : (part + 1) * q_len]
        summed = jnp.sum(jnp.where(live_rows(first, length, q_len), piece, 0.0), 0, keepdims=True)
        in_slot = lax.broadcasted_iota(jnp.int32, (SLOTS, 1), 0) == slot
        pool_ref[...] += jnp.where(in_slot, summed / length.astype(F32), 0.0)

    @pl.when(block < query_blocks)
    def _():
        yq_ref[...] = y2.astype(LOW)

    @pl.when(block >= query_blocks)
    def _():
        yp_ref[...] = y2.astype(LOW)

    @pl.when(block == pl.num_programs(0) - 1)
    def _():
        pooled = pool_ref[...]
        emb = pooled * lax.rsqrt(jnp.sum(pooled * pooled, -1, keepdims=True) + EPS_POOL)
        pay_ref[:, :width] = emb.astype(LOW)
        row = lax.broadcasted_iota(jnp.int32, (SLOTS, 128), 0)
        col = lax.broadcasted_iota(jnp.int32, (SLOTS, 128), 1)
        place = jnp.zeros((SLOTS, 128), jnp.int32)
        for j in range(q_dev):
            high = pos_ref[j] // 128
            low = pos_ref[j] - high * 128
            place = jnp.where(row == j, jnp.where(col == 0, high, jnp.where(col == 1, low, 0)), place)
        pay_ref[:, width:] = place.astype(F32).astype(LOW)


def loss_kernel(
    dims, me_ref, qlen_ref, plen_ref, own_ref, all_ref, pool_ref, loss_ref, gvec_ref
):
    q_dev, p_dev, width, col_count = dims
    count = all_ref.shape[0]
    every = all_ref[:, :width]
    own = own_ref[:, :width]

    def passage_mask(index):
        spot, place = index % SLOTS, index // SLOTS
        per_core = count // SLOTS // 2
        core, rest = place // per_core, place % per_core
        device = (rest // col_count * 2 + core) * col_count + rest % col_count
        return (spot >= q_dev) & (spot < q_dev + p_dev), device * p_dev + spot - q_dev

    scores = mm_nt(own, every) * INV_TEMP
    valid, ident = passage_mask(lax.broadcasted_iota(jnp.int32, (SLOTS, count), 1))
    scores = jnp.where(valid, scores, -1e30)
    top = jnp.max(scores, -1, keepdims=True)
    totals = top + jnp.log(jnp.sum(jnp.exp(scores - top), -1, keepdims=True))
    marks = own_ref[:, width:].astype(F32)
    wanted = marks[:, 0:1] * 128.0 + marks[:, 1:2]
    target = (valid & (ident.astype(F32) == wanted)).astype(F32)
    raw = (INV_TEMP * (SCALE_LOSS * (jnp.exp(scores - totals) - target))).astype(LOW)
    grad_q = mm(raw, every)

    picker_col = lax.broadcasted_iota(jnp.int32, (SLOTS, 128), 1)
    picker = jnp.where(picker_col == 0, 128.0, jnp.where(picker_col == 1, 1.0, 0.0)).astype(LOW)
    own_row = lax.broadcasted_iota(jnp.int32, (SLOTS, TILE), 0)
    own_valid = (own_row >= q_dev) & (own_row < q_dev + p_dev)
    own_ident = (me_ref[0] * p_dev + own_row - q_dev).astype(F32)

    def body(step, carry):
        total_loss, grad_p = carry
        rows = rows_of(step, TILE)
        some = all_ref[rows, :width]
        place = mm_nt(picker, all_ref[rows, width:])[0:1]
        table = mm_nt(every, some) * INV_TEMP
        ok, names = passage_mask(lax.broadcasted_iota(jnp.int32, (count, TILE), 0))
        picked = jnp.sum(jnp.where(ok & (names.astype(F32) == place), table, 0.0), 0, keepdims=True)
        table = jnp.where(ok, table, -1e30)
        high = jnp.max(table, 0, keepdims=True)
        lse = high + jnp.log(jnp.sum(jnp.exp(table - high), 0, keepdims=True))
        is_query = lax.broadcasted_iota(jnp.int32, (1, TILE), 1) % SLOTS < q_dev
        losses = jnp.where(is_query, lse - picked, 0.0)
        mine = mm_nt(own, some) * INV_TEMP
        hit = (own_ident == place).astype(F32)
        grads = INV_TEMP * (SCALE_LOSS * (jnp.exp(mine - lse) - hit))
        grads = jnp.where(own_valid & is_query, grads, 0.0).astype(LOW)
        return total_loss + jnp.sum(losses, 1, keepdims=True), grad_p + mm(grads, some)

    start = (jnp.zeros((1, 1), F32), jnp.zeros((SLOTS, width), F32))
    total_loss, grad_p = lax.fori_loop(0, count // TILE, body, start)
    loss_ref[...] = jnp.broadcast_to(total_loss / float(count // SLOTS * q_dev), loss_ref.shape)

    slot = lax.broadcasted_iota(jnp.int32, (SLOTS, 1), 0)
    grad = jnp.where(slot < q_dev, grad_q, grad_p)
    pooled = pool_ref[...]
    r = lax.rsqrt(jnp.sum(pooled * pooled, -1, keepdims=True) + EPS_POOL)
    inside = jnp.sum(pooled * grad, -1, keepdims=True)
    length = jnp.ones((SLOTS, 1), F32)
    for j in range(q_dev):
        length = jnp.where(slot == j, qlen_ref[j].astype(F32), length)
    for j in range(p_dev):
        length = jnp.where(slot == q_dev + j, plen_ref[j].astype(F32), length)
    gvec_ref[...] = (r * grad - r * r * r * inside * pooled) / length


def store_shards(core_ref, result, send_ref, keep_ref, by_row=True, tails=None):
    count = send_ref.shape[0] * 2
    size = result.shape[0 if by_row else 1] // count

    def store(even, odd):
        for shard in range(count):
            spot = slice(shard * size, (shard + 1) * size)
            piece = (result[spot, :] if by_row else result[:, spot]).astype(LOW)
            target = odd if shard % 2 else even
            if tails is None:
                target[shard // 2] = piece
            else:
                target[shard // 2, :size] = piece
                target[shard // 2, size:] = tails[shard]

    @pl.when(core_ref[0] == 0)
    def _():
        store(keep_ref, send_ref)

    @pl.when(core_ref[0] == 1)
    def _():
        store(send_ref, keep_ref)


def outer_grad_kernel(
    dims, core_ref, qlen_ref, plen_ref, gvec_ref, h2_ref, g2_ref, act_ref,
    gf_ref, stat_ref, send_ref, keep_ref, gf_t_ref,
):
    q_dev, q_len, p_len = dims

    @pl.when(pl.program_id(0) == 0)
    def _():
        stat_ref[...] = jnp.zeros_like(stat_ref)

        def body(part, carry):
            rows = rows_of(part, q_len)
            slot, length, first = part_owner(part, q_dev, q_len, p_len, qlen_ref, plen_ref)
            in_slot = lax.broadcasted_iota(jnp.int32, (SLOTS, 1), 0) == slot
            grad_y = jnp.sum(jnp.where(in_slot, gvec_ref[...], 0.0), 0, keepdims=True)
            live = live_rows(first, length, q_len)
            n2, r2 = norm_parts(h2_ref[rows, :].astype(F32))
            g = grad_y * vec(g2_ref)
            grad = r2 * (g - jnp.mean(g, -1, keepdims=True) - n2 * jnp.mean(g * n2, -1, keepdims=True))
            grad = jnp.where(live, grad, 0.0)
            low = grad.astype(LOW)
            gf_ref[rows, :] = low
            gf_t_ref[:, rows] = low.T
            stat_ref[0:1, :] += grad_y * jnp.sum(jnp.where(live, n2, 0.0), 0, keepdims=True)
            stat_ref[1:2, :] += grad_y * jnp.sum(live.astype(F32), 0, keepdims=True)
            stat_ref[2:3, :] += jnp.sum(low.astype(F32), 0, keepdims=True)
            return carry

        lax.fori_loop(0, h2_ref.shape[0] // q_len, body, 0)

    store_shards(core_ref, mm(gf_t_ref[...], act_ref[...]), send_ref, keep_ref, by_row=False)


def dense_back_kernel(
    dims, gf_ref, dg_ref, h1_ref, wf_hbm, wi_hbm, wo_hbm, g1_ref,
    gu_ref, ga_ref, gc_ref, stat_ref, bi_ref,
    wf_ref, wi_ref, wo_ref, sems,
):
    inner = dims
    block = pl.program_id(0)
    copies = [
        fetch(source, target, sems, index)
        for index, (source, target) in enumerate([(wf_hbm, wf_ref), (wi_hbm, wi_ref), (wo_hbm, wo_ref)])
    ]

    @pl.when(block == 0)
    def _():
        for copy in copies:
            copy.start()
        stat_ref[...] = jnp.zeros_like(stat_ref)
        bi_ref[...] = jnp.zeros_like(bi_ref)
        copies[0].wait()

    gf = gf_ref[...]
    raw, made, biases = {}, {}, []

    def spread(i):
        raw[i] = mm_nt(gf, wf_ref[i * TILE : (i + 1) * TILE, :])

    def slope(i):
        cols = slice(i * TILE, (i + 1) * TILE)
        made[i] = (raw.pop(i) * dg_ref[:, cols].astype(F32)).astype(LOW)
        gu_ref[:, cols] = made[i]
        biases.append(jnp.sum(made[i].astype(F32), 0, keepdims=True))

    staged(inner // TILE, spread, slope)
    bi_ref[0:1, :] += jnp.concatenate(biases, 1)
    left = jnp.concatenate([made[i] for i in range(inner // TILE)], 1)

    @pl.when(block == 0)
    def _():
        for copy in copies[1:]:
            copy.wait()

    total = gf.astype(F32) + mm_nt(left, wi_ref[...])
    n1, r1 = norm_parts(h1_ref[...].astype(F32))
    stat_ref[0:1, :] += jnp.sum(total * n1, 0, keepdims=True)
    stat_ref[1:2, :] += jnp.sum(total, 0, keepdims=True)
    g = total * vec(g1_ref)
    grad = r1 * (g - jnp.mean(g, -1, keepdims=True) - n1 * jnp.mean(g * n1, -1, keepdims=True))
    low = grad.astype(LOW)
    ga_ref[...] = low
    stat_ref[2:3, :] += jnp.sum(low.astype(F32), 0, keepdims=True)
    gc_ref[...] = mm_nt(low, wo_ref[...]).astype(LOW)


def attend_back_kernel(
    dims, core_ref, qlen_ref, plen_ref, q_ref, k_ref, v_ref, ctx_t_ref, lse_ref, gc_ref, x_t_ref, *refs
):
    *extra, out_ref, stat_ref, send_ref, keep_ref, sum_ref = refs
    q_dev, q_len, rows_all, head_dim = dims
    block = pl.program_id(0)
    pair_dim = 2 * head_dim
    width = q_ref.shape[1]
    pairs = width // pair_dim

    @pl.when(block == 0)
    def _():
        stat_ref[...] = jnp.zeros_like(stat_ref)

    def attend(size, starts, lengths, fresh):
        lane = lax.broadcasted_iota(jnp.int32, (size, pair_dim), 1)
        items = [(s, p, which) for p in range(pairs) for s in range(len(starts)) for which in range(2)]
        held, raw, made, grads = {}, {}, {}, {}

        def pair_of(s, p):
            if (s, p) not in held:
                here, cols = slice(starts[s], starts[s] + size), slice(p * pair_dim, (p + 1) * pair_dim)
                q, k, v, gc = q_ref[here, cols], k_ref[here, cols], v_ref[here, cols], gc_ref[here, cols]
                held[s, p] = here, cols, q, k, v, gc, q.T, k.T, gc.T
            return held[s, p]

        def compare(i):
            s, p, which = items[i]
            here, cols, q, k, v, gc, q_t, k_t, gc_t = pair_of(s, p)
            raw[i] = mm(k, half_only(q_t, which)), mm(v, half_only(gc_t, which))

        def weigh(i):
            s, p, which = items[i]
            here, cols, q, k, v, gc, q_t, k_t, gc_t = pair_of(s, p)
            head = slice((p * 2 + which) * head_dim, (p * 2 + which + 1) * head_dim)
            scores, grad_p = raw.pop(i)
            lse = lse_ref[0, p, which : which + 1, here]
            edge = sure_rows(size)
            late = jnp.where(live_rows(edge, lengths[s], size - edge), scores[edge:], -1e30)
            probs = jnp.concatenate([jnp.exp(scores[:edge] - lse), jnp.exp(late - lse)], 0)
            half = slice(which * head_dim, (which + 1) * head_dim)
            delta = jnp.sum(gc_t[half].astype(F32) * ctx_t_ref[head, here].astype(F32), 0, keepdims=True)
            made[i] = probs.astype(LOW), (probs * (grad_p - delta)).astype(LOW)

        def combine(i):
            s, p, which = items[i]
            here, cols, q, k, v, gc, q_t, k_t, gc_t = pair_of(s, p)
            mine = (lane >= head_dim) if which else (lane < head_dim)
            zero = jnp.zeros_like(q)
            probs, grad_s = made.pop(i)
            add_v = mm(probs, jnp.where(mine, gc, zero))
            add_k = mm(grad_s, jnp.where(mine, q, zero))
            add_q = mm(k_t[which * head_dim : (which + 1) * head_dim], grad_s)
            if which == 0:
                made[s, p] = add_v, add_k, add_q
                return
            old_v, old_k, old_q = made.pop((s, p))
            grad_q = (jnp.concatenate([old_q, add_q], 0).T * head_dim**-0.5).astype(LOW)
            grad_k = (old_k + add_k).astype(LOW)
            grad_v = (old_v + add_v).astype(LOW)
            for number, grad in enumerate((grad_q, grad_k, grad_v)):
                out_ref[here, number * width + cols.start : number * width + cols.stop] = grad
                grads[number, s, p] = grad
            stat_ref[0:1, cols] += jnp.sum(grad_q.astype(F32), 0, keepdims=True)
            stat_ref[1:2, cols] += jnp.sum(grad_v.astype(F32), 0, keepdims=True)

            if p % 2 and s == len(starts) - 1:
                project(p - 1)

        def project(p):
            for number in range(3):
                rows = [
                    jnp.concatenate([grads.pop((number, s, p)), grads.pop((number, s, p + 1))], 1)
                    for s in range(len(starts))
                ]
                product = mm(x_t_ref[...], jnp.concatenate(rows, 0))
                cols = slice(number * width + p * pair_dim, number * width + (p + 2) * pair_dim)
                if fresh:
                    sum_ref[:, cols] = product
                else:
                    sum_ref[:, cols] += product

        staged(len(items), compare, weigh, combine)

    @pl.when(block == 0)
    def _():
        attend(q_len, [s * q_len for s in range(q_dev)], [qlen_ref[s] for s in range(q_dev)], True)

    @pl.when(block > 0)
    def _():
        attend(rows_all, [0], [plen_ref[jnp.maximum(block - 1, 0)]], False)

    @pl.when(block == pl.num_programs(0) - 1)
    def _():
        tails = None
        if extra:
            tails = small_rows([*extra, stat_ref], send_ref.shape[0] * 2, send_ref.shape[2])
        store_shards(core_ref, sum_ref[...], send_ref, keep_ref, tails=tails)


def input_grad_kernel(groups, *refs):
    grads, (base_ref, wq_ref, wk_ref, wv_ref, gq_ref, gp_ref) = refs[: len(groups)], refs[len(groups) :]
    total = base_ref[...].astype(F32)
    for grad_ref, (start, wide) in zip(grads, groups):
        for number, w_ref in enumerate((wq_ref, wk_ref, wv_ref)):
            total = total + mm_nt(grad_ref[:, number * wide : (number + 1) * wide], w_ref[:, start : start + wide])
    low = total.astype(LOW)

    @pl.when(pl.program_id(0) == 0)
    def _():
        gq_ref[...] = low

    @pl.when(pl.program_id(0) > 0)
    def _():
        gp_ref[...] = low


def weight_grad_kernel(core_ref, left_ref, right_ref, send_ref, keep_ref):
    store_shards(core_ref, mm(left_ref[...], right_ref[...]), send_ref, keep_ref)


def small_rows(refs, count, wide):
    two, one, inner, *attn = [ref[...] for ref in refs]
    eight = jnp.concatenate(
        [jnp.concatenate([item[0:2] for item in attn], 1), one[2:3], two[2:3], one[0:2], two[0:2]], 0
    )
    inner = inner[0:1]
    short, long = eight.shape[1] // count, inner.shape[1] // count
    rows = []
    for shard in range(count):
        top = eight[:, shard * short : (shard + 1) * short]
        low = inner[:, shard * long : (shard + 1) * long]
        top = jnp.concatenate([top, jnp.zeros((8, wide - short), F32)], 1)
        low = jnp.concatenate([low, jnp.zeros((1, wide - long), F32)], 1)
        rows.append(jnp.concatenate([top, low, jnp.zeros((7, wide), F32)], 0).astype(LOW))
    return rows


def turn_kernel(part_ref, out_ref):
    out_ref[...] = part_ref[...].astype(F32).T


def turn_low_kernel(*refs):
    *inputs, out_ref = refs
    if len(inputs) == 1:
        out_ref[...] = inputs[0][...].T
        return

    @pl.when(pl.program_id(0) == 0)
    def _():
        out_ref[...] = inputs[0][...].T

    @pl.when(pl.program_id(0) > 0)
    def _():
        out_ref[...] = inputs[1][...].T


def const_spec(shape):
    return pl.BlockSpec(shape, lambda i: (0,) * len(shape), pipeline_mode=pl.Buffered(1))


def call(body, operands, in_specs, outs, grid, room, deps=(), old=(), into=0, name=None, scratch=(), us=12):
    count, extra = len(operands), len(old)
    if deps:
        tied = min(range(count), key=lambda i: operands[i].size)
        operands = list(operands)
        operands[tied] = lax.optimization_barrier((operands[tied], *deps))[0]

    def kernel(*refs):
        body(*refs[:count], *refs[count + extra :])

    return pl.pallas_call(
        kernel,
        grid=grid,
        in_specs=list(in_specs) + [pl.BlockSpec(memory_space=pl.ANY)] * extra,
        out_specs=[spec for spec, _ in outs],
        out_shape=[jax.ShapeDtypeStruct(kind.shape, kind.dtype) for _, kind in outs],
        scratch_shapes=scratch,
        input_output_aliases={count + i: into + i for i in range(extra)},
        compiler_params=pltpu.CompilerParams(vmem_limit_bytes=room * 1024 * 1024),
        cost_estimate=pl.CostEstimate(flops=int(us * 1.15e9), bytes_accessed=0, transcendentals=0),
        name=name,
    )(*operands, *old)


def weight_grad(left_t, right, row_count, core, deps, old=(), at=0, us=12):
    height, depth = left_t.shape
    wide = right.shape[1]
    block = min(wide, 768)
    shape = old[0].shape if old else (row_count // 2, height // row_count, wide)
    spec = pl.BlockSpec((*shape[:2], block), lambda i: (0, 0, i + at))
    return call(
        weight_grad_kernel,
        (core, left_t, right),
        [
            pl.BlockSpec(memory_space=pltpu.SMEM),
            const_spec((height, depth)),
            pl.BlockSpec((depth, block), lambda i: (0, i)),
        ],
        [(spec, jax.ShapeDtypeStruct(shape, LOW))] * 2,
        (wide // block,),
        56,
        deps,
        old,
        name="weight_grad",
        us=us,
    )


def add_kernel(*refs):
    *terms, out_ref = refs
    out_ref[...] = sum([ref[...].astype(F32) for ref in terms[1:]], terms[0][...].astype(F32)).astype(LOW)


def add_all(terms):
    shape = terms[0].shape
    spec = pl.BlockSpec(shape, lambda i: (0,) * len(shape), pipeline_mode=pl.Buffered(1))
    outs = [(spec, jax.ShapeDtypeStruct(shape, LOW))]
    return call(add_kernel, terms, [spec] * len(terms), outs, (1,), 24, name="add_all", us=12)[0]


def masks_of(bits):
    return [
        sum(1 << bit for i, bit in enumerate(bits) if other >> i & 1) for other in range(1, 1 << len(bits))
    ]


def in_order(pieces, name, bits):
    here = lax.axis_index(name)
    for i, bit in enumerate(bits):
        high = ((here >> bit) & 1) == 1
        pieces = [jnp.where(high, pieces[place ^ (1 << i)], pieces[place]) for place in range(len(pieces))]
    return jnp.concatenate(pieces, 0)


class Flow:
    def __init__(self, sent, kept, line=False, fused=False, split=False, wide=2):
        bits = lax.axis_size("row").bit_length() - 1
        self.order = [(0,)] + [tuple(range(i, min(i + wide, bits))) for i in range(1, bits, wide)]
        self.left = list(range(bits - 1, 0, -1))
        count = lax.axis_size("col")
        self.line = [(None, [(i, i ^ (1 << bit)) for i in range(count)]) for bit in range(count.bit_length() - 1)]
        if line:
            half = count // 2
            self.line = [(None, [(i, i + 1), (count - 1 - i, count - 2 - i)]) for i in range(half - 1)]
            self.line += [(None, [(half - 1, half), (half, half - 1)])]
            self.line += [
                ((i, count - 1 - i), [(i + 1, i), (count - 2 - i, count - 1 - i)])
                for i in range(half - 2, -1, -1)
            ]
        if split:
            bits = count.bit_length() - 1
            groups = [tuple(range(i, min(i + 2, bits))) for i in range(0, bits, 2)]
            self.line = [("scatter", group) for group in groups[::-1]] + [("gather", group) for group in groups]
        self.sent, self.kept, self.got, self.fused, self.split = [sent], kept, None, fused, split

    def shard(self, terms, bits, mask, name="row"):
        here = lax.axis_index(name)
        order = [self.left.index(bit) for bit in bits]
        total = None
        for term in terms:
            starts, sizes = [0] * term.ndim, list(term.shape)
            for axis, bit in zip(order, bits):
                starts[axis], sizes[axis] = ((here ^ mask) >> bit) & 1, 1
            piece = lax.dynamic_slice(term, starts, sizes)
            piece = piece.reshape([size for i, size in enumerate(sizes) if i not in order]).astype(F32)
            total = piece if total is None else total + piece
        return total.astype(LOW)

    def step(self):
        if self.order:
            bits = self.order[0]
            masks = masks_of(bits)
            if bits != (0,):
                terms = [self.kept, *self.got]
                self.sent = [self.shard(terms, bits, mask) for mask in masks]
                self.kept = self.shard(terms, bits, 0)
                self.left = [bit for bit in self.left if bit not in bits]
            size = lax.axis_size("row")
            self.got = [
                lax.ppermute(sent, "row", [(i, i ^ mask) for i in range(size)])
                for sent, mask in zip(self.sent, masks)
            ]
        elif self.split:
            kind, bits = self.line[0]
            masks = masks_of(bits)
            size = lax.axis_size("col")
            if kind == "scatter":
                terms = [self.kept, *self.got]
                if not self.left:
                    self.left = list(range(size.bit_length() - 2, -1, -1))
                    rows, wide = self.kept.shape
                    dims = (2,) * len(self.left) + (rows // size, wide)
                    terms = [term.reshape(dims) for term in terms]
                self.sent = [self.shard(terms, bits, mask, "col") for mask in masks]
                self.kept = self.shard(terms, bits, 0, "col")
                self.left = [bit for bit in self.left if bit not in bits]
            else:
                self.sent = [self.kept] * len(masks)
            self.got = [
                lax.ppermute(sent, "col", [(i, i ^ mask) for i in range(size)])
                for sent, mask in zip(self.sent, masks)
            ]
        else:
            self.sent = [self.kept]
            self.got = [lax.ppermute(self.kept, "col", self.line[0][1])]

    def land(self, token=None):
        if token is not None:
            self.kept = lax.optimization_barrier((self.kept, token))[0]
        got = self.got
        if self.order:
            bits = self.order.pop(0)
            if bits == (0,):
                dims = (2,) * len(self.left) + self.kept.shape[1:]
                self.kept, self.got = self.kept.reshape(dims), [item.reshape(dims) for item in self.got]
            if not self.order and self.fused:
                self.kept = add_all([self.kept, *self.got])
            elif not self.order and not self.split:
                self.kept = sum([item.astype(F32) for item in self.got], self.kept.astype(F32)).astype(LOW)
        elif self.split:
            kind, bits = self.line.pop(0)
            if kind == "gather":
                self.kept = in_order([self.kept, *self.got], "col", bits)
            elif self.line[0][0] == "gather":
                self.kept = sum([item.astype(F32) for item in self.got], self.kept.astype(F32)).astype(LOW)
        else:
            ends, _ = self.line.pop(0)
            if ends is None:
                self.kept = self.kept + self.got[0]
            else:
                here = lax.axis_index("col")
                self.kept = jnp.where((here == ends[0]) | (here == ends[1]), self.got[0], self.kept)
        return got

    def turn(self, token=None):
        got = self.land(token)
        if self.done:
            return got
        self.step()
        return got + self.sent

    @property
    def done(self):
        return not self.order and not self.line


def gather_all(piece):
    row_bits = lax.axis_size("row").bit_length() - 1
    col_bits = lax.axis_size("col").bit_length() - 1
    steps = [("col", tuple(range(i, min(i + 2, col_bits)))) for i in range(0, col_bits, 2)]
    steps += [("row", tuple(range(i, min(i + 2, row_bits)))) for i in range(1, row_bits, 2)]
    for name, bits in steps + [("row", (0,))]:
        size = lax.axis_size(name)
        got = [lax.ppermute(piece, name, [(i, i ^ mask) for i in range(size)]) for mask in masks_of(bits)]
        piece = in_order([piece, *got], name, bits)
    return piece


def per_device(
    query_tokens, passage_tokens, query_lengths, passage_lengths, positives,
    w_query, w_key, w_value, w_attn_out, w_inner, w_outer,
    bias_query, bias_value, bias_attn_out, bias_inner, bias_outer,
    gain_one, shift_one, gain_two, shift_two,
):
    q_dev, q_len, width = query_tokens.shape
    p_dev, p_len, _ = passage_tokens.shape
    inner = w_inner.shape[1]
    rows_all = p_len
    assert q_dev * q_len == rows_all and q_dev + p_dev <= SLOTS
    blocks = 1 + p_dev
    total_rows = blocks * rows_all
    row_count = lax.axis_size("row")
    col_count = lax.axis_size("col")
    row_here = lax.axis_index("row")
    core = (row_here & 1).reshape(1)
    me = (row_here * col_count + lax.axis_index("col")).reshape(1)
    params = pltpu.CompilerParams(vmem_limit_bytes=VMEM)
    smem = pl.BlockSpec(memory_space=pltpu.SMEM)

    def by_block(wide):
        return pl.BlockSpec((rows_all, wide), lambda i: (i, 0))

    def by_block_t(high):
        return pl.BlockSpec((high, rows_all), lambda i: (0, i))

    def fixed(shape):
        return pl.BlockSpec(shape, lambda i: (0,) * len(shape))

    queries_spec = pl.BlockSpec((rows_all, width), lambda i: (0, 0))
    passages_spec = pl.BlockSpec((rows_all, width), lambda i: (jnp.maximum(i - 1, 0), 0))

    lse_spec = pl.BlockSpec((1, HEADS // 2, 8, rows_all), lambda i: (i, 0, 0, 0))

    def shape(*dims, kind=LOW):
        return jax.ShapeDtypeStruct(dims, kind)

    queries = query_tokens.reshape(rows_all, width)
    passages = passage_tokens.reshape(p_dev * rows_all, width)
    square = const_spec((width, width))
    anywhere = pl.BlockSpec(memory_space=pl.ANY)
    thin = const_spec((width,))

    q, k, v, ctx_t, lse = call(
        partial(attend_kernel, (q_dev, q_len, rows_all, width)),
        (query_lengths, passage_lengths, queries, passages, w_query, w_key, w_value, bias_query, bias_value),
        [smem, smem, queries_spec, passages_spec, square, square, square, thin, thin],
        [(by_block(width), shape(total_rows, width))] * 3
        + [
            (by_block_t(width), shape(width, total_rows)),
            (lse_spec, shape(blocks, HEADS // 2, 8, rows_all, kind=F32)),
        ],
        (blocks,),
        56,
        name="attend",

    )

    rows_part = rows_all
    parts = blocks

    def by_part(wide):
        return pl.BlockSpec((rows_part, wide), lambda i: (i, 0))

    queries_part = pl.BlockSpec((rows_part, width), lambda i: (0, 0))
    passages_part = pl.BlockSpec((rows_part, width), lambda i: (jnp.maximum(i - 1, 0), 0))
    h1, y1, act, slope, h2, query_out, passage_out, pooled, payload = call(
        partial(dense_kernel, (q_dev, q_len, p_len, width, inner)),
        (
            query_lengths, passage_lengths, positives, queries, passages, ctx_t, w_attn_out, w_inner, w_outer,
            bias_attn_out, bias_inner, bias_outer, gain_one, shift_one, gain_two, shift_two,
        ),
        [smem, smem, smem, queries_part, passages_part, pl.BlockSpec((width, rows_part), lambda i: (0, i))]
        + [anywhere] * 3
        + [thin, const_spec((inner,))]
        + [thin] * 5,
        [
            (by_part(width), shape(total_rows, width)),
            (by_part(width), shape(total_rows, width)),
            (by_part(inner), shape(total_rows, inner)),
            (by_part(inner), shape(total_rows, inner)),
            (by_part(width), shape(total_rows, width)),
            (queries_part, shape(rows_all, width)),
            (passages_part, shape(p_dev * rows_all, width)),
            (fixed((SLOTS, width)), shape(SLOTS, width, kind=F32)),
            (fixed((SLOTS, width + 128)), shape(SLOTS, width + 128)),
        ],
        (parts,),
        56,
        name="dense",
        scratch=[
            pltpu.VMEM((width, width), LOW),
            pltpu.VMEM((width, inner), LOW),
            pltpu.VMEM((inner, width), LOW),
            pltpu.SemaphoreType.DMA((3,)),
        ],

    )

    gathered = gather_all(payload)
    loss, gvec = pl.pallas_call(
        partial(loss_kernel, (q_dev, p_dev, width, col_count)),
        in_specs=[smem] * 3 + [pl.BlockSpec(memory_space=pltpu.VMEM)] * 3,
        out_specs=[pl.BlockSpec(memory_space=pltpu.VMEM)] * 2,
        out_shape=[shape(8, 128, kind=F32), shape(SLOTS, width, kind=F32)],
        compiler_params=params,
        name="loss",
    )(me, query_lengths, passage_lengths, payload, gathered, pooled)

    smalls = shape(8, width, kind=F32)
    cut = width // row_count
    cut_inner = inner // row_count
    half = row_count // 2
    step_cols = 768
    per_step = step_cols // cut_inner
    outer_spec = pl.BlockSpec((per_step // 2, width, cut_inner), lambda i: (i, 0, 0))
    grad_f, stat_two, *outer_parts = call(
        partial(outer_grad_kernel, (q_dev, q_len, p_len)),
        (core, query_lengths, passage_lengths, gvec, h2, gain_two, act),
        [smem, smem, smem, fixed((SLOTS, width)), const_spec((total_rows, width)), thin]
        + [pl.BlockSpec((total_rows, step_cols), lambda i: (0, i))],
        [
            (fixed((total_rows, width)), shape(total_rows, width)),
            (fixed((8, width)), smalls),
            (outer_spec, shape(half, width, cut_inner)),
            (outer_spec, shape(half, width, cut_inner)),
        ],
        (inner // step_cols,),
        56,
        name="outer_grad",
        scratch=[pltpu.VMEM((width, total_rows), LOW)],
    )
    outer = Flow(*outer_parts)
    outer.step()

    def turn(arrays, specs, deps):
        outs = [(by_block_t(width), shape(width, total_rows))]
        return call(turn_low_kernel, arrays, specs, outs, (blocks,), 56, deps, name="turn", us=40)[0]

    y1_t = turn([y1], [by_block(width)], outer.sent)
    deps = outer.turn(y1_t)
    head_dim = width // HEADS
    third = 4 * head_dim
    groups = [(0, 2 * third), (2 * third, third)]
    grad_u, grad_attn, grad_ctx, stat_one, grad_bias_inner = call(
        partial(dense_back_kernel, inner),
        (grad_f, slope, h1, w_outer, w_inner, w_attn_out, gain_one),
        [by_block(width), by_block(inner), by_block(width), anywhere, anywhere, anywhere, thin],
        [
            (by_block(inner), shape(total_rows, inner)),
            (by_block(width), shape(total_rows, width)),
            (by_block(width), shape(total_rows, width)),
            (fixed((8, width)), smalls),
            (fixed((8, inner)), shape(8, inner, kind=F32)),
        ],
        (blocks,),
        60,
        deps,
        name="dense_back",
        scratch=[
            pltpu.VMEM((inner, width), LOW),
            pltpu.VMEM((width, inner), LOW),
            pltpu.VMEM((width, width), LOW),
            pltpu.SemaphoreType.DMA((3,)),
        ],
    )
    deps = outer.turn(stat_one)
    up_flow = Flow(*weight_grad(y1_t, grad_u, row_count, core, deps), fused=True)
    up_flow.step()
    deps = up_flow.sent + outer.turn(up_flow.sent[0])
    x_t = turn([queries, passages], [queries_spec, passages_spec], deps)
    deps = up_flow.turn(x_t)

    def attend_back(start, wide, deps, extra=(), room=None):
        pairs = wide // (2 * head_dim)
        index = start // wide
        cols = pl.BlockSpec((rows_all, wide), lambda i: (i, index))
        rows = cut + (16 if extra else 0)
        return call(
            partial(attend_back_kernel, (q_dev, q_len, rows_all, head_dim)),
            (core, query_lengths, passage_lengths, q, k, v, ctx_t, lse, grad_ctx, x_t, *extra),
            [smem, smem, smem]
            + [cols] * 3
            + [
                pl.BlockSpec((wide, rows_all), lambda i: (index, i)),
                pl.BlockSpec((1, pairs, 8, rows_all), lambda i: (i, index, 0, 0)),
                cols,
                by_block_t(width),
            ]
            + [const_spec(item.shape) for item in extra],
            [
                (by_block(3 * wide), shape(total_rows, 3 * wide)),
                (fixed((8, wide)), shape(8, wide, kind=F32)),
            ]
            + [(fixed((half, rows, 3 * wide)), shape(half, rows, room or 3 * wide))] * 2,
            (blocks,),
            56,
            deps,
            name="attend_back",
            scratch=[pltpu.VMEM((width, 3 * wide), F32)],
            us=12 if room else 40,
        )

    grad_a, stat_a, *mixed_parts = attend_back(*groups[0], deps, room=6 * third + width)
    at = 6 * third // width
    mixed_parts = weight_grad(ctx_t, grad_attn, row_count, core, [stat_a], mixed_parts, at, us=0)
    mixed_flow = Flow(*mixed_parts, split=True)
    mixed_flow.step()
    token = mixed_flow.sent[0]
    deps = mixed_flow.sent + outer.turn(token) + up_flow.turn(token)
    extra = (stat_two, stat_one, grad_bias_inner, stat_a)
    grad_b, stat_b, *last_parts = attend_back(*groups[1], deps, extra)
    last_flow = Flow(*last_parts, wide=1)
    last_flow.step()
    deps = last_flow.sent + mixed_flow.turn(stat_b) + up_flow.turn(stat_b)
    query_grad, passage_grad = call(
        partial(input_grad_kernel, groups),
        (grad_a, grad_b, grad_attn, w_query, w_key, w_value),
        [by_block(3 * wide) for _, wide in groups] + [by_block(width), square, square, square],
        [
            (queries_spec, shape(rows_all, width)),
            (passages_spec, shape(p_dev * rows_all, width)),
        ],
        (blocks,),
        56,
        deps,
        name="input_grad",
        us=40,
    )
    mixed_flow.turn(passage_grad)
    last_flow.turn(mixed_flow.kept)
    outs = [(fixed((cut_inner, width)), shape(cut_inner, width, kind=F32))]
    (turned,) = call(
        turn_kernel, (outer.kept,), [const_spec((width, cut_inner))], outs, (1,), 56, [last_flow.kept], name="turn", us=40
    )
    up_flow.turn(turned)
    last_flow.turn(up_flow.kept)
    mixed_flow.turn(last_flow.kept)
    last_flow.turn(mixed_flow.kept)
    last_flow.turn()
    mixed_flow.turn(last_flow.kept)
    flows = [outer, up_flow, mixed_flow, last_flow]
    while not all(flow.done for flow in flows):
        for flow in flows:
            if not flow.done:
                flow.turn()
    mixed, last = mixed_flow.kept, last_flow.kept
    qkv = [
        jnp.concatenate(
            [mixed[:, i * 2 * third : (i + 1) * 2 * third], last[:cut, i * third : (i + 1) * third]], 1
        ).astype(F32)
        for i in range(3)
    ]
    small = last[cut:].astype(F32)
    return (
        loss[0, 0],
        query_out.reshape(query_tokens.shape),
        passage_out.reshape(passage_tokens.shape),
        query_grad.reshape(query_tokens.shape),
        passage_grad.reshape(passage_tokens.shape),
        *qkv,
        mixed[:, 6 * third :].astype(F32),
        up_flow.kept.astype(F32),
        turned,
        *[small[i, :cut] for i in range(3)],
        small[8, : inner // row_count],
        *[small[i, :cut] for i in range(3, 8)],
    )


def solution(mesh):
    in_specs = (
        P(("row", "col"), None, None),
        P(("row", "col"), None, None),
        P(("row", "col")),
        P(("row", "col")),
        P(("row", "col")),
        P(),
        P(),
        P(),
        P(),
        P(),
        P(),
        P(),
        P(),
        P(),
        P(),
        P(),
        P(),
        P(),
        P(),
        P(),
    )
    out_specs = (
        P(),
        P(("row", "col"), None, None),
        P(("row", "col"), None, None),
        P(("row", "col"), None, None),
        P(("row", "col"), None, None),
        P("row", None),
        P("row", None),
        P("row", None),
        P("row", None),
        P("row", None),
        P("row", None),
        P("row"),
        P("row"),
        P("row"),
        P("row"),
        P("row"),
        P("row"),
        P("row"),
        P("row"),
        P("row"),
    )
    return jax.shard_map(
        per_device, mesh=mesh, in_specs=in_specs, out_specs=out_specs, check_vma=False
    )
```

```python
from functools import partial

import jax
import jax.numpy as jnp
from jax import lax
from jax.experimental import pallas as pl
from jax.experimental.pallas import tpu as pltpu
from jax.sharding import PartitionSpec as P

HEADS = 12
EPS_NORM = 1e-12
EPS_POOL = 1e-06
SCALE_LOSS = 128.0
INV_TEMP = 100.0
TILE = 256
SLOTS = 8
VMEM = 60 * 1024 * 1024
LOW = jnp.bfloat16
F32 = jnp.float32


def mm(left, right):
    return lax.dot_general(left, right, (((1,), (0,)), ((), ())), preferred_element_type=F32)


def mm_nt(left, right):
    return lax.dot_general(left, right, (((1,), (1,)), ((), ())), preferred_element_type=F32)


def norm_parts(hidden):
    center = hidden - jnp.mean(hidden, -1, keepdims=True)
    spread = jnp.mean(center * center, -1, keepdims=True)
    scale = lax.rsqrt(spread + EPS_NORM)
    return center * scale, scale


def gelu_parts(u):
    square = u * u
    q = 1.4250060785476853e-06
    for factor in (-3.669345091379551e-05, -8.782652731110375e-05, 0.03639228618131223, 0.7978697123041883):
        q = q * square + factor
    share = 0.5 + 0.5 * jnp.tanh(u * q)
    bell = jnp.exp(-0.5 * square)
    return u * share, share + (0.3989422804014327 * u) * bell


def vec(ref, cols=slice(None)):
    return ref[cols].reshape(1, -1)


def rows_of(step, size):
    return pl.ds(pl.multiple_of(step * size, size), size)


def part_owner(part, q_dev, q_len, p_len, qlen_ref, plen_ref):
    per = p_len // q_len
    beyond = jnp.maximum(part - q_dev, 0)
    is_query = part < q_dev
    slot = jnp.where(is_query, part, q_dev + beyond // per)
    length = jnp.where(is_query, qlen_ref[jnp.where(is_query, part, 0)], plen_ref[beyond // per])
    first = jnp.where(is_query, 0, beyond % per * q_len)
    return slot, length, first


def live_rows(first, length, size):
    return (first + lax.broadcasted_iota(jnp.int32, (size, 1), 0)) < length


def sure_rows(size):
    return size * 4 // 5 // 16 * 16


def half_only(pair_t, which):
    half = pair_t.shape[0] // 2
    zeros = jnp.zeros((half, pair_t.shape[1]), pair_t.dtype)
    if which == 0:
        return jnp.concatenate([pair_t[:half], zeros], 0)
    return jnp.concatenate([zeros, pair_t[half:]], 0)


def staged(count, *stages):
    for step in range(count + len(stages) - 1):
        for late, stage in enumerate(stages):
            if 0 <= step - late < count:
                stage(step - late)


def fetch(source, target, sems, index):
    return pltpu.make_async_copy(source, target, sems.at[index])


def attend_kernel(
    dims, qlen_ref, plen_ref, xq_ref, xp_ref, wq_ref, wk_ref, wv_ref, bq_ref, bv_ref,
    q_ref, k_ref, v_ref, ctx_t_ref, lse_ref,
):
    q_dev, q_len, rows_all, width = dims
    block = pl.program_id(0)
    head_dim = width // HEADS
    x = jnp.where(block == 0, xq_ref[...], xp_ref[...])
    q = ((mm(x, wq_ref[...]) + vec(bq_ref)) * head_dim**-0.5).astype(LOW)
    k = mm(x, wk_ref[...]).astype(LOW)
    v = (mm(x, wv_ref[...]) + vec(bv_ref)).astype(LOW)
    q_ref[...] = q
    k_ref[...] = k
    v_ref[...] = v
    q_t, v_t = q.T, v.T

    def attend(size, starts, lengths):
        items = [(start, length, head) for head in range(HEADS) for start, length in zip(starts, lengths)]
        scores, weights = {}, {}

        def compare(i):
            start, length, head = items[i]
            cols = slice(head // 2 * 2 * head_dim, (head // 2 + 1) * 2 * head_dim)
            here = slice(start, start + size)
            scores[i] = mm(k[here, cols], half_only(q_t[cols, here], head % 2))

        def weigh(i):
            start, length, head = items[i]
            edge = sure_rows(size)
            early, late = scores[i][:edge], scores.pop(i)[edge:]
            late = jnp.where(live_rows(edge, length, size - edge), late, -1e30)
            top = jnp.maximum(jnp.max(early, 0, keepdims=True), jnp.max(late, 0, keepdims=True))
            weights[i] = top, jnp.concatenate([jnp.exp(early - top).astype(LOW), jnp.exp(late - top).astype(LOW)], 0)

        def combine(i):
            start, length, head = items[i]
            here, rows = slice(start, start + size), slice(head * head_dim, (head + 1) * head_dim)
            top, weight = weights.pop(i)
            values = jnp.concatenate([v_t[rows, here], jnp.ones((16, size), LOW)], 0)
            result = mm(values, weight)
            total = result[head_dim : head_dim + 1]
            lse_ref[0, head // 2, head % 2 : head % 2 + 1, here] = top + jnp.log(total)
            ctx_t_ref[rows, here] = (result[:head_dim] * (1.0 / total)).astype(LOW)

        staged(len(items), compare, weigh, combine)

    @pl.when(block == 0)
    def _():
        attend(q_len, [s * q_len for s in range(q_dev)], [qlen_ref[s] for s in range(q_dev)])

    @pl.when(block > 0)
    def _():
        attend(rows_all, [0], [plen_ref[jnp.maximum(block - 1, 0)]])


def dense_kernel(
    dims, qlen_ref, plen_ref, pos_ref, xq_ref, xp_ref, ctx_t_ref, wo_hbm, wi_hbm, wf_hbm,
    bo_ref, bi_ref, bf_ref, g1_ref, s1_ref, g2_ref, s2_ref,
    h1_ref, y1_ref, act_ref, dg_ref, h2_ref, yq_ref, yp_ref, pool_ref, pay_ref,
    wo_ref, wi_ref, wf_ref, sems,
):
    q_dev, q_len, p_len, width, inner = dims
    block = pl.program_id(0)
    rows_all = xq_ref.shape[0]
    query_blocks = q_dev * q_len // rows_all
    copies = [
        fetch(source, target, sems, index)
        for index, (source, target) in enumerate([(wo_hbm, wo_ref), (wi_hbm, wi_ref), (wf_hbm, wf_ref)])
    ]

    @pl.when(block == 0)
    def _():
        for copy in copies:
            copy.start()
        pool_ref[...] = jnp.zeros_like(pool_ref)
        copies[0].wait()

    x = jnp.where(block < query_blocks, xq_ref[...], xp_ref[...])
    hidden = x.astype(F32) + (mm(ctx_t_ref[...].T, wo_ref[...]) + vec(bo_ref))
    h1_ref[...] = hidden.astype(LOW)
    y1 = norm_parts(hidden)[0] * vec(g1_ref) + vec(s1_ref)
    y1_low = y1.astype(LOW)
    y1_ref[...] = y1_low

    @pl.when(block == 0)
    def _():
        copies[1].wait()
        copies[2].wait()

    raw, made = {}, {}

    def expand(i):
        cols = slice(i * TILE, (i + 1) * TILE)
        raw[i] = mm(y1_low, wi_ref[:, cols]) + vec(bi_ref, cols)

    def activate(i):
        cols = slice(i * TILE, (i + 1) * TILE)
        act, slope = gelu_parts(raw.pop(i))
        made[i] = act.astype(LOW)
        act_ref[:, cols] = made[i]
        dg_ref[:, cols] = slope.astype(LOW)

    staged(inner // TILE, expand, activate)
    left = jnp.concatenate([made[i] for i in range(inner // TILE)], 1)
    total = (y1 + vec(bf_ref)) + mm(left, wf_ref[...])
    h2_ref[...] = total.astype(LOW)
    y2 = norm_parts(total)[0] * vec(g2_ref) + vec(s2_ref)
    for part in range(rows_all // q_len):
        number = block * (rows_all // q_len) + part
        slot, length, first = part_owner(number, q_dev, q_len, p_len, qlen_ref, plen_ref)
        piece = y2[part * q_len : (part + 1) * q_len]
        summed = jnp.sum(jnp.where(live_rows(first, length, q_len), piece, 0.0), 0, keepdims=True)
        in_slot = lax.broadcasted_iota(jnp.int32, (SLOTS, 1), 0) == slot
        pool_ref[...] += jnp.where(in_slot, summed / length.astype(F32), 0.0)

    @pl.when(block < query_blocks)
    def _():
        yq_ref[...] = y2.astype(LOW)

    @pl.when(block >= query_blocks)
    def _():
        yp_ref[...] = y2.astype(LOW)

    @pl.when(block == pl.num_programs(0) - 1)
    def _():
        pooled = pool_ref[...]
        emb = pooled * lax.rsqrt(jnp.sum(pooled * pooled, -1, keepdims=True) + EPS_POOL)
        pay_ref[:, :width] = emb.astype(LOW)
        row = lax.broadcasted_iota(jnp.int32, (SLOTS, 128), 0)
        col = lax.broadcasted_iota(jnp.int32, (SLOTS, 128), 1)
        place = jnp.zeros((SLOTS, 128), jnp.int32)
        for j in range(q_dev):
            high = pos_ref[j] // 128
            low = pos_ref[j] - high * 128
            place = jnp.where(row == j, jnp.where(col == 0, high, jnp.where(col == 1, low, 0)), place)
        pay_ref[:, width:] = place.astype(F32).astype(LOW)


def loss_kernel(
    dims, me_ref, qlen_ref, plen_ref, own_ref, all_ref, pool_ref, loss_ref, gvec_ref
):
    q_dev, p_dev, width, col_count = dims
    count = all_ref.shape[0]
    every = all_ref[:, :width]
    own = own_ref[:, :width]

    def passage_mask(index):
        spot, place = index % SLOTS, index // SLOTS
        per_core = count // SLOTS // 2
        core, rest = place // per_core, place % per_core
        device = (rest // col_count * 2 + core) * col_count + rest % col_count
        return (spot >= q_dev) & (spot < q_dev + p_dev), device * p_dev + spot - q_dev

    scores = mm_nt(own, every) * INV_TEMP
    valid, ident = passage_mask(lax.broadcasted_iota(jnp.int32, (SLOTS, count), 1))
    scores = jnp.where(valid, scores, -1e30)
    top = jnp.max(scores, -1, keepdims=True)
    totals = top + jnp.log(jnp.sum(jnp.exp(scores - top), -1, keepdims=True))
    marks = own_ref[:, width:].astype(F32)
    wanted = marks[:, 0:1] * 128.0 + marks[:, 1:2]
    target = (valid & (ident.astype(F32) == wanted)).astype(F32)
    raw = (INV_TEMP * (SCALE_LOSS * (jnp.exp(scores - totals) - target))).astype(LOW)
    grad_q = mm(raw, every)

    picker_col = lax.broadcasted_iota(jnp.int32, (SLOTS, 128), 1)
    picker = jnp.where(picker_col == 0, 128.0, jnp.where(picker_col == 1, 1.0, 0.0)).astype(LOW)
    own_row = lax.broadcasted_iota(jnp.int32, (SLOTS, TILE), 0)
    own_valid = (own_row >= q_dev) & (own_row < q_dev + p_dev)
    own_ident = (me_ref[0] * p_dev + own_row - q_dev).astype(F32)

    def body(step, carry):
        total_loss, grad_p = carry
        rows = rows_of(step, TILE)
        some = all_ref[rows, :width]
        place = mm_nt(picker, all_ref[rows, width:])[0:1]
        table = mm_nt(every, some) * INV_TEMP
        ok, names = passage_mask(lax.broadcasted_iota(jnp.int32, (count, TILE), 0))
        picked = jnp.sum(jnp.where(ok & (names.astype(F32) == place), table, 0.0), 0, keepdims=True)
        table = jnp.where(ok, table, -1e30)
        high = jnp.max(table, 0, keepdims=True)
        lse = high + jnp.log(jnp.sum(jnp.exp(table - high), 0, keepdims=True))
        is_query = lax.broadcasted_iota(jnp.int32, (1, TILE), 1) % SLOTS < q_dev
        losses = jnp.where(is_query, lse - picked, 0.0)
        mine = mm_nt(own, some) * INV_TEMP
        hit = (own_ident == place).astype(F32)
        grads = INV_TEMP * (SCALE_LOSS * (jnp.exp(mine - lse) - hit))
        grads = jnp.where(own_valid & is_query, grads, 0.0).astype(LOW)
        return total_loss + jnp.sum(losses, 1, keepdims=True), grad_p + mm(grads, some)

    start = (jnp.zeros((1, 1), F32), jnp.zeros((SLOTS, width), F32))
    total_loss, grad_p = lax.fori_loop(0, count // TILE, body, start)
    loss_ref[...] = jnp.broadcast_to(total_loss / float(count // SLOTS * q_dev), loss_ref.shape)

    slot = lax.broadcasted_iota(jnp.int32, (SLOTS, 1), 0)
    grad = jnp.where(slot < q_dev, grad_q, grad_p)
    pooled = pool_ref[...]
    r = lax.rsqrt(jnp.sum(pooled * pooled, -1, keepdims=True) + EPS_POOL)
    inside = jnp.sum(pooled * grad, -1, keepdims=True)
    length = jnp.ones((SLOTS, 1), F32)
    for j in range(q_dev):
        length = jnp.where(slot == j, qlen_ref[j].astype(F32), length)
    for j in range(p_dev):
        length = jnp.where(slot == q_dev + j, plen_ref[j].astype(F32), length)
    gvec_ref[...] = (r * grad - r * r * r * inside * pooled) / length


def store_shards(core_ref, result, send_ref, keep_ref, by_row=True, tails=None):
    count = send_ref.shape[0] * 2
    size = result.shape[0 if by_row else 1] // count

    def store(even, odd):
        for shard in range(count):
            spot = slice(shard * size, (shard + 1) * size)
            piece = (result[spot, :] if by_row else result[:, spot]).astype(LOW)
            target = odd if shard % 2 else even
            if tails is None:
                target[shard // 2] = piece
            else:
                target[shard // 2, :size] = piece
                target[shard // 2, size:] = tails[shard]

    @pl.when(core_ref[0] == 0)
    def _():
        store(keep_ref, send_ref)

    @pl.when(core_ref[0] == 1)
    def _():
        store(send_ref, keep_ref)


def outer_grad_kernel(
    dims, core_ref, qlen_ref, plen_ref, gvec_ref, h2_ref, g2_ref, act_ref,
    gf_ref, stat_ref, send_ref, keep_ref, gf_t_ref,
):
    q_dev, q_len, p_len = dims

    @pl.when(pl.program_id(0) == 0)
    def _():
        stat_ref[...] = jnp.zeros_like(stat_ref)

        def body(part, carry):
            rows = rows_of(part, q_len)
            slot, length, first = part_owner(part, q_dev, q_len, p_len, qlen_ref, plen_ref)
            in_slot = lax.broadcasted_iota(jnp.int32, (SLOTS, 1), 0) == slot
            grad_y = jnp.sum(jnp.where(in_slot, gvec_ref[...], 0.0), 0, keepdims=True)
            live = live_rows(first, length, q_len)
            n2, r2 = norm_parts(h2_ref[rows, :].astype(F32))
            g = grad_y * vec(g2_ref)
            grad = r2 * (g - jnp.mean(g, -1, keepdims=True) - n2 * jnp.mean(g * n2, -1, keepdims=True))
            grad = jnp.where(live, grad, 0.0)
            low = grad.astype(LOW)
            gf_ref[rows, :] = low
            gf_t_ref[:, rows] = low.T
            stat_ref[0:1, :] += grad_y * jnp.sum(jnp.where(live, n2, 0.0), 0, keepdims=True)
            stat_ref[1:2, :] += grad_y * jnp.sum(live.astype(F32), 0, keepdims=True)
            stat_ref[2:3, :] += jnp.sum(low.astype(F32), 0, keepdims=True)
            return carry

        lax.fori_loop(0, h2_ref.shape[0] // q_len, body, 0)

    store_shards(core_ref, mm(gf_t_ref[...], act_ref[...]), send_ref, keep_ref, by_row=False)


def dense_back_kernel(
    dims, gf_ref, dg_ref, h1_ref, wf_hbm, wi_hbm, wo_hbm, g1_ref,
    gu_ref, ga_ref, gc_ref, stat_ref, bi_ref,
    wf_ref, wi_ref, wo_ref, sems,
):
    inner = dims
    block = pl.program_id(0)
    copies = [
        fetch(source, target, sems, index)
        for index, (source, target) in enumerate([(wf_hbm, wf_ref), (wi_hbm, wi_ref), (wo_hbm, wo_ref)])
    ]

    @pl.when(block == 0)
    def _():
        for copy in copies:
            copy.start()
        stat_ref[...] = jnp.zeros_like(stat_ref)
        bi_ref[...] = jnp.zeros_like(bi_ref)
        copies[0].wait()

    gf = gf_ref[...]
    raw, made, biases = {}, {}, []

    def spread(i):
        raw[i] = mm_nt(gf, wf_ref[i * TILE : (i + 1) * TILE, :])

    def slope(i):
        cols = slice(i * TILE, (i + 1) * TILE)
        made[i] = (raw.pop(i) * dg_ref[:, cols].astype(F32)).astype(LOW)
        gu_ref[:, cols] = made[i]
        biases.append(jnp.sum(made[i].astype(F32), 0, keepdims=True))

    staged(inner // TILE, spread, slope)
    bi_ref[0:1, :] += jnp.concatenate(biases, 1)
    left = jnp.concatenate([made[i] for i in range(inner // TILE)], 1)

    @pl.when(block == 0)
    def _():
        for copy in copies[1:]:
            copy.wait()

    total = gf.astype(F32) + mm_nt(left, wi_ref[...])
    n1, r1 = norm_parts(h1_ref[...].astype(F32))
    stat_ref[0:1, :] += jnp.sum(total * n1, 0, keepdims=True)
    stat_ref[1:2, :] += jnp.sum(total, 0, keepdims=True)
    g = total * vec(g1_ref)
    grad = r1 * (g - jnp.mean(g, -1, keepdims=True) - n1 * jnp.mean(g * n1, -1, keepdims=True))
    low = grad.astype(LOW)
    ga_ref[...] = low
    stat_ref[2:3, :] += jnp.sum(low.astype(F32), 0, keepdims=True)
    gc_ref[...] = mm_nt(low, wo_ref[...]).astype(LOW)


def attend_back_kernel(
    dims, core_ref, qlen_ref, plen_ref, q_ref, k_ref, v_ref, ctx_t_ref, lse_ref, gc_ref, x_t_ref, *refs
):
    *extra, out_ref, stat_ref, send_ref, keep_ref, sum_ref = refs
    q_dev, q_len, rows_all, head_dim = dims
    block = pl.program_id(0)
    pair_dim = 2 * head_dim
    width = q_ref.shape[1]
    pairs = width // pair_dim

    @pl.when(block == 0)
    def _():
        stat_ref[...] = jnp.zeros_like(stat_ref)

    def attend(size, starts, lengths, fresh):
        lane = lax.broadcasted_iota(jnp.int32, (size, pair_dim), 1)
        items = [(s, p, which) for p in range(pairs) for s in range(len(starts)) for which in range(2)]
        held, raw, made, grads = {}, {}, {}, {}

        def pair_of(s, p):
            if (s, p) not in held:
                here, cols = slice(starts[s], starts[s] + size), slice(p * pair_dim, (p + 1) * pair_dim)
                q, k, v, gc = q_ref[here, cols], k_ref[here, cols], v_ref[here, cols], gc_ref[here, cols]
                held[s, p] = here, cols, q, k, v, gc, q.T, k.T, gc.T
            return held[s, p]

        def compare(i):
            s, p, which = items[i]
            here, cols, q, k, v, gc, q_t, k_t, gc_t = pair_of(s, p)
            raw[i] = mm(k, half_only(q_t, which)), mm(v, half_only(gc_t, which))

        def weigh(i):
            s, p, which = items[i]
            here, cols, q, k, v, gc, q_t, k_t, gc_t = pair_of(s, p)
            head = slice((p * 2 + which) * head_dim, (p * 2 + which + 1) * head_dim)
            scores, grad_p = raw.pop(i)
            lse = lse_ref[0, p, which : which + 1, here]
            edge = sure_rows(size)
            late = jnp.where(live_rows(edge, lengths[s], size - edge), scores[edge:], -1e30)
            probs = jnp.concatenate([jnp.exp(scores[:edge] - lse), jnp.exp(late - lse)], 0)
            half = slice(which * head_dim, (which + 1) * head_dim)
            delta = jnp.sum(gc_t[half].astype(F32) * ctx_t_ref[head, here].astype(F32), 0, keepdims=True)
            made[i] = probs.astype(LOW), (probs * (grad_p - delta)).astype(LOW)

        def combine(i):
            s, p, which = items[i]
            here, cols, q, k, v, gc, q_t, k_t, gc_t = pair_of(s, p)
            mine = (lane >= head_dim) if which else (lane < head_dim)
            zero = jnp.zeros_like(q)
            probs, grad_s = made.pop(i)
            add_v = mm(probs, jnp.where(mine, gc, zero))
            add_k = mm(grad_s, jnp.where(mine, q, zero))
            add_q = mm(k_t[which * head_dim : (which + 1) * head_dim], grad_s)
            if which == 0:
                made[s, p] = add_v, add_k, add_q
                return
            old_v, old_k, old_q = made.pop((s, p))
            grad_q = (jnp.concatenate([old_q, add_q], 0).T * head_dim**-0.5).astype(LOW)
            grad_k = (old_k + add_k).astype(LOW)
            grad_v = (old_v + add_v).astype(LOW)
            for number, grad in enumerate((grad_q, grad_k, grad_v)):
                out_ref[here, number * width + cols.start : number * width + cols.stop] = grad
                grads[number, s, p] = grad
            stat_ref[0:1, cols] += jnp.sum(grad_q.astype(F32), 0, keepdims=True)
            stat_ref[1:2, cols] += jnp.sum(grad_v.astype(F32), 0, keepdims=True)

            if p % 2 and s == len(starts) - 1:
                project(p - 1)

        def project(p):
            for number in range(3):
                rows = [
                    jnp.concatenate([grads.pop((number, s, p)), grads.pop((number, s, p + 1))], 1)
                    for s in range(len(starts))
                ]
                product = mm(x_t_ref[...], jnp.concatenate(rows, 0))
                cols = slice(number * width + p * pair_dim, number * width + (p + 2) * pair_dim)
                if fresh:
                    sum_ref[:, cols] = product
                else:
                    sum_ref[:, cols] += product

        staged(len(items), compare, weigh, combine)

    @pl.when(block == 0)
    def _():
        attend(q_len, [s * q_len for s in range(q_dev)], [qlen_ref[s] for s in range(q_dev)], True)

    @pl.when(block > 0)
    def _():
        attend(rows_all, [0], [plen_ref[jnp.maximum(block - 1, 0)]], False)

    @pl.when(block == pl.num_programs(0) - 1)
    def _():
        tails = None
        if extra:
            tails = small_rows([*extra, stat_ref], send_ref.shape[0] * 2, send_ref.shape[2])
        store_shards(core_ref, sum_ref[...], send_ref, keep_ref, tails=tails)


def input_grad_kernel(groups, *refs):
    grads, (base_ref, wq_ref, wk_ref, wv_ref, gq_ref, gp_ref) = refs[: len(groups)], refs[len(groups) :]
    total = base_ref[...].astype(F32)
    for grad_ref, (start, wide) in zip(grads, groups):
        for number, w_ref in enumerate((wq_ref, wk_ref, wv_ref)):
            total = total + mm_nt(grad_ref[:, number * wide : (number + 1) * wide], w_ref[:, start : start + wide])
    low = total.astype(LOW)

    @pl.when(pl.program_id(0) == 0)
    def _():
        gq_ref[...] = low

    @pl.when(pl.program_id(0) > 0)
    def _():
        gp_ref[...] = low


def weight_grad_kernel(core_ref, left_ref, right_ref, send_ref, keep_ref):
    store_shards(core_ref, mm(left_ref[...], right_ref[...]), send_ref, keep_ref)


def small_rows(refs, count, wide):
    two, one, inner, *attn = [ref[...] for ref in refs]
    eight = jnp.concatenate(
        [jnp.concatenate([item[0:2] for item in attn], 1), one[2:3], two[2:3], one[0:2], two[0:2]], 0
    )
    inner = inner[0:1]
    short, long = eight.shape[1] // count, inner.shape[1] // count
    rows = []
    for shard in range(count):
        top = eight[:, shard * short : (shard + 1) * short]
        low = inner[:, shard * long : (shard + 1) * long]
        top = jnp.concatenate([top, jnp.zeros((8, wide - short), F32)], 1)
        low = jnp.concatenate([low, jnp.zeros((1, wide - long), F32)], 1)
        rows.append(jnp.concatenate([top, low, jnp.zeros((7, wide), F32)], 0).astype(LOW))
    return rows


def turn_kernel(part_ref, out_ref):
    out_ref[...] = part_ref[...].astype(F32).T


def turn_low_kernel(*refs):
    *inputs, out_ref = refs
    if len(inputs) == 1:
        out_ref[...] = inputs[0][...].T
        return

    @pl.when(pl.program_id(0) == 0)
    def _():
        out_ref[...] = inputs[0][...].T

    @pl.when(pl.program_id(0) > 0)
    def _():
        out_ref[...] = inputs[1][...].T


def const_spec(shape):
    return pl.BlockSpec(shape, lambda i: (0,) * len(shape), pipeline_mode=pl.Buffered(1))


def call(body, operands, in_specs, outs, grid, room, deps=(), old=(), into=0, name=None, scratch=(), us=12):
    count, extra = len(operands), len(old)
    if deps:
        tied = min(range(count), key=lambda i: operands[i].size)
        operands = list(operands)
        operands[tied] = lax.optimization_barrier((operands[tied], *deps))[0]

    def kernel(*refs):
        body(*refs[:count], *refs[count + extra :])

    return pl.pallas_call(
        kernel,
        grid=grid,
        in_specs=list(in_specs) + [pl.BlockSpec(memory_space=pl.ANY)] * extra,
        out_specs=[spec for spec, _ in outs],
        out_shape=[jax.ShapeDtypeStruct(kind.shape, kind.dtype) for _, kind in outs],
        scratch_shapes=scratch,
        input_output_aliases={count + i: into + i for i in range(extra)},
        compiler_params=pltpu.CompilerParams(vmem_limit_bytes=room * 1024 * 1024),
        cost_estimate=pl.CostEstimate(flops=int(us * 1.15e9), bytes_accessed=0, transcendentals=0),
        name=name,
    )(*operands, *old)


def weight_grad(left_t, right, row_count, core, deps, old=(), at=0, us=12):
    height, depth = left_t.shape
    wide = right.shape[1]
    block = min(wide, 768)
    shape = old[0].shape if old else (row_count // 2, height // row_count, wide)
    spec = pl.BlockSpec((*shape[:2], block), lambda i: (0, 0, i + at))
    return call(
        weight_grad_kernel,
        (core, left_t, right),
        [
            pl.BlockSpec(memory_space=pltpu.SMEM),
            const_spec((height, depth)),
            pl.BlockSpec((depth, block), lambda i: (0, i)),
        ],
        [(spec, jax.ShapeDtypeStruct(shape, LOW))] * 2,
        (wide // block,),
        56,
        deps,
        old,
        name="weight_grad",
        us=us,
    )


def add_kernel(*refs):
    *terms, out_ref = refs
    out_ref[...] = sum([ref[...].astype(F32) for ref in terms[1:]], terms[0][...].astype(F32)).astype(LOW)


def add_all(terms):
    shape = terms[0].shape
    spec = pl.BlockSpec(shape, lambda i: (0,) * len(shape), pipeline_mode=pl.Buffered(1))
    outs = [(spec, jax.ShapeDtypeStruct(shape, LOW))]
    return call(add_kernel, terms, [spec] * len(terms), outs, (1,), 24, name="add_all", us=12)[0]


def masks_of(bits):
    return [
        sum(1 << bit for i, bit in enumerate(bits) if other >> i & 1) for other in range(1, 1 << len(bits))
    ]


def in_order(pieces, name, bits):
    here = lax.axis_index(name)
    for i, bit in enumerate(bits):
        high = ((here >> bit) & 1) == 1
        pieces = [jnp.where(high, pieces[place ^ (1 << i)], pieces[place]) for place in range(len(pieces))]
    return jnp.concatenate(pieces, 0)


class Flow:
    def __init__(self, sent, kept, line=False, fused=False, split=False, wide=2):
        bits = lax.axis_size("row").bit_length() - 1
        self.order = [(0,)] + [tuple(range(i, min(i + wide, bits))) for i in range(1, bits, wide)]
        self.left = list(range(bits - 1, 0, -1))
        count = lax.axis_size("col")
        self.line = [(None, [(i, i ^ (1 << bit)) for i in range(count)]) for bit in range(count.bit_length() - 1)]
        if line:
            half = count // 2
            self.line = [(None, [(i, i + 1), (count - 1 - i, count - 2 - i)]) for i in range(half - 1)]
            self.line += [(None, [(half - 1, half), (half, half - 1)])]
            self.line += [
                ((i, count - 1 - i), [(i + 1, i), (count - 2 - i, count - 1 - i)])
                for i in range(half - 2, -1, -1)
            ]
        if split:
            bits = count.bit_length() - 1
            groups = [tuple(range(i, min(i + 2, bits))) for i in range(0, bits, 2)]
            self.line = [("scatter", group) for group in groups[::-1]] + [("gather", group) for group in groups]
        self.sent, self.kept, self.got, self.fused, self.split = [sent], kept, None, fused, split

    def shard(self, terms, bits, mask, name="row"):
        here = lax.axis_index(name)
        order = [self.left.index(bit) for bit in bits]
        total = None
        for term in terms:
            starts, sizes = [0] * term.ndim, list(term.shape)
            for axis, bit in zip(order, bits):
                starts[axis], sizes[axis] = ((here ^ mask) >> bit) & 1, 1
            piece = lax.dynamic_slice(term, starts, sizes)
            piece = piece.reshape([size for i, size in enumerate(sizes) if i not in order]).astype(F32)
            total = piece if total is None else total + piece
        return total.astype(LOW)

    def step(self):
        if self.order:
            bits = self.order[0]
            masks = masks_of(bits)
            if bits != (0,):
                terms = [self.kept, *self.got]
                self.sent = [self.shard(terms, bits, mask) for mask in masks]
                self.kept = self.shard(terms, bits, 0)
                self.left = [bit for bit in self.left if bit not in bits]
            size = lax.axis_size("row")
            self.got = [
                lax.ppermute(sent, "row", [(i, i ^ mask) for i in range(size)])
                for sent, mask in zip(self.sent, masks)
            ]
        elif self.split:
            kind, bits = self.line[0]
            masks = masks_of(bits)
            size = lax.axis_size("col")
            if kind == "scatter":
                terms = [self.kept, *self.got]
                if not self.left:
                    self.left = list(range(size.bit_length() - 2, -1, -1))
                    rows, wide = self.kept.shape
                    dims = (2,) * len(self.left) + (rows // size, wide)
                    terms = [term.reshape(dims) for term in terms]
                self.sent = [self.shard(terms, bits, mask, "col") for mask in masks]
                self.kept = self.shard(terms, bits, 0, "col")
                self.left = [bit for bit in self.left if bit not in bits]
            else:
                self.sent = [self.kept] * len(masks)
            self.got = [
                lax.ppermute(sent, "col", [(i, i ^ mask) for i in range(size)])
                for sent, mask in zip(self.sent, masks)
            ]
        else:
            self.sent = [self.kept]
            self.got = [lax.ppermute(self.kept, "col", self.line[0][1])]

    def land(self, token=None):
        if token is not None:
            self.kept = lax.optimization_barrier((self.kept, token))[0]
        got = self.got
        if self.order:
            bits = self.order.pop(0)
            if bits == (0,):
                dims = (2,) * len(self.left) + self.kept.shape[1:]
                self.kept, self.got = self.kept.reshape(dims), [item.reshape(dims) for item in self.got]
            if not self.order and self.fused:
                self.kept = add_all([self.kept, *self.got])
            elif not self.order and not self.split:
                self.kept = sum([item.astype(F32) for item in self.got], self.kept.astype(F32)).astype(LOW)
        elif self.split:
            kind, bits = self.line.pop(0)
            if kind == "gather":
                self.kept = in_order([self.kept, *self.got], "col", bits)
            elif self.line[0][0] == "gather":
                self.kept = sum([item.astype(F32) for item in self.got], self.kept.astype(F32)).astype(LOW)
        else:
            ends, _ = self.line.pop(0)
            if ends is None:
                self.kept = self.kept + self.got[0]
            else:
                here = lax.axis_index("col")
                self.kept = jnp.where((here == ends[0]) | (here == ends[1]), self.got[0], self.kept)
        return got

    def turn(self, token=None):
        got = self.land(token)
        if self.done:
            return got
        self.step()
        return got + self.sent

    @property
    def done(self):
        return not self.order and not self.line


def gather_all(piece):
    row_bits = lax.axis_size("row").bit_length() - 1
    col_bits = lax.axis_size("col").bit_length() - 1
    steps = [("col", tuple(range(i, min(i + 2, col_bits)))) for i in range(0, col_bits, 2)]
    steps += [("row", tuple(range(i, min(i + 2, row_bits)))) for i in range(1, row_bits, 2)]
    for name, bits in steps + [("row", (0,))]:
        size = lax.axis_size(name)
        got = [lax.ppermute(piece, name, [(i, i ^ mask) for i in range(size)]) for mask in masks_of(bits)]
        piece = in_order([piece, *got], name, bits)
    return piece


def per_device(
    query_tokens, passage_tokens, query_lengths, passage_lengths, positives,
    w_query, w_key, w_value, w_attn_out, w_inner, w_outer,
    bias_query, bias_value, bias_attn_out, bias_inner, bias_outer,
    gain_one, shift_one, gain_two, shift_two,
):
    q_dev, q_len, width = query_tokens.shape
    p_dev, p_len, _ = passage_tokens.shape
    inner = w_inner.shape[1]
    rows_all = p_len
    assert q_dev * q_len == rows_all and q_dev + p_dev <= SLOTS
    blocks = 1 + p_dev
    total_rows = blocks * rows_all
    row_count = lax.axis_size("row")
    col_count = lax.axis_size("col")
    row_here = lax.axis_index("row")
    core = (row_here & 1).reshape(1)
    me = (row_here * col_count + lax.axis_index("col")).reshape(1)
    params = pltpu.CompilerParams(vmem_limit_bytes=VMEM)
    smem = pl.BlockSpec(memory_space=pltpu.SMEM)

    def by_block(wide):
        return pl.BlockSpec((rows_all, wide), lambda i: (i, 0))

    def by_block_t(high):
        return pl.BlockSpec((high, rows_all), lambda i: (0, i))

    def fixed(shape):
        return pl.BlockSpec(shape, lambda i: (0,) * len(shape))

    queries_spec = pl.BlockSpec((rows_all, width), lambda i: (0, 0))
    passages_spec = pl.BlockSpec((rows_all, width), lambda i: (jnp.maximum(i - 1, 0), 0))

    lse_spec = pl.BlockSpec((1, HEADS // 2, 8, rows_all), lambda i: (i, 0, 0, 0))

    def shape(*dims, kind=LOW):
        return jax.ShapeDtypeStruct(dims, kind)

    queries = query_tokens.reshape(rows_all, width)
    passages = passage_tokens.reshape(p_dev * rows_all, width)
    square = const_spec((width, width))
    anywhere = pl.BlockSpec(memory_space=pl.ANY)
    thin = const_spec((width,))

    q, k, v, ctx_t, lse = call(
        partial(attend_kernel, (q_dev, q_len, rows_all, width)),
        (query_lengths, passage_lengths, queries, passages, w_query, w_key, w_value, bias_query, bias_value),
        [smem, smem, queries_spec, passages_spec, square, square, square, thin, thin],
        [(by_block(width), shape(total_rows, width))] * 3
        + [
            (by_block_t(width), shape(width, total_rows)),
            (lse_spec, shape(blocks, HEADS // 2, 8, rows_all, kind=F32)),
        ],
        (blocks,),
        56,
        name="attend",

    )

    rows_part = rows_all
    parts = blocks

    def by_part(wide):
        return pl.BlockSpec((rows_part, wide), lambda i: (i, 0))

    queries_part = pl.BlockSpec((rows_part, width), lambda i: (0, 0))
    passages_part = pl.BlockSpec((rows_part, width), lambda i: (jnp.maximum(i - 1, 0), 0))
    h1, y1, act, slope, h2, query_out, passage_out, pooled, payload = call(
        partial(dense_kernel, (q_dev, q_len, p_len, width, inner)),
        (
            query_lengths, passage_lengths, positives, queries, passages, ctx_t, w_attn_out, w_inner, w_outer,
            bias_attn_out, bias_inner, bias_outer, gain_one, shift_one, gain_two, shift_two,
        ),
        [smem, smem, smem, queries_part, passages_part, pl.BlockSpec((width, rows_part), lambda i: (0, i))]
        + [anywhere] * 3
        + [thin, const_spec((inner,))]
        + [thin] * 5,
        [
            (by_part(width), shape(total_rows, width)),
            (by_part(width), shape(total_rows, width)),
            (by_part(inner), shape(total_rows, inner)),
            (by_part(inner), shape(total_rows, inner)),
            (by_part(width), shape(total_rows, width)),
            (queries_part, shape(rows_all, width)),
            (passages_part, shape(p_dev * rows_all, width)),
            (fixed((SLOTS, width)), shape(SLOTS, width, kind=F32)),
            (fixed((SLOTS, width + 128)), shape(SLOTS, width + 128)),
        ],
        (parts,),
        56,
        name="dense",
        scratch=[
            pltpu.VMEM((width, width), LOW),
            pltpu.VMEM((width, inner), LOW),
            pltpu.VMEM((inner, width), LOW),
            pltpu.SemaphoreType.DMA((3,)),
        ],

    )

    gathered = gather_all(payload)
    loss, gvec = pl.pallas_call(
        partial(loss_kernel, (q_dev, p_dev, width, col_count)),
        in_specs=[smem] * 3 + [pl.BlockSpec(memory_space=pltpu.VMEM)] * 3,
        out_specs=[pl.BlockSpec(memory_space=pltpu.VMEM)] * 2,
        out_shape=[shape(8, 128, kind=F32), shape(SLOTS, width, kind=F32)],
        compiler_params=params,
        name="loss",
    )(me, query_lengths, passage_lengths, payload, gathered, pooled)

    smalls = shape(8, width, kind=F32)
    cut = width // row_count
    cut_inner = inner // row_count
    half = row_count // 2
    step_cols = 768
    per_step = step_cols // cut_inner
    outer_spec = pl.BlockSpec((per_step // 2, width, cut_inner), lambda i: (i, 0, 0))
    grad_f, stat_two, *outer_parts = call(
        partial(outer_grad_kernel, (q_dev, q_len, p_len)),
        (core, query_lengths, passage_lengths, gvec, h2, gain_two, act),
        [smem, smem, smem, fixed((SLOTS, width)), const_spec((total_rows, width)), thin]
        + [pl.BlockSpec((total_rows, step_cols), lambda i: (0, i))],
        [
            (fixed((total_rows, width)), shape(total_rows, width)),
            (fixed((8, width)), smalls),
            (outer_spec, shape(half, width, cut_inner)),
            (outer_spec, shape(half, width, cut_inner)),
        ],
        (inner // step_cols,),
        56,
        name="outer_grad",
        scratch=[pltpu.VMEM((width, total_rows), LOW)],
    )
    outer = Flow(*outer_parts)
    outer.step()

    def turn(arrays, specs, deps):
        outs = [(by_block_t(width), shape(width, total_rows))]
        return call(turn_low_kernel, arrays, specs, outs, (blocks,), 56, deps, name="turn", us=40)[0]

    y1_t = turn([y1], [by_block(width)], outer.sent)
    deps = outer.turn(y1_t)
    head_dim = width // HEADS
    third = 4 * head_dim
    groups = [(0, 2 * third), (2 * third, third)]
    grad_u, grad_attn, grad_ctx, stat_one, grad_bias_inner = call(
        partial(dense_back_kernel, inner),
        (grad_f, slope, h1, w_outer, w_inner, w_attn_out, gain_one),
        [by_block(width), by_block(inner), by_block(width), anywhere, anywhere, anywhere, thin],
        [
            (by_block(inner), shape(total_rows, inner)),
            (by_block(width), shape(total_rows, width)),
            (by_block(width), shape(total_rows, width)),
            (fixed((8, width)), smalls),
            (fixed((8, inner)), shape(8, inner, kind=F32)),
        ],
        (blocks,),
        60,
        deps,
        name="dense_back",
        scratch=[
            pltpu.VMEM((inner, width), LOW),
            pltpu.VMEM((width, inner), LOW),
            pltpu.VMEM((width, width), LOW),
            pltpu.SemaphoreType.DMA((3,)),
        ],
    )
    deps = outer.turn(stat_one)
    up_flow = Flow(*weight_grad(y1_t, grad_u, row_count, core, deps), fused=True)
    up_flow.step()
    deps = up_flow.sent + outer.turn(up_flow.sent[0])
    x_t = turn([queries, passages], [queries_spec, passages_spec], deps)
    deps = up_flow.turn(x_t)

    def attend_back(start, wide, deps, extra=(), room=None):
        pairs = wide // (2 * head_dim)
        index = start // wide
        cols = pl.BlockSpec((rows_all, wide), lambda i: (i, index))
        rows = cut + (16 if extra else 0)
        return call(
            partial(attend_back_kernel, (q_dev, q_len, rows_all, head_dim)),
            (core, query_lengths, passage_lengths, q, k, v, ctx_t, lse, grad_ctx, x_t, *extra),
            [smem, smem, smem]
            + [cols] * 3
            + [
                pl.BlockSpec((wide, rows_all), lambda i: (index, i)),
                pl.BlockSpec((1, pairs, 8, rows_all), lambda i: (i, index, 0, 0)),
                cols,
                by_block_t(width),
            ]
            + [const_spec(item.shape) for item in extra],
            [
                (by_block(3 * wide), shape(total_rows, 3 * wide)),
                (fixed((8, wide)), shape(8, wide, kind=F32)),
            ]
            + [(fixed((half, rows, 3 * wide)), shape(half, rows, room or 3 * wide))] * 2,
            (blocks,),
            56,
            deps,
            name="attend_back",
            scratch=[pltpu.VMEM((width, 3 * wide), F32)],
            us=12 if room else 40,
        )

    grad_a, stat_a, *mixed_parts = attend_back(*groups[0], deps, room=6 * third + width)
    at = 6 * third // width
    mixed_parts = weight_grad(ctx_t, grad_attn, row_count, core, [stat_a], mixed_parts, at, us=0)
    mixed_flow = Flow(*mixed_parts, split=True)
    mixed_flow.step()
    token = mixed_flow.sent[0]
    deps = mixed_flow.sent + outer.turn(token) + up_flow.turn(token)
    extra = (stat_two, stat_one, grad_bias_inner, stat_a)
    grad_b, stat_b, *last_parts = attend_back(*groups[1], deps, extra)
    last_flow = Flow(*last_parts, wide=1)
    last_flow.step()
    deps = last_flow.sent + mixed_flow.turn(stat_b) + up_flow.turn(stat_b)
    query_grad, passage_grad = call(
        partial(input_grad_kernel, groups),
        (grad_a, grad_b, grad_attn, w_query, w_key, w_value),
        [by_block(3 * wide) for _, wide in groups] + [by_block(width), square, square, square],
        [
            (queries_spec, shape(rows_all, width)),
            (passages_spec, shape(p_dev * rows_all, width)),
        ],
        (blocks,),
        56,
        deps,
        name="input_grad",
        us=40,
    )
    last_flow.turn(passage_grad)
    mixed_flow.turn(last_flow.kept)
    outs = [(fixed((cut_inner, width)), shape(cut_inner, width, kind=F32))]
    (turned,) = call(
        turn_kernel, (outer.kept,), [const_spec((width, cut_inner))], outs, (1,), 56, [mixed_flow.kept], name="turn", us=40
    )
    last_flow.turn(turned)
    up_flow.turn(last_flow.kept)
    last_flow.turn(up_flow.kept)
    mixed_flow.turn(last_flow.kept)
    last_flow.turn(mixed_flow.kept)
    mixed_flow.turn(last_flow.kept)
    flows = [outer, up_flow, mixed_flow, last_flow]
    while not all(flow.done for flow in flows):
        for flow in flows:
            if not flow.done:
                flow.turn()
    mixed, last = mixed_flow.kept, last_flow.kept
    qkv = [
        jnp.concatenate(
            [mixed[:, i * 2 * third : (i + 1) * 2 * third], last[:cut, i * third : (i + 1) * third]], 1
        ).astype(F32)
        for i in range(3)
    ]
    small = last[cut:].astype(F32)
    return (
        loss[0, 0],
        query_out.reshape(query_tokens.shape),
        passage_out.reshape(passage_tokens.shape),
        query_grad.reshape(query_tokens.shape),
        passage_grad.reshape(passage_tokens.shape),
        *qkv,
        mixed[:, 6 * third :].astype(F32),
        up_flow.kept.astype(F32),
        turned,
        *[small[i, :cut] for i in range(3)],
        small[8, : inner // row_count],
        *[small[i, :cut] for i in range(3, 8)],
    )


def solution(mesh):
    in_specs = (
        P(("row", "col"), None, None),
        P(("row", "col"), None, None),
        P(("row", "col")),
        P(("row", "col")),
        P(("row", "col")),
        P(),
        P(),
        P(),
        P(),
        P(),
        P(),
        P(),
        P(),
        P(),
        P(),
        P(),
        P(),
        P(),
        P(),
        P(),
    )
    out_specs = (
        P(),
        P(("row", "col"), None, None),
        P(("row", "col"), None, None),
        P(("row", "col"), None, None),
        P(("row", "col"), None, None),
        P("row", None),
        P("row", None),
        P("row", None),
        P("row", None),
        P("row", None),
        P("row", None),
        P("row"),
        P("row"),
        P("row"),
        P("row"),
        P("row"),
        P("row"),
        P("row"),
        P("row"),
        P("row"),
    )
    return jax.shard_map(
        per_device, mesh=mesh, in_specs=in_specs, out_specs=out_specs, check_vma=False
    )
```

```python
from functools import partial

import jax
import jax.numpy as jnp
from jax import lax
from jax.experimental import pallas as pl
from jax.experimental.pallas import tpu as pltpu
from jax.sharding import PartitionSpec as P

HEADS = 12
EPS_NORM = 1e-12
EPS_POOL = 1e-06
SCALE_LOSS = 128.0
INV_TEMP = 100.0
TILE = 256
SLOTS = 8
VMEM = 60 * 1024 * 1024
LOW = jnp.bfloat16
F32 = jnp.float32


def mm(left, right):
    return lax.dot_general(left, right, (((1,), (0,)), ((), ())), preferred_element_type=F32)


def mm_nt(left, right):
    return lax.dot_general(left, right, (((1,), (1,)), ((), ())), preferred_element_type=F32)


def norm_parts(hidden):
    center = hidden - jnp.mean(hidden, -1, keepdims=True)
    spread = jnp.mean(center * center, -1, keepdims=True)
    scale = lax.rsqrt(spread + EPS_NORM)
    return center * scale, scale


def gelu_parts(u):
    square = u * u
    q = 1.4250060785476853e-06
    for factor in (-3.669345091379551e-05, -8.782652731110375e-05, 0.03639228618131223, 0.7978697123041883):
        q = q * square + factor
    share = 0.5 + 0.5 * jnp.tanh(u * q)
    bell = jnp.exp(-0.5 * square)
    return u * share, share + (0.3989422804014327 * u) * bell


def vec(ref, cols=slice(None)):
    return ref[cols].reshape(1, -1)


def rows_of(step, size):
    return pl.ds(pl.multiple_of(step * size, size), size)


def part_owner(part, q_dev, q_len, p_len, qlen_ref, plen_ref):
    per = p_len // q_len
    beyond = jnp.maximum(part - q_dev, 0)
    is_query = part < q_dev
    slot = jnp.where(is_query, part, q_dev + beyond // per)
    length = jnp.where(is_query, qlen_ref[jnp.where(is_query, part, 0)], plen_ref[beyond // per])
    first = jnp.where(is_query, 0, beyond % per * q_len)
    return slot, length, first


def live_rows(first, length, size):
    return (first + lax.broadcasted_iota(jnp.int32, (size, 1), 0)) < length


def sure_rows(size):
    return size * 4 // 5 // 16 * 16


def half_only(pair_t, which):
    half = pair_t.shape[0] // 2
    zeros = jnp.zeros((half, pair_t.shape[1]), pair_t.dtype)
    if which == 0:
        return jnp.concatenate([pair_t[:half], zeros], 0)
    return jnp.concatenate([zeros, pair_t[half:]], 0)


def staged(count, *stages):
    for step in range(count + len(stages) - 1):
        for late, stage in enumerate(stages):
            if 0 <= step - late < count:
                stage(step - late)


def fetch(source, target, sems, index):
    return pltpu.make_async_copy(source, target, sems.at[index])


def attend_kernel(
    dims, qlen_ref, plen_ref, xq_ref, xp_ref, wq_ref, wk_ref, wv_ref, bq_ref, bv_ref,
    q_ref, k_ref, v_ref, ctx_t_ref, lse_ref,
):
    q_dev, q_len, rows_all, width = dims
    block = pl.program_id(0)
    head_dim = width // HEADS
    x = jnp.where(block == 0, xq_ref[...], xp_ref[...])
    q = ((mm(x, wq_ref[...]) + vec(bq_ref)) * head_dim**-0.5).astype(LOW)
    k = mm(x, wk_ref[...]).astype(LOW)
    v = (mm(x, wv_ref[...]) + vec(bv_ref)).astype(LOW)
    q_ref[...] = q
    k_ref[...] = k
    v_ref[...] = v
    q_t, v_t = q.T, v.T

    def attend(size, starts, lengths):
        items = [(start, length, head) for head in range(HEADS) for start, length in zip(starts, lengths)]
        scores, weights = {}, {}

        def compare(i):
            start, length, head = items[i]
            cols = slice(head // 2 * 2 * head_dim, (head // 2 + 1) * 2 * head_dim)
            here = slice(start, start + size)
            scores[i] = mm(k[here, cols], half_only(q_t[cols, here], head % 2))

        def weigh(i):
            start, length, head = items[i]
            edge = sure_rows(size)
            early, late = scores[i][:edge], scores.pop(i)[edge:]
            late = jnp.where(live_rows(edge, length, size - edge), late, -1e30)
            top = jnp.maximum(jnp.max(early, 0, keepdims=True), jnp.max(late, 0, keepdims=True))
            weights[i] = top, jnp.concatenate([jnp.exp(early - top).astype(LOW), jnp.exp(late - top).astype(LOW)], 0)

        def combine(i):
            start, length, head = items[i]
            here, rows = slice(start, start + size), slice(head * head_dim, (head + 1) * head_dim)
            top, weight = weights.pop(i)
            values = jnp.concatenate([v_t[rows, here], jnp.ones((16, size), LOW)], 0)
            result = mm(values, weight)
            total = result[head_dim : head_dim + 1]
            lse_ref[0, head // 2, head % 2 : head % 2 + 1, here] = top + jnp.log(total)
            ctx_t_ref[rows, here] = (result[:head_dim] * (1.0 / total)).astype(LOW)

        staged(len(items), compare, weigh, combine)

    @pl.when(block == 0)
    def _():
        attend(q_len, [s * q_len for s in range(q_dev)], [qlen_ref[s] for s in range(q_dev)])

    @pl.when(block > 0)
    def _():
        attend(rows_all, [0], [plen_ref[jnp.maximum(block - 1, 0)]])


def dense_kernel(
    dims, qlen_ref, plen_ref, pos_ref, xq_ref, xp_ref, ctx_t_ref, wo_hbm, wi_hbm, wf_hbm,
    bo_ref, bi_ref, bf_ref, g1_ref, s1_ref, g2_ref, s2_ref,
    h1_ref, y1_ref, act_ref, dg_ref, h2_ref, yq_ref, yp_ref, pool_ref, pay_ref,
    wo_ref, wi_ref, wf_ref, sems,
):
    q_dev, q_len, p_len, width, inner = dims
    block = pl.program_id(0)
    rows_all = xq_ref.shape[0]
    query_blocks = q_dev * q_len // rows_all
    copies = [
        fetch(source, target, sems, index)
        for index, (source, target) in enumerate([(wo_hbm, wo_ref), (wi_hbm, wi_ref), (wf_hbm, wf_ref)])
    ]

    @pl.when(block == 0)
    def _():
        for copy in copies:
            copy.start()
        pool_ref[...] = jnp.zeros_like(pool_ref)
        copies[0].wait()

    x = jnp.where(block < query_blocks, xq_ref[...], xp_ref[...])
    hidden = x.astype(F32) + (mm(ctx_t_ref[...].T, wo_ref[...]) + vec(bo_ref))
    h1_ref[...] = hidden.astype(LOW)
    y1 = norm_parts(hidden)[0] * vec(g1_ref) + vec(s1_ref)
    y1_low = y1.astype(LOW)
    y1_ref[...] = y1_low

    @pl.when(block == 0)
    def _():
        copies[1].wait()
        copies[2].wait()

    raw, made = {}, {}

    def expand(i):
        cols = slice(i * TILE, (i + 1) * TILE)
        raw[i] = mm(y1_low, wi_ref[:, cols]) + vec(bi_ref, cols)

    def activate(i):
        cols = slice(i * TILE, (i + 1) * TILE)
        act, slope = gelu_parts(raw.pop(i))
        made[i] = act.astype(LOW)
        act_ref[:, cols] = made[i]
        dg_ref[:, cols] = slope.astype(LOW)

    staged(inner // TILE, expand, activate)
    left = jnp.concatenate([made[i] for i in range(inner // TILE)], 1)
    total = (y1 + vec(bf_ref)) + mm(left, wf_ref[...])
    h2_ref[...] = total.astype(LOW)
    y2 = norm_parts(total)[0] * vec(g2_ref) + vec(s2_ref)
    for part in range(rows_all // q_len):
        number = block * (rows_all // q_len) + part
        slot, length, first = part_owner(number, q_dev, q_len, p_len, qlen_ref, plen_ref)
        piece = y2[part * q_len : (part + 1) * q_len]
        summed = jnp.sum(jnp.where(live_rows(first, length, q_len), piece, 0.0), 0, keepdims=True)
        in_slot = lax.broadcasted_iota(jnp.int32, (SLOTS, 1), 0) == slot
        pool_ref[...] += jnp.where(in_slot, summed / length.astype(F32), 0.0)

    @pl.when(block < query_blocks)
    def _():
        yq_ref[...] = y2.astype(LOW)

    @pl.when(block >= query_blocks)
    def _():
        yp_ref[...] = y2.astype(LOW)

    @pl.when(block == pl.num_programs(0) - 1)
    def _():
        pooled = pool_ref[...]
        emb = pooled * lax.rsqrt(jnp.sum(pooled * pooled, -1, keepdims=True) + EPS_POOL)
        pay_ref[:, :width] = emb.astype(LOW)
        row = lax.broadcasted_iota(jnp.int32, (SLOTS, 128), 0)
        col = lax.broadcasted_iota(jnp.int32, (SLOTS, 128), 1)
        place = jnp.zeros((SLOTS, 128), jnp.int32)
        for j in range(q_dev):
            high = pos_ref[j] // 128
            low = pos_ref[j] - high * 128
            place = jnp.where(row == j, jnp.where(col == 0, high, jnp.where(col == 1, low, 0)), place)
        pay_ref[:, width:] = place.astype(F32).astype(LOW)


def loss_kernel(
    dims, me_ref, qlen_ref, plen_ref, own_ref, all_ref, pool_ref, loss_ref, gvec_ref
):
    q_dev, p_dev, width, col_count = dims
    count = all_ref.shape[0]
    every = all_ref[:, :width]
    own = own_ref[:, :width]

    def passage_mask(index):
        spot, place = index % SLOTS, index // SLOTS
        per_core = count // SLOTS // 2
        core, rest = place // per_core, place % per_core
        device = (rest // col_count * 2 + core) * col_count + rest % col_count
        return (spot >= q_dev) & (spot < q_dev + p_dev), device * p_dev + spot - q_dev

    scores = mm_nt(own, every) * INV_TEMP
    valid, ident = passage_mask(lax.broadcasted_iota(jnp.int32, (SLOTS, count), 1))
    scores = jnp.where(valid, scores, -1e30)
    top = jnp.max(scores, -1, keepdims=True)
    totals = top + jnp.log(jnp.sum(jnp.exp(scores - top), -1, keepdims=True))
    marks = own_ref[:, width:].astype(F32)
    wanted = marks[:, 0:1] * 128.0 + marks[:, 1:2]
    target = (valid & (ident.astype(F32) == wanted)).astype(F32)
    raw = (INV_TEMP * (SCALE_LOSS * (jnp.exp(scores - totals) - target))).astype(LOW)
    grad_q = mm(raw, every)

    picker_col = lax.broadcasted_iota(jnp.int32, (SLOTS, 128), 1)
    picker = jnp.where(picker_col == 0, 128.0, jnp.where(picker_col == 1, 1.0, 0.0)).astype(LOW)
    own_row = lax.broadcasted_iota(jnp.int32, (SLOTS, TILE), 0)
    own_valid = (own_row >= q_dev) & (own_row < q_dev + p_dev)
    own_ident = (me_ref[0] * p_dev + own_row - q_dev).astype(F32)

    def body(step, carry):
        total_loss, grad_p = carry
        rows = rows_of(step, TILE)
        some = all_ref[rows, :width]
        place = mm_nt(picker, all_ref[rows, width:])[0:1]
        table = mm_nt(every, some) * INV_TEMP
        ok, names = passage_mask(lax.broadcasted_iota(jnp.int32, (count, TILE), 0))
        picked = jnp.sum(jnp.where(ok & (names.astype(F32) == place), table, 0.0), 0, keepdims=True)
        table = jnp.where(ok, table, -1e30)
        high = jnp.max(table, 0, keepdims=True)
        lse = high + jnp.log(jnp.sum(jnp.exp(table - high), 0, keepdims=True))
        is_query = lax.broadcasted_iota(jnp.int32, (1, TILE), 1) % SLOTS < q_dev
        losses = jnp.where(is_query, lse - picked, 0.0)
        mine = mm_nt(own, some) * INV_TEMP
        hit = (own_ident == place).astype(F32)
        grads = INV_TEMP * (SCALE_LOSS * (jnp.exp(mine - lse) - hit))
        grads = jnp.where(own_valid & is_query, grads, 0.0).astype(LOW)
        return total_loss + jnp.sum(losses, 1, keepdims=True), grad_p + mm(grads, some)

    start = (jnp.zeros((1, 1), F32), jnp.zeros((SLOTS, width), F32))
    total_loss, grad_p = lax.fori_loop(0, count // TILE, body, start)
    loss_ref[...] = jnp.broadcast_to(total_loss / float(count // SLOTS * q_dev), loss_ref.shape)

    slot = lax.broadcasted_iota(jnp.int32, (SLOTS, 1), 0)
    grad = jnp.where(slot < q_dev, grad_q, grad_p)
    pooled = pool_ref[...]
    r = lax.rsqrt(jnp.sum(pooled * pooled, -1, keepdims=True) + EPS_POOL)
    inside = jnp.sum(pooled * grad, -1, keepdims=True)
    length = jnp.ones((SLOTS, 1), F32)
    for j in range(q_dev):
        length = jnp.where(slot == j, qlen_ref[j].astype(F32), length)
    for j in range(p_dev):
        length = jnp.where(slot == q_dev + j, plen_ref[j].astype(F32), length)
    gvec_ref[...] = (r * grad - r * r * r * inside * pooled) / length


def store_shards(core_ref, result, send_ref, keep_ref, by_row=True, tails=None):
    count = send_ref.shape[0] * 2
    size = result.shape[0 if by_row else 1] // count

    def store(even, odd):
        for shard in range(count):
            spot = slice(shard * size, (shard + 1) * size)
            piece = (result[spot, :] if by_row else result[:, spot]).astype(LOW)
            target = odd if shard % 2 else even
            if tails is None:
                target[shard // 2] = piece
            else:
                target[shard // 2, :size] = piece
                target[shard // 2, size:] = tails[shard]

    @pl.when(core_ref[0] == 0)
    def _():
        store(keep_ref, send_ref)

    @pl.when(core_ref[0] == 1)
    def _():
        store(send_ref, keep_ref)


def outer_grad_kernel(
    dims, core_ref, qlen_ref, plen_ref, gvec_ref, h2_ref, g2_ref, act_ref,
    gf_ref, stat_ref, send_ref, keep_ref, gf_t_ref,
):
    q_dev, q_len, p_len = dims

    @pl.when(pl.program_id(0) == 0)
    def _():
        stat_ref[...] = jnp.zeros_like(stat_ref)

        def body(part, carry):
            rows = rows_of(part, q_len)
            slot, length, first = part_owner(part, q_dev, q_len, p_len, qlen_ref, plen_ref)
            in_slot = lax.broadcasted_iota(jnp.int32, (SLOTS, 1), 0) == slot
            grad_y = jnp.sum(jnp.where(in_slot, gvec_ref[...], 0.0), 0, keepdims=True)
            live = live_rows(first, length, q_len)
            n2, r2 = norm_parts(h2_ref[rows, :].astype(F32))
            g = grad_y * vec(g2_ref)
            grad = r2 * (g - jnp.mean(g, -1, keepdims=True) - n2 * jnp.mean(g * n2, -1, keepdims=True))
            grad = jnp.where(live, grad, 0.0)
            low = grad.astype(LOW)
            gf_ref[rows, :] = low
            gf_t_ref[:, rows] = low.T
            stat_ref[0:1, :] += grad_y * jnp.sum(jnp.where(live, n2, 0.0), 0, keepdims=True)
            stat_ref[1:2, :] += grad_y * jnp.sum(live.astype(F32), 0, keepdims=True)
            stat_ref[2:3, :] += jnp.sum(low.astype(F32), 0, keepdims=True)
            return carry

        lax.fori_loop(0, h2_ref.shape[0] // q_len, body, 0)

    store_shards(core_ref, mm(gf_t_ref[...], act_ref[...]), send_ref, keep_ref, by_row=False)


def dense_back_kernel(
    dims, gf_ref, dg_ref, h1_ref, wf_hbm, wi_hbm, wo_hbm, g1_ref,
    gu_ref, ga_ref, gc_ref, stat_ref, bi_ref,
    wf_ref, wi_ref, wo_ref, sems,
):
    inner = dims
    block = pl.program_id(0)
    copies = [
        fetch(source, target, sems, index)
        for index, (source, target) in enumerate([(wf_hbm, wf_ref), (wi_hbm, wi_ref), (wo_hbm, wo_ref)])
    ]

    @pl.when(block == 0)
    def _():
        for copy in copies:
            copy.start()
        stat_ref[...] = jnp.zeros_like(stat_ref)
        bi_ref[...] = jnp.zeros_like(bi_ref)
        copies[0].wait()

    gf = gf_ref[...]
    raw, made, biases = {}, {}, []

    def spread(i):
        raw[i] = mm_nt(gf, wf_ref[i * TILE : (i + 1) * TILE, :])

    def slope(i):
        cols = slice(i * TILE, (i + 1) * TILE)
        made[i] = (raw.pop(i) * dg_ref[:, cols].astype(F32)).astype(LOW)
        gu_ref[:, cols] = made[i]
        biases.append(jnp.sum(made[i].astype(F32), 0, keepdims=True))

    staged(inner // TILE, spread, slope)
    bi_ref[0:1, :] += jnp.concatenate(biases, 1)
    left = jnp.concatenate([made[i] for i in range(inner // TILE)], 1)

    @pl.when(block == 0)
    def _():
        for copy in copies[1:]:
            copy.wait()

    total = gf.astype(F32) + mm_nt(left, wi_ref[...])
    n1, r1 = norm_parts(h1_ref[...].astype(F32))
    stat_ref[0:1, :] += jnp.sum(total * n1, 0, keepdims=True)
    stat_ref[1:2, :] += jnp.sum(total, 0, keepdims=True)
    g = total * vec(g1_ref)
    grad = r1 * (g - jnp.mean(g, -1, keepdims=True) - n1 * jnp.mean(g * n1, -1, keepdims=True))
    low = grad.astype(LOW)
    ga_ref[...] = low
    stat_ref[2:3, :] += jnp.sum(low.astype(F32), 0, keepdims=True)
    gc_ref[...] = mm_nt(low, wo_ref[...]).astype(LOW)


def attend_back_kernel(
    dims, core_ref, qlen_ref, plen_ref, q_ref, k_ref, v_ref, ctx_t_ref, lse_ref, gc_ref, x_t_ref, *refs
):
    *extra, out_ref, stat_ref, send_ref, keep_ref, sum_ref = refs
    q_dev, q_len, rows_all, head_dim = dims
    block = pl.program_id(0)
    pair_dim = 2 * head_dim
    width = q_ref.shape[1]
    pairs = width // pair_dim

    @pl.when(block == 0)
    def _():
        stat_ref[...] = jnp.zeros_like(stat_ref)

    def attend(size, starts, lengths, fresh):
        lane = lax.broadcasted_iota(jnp.int32, (size, pair_dim), 1)
        items = [(s, p, which) for p in range(pairs) for s in range(len(starts)) for which in range(2)]
        held, raw, made, grads = {}, {}, {}, {}

        def pair_of(s, p):
            if (s, p) not in held:
                here, cols = slice(starts[s], starts[s] + size), slice(p * pair_dim, (p + 1) * pair_dim)
                q, k, v, gc = q_ref[here, cols], k_ref[here, cols], v_ref[here, cols], gc_ref[here, cols]
                held[s, p] = here, cols, q, k, v, gc, q.T, k.T, gc.T
            return held[s, p]

        def compare(i):
            s, p, which = items[i]
            here, cols, q, k, v, gc, q_t, k_t, gc_t = pair_of(s, p)
            raw[i] = mm(k, half_only(q_t, which)), mm(v, half_only(gc_t, which))

        def weigh(i):
            s, p, which = items[i]
            here, cols, q, k, v, gc, q_t, k_t, gc_t = pair_of(s, p)
            head = slice((p * 2 + which) * head_dim, (p * 2 + which + 1) * head_dim)
            scores, grad_p = raw.pop(i)
            lse = lse_ref[0, p, which : which + 1, here]
            edge = sure_rows(size)
            late = jnp.where(live_rows(edge, lengths[s], size - edge), scores[edge:], -1e30)
            probs = jnp.concatenate([jnp.exp(scores[:edge] - lse), jnp.exp(late - lse)], 0)
            half = slice(which * head_dim, (which + 1) * head_dim)
            delta = jnp.sum(gc_t[half].astype(F32) * ctx_t_ref[head, here].astype(F32), 0, keepdims=True)
            made[i] = probs.astype(LOW), (probs * (grad_p - delta)).astype(LOW)

        def combine(i):
            s, p, which = items[i]
            here, cols, q, k, v, gc, q_t, k_t, gc_t = pair_of(s, p)
            mine = (lane >= head_dim) if which else (lane < head_dim)
            zero = jnp.zeros_like(q)
            probs, grad_s = made.pop(i)
            add_v = mm(probs, jnp.where(mine, gc, zero))
            add_k = mm(grad_s, jnp.where(mine, q, zero))
            add_q = mm(k_t[which * head_dim : (which + 1) * head_dim], grad_s)
            if which == 0:
                made[s, p] = add_v, add_k, add_q
                return
            old_v, old_k, old_q = made.pop((s, p))
            grad_q = (jnp.concatenate([old_q, add_q], 0).T * head_dim**-0.5).astype(LOW)
            grad_k = (old_k + add_k).astype(LOW)
            grad_v = (old_v + add_v).astype(LOW)
            for number, grad in enumerate((grad_q, grad_k, grad_v)):
                out_ref[here, number * width + cols.start : number * width + cols.stop] = grad
                grads[number, s, p] = grad
            stat_ref[0:1, cols] += jnp.sum(grad_q.astype(F32), 0, keepdims=True)
            stat_ref[1:2, cols] += jnp.sum(grad_v.astype(F32), 0, keepdims=True)

            if p % 2 and s == len(starts) - 1:
                project(p - 1)

        def project(p):
            for number in range(3):
                rows = [
                    jnp.concatenate([grads.pop((number, s, p)), grads.pop((number, s, p + 1))], 1)
                    for s in range(len(starts))
                ]
                product = mm(x_t_ref[...], jnp.concatenate(rows, 0))
                cols = slice(number * width + p * pair_dim, number * width + (p + 2) * pair_dim)
                if fresh:
                    sum_ref[:, cols] = product
                else:
                    sum_ref[:, cols] += product

        staged(len(items), compare, weigh, combine)

    @pl.when(block == 0)
    def _():
        attend(q_len, [s * q_len for s in range(q_dev)], [qlen_ref[s] for s in range(q_dev)], True)

    @pl.when(block > 0)
    def _():
        attend(rows_all, [0], [plen_ref[jnp.maximum(block - 1, 0)]], False)

    @pl.when(block == pl.num_programs(0) - 1)
    def _():
        tails = None
        if extra:
            tails = small_rows([*extra, stat_ref], send_ref.shape[0] * 2, send_ref.shape[2])
        store_shards(core_ref, sum_ref[...], send_ref, keep_ref, tails=tails)


def input_grad_kernel(groups, *refs):
    grads, (base_ref, wq_ref, wk_ref, wv_ref, gq_ref, gp_ref) = refs[: len(groups)], refs[len(groups) :]
    total = base_ref[...].astype(F32)
    for grad_ref, (start, wide) in zip(grads, groups):
        for number, w_ref in enumerate((wq_ref, wk_ref, wv_ref)):
            total = total + mm_nt(grad_ref[:, number * wide : (number + 1) * wide], w_ref[:, start : start + wide])
    low = total.astype(LOW)

    @pl.when(pl.program_id(0) == 0)
    def _():
        gq_ref[...] = low

    @pl.when(pl.program_id(0) > 0)
    def _():
        gp_ref[...] = low


def weight_grad_kernel(core_ref, left_ref, right_ref, send_ref, keep_ref):
    store_shards(core_ref, mm(left_ref[...], right_ref[...]), send_ref, keep_ref)


def small_rows(refs, count, wide):
    two, one, inner, *attn = [ref[...] for ref in refs]
    eight = jnp.concatenate(
        [jnp.concatenate([item[0:2] for item in attn], 1), one[2:3], two[2:3], one[0:2], two[0:2]], 0
    )
    inner = inner[0:1]
    short, long = eight.shape[1] // count, inner.shape[1] // count
    rows = []
    for shard in range(count):
        top = eight[:, shard * short : (shard + 1) * short]
        low = inner[:, shard * long : (shard + 1) * long]
        top = jnp.concatenate([top, jnp.zeros((8, wide - short), F32)], 1)
        low = jnp.concatenate([low, jnp.zeros((1, wide - long), F32)], 1)
        rows.append(jnp.concatenate([top, low, jnp.zeros((7, wide), F32)], 0).astype(LOW))
    return rows


def turn_kernel(part_ref, out_ref):
    out_ref[...] = part_ref[...].astype(F32).T


def turn_low_kernel(*refs):
    *inputs, out_ref = refs
    if len(inputs) == 1:
        out_ref[...] = inputs[0][...].T
        return

    @pl.when(pl.program_id(0) == 0)
    def _():
        out_ref[...] = inputs[0][...].T

    @pl.when(pl.program_id(0) > 0)
    def _():
        out_ref[...] = inputs[1][...].T


def const_spec(shape):
    return pl.BlockSpec(shape, lambda i: (0,) * len(shape), pipeline_mode=pl.Buffered(1))


def call(body, operands, in_specs, outs, grid, room, deps=(), old=(), into=0, name=None, scratch=(), us=12):
    count, extra = len(operands), len(old)
    if deps:
        tied = min(range(count), key=lambda i: operands[i].size)
        operands = list(operands)
        operands[tied] = lax.optimization_barrier((operands[tied], *deps))[0]

    def kernel(*refs):
        body(*refs[:count], *refs[count + extra :])

    return pl.pallas_call(
        kernel,
        grid=grid,
        in_specs=list(in_specs) + [pl.BlockSpec(memory_space=pl.ANY)] * extra,
        out_specs=[spec for spec, _ in outs],
        out_shape=[jax.ShapeDtypeStruct(kind.shape, kind.dtype) for _, kind in outs],
        scratch_shapes=scratch,
        input_output_aliases={count + i: into + i for i in range(extra)},
        compiler_params=pltpu.CompilerParams(vmem_limit_bytes=room * 1024 * 1024),
        cost_estimate=pl.CostEstimate(flops=int(us * 1.15e9), bytes_accessed=0, transcendentals=0),
        name=name,
    )(*operands, *old)


def weight_grad(left_t, right, row_count, core, deps, old=(), at=0, us=12):
    height, depth = left_t.shape
    wide = right.shape[1]
    block = min(wide, 768)
    shape = old[0].shape if old else (row_count // 2, height // row_count, wide)
    spec = pl.BlockSpec((*shape[:2], block), lambda i: (0, 0, i + at))
    return call(
        weight_grad_kernel,
        (core, left_t, right),
        [
            pl.BlockSpec(memory_space=pltpu.SMEM),
            const_spec((height, depth)),
            pl.BlockSpec((depth, block), lambda i: (0, i)),
        ],
        [(spec, jax.ShapeDtypeStruct(shape, LOW))] * 2,
        (wide // block,),
        56,
        deps,
        old,
        name="weight_grad",
        us=us,
    )


def add_kernel(*refs):
    *terms, out_ref = refs
    out_ref[...] = sum([ref[...].astype(F32) for ref in terms[1:]], terms[0][...].astype(F32)).astype(LOW)


def add_all(terms):
    shape = terms[0].shape
    spec = pl.BlockSpec(shape, lambda i: (0,) * len(shape), pipeline_mode=pl.Buffered(1))
    outs = [(spec, jax.ShapeDtypeStruct(shape, LOW))]
    return call(add_kernel, terms, [spec] * len(terms), outs, (1,), 24, name="add_all", us=12)[0]


def masks_of(bits):
    return [
        sum(1 << bit for i, bit in enumerate(bits) if other >> i & 1) for other in range(1, 1 << len(bits))
    ]


def in_order(pieces, name, bits):
    here = lax.axis_index(name)
    for i, bit in enumerate(bits):
        high = ((here >> bit) & 1) == 1
        pieces = [jnp.where(high, pieces[place ^ (1 << i)], pieces[place]) for place in range(len(pieces))]
    return jnp.concatenate(pieces, 0)


class Flow:
    def __init__(self, sent, kept, line=False, fused=False, split=False, wide=2):
        bits = lax.axis_size("row").bit_length() - 1
        self.order = [(0,)] + [tuple(range(i, min(i + wide, bits))) for i in range(1, bits, wide)]
        self.left = list(range(bits - 1, 0, -1))
        count = lax.axis_size("col")
        self.line = [(None, [(i, i ^ (1 << bit)) for i in range(count)]) for bit in range(count.bit_length() - 1)]
        if line:
            half = count // 2
            self.line = [(None, [(i, i + 1), (count - 1 - i, count - 2 - i)]) for i in range(half - 1)]
            self.line += [(None, [(half - 1, half), (half, half - 1)])]
            self.line += [
                ((i, count - 1 - i), [(i + 1, i), (count - 2 - i, count - 1 - i)])
                for i in range(half - 2, -1, -1)
            ]
        if split:
            bits = count.bit_length() - 1
            groups = [tuple(range(i, min(i + 2, bits))) for i in range(0, bits, 2)]
            self.line = [("scatter", group) for group in groups[::-1]] + [("gather", group) for group in groups]
        self.sent, self.kept, self.got, self.fused, self.split = [sent], kept, None, fused, split

    def shard(self, terms, bits, mask, name="row"):
        here = lax.axis_index(name)
        order = [self.left.index(bit) for bit in bits]
        total = None
        for term in terms:
            starts, sizes = [0] * term.ndim, list(term.shape)
            for axis, bit in zip(order, bits):
                starts[axis], sizes[axis] = ((here ^ mask) >> bit) & 1, 1
            piece = lax.dynamic_slice(term, starts, sizes)
            piece = piece.reshape([size for i, size in enumerate(sizes) if i not in order]).astype(F32)
            total = piece if total is None else total + piece
        return total.astype(LOW)

    def step(self):
        if self.order:
            bits = self.order[0]
            masks = masks_of(bits)
            if bits != (0,):
                terms = [self.kept, *self.got]
                self.sent = [self.shard(terms, bits, mask) for mask in masks]
                self.kept = self.shard(terms, bits, 0)
                self.left = [bit for bit in self.left if bit not in bits]
            size = lax.axis_size("row")
            self.got = [
                lax.ppermute(sent, "row", [(i, i ^ mask) for i in range(size)])
                for sent, mask in zip(self.sent, masks)
            ]
        elif self.split:
            kind, bits = self.line[0]
            masks = masks_of(bits)
            size = lax.axis_size("col")
            if kind == "scatter":
                terms = [self.kept, *self.got]
                if not self.left:
                    self.left = list(range(size.bit_length() - 2, -1, -1))
                    rows, wide = self.kept.shape
                    dims = (2,) * len(self.left) + (rows // size, wide)
                    terms = [term.reshape(dims) for term in terms]
                self.sent = [self.shard(terms, bits, mask, "col") for mask in masks]
                self.kept = self.shard(terms, bits, 0, "col")
                self.left = [bit for bit in self.left if bit not in bits]
            else:
                self.sent = [self.kept] * len(masks)
            self.got = [
                lax.ppermute(sent, "col", [(i, i ^ mask) for i in range(size)])
                for sent, mask in zip(self.sent, masks)
            ]
        else:
            self.sent = [self.kept]
            self.got = [lax.ppermute(self.kept, "col", self.line[0][1])]

    def land(self, token=None):
        if token is not None:
            self.kept = lax.optimization_barrier((self.kept, token))[0]
        got = self.got
        if self.order:
            bits = self.order.pop(0)
            if bits == (0,):
                dims = (2,) * len(self.left) + self.kept.shape[1:]
                self.kept, self.got = self.kept.reshape(dims), [item.reshape(dims) for item in self.got]
            if not self.order and self.fused:
                self.kept = add_all([self.kept, *self.got])
            elif not self.order and not self.split:
                self.kept = sum([item.astype(F32) for item in self.got], self.kept.astype(F32)).astype(LOW)
        elif self.split:
            kind, bits = self.line.pop(0)
            if kind == "gather":
                self.kept = in_order([self.kept, *self.got], "col", bits)
            elif self.line[0][0] == "gather":
                self.kept = sum([item.astype(F32) for item in self.got], self.kept.astype(F32)).astype(LOW)
        else:
            ends, _ = self.line.pop(0)
            if ends is None:
                self.kept = self.kept + self.got[0]
            else:
                here = lax.axis_index("col")
                self.kept = jnp.where((here == ends[0]) | (here == ends[1]), self.got[0], self.kept)
        return got

    def turn(self, token=None):
        got = self.land(token)
        if self.done:
            return got
        self.step()
        return got + self.sent

    @property
    def done(self):
        return not self.order and not self.line


def gather_all(piece):
    row_bits = lax.axis_size("row").bit_length() - 1
    col_bits = lax.axis_size("col").bit_length() - 1
    steps = [("col", tuple(range(i, min(i + 2, col_bits)))) for i in range(0, col_bits, 2)]
    steps += [("row", tuple(range(i, min(i + 2, row_bits)))) for i in range(1, row_bits, 2)]
    for name, bits in steps + [("row", (0,))]:
        size = lax.axis_size(name)
        got = [lax.ppermute(piece, name, [(i, i ^ mask) for i in range(size)]) for mask in masks_of(bits)]
        piece = in_order([piece, *got], name, bits)
    return piece


def per_device(
    query_tokens, passage_tokens, query_lengths, passage_lengths, positives,
    w_query, w_key, w_value, w_attn_out, w_inner, w_outer,
    bias_query, bias_value, bias_attn_out, bias_inner, bias_outer,
    gain_one, shift_one, gain_two, shift_two,
):
    q_dev, q_len, width = query_tokens.shape
    p_dev, p_len, _ = passage_tokens.shape
    inner = w_inner.shape[1]
    rows_all = p_len
    assert q_dev * q_len == rows_all and q_dev + p_dev <= SLOTS
    blocks = 1 + p_dev
    total_rows = blocks * rows_all
    row_count = lax.axis_size("row")
    col_count = lax.axis_size("col")
    row_here = lax.axis_index("row")
    core = (row_here & 1).reshape(1)
    me = (row_here * col_count + lax.axis_index("col")).reshape(1)
    params = pltpu.CompilerParams(vmem_limit_bytes=VMEM)
    smem = pl.BlockSpec(memory_space=pltpu.SMEM)

    def by_block(wide):
        return pl.BlockSpec((rows_all, wide), lambda i: (i, 0))

    def by_block_t(high):
        return pl.BlockSpec((high, rows_all), lambda i: (0, i))

    def fixed(shape):
        return pl.BlockSpec(shape, lambda i: (0,) * len(shape))

    queries_spec = pl.BlockSpec((rows_all, width), lambda i: (0, 0))
    passages_spec = pl.BlockSpec((rows_all, width), lambda i: (jnp.maximum(i - 1, 0), 0))

    lse_spec = pl.BlockSpec((1, HEADS // 2, 8, rows_all), lambda i: (i, 0, 0, 0))

    def shape(*dims, kind=LOW):
        return jax.ShapeDtypeStruct(dims, kind)

    queries = query_tokens.reshape(rows_all, width)
    passages = passage_tokens.reshape(p_dev * rows_all, width)
    square = const_spec((width, width))
    anywhere = pl.BlockSpec(memory_space=pl.ANY)
    thin = const_spec((width,))

    q, k, v, ctx_t, lse = call(
        partial(attend_kernel, (q_dev, q_len, rows_all, width)),
        (query_lengths, passage_lengths, queries, passages, w_query, w_key, w_value, bias_query, bias_value),
        [smem, smem, queries_spec, passages_spec, square, square, square, thin, thin],
        [(by_block(width), shape(total_rows, width))] * 3
        + [
            (by_block_t(width), shape(width, total_rows)),
            (lse_spec, shape(blocks, HEADS // 2, 8, rows_all, kind=F32)),
        ],
        (blocks,),
        56,
        name="attend",

    )

    rows_part = rows_all
    parts = blocks

    def by_part(wide):
        return pl.BlockSpec((rows_part, wide), lambda i: (i, 0))

    queries_part = pl.BlockSpec((rows_part, width), lambda i: (0, 0))
    passages_part = pl.BlockSpec((rows_part, width), lambda i: (jnp.maximum(i - 1, 0), 0))
    h1, y1, act, slope, h2, query_out, passage_out, pooled, payload = call(
        partial(dense_kernel, (q_dev, q_len, p_len, width, inner)),
        (
            query_lengths, passage_lengths, positives, queries, passages, ctx_t, w_attn_out, w_inner, w_outer,
            bias_attn_out, bias_inner, bias_outer, gain_one, shift_one, gain_two, shift_two,
        ),
        [smem, smem, smem, queries_part, passages_part, pl.BlockSpec((width, rows_part), lambda i: (0, i))]
        + [anywhere] * 3
        + [thin, const_spec((inner,))]
        + [thin] * 5,
        [
            (by_part(width), shape(total_rows, width)),
            (by_part(width), shape(total_rows, width)),
            (by_part(inner), shape(total_rows, inner)),
            (by_part(inner), shape(total_rows, inner)),
            (by_part(width), shape(total_rows, width)),
            (queries_part, shape(rows_all, width)),
            (passages_part, shape(p_dev * rows_all, width)),
            (fixed((SLOTS, width)), shape(SLOTS, width, kind=F32)),
            (fixed((SLOTS, width + 128)), shape(SLOTS, width + 128)),
        ],
        (parts,),
        56,
        name="dense",
        scratch=[
            pltpu.VMEM((width, width), LOW),
            pltpu.VMEM((width, inner), LOW),
            pltpu.VMEM((inner, width), LOW),
            pltpu.SemaphoreType.DMA((3,)),
        ],

    )

    gathered = gather_all(payload)
    loss, gvec = pl.pallas_call(
        partial(loss_kernel, (q_dev, p_dev, width, col_count)),
        in_specs=[smem] * 3 + [pl.BlockSpec(memory_space=pltpu.VMEM)] * 3,
        out_specs=[pl.BlockSpec(memory_space=pltpu.VMEM)] * 2,
        out_shape=[shape(8, 128, kind=F32), shape(SLOTS, width, kind=F32)],
        compiler_params=params,
        name="loss",
    )(me, query_lengths, passage_lengths, payload, gathered, pooled)

    smalls = shape(8, width, kind=F32)
    cut = width // row_count
    cut_inner = inner // row_count
    half = row_count // 2
    step_cols = 768
    per_step = step_cols // cut_inner
    outer_spec = pl.BlockSpec((per_step // 2, width, cut_inner), lambda i: (i, 0, 0))
    grad_f, stat_two, *outer_parts = call(
        partial(outer_grad_kernel, (q_dev, q_len, p_len)),
        (core, query_lengths, passage_lengths, gvec, h2, gain_two, act),
        [smem, smem, smem, fixed((SLOTS, width)), const_spec((total_rows, width)), thin]
        + [pl.BlockSpec((total_rows, step_cols), lambda i: (0, i))],
        [
            (fixed((total_rows, width)), shape(total_rows, width)),
            (fixed((8, width)), smalls),
            (outer_spec, shape(half, width, cut_inner)),
            (outer_spec, shape(half, width, cut_inner)),
        ],
        (inner // step_cols,),
        56,
        name="outer_grad",
        scratch=[pltpu.VMEM((width, total_rows), LOW)],
    )
    outer = Flow(*outer_parts)
    outer.step()

    def turn(arrays, specs, deps):
        outs = [(by_block_t(width), shape(width, total_rows))]
        return call(turn_low_kernel, arrays, specs, outs, (blocks,), 56, deps, name="turn", us=40)[0]

    y1_t = turn([y1], [by_block(width)], outer.sent)
    deps = outer.turn(y1_t)
    head_dim = width // HEADS
    third = 4 * head_dim
    groups = [(0, 2 * third), (2 * third, third)]
    grad_u, grad_attn, grad_ctx, stat_one, grad_bias_inner = call(
        partial(dense_back_kernel, inner),
        (grad_f, slope, h1, w_outer, w_inner, w_attn_out, gain_one),
        [by_block(width), by_block(inner), by_block(width), anywhere, anywhere, anywhere, thin],
        [
            (by_block(inner), shape(total_rows, inner)),
            (by_block(width), shape(total_rows, width)),
            (by_block(width), shape(total_rows, width)),
            (fixed((8, width)), smalls),
            (fixed((8, inner)), shape(8, inner, kind=F32)),
        ],
        (blocks,),
        60,
        deps,
        name="dense_back",
        scratch=[
            pltpu.VMEM((inner, width), LOW),
            pltpu.VMEM((width, inner), LOW),
            pltpu.VMEM((width, width), LOW),
            pltpu.SemaphoreType.DMA((3,)),
        ],
    )
    deps = outer.turn(stat_one)
    up_flow = Flow(*weight_grad(y1_t, grad_u, row_count, core, deps), fused=True)
    up_flow.step()
    deps = up_flow.sent + outer.turn(up_flow.sent[0])
    x_t = turn([queries, passages], [queries_spec, passages_spec], deps)
    deps = up_flow.turn(x_t)

    def attend_back(start, wide, deps, extra=(), room=None):
        pairs = wide // (2 * head_dim)
        index = start // wide
        cols = pl.BlockSpec((rows_all, wide), lambda i: (i, index))
        rows = cut + (16 if extra else 0)
        return call(
            partial(attend_back_kernel, (q_dev, q_len, rows_all, head_dim)),
            (core, query_lengths, passage_lengths, q, k, v, ctx_t, lse, grad_ctx, x_t, *extra),
            [smem, smem, smem]
            + [cols] * 3
            + [
                pl.BlockSpec((wide, rows_all), lambda i: (index, i)),
                pl.BlockSpec((1, pairs, 8, rows_all), lambda i: (i, index, 0, 0)),
                cols,
                by_block_t(width),
            ]
            + [const_spec(item.shape) for item in extra],
            [
                (by_block(3 * wide), shape(total_rows, 3 * wide)),
                (fixed((8, wide)), shape(8, wide, kind=F32)),
            ]
            + [(fixed((half, rows, 3 * wide)), shape(half, rows, room or 3 * wide))] * 2,
            (blocks,),
            56,
            deps,
            name="attend_back",
            scratch=[pltpu.VMEM((width, 3 * wide), F32)],
            us=12 if room else 40,
        )

    grad_a, stat_a, *mixed_parts = attend_back(*groups[0], deps, room=6 * third + width)
    at = 6 * third // width
    mixed_parts = weight_grad(ctx_t, grad_attn, row_count, core, [stat_a], mixed_parts, at, us=0)
    mixed_flow = Flow(*mixed_parts, split=True)
    mixed_flow.step()
    token = mixed_flow.sent[0]
    deps = mixed_flow.sent + outer.turn(token) + up_flow.turn(token)
    extra = (stat_two, stat_one, grad_bias_inner, stat_a)
    grad_b, stat_b, *last_parts = attend_back(*groups[1], deps, extra)
    last_flow = Flow(*last_parts, wide=1)
    last_flow.step()
    deps = last_flow.sent + mixed_flow.turn(stat_b) + up_flow.turn(stat_b)
    query_grad, passage_grad = call(
        partial(input_grad_kernel, groups),
        (grad_a, grad_b, grad_attn, w_query, w_key, w_value),
        [by_block(3 * wide) for _, wide in groups] + [by_block(width), square, square, square],
        [
            (queries_spec, shape(rows_all, width)),
            (passages_spec, shape(p_dev * rows_all, width)),
        ],
        (blocks,),
        56,
        deps,
        name="input_grad",
        us=40,
    )
    last_flow.turn(passage_grad)
    mixed_flow.turn(last_flow.kept)
    outs = [(fixed((cut_inner, width)), shape(cut_inner, width, kind=F32))]
    (turned,) = call(
        turn_kernel, (outer.kept,), [const_spec((width, cut_inner))], outs, (1,), 56, [mixed_flow.kept], name="turn", us=40
    )
    last_flow.turn(turned)
    up_flow.turn(last_flow.kept)
    last_flow.turn(up_flow.kept)
    last_flow.turn()
    mixed_flow.turn(last_flow.kept)
    mixed_flow.turn()
    flows = [outer, up_flow, mixed_flow, last_flow]
    while not all(flow.done for flow in flows):
        for flow in flows:
            if not flow.done:
                flow.turn()
    mixed, last = mixed_flow.kept, last_flow.kept
    qkv = [
        jnp.concatenate(
            [mixed[:, i * 2 * third : (i + 1) * 2 * third], last[:cut, i * third : (i + 1) * third]], 1
        ).astype(F32)
        for i in range(3)
    ]
    small = last[cut:].astype(F32)
    return (
        loss[0, 0],
        query_out.reshape(query_tokens.shape),
        passage_out.reshape(passage_tokens.shape),
        query_grad.reshape(query_tokens.shape),
        passage_grad.reshape(passage_tokens.shape),
        *qkv,
        mixed[:, 6 * third :].astype(F32),
        up_flow.kept.astype(F32),
        turned,
        *[small[i, :cut] for i in range(3)],
        small[8, : inner // row_count],
        *[small[i, :cut] for i in range(3, 8)],
    )


def solution(mesh):
    in_specs = (
        P(("row", "col"), None, None),
        P(("row", "col"), None, None),
        P(("row", "col")),
        P(("row", "col")),
        P(("row", "col")),
        P(),
        P(),
        P(),
        P(),
        P(),
        P(),
        P(),
        P(),
        P(),
        P(),
        P(),
        P(),
        P(),
        P(),
        P(),
    )
    out_specs = (
        P(),
        P(("row", "col"), None, None),
        P(("row", "col"), None, None),
        P(("row", "col"), None, None),
        P(("row", "col"), None, None),
        P("row", None),
        P("row", None),
        P("row", None),
        P("row", None),
        P("row", None),
        P("row", None),
        P("row"),
        P("row"),
        P("row"),
        P("row"),
        P("row"),
        P("row"),
        P("row"),
        P("row"),
        P("row"),
    )
    return jax.shard_map(
        per_device, mesh=mesh, in_specs=in_specs, out_specs=out_specs, check_vma=False
    )
```
